32 devices in a mesh: rows: 8 (over z, y), cols: 4 (over x, core).
Axes of the slice: x: 2, y: 2, z: 4, core: 2. Of those that a mesh axis runs over, the one named last changes fastest.
Arguments:
- image_pair: bfloat16 [1, 256, 256, 6], P(None, 'rows', 'cols'), may hold values from -6 to 6
- noise_target: float32 [1, 256, 256, 3], P(None, 'rows', 'cols'), may hold values from -6 to 6
- timesteps: int32 [1, 5, 5], replicated, may hold values from 0 to 999
- text_pooled: bfloat16 [1, 5, 5, 4096], replicated, may hold values from -6 to 6
- slot_live: int32 [1, 5, 5], replicated, may hold values 0 or 1
- edgeconv_weight: float32 [9, 128, 9], replicated
- edgeconv_first: float32 [9, 128, 9], replicated, may hold values from -7.6293945e-05 to 7.6293945e-05
- edgeconv_second: float32 [9, 128, 9], replicated, may hold values from 4.4475685e-12 to 1.9766971e-10
- convlow_weight: float32 [4, 9, 128, 128], P(None, None, 'rows', 'cols')
- convlow_first: float32 [4, 9, 128, 128], P(None, None, 'rows', 'cols'), may hold values from -1.5258789e-05 to 1.5258789e-05
- convlow_second: float32 [4, 9, 128, 128], P(None, None, 'rows', 'cols'), may hold values from 4.9417425e-13 to 1.976697e-12
- convhigh_weight: float32 [2, 9, 256, 256], P(None, None, 'rows', 'cols')
- convhigh_first: float32 [2, 9, 256, 256], P(None, None, 'rows', 'cols'), may hold values from -1.5258789e-05 to 1.5258789e-05
- convhigh_second: float32 [2, 9, 256, 256], P(None, None, 'rows', 'cols'), may hold values from 4.9417425e-13 to 1.976697e-12
- downconv_weight: float32 [9, 128, 256], P(None, 'rows', 'cols')
- downconv_first: float32 [9, 128, 256], P(None, 'rows', 'cols'), may hold values from -1.5258789e-05 to 1.5258789e-05
- downconv_second: float32 [9, 128, 256], P(None, 'rows', 'cols'), may hold values from 4.9417425e-13 to 1.976697e-12
- upconv_weight: float32 [9, 256, 128], P(None, 'rows', 'cols')
- upconv_first: float32 [9, 256, 128], P(None, 'rows', 'cols'), may hold values from -1.5258789e-05 to 1.5258789e-05
- upconv_second: float32 [9, 256, 128], P(None, 'rows', 'cols'), may hold values from 4.9417425e-13 to 1.976697e-12
- condproj_weight: float32 [4224, 512], P(None, ('rows', 'cols'))
- condproj_first: float32 [4224, 512], P(None, ('rows', 'cols')), may hold values from -1.5258789e-05 to 1.5258789e-05
- condproj_second: float32 [4224, 512], P(None, ('rows', 'cols')), may hold values from 4.9417425e-13 to 1.976697e-12
- filmproj_weight: float32 [512, 1024], P('rows', 'cols')
- filmproj_first: float32 [512, 1024], P('rows', 'cols'), may hold values from -1.5258789e-05 to 1.5258789e-05
- filmproj_second: float32 [512, 1024], P('rows', 'cols'), may hold values from 4.9417425e-13 to 1.976697e-12
- normparams_weight: float32 [2, 1152], replicated, may hold values from -0.5 to 1.3, as said below
- normparams_first: float32 [2, 1152], replicated, may hold values from -7.6293945e-05 to 7.6293945e-05
- normparams_second: float32 [2, 1152], replicated, may hold values from 1.2354357e-11 to 4.941743e-11
Outputs:
- edgeconv_grad: float32 [9, 128, 9], replicated
- edgeconv_moment: float32 [9, 128, 9], replicated
- edgeconv_new: float32 [9, 128, 9], replicated
- convlow_grad: float32 [4, 9, 128, 128], P(None, None, 'rows', 'cols')
- convlow_moment: float32 [4, 9, 128, 128], P(None, None, 'rows', 'cols')
- convlow_new: float32 [4, 9, 128, 128], P(None, None, 'rows', 'cols')
- convhigh_grad: float32 [2, 9, 256, 256], P(None, None, 'rows', 'cols')
- convhigh_moment: float32 [2, 9, 256, 256], P(None, None, 'rows', 'cols')
- convhigh_new: float32 [2, 9, 256, 256], P(None, None, 'rows', 'cols')
- downconv_grad: float32 [9, 128, 256], P(None, 'rows', 'cols')
- downconv_moment: float32 [9, 128, 256], P(None, 'rows', 'cols')
- downconv_new: float32 [9, 128, 256], P(None, 'rows', 'cols')
- upconv_grad: float32 [9, 256, 128], P(None, 'rows', 'cols')
- upconv_moment: float32 [9, 256, 128], P(None, 'rows', 'cols')
- upconv_new: float32 [9, 256, 128], P(None, 'rows', 'cols')
- condproj_grad: float32 [4224, 512], P(None, ('rows', 'cols'))
- condproj_moment: float32 [4224, 512], P(None, ('rows', 'cols'))
- condproj_new: float32 [4224, 512], P(None, ('rows', 'cols'))
- filmproj_grad: float32 [512, 1024], P('rows', 'cols')
- filmproj_moment: float32 [512, 1024], P('rows', 'cols')
- filmproj_new: float32 [512, 1024], P('rows', 'cols')
- normparams_grad: float32 [2, 1152], replicated
- normparams_moment: float32 [2, 1152], replicated
- normparams_new: float32 [2, 1152], replicated
- loss_sum: float32 [], replicated
- loss_count: float32 [], replicated
- clip_norm: float32 [], replicated
- image_grad: float32 [1, 256, 256, 6], P(None, 'rows', 'cols')
The draws below stay inside these ranges and needn't reach their ends.
Inputs may be any that keep to these rules, and one draw needn't show every extreme that they name: `normparams_weight`: row 0 holds the norms' gains, row 1 their biases.
All inputs are finite; a program needn't handle non-finite values.
Results may differ from the reference program's by a relative error of at most 0.018.
Values may be sent and summed in bfloat16 or wider, within the bound.
A program may use at most 256 MiB of HBM per device.

```python
import math
import jax
import jax.numpy as jnp
from jax import lax

IMG = 256
SLOT = 64
SLOTS = 5
CANVAS = 1
C1 = 128
C2 = 256
GROUPS = 32
TEXT = 4096
TEMB = 128
COND = 512
FILM = 1024
NORMS = 1152
PARAMS = 5058944
STEP = 10


def rising(key, shape, axis, fan_in, top):
    values = jax.random.truncated_normal(key, -6.0, 6.0, shape, jnp.float32)
    length = shape[axis]
    slope = top - 1.0
    norm = (1.0 + slope + slope * slope * (2 * length - 1) / (6.0 * (length - 1))) ** 0.5
    gain = (1.0 + slope * jnp.arange(length, dtype=jnp.float32) / (length - 1)) / norm
    view = [1] * len(shape)
    view[axis] = length
    return values * gain.reshape(tuple(view)) / fan_in ** 0.5


def draw_convlow_weight(key, part):
    key = jax.random.fold_in(key, 31)
    top = 8.0
    return rising(key, (4, 9, C1, C1), 2, 9 * C1, top)


def draw_convhigh_weight(key, part):
    key = jax.random.fold_in(key, 37)
    top = 8.0
    return rising(key, (2, 9, C2, C2), 2, 9 * C2, top)


def draw_downconv_weight(key, part):
    key = jax.random.fold_in(key, 41)
    top = 8.0
    return rising(key, (9, C1, C2), 1, 9 * C1, top)


def draw_upconv_weight(key, part):
    key = jax.random.fold_in(key, 43)
    top = 8.0
    return rising(key, (9, C2, C1), 1, 9 * C2, top)


def draw_condproj_weight(key, part):
    key = jax.random.fold_in(key, 47)
    top = 8.0
    return rising(key, (TEMB + TEXT, COND), 1, TEMB + TEXT, top)


def draw_filmproj_weight(key, part):
    key = jax.random.fold_in(key, 53)
    top = 8.0
    return rising(key, (COND, FILM), 0, COND, top)


def draw_edgeconv_weight(key, part):
    key = jax.random.fold_in(key, 59)
    values = jax.random.truncated_normal(key, -6.0, 6.0, (9, C1, 9), jnp.float32)
    column = jnp.arange(9)
    scale = jnp.where(column < 6, 54.0 ** (-0.5), (9.0 * C1) ** (-0.5))
    return values * scale[None, None, :]


def draw_edgeconv_second(key, part):
    key = jax.random.fold_in(key, 61)
    values = jnp.exp(jax.random.uniform(key, (9, C1, 9), jnp.float32, 0.0, 1.3862944))
    column = jnp.arange(9)
    scale = jnp.where(column < 6, 9.0, 100.0) * 0.001 * 0.0025 / PARAMS
    return values * scale[None, None, :]


def draw_normparams_weight(key, part):
    gain_key = jax.random.fold_in(key, 11)
    bias_key = jax.random.fold_in(key, 23)
    gains = jax.random.uniform(gain_key, (NORMS,), jnp.float32, 0.7, 1.3)
    biases = jax.random.uniform(bias_key, (NORMS,), jnp.float32, -0.5, 0.5)
    return jnp.stack([gains, biases])


def place_ends(result, rng, low, top_value):
    spot = [jax.random.randint(jax.random.fold_in(rng, axis), (), 0, length) for axis, length in enumerate(result.shape)]
    widest = result.shape.index(max(result.shape))
    beside = spot[:widest] + [(spot[widest] + 1) % result.shape[widest]] + spot[widest + 1:]
    return result.at[tuple(spot)].set(low).at[tuple(beside)].set(top_value)


def steps_of(rng, shape, cuts, low, high):
    def one(axis_at, shards_of):
        steps = jax.random.uniform(jax.random.fold_in(jax.random.fold_in(rng, 6), axis_at), (shards_of,), jnp.float32, low / len(cuts), high / len(cuts))
        return jnp.repeat(jnp.exp(steps), shape[axis_at] // shards_of).reshape((-1,) + (1,) * (len(shape) - axis_at - 1))

    loudness = one(*cuts[0])
    for cut in cuts[1:]:
        loudness = loudness * one(*cut)
    return loudness


def bell_draw(stream_key, shape, deviation, bound, split=(), kind=jnp.bfloat16):
    values = deviation * jax.random.normal(stream_key, shape, jnp.float32)
    if split:
        values = values * steps_of(stream_key, shape, split, -0.22, 0.18)
    return jnp.clip(values, -bound, bound).astype(kind)


def setup_inputs(seed: int = 0) -> dict:
    arg_keys = jax.random.split(jax.random.key(seed), 30)
    return {
        "image_pair": bell_draw(arg_keys[0], (CANVAS, IMG, IMG, 6), 1.0, 6.0, ((1, 8), (2, 4))),
        "noise_target": bell_draw(arg_keys[1], (CANVAS, IMG, IMG, 3), 1.0, 6.0, ((1, 8), (2, 4)), jnp.float32),
        "timesteps": place_ends(jax.random.randint(arg_keys[2], (CANVAS, SLOTS, SLOTS), 0, 1000), jax.random.fold_in(arg_keys[2], 1), 0, 999).astype(jnp.int32),
        "text_pooled": bell_draw(arg_keys[3], (CANVAS, SLOTS, SLOTS, TEXT), 1.0, 6.0),
        "slot_live": place_ends((jax.random.randint(arg_keys[4], (CANVAS, SLOTS, SLOTS), 0, 8) < 7).astype(jnp.int32), jax.random.fold_in(arg_keys[4], 1), 0, 1),
        "edgeconv_weight": draw_edgeconv_weight(jax.random.fold_in(arg_keys[29], 71), 0),
        "edgeconv_first": bell_draw(arg_keys[6], (9, C1, 9), (0.111 * 5 * 0.05 / PARAMS ** 0.5), 7.62939453125e-05, (), jnp.float32),
        "edgeconv_second": draw_edgeconv_second(jax.random.fold_in(arg_keys[29], 71), 0),
        "convlow_weight": draw_convlow_weight(jax.random.fold_in(arg_keys[29], 71), 0),
        "convlow_first": bell_draw(arg_keys[9], (4, 9, C1, C1), (0.111 * 0.05 / PARAMS ** 0.5), 1.52587890625e-05, ((2, 8), (3, 4)), jnp.float32),
        "convlow_second": jnp.clip(jnp.exp(math.log(1.976697017874729e-12) - 1.3862944 * jax.random.uniform(arg_keys[10], (4, 9, C1, C1), jnp.float32) ** steps_of(arg_keys[10], (4, 9, C1, C1), ((2, 8), (3, 4)), -0.2, 0.2)), 4.941742544686822e-13, 1.976697017874729e-12),
        "convhigh_weight": draw_convhigh_weight(jax.random.fold_in(arg_keys[29], 71), 0),
        "convhigh_first": bell_draw(arg_keys[12], (2, 9, C2, C2), (0.111 * 0.05 / PARAMS ** 0.5), 1.52587890625e-05, ((2, 8), (3, 4)), jnp.float32),
        "convhigh_second": jnp.clip(jnp.exp(math.log(1.976697017874729e-12) - 1.3862944 * jax.random.uniform(arg_keys[13], (2, 9, C2, C2), jnp.float32) ** steps_of(arg_keys[13], (2, 9, C2, C2), ((2, 8), (3, 4)), -0.2, 0.2)), 4.941742544686822e-13, 1.976697017874729e-12),
        "downconv_weight": draw_downconv_weight(jax.random.fold_in(arg_keys[29], 71), 0),
        "downconv_first": bell_draw(arg_keys[15], (9, C1, C2), (0.111 * 0.05 / PARAMS ** 0.5), 1.52587890625e-05, ((1, 8), (2, 4)), jnp.float32),
        "downconv_second": jnp.clip(jnp.exp(math.log(1.976697017874729e-12) - 1.3862944 * jax.random.uniform(arg_keys[16], (9, C1, C2), jnp.float32) ** steps_of(arg_keys[16], (9, C1, C2), ((1, 8), (2, 4)), -0.2, 0.2)), 4.941742544686822e-13, 1.976697017874729e-12),
        "upconv_weight": draw_upconv_weight(jax.random.fold_in(arg_keys[29], 71), 0),
        "upconv_first": bell_draw(arg_keys[18], (9, C2, C1), (0.111 * 0.05 / PARAMS ** 0.5), 1.52587890625e-05, ((1, 8), (2, 4)), jnp.float32),
        "upconv_second": jnp.clip(jnp.exp(math.log(1.976697017874729e-12) - 1.3862944 * jax.random.uniform(arg_keys[19], (9, C2, C1), jnp.float32) ** steps_of(arg_keys[19], (9, C2, C1), ((1, 8), (2, 4)), -0.2, 0.2)), 4.941742544686822e-13, 1.976697017874729e-12),
        "condproj_weight": draw_condproj_weight(jax.random.fold_in(arg_keys[29], 71), 0),
        "condproj_first": bell_draw(arg_keys[21], (TEMB + TEXT, COND), (0.111 * 0.05 / PARAMS ** 0.5), 1.52587890625e-05, ((1, 32),), jnp.float32),
        "condproj_second": jnp.clip(jnp.exp(math.log(1.976697017874729e-12) - 1.3862944 * jax.random.uniform(arg_keys[22], (TEMB + TEXT, COND), jnp.float32) ** steps_of(arg_keys[22], (TEMB + TEXT, COND), ((1, 32),), -0.2, 0.2)), 4.941742544686822e-13, 1.976697017874729e-12),
        "filmproj_weight": draw_filmproj_weight(jax.random.fold_in(arg_keys[29], 71), 0),
        "filmproj_first": bell_draw(arg_keys[24], (COND, FILM), (0.111 * 0.05 / PARAMS ** 0.5), 1.52587890625e-05, ((0, 8), (1, 4)), jnp.float32),
        "filmproj_second": jnp.clip(jnp.exp(math.log(1.976697017874729e-12) - 1.3862944 * jax.random.uniform(arg_keys[25], (COND, FILM), jnp.float32) ** steps_of(arg_keys[25], (COND, FILM), ((0, 8), (1, 4)), -0.2, 0.2)), 4.941742544686822e-13, 1.976697017874729e-12),
        "normparams_weight": draw_normparams_weight(jax.random.fold_in(arg_keys[29], 71), 0),
        "normparams_first": bell_draw(arg_keys[27], (2, NORMS), (0.111 * 5 * 0.05 / PARAMS ** 0.5), 7.62939453125e-05, (), jnp.float32),
        "normparams_second": jnp.clip(jnp.exp(jax.random.uniform(arg_keys[28], (2, NORMS), jnp.float32, math.log(1.2354357120658577e-11), math.log(4.941742848263431e-11))), 1.2354357120658577e-11, 4.941742848263431e-11),
    }


HIGH = lax.Precision.HIGHEST
EPS_NORM = 1e-05
CLIP_AT = 0.05
RATE = 0.5
BETA_ONE = 0.9
BETA_TWO = 0.999
EPS_ADAM = 1e-06
DECAY = 0.01

@jax.custom_vjp
def low(v):
    return lax.optimization_barrier(v.astype(jnp.bfloat16)).astype(jnp.float32)

@jax.custom_vjp
def low_back(v):
    return v

def low_keep(v):
    return (low(v), None)

def low_pass(kept, grad):
    return (grad,)

def back_keep(v):
    return (v, None)

def back_low(kept, grad):
    return (low(grad),)
low.defvjp(low_keep, low_pass)
low_back.defvjp(back_keep, back_low)

def time_embed(steps):
    half = TEMB // 2
    freq = jnp.exp(-math.log(10000.0) * jnp.arange(half, dtype=jnp.float32) / half)
    angle = steps.astype(jnp.float32)[..., None] * freq
    return jnp.concatenate([jnp.sin(angle), jnp.cos(angle)], axis=-1)

def tap_masks(size, slot):
    places = jnp.arange(size)
    half = slot // 2
    return [((places + offset + half) // slot == (places + half) // slot).astype(jnp.float32) for offset in (-1, 0, 1)]

def conv_plain(inputs, weight, slot, stride):
    size = inputs.shape[0]
    masks = tap_masks(size, slot)
    padded = jnp.pad(inputs, ((1, 1), (1, 1), (0, 0)))
    total = jnp.zeros((size // stride, size // stride, weight.shape[2]), jnp.float32)
    for tap in range(9):
        row_off, col_off = (tap // 3, tap % 3)
        patch = padded[row_off:row_off + size:stride, col_off:col_off + size:stride, :]
        window = masks[row_off][::stride][:, None] * masks[col_off][::stride][None, :]
        total = total + jnp.einsum('hwc,cd->hwd', patch * window[:, :, None], weight[tap], precision=HIGH)
    return total
conv = jax.checkpoint(conv_plain, static_argnums=(2, 3))

def group_norm(values, gain, bias, slot, scale, shift):
    size, _, width = values.shape
    half = slot // 2
    count = size // slot + 1
    padded = jnp.pad(values, ((half, half), (half, half), (0, 0)))
    grouped = padded.reshape(count, slot, count, slot, GROUPS, width // GROUPS)
    labels = jnp.arange(count)
    side = jnp.where((labels == 0) | (labels == count - 1), half, slot).astype(jnp.float32)
    area = (side[:, None] * side[None, :] * (width // GROUPS))[:, None, :, None, None, None]
    mean = lax.optimization_barrier(jnp.sum(grouped, axis=(1, 3, 5), keepdims=True)) / area
    var = lax.optimization_barrier(jnp.sum(grouped * grouped, axis=(1, 3, 5), keepdims=True)) / area - mean * mean
    hat = ((grouped - mean) * lax.rsqrt(var + EPS_NORM)).reshape(count, slot, count, slot, width)
    normed = hat * gain + bias
    out = normed * (1.0 + scale[:, None, :, None, :]) + shift[:, None, :, None, :]
    return out.reshape(count * slot, count * slot, width)[half:half + size, half:half + size]

def block(hidden, weights, gains, film, slot):
    zeros = jnp.zeros((SLOTS, SLOTS, hidden.shape[2]), jnp.float32)
    act_one = low(jax.nn.silu(group_norm(hidden, gains[0], gains[1], slot, zeros, zeros)))
    conv_one = low_back(conv(act_one, low(weights[0]), slot, 1))
    act_two = low(jax.nn.silu(group_norm(conv_one, gains[2], gains[3], slot, film[0], film[1])))
    return hidden + low_back(conv(act_two, low(weights[1]), slot, 1))

def forward(params, image, target, live, steps, text):
    edgeconv, convlow, convhigh, downconv, upconv, condproj, filmproj, norms = params
    inconv = jnp.swapaxes(edgeconv[:, :, 0:6], 1, 2)
    headconv = edgeconv[:, :, 6:9]
    joined = jnp.concatenate([low(time_embed(steps)), text], axis=-1)
    pre = jnp.einsum('abk,kf->abf', joined, low(condproj), precision=HIGH)
    film = jnp.einsum('abk,kf->abf', low(jax.nn.silu(pre)), low(filmproj), precision=HIGH)
    offsets = [0, C1, 2 * C1, 3 * C1, 4 * C1, 4 * C1 + C2, 4 * C1 + 2 * C2, 5 * C1 + 2 * C2]
    gains = [(norms[0, offsets[k]:offsets[k + 1]], norms[1, offsets[k]:offsets[k + 1]]) for k in range(7)]
    hidden = low_back(conv(image, low(inconv), SLOT, 1))
    for index in range(2):
        base = 2 * C1 * index
        hidden = block(hidden, (convlow[2 * index], convlow[2 * index + 1]), gains[2 * index] + gains[2 * index + 1], (film[:, :, base:base + C1], film[:, :, base + C1:base + 2 * C1]), SLOT)
    skip = hidden
    deep = low_back(conv(low(skip), low(downconv), SLOT, 2))
    base = 4 * C1
    deep = block(deep, (convhigh[0], convhigh[1]), gains[4] + gains[5], (film[:, :, base:base + C2], film[:, :, base + C2:base + 2 * C2]), SLOT // 2)
    upsampled = jnp.repeat(jnp.repeat(low(deep), 2, axis=0), 2, axis=1)
    merged = low_back(conv(upsampled, low(upconv), SLOT, 1)) + skip
    zeros = jnp.zeros((SLOTS, SLOTS, C1), jnp.float32)
    act = low(jax.nn.silu(group_norm(merged, gains[6][0], gains[6][1], SLOT, zeros, zeros)))
    pred = low_back(conv(act, low(headconv), SLOT, 1))
    diff = pred - target
    return jnp.sum(live[:, :, None] * diff * diff)

def lamb(weight, first, second, grad, mode):
    first_new = BETA_ONE * first + (1.0 - BETA_ONE) * grad
    second_new = BETA_TWO * second + (1.0 - BETA_TWO) * grad * grad
    first_hat = first_new / (1.0 - BETA_ONE ** STEP)
    second_hat = second_new / (1.0 - BETA_TWO ** STEP)
    update = first_hat / (jnp.sqrt(second_hat) + EPS_ADAM) + DECAY * weight
    if mode == 2:
        part = (jnp.arange(9) < 6)[None, None, :]

        def ratio_of(sel):
            return jnp.sqrt(jnp.sum(jnp.where(sel, weight * weight, 0.0))) / jnp.sqrt(jnp.sum(jnp.where(sel, update * update, 0.0)))
        ratio = jnp.where(part, ratio_of(part), ratio_of(jnp.logical_not(part)))
    else:
        axes = tuple(range(1, weight.ndim)) if mode == 1 else tuple(range(weight.ndim))
        ratio = jnp.sqrt(lax.optimization_barrier(jnp.sum(weight * weight, axis=axes, keepdims=True))) / jnp.sqrt(lax.optimization_barrier(jnp.sum(update * update, axis=axes, keepdims=True)))
    return (second_new, weight - RATE * ratio * update)

def reference(image_pair, noise_target, timesteps, text_pooled, slot_live, edgeconv_weight, edgeconv_first, edgeconv_second, convlow_weight, convlow_first, convlow_second, convhigh_weight, convhigh_first, convhigh_second, downconv_weight, downconv_first, downconv_second, upconv_weight, upconv_first, upconv_second, condproj_weight, condproj_first, condproj_second, filmproj_weight, filmproj_first, filmproj_second, normparams_weight, normparams_first, normparams_second):
    weights = (edgeconv_weight, convlow_weight, convhigh_weight, downconv_weight, upconv_weight, condproj_weight, filmproj_weight, normparams_weight)
    firsts = (edgeconv_first, convlow_first, convhigh_first, downconv_first, upconv_first, condproj_first, filmproj_first, normparams_first)
    seconds = (edgeconv_second, convlow_second, convhigh_second, downconv_second, upconv_second, condproj_second, filmproj_second, normparams_second)
    half = SLOT // 2
    live_slots = slot_live.astype(jnp.float32)
    live = jnp.repeat(jnp.repeat(live_slots, SLOT, axis=1), SLOT, axis=2)[:, half:half + IMG, half:half + IMG]
    count = 3.0 * jnp.sum(live)
    images = image_pair.astype(jnp.float32)
    texts = text_pooled.astype(jnp.float32)

    def per_canvas(carry, item):
        grads, total = carry
        image, target, mask, steps, text = item
        loss, pull = jax.vjp(lambda params, picture: forward(params, picture, target, mask, steps, text), weights, image)
        back, picture_back = pull(1.0 / count)
        return ((jax.tree.map(jnp.add, grads, back), total + loss), picture_back * count)
    zero = jax.tree.map(jnp.zeros_like, weights)
    (grads, loss_sum), image_grad = lax.scan(per_canvas, (zero, jnp.zeros((), jnp.float32)), (images, noise_target, live, timesteps, texts))
    clip_norm = jnp.sqrt(sum((jnp.sum(grad * grad) for grad in grads)))
    factor = jnp.minimum(1.0, CLIP_AT / clip_norm)
    results = []
    for index in range(8):
        grad = grads[index] * factor
        mode = 2 if index == 0 else 1 if index in (1, 2) else 0
        moment, updated = lamb(weights[index], firsts[index], seconds[index], grad, mode)
        results.extend([grad, moment, updated])
    return (results[0], results[1], results[2], results[3], results[4], results[5], results[6], results[7], results[8], results[9], results[10], results[11], results[12], results[13], results[14], results[15], results[16], results[17], results[18], results[19], results[20], results[21], results[22], results[23], loss_sum, count, clip_norm, image_grad)
```

```python
import math

import jax
import jax.numpy as jnp
import numpy as np
from jax import lax
from jax.experimental import pallas as pl
from jax.experimental.pallas import tpu as pltpu
from jax.sharding import PartitionSpec as P

SLOT = 64
SLOTS = 5
C1 = 128
C2 = 256
GROUPS = 32
TEMB = 128
STEP = 10


HIGH = lax.Precision.HIGHEST
EPS_NORM = 1e-05
CLIP_AT = 0.05
RATE = 0.5
BETA_ONE = 0.9
BETA_TWO = 0.999
EPS_ADAM = 1e-06
DECAY = 0.01


def entering(part, axis, combine, identity, reverse):
    count = lax.axis_size(axis)
    place = lax.axis_index(axis)
    ahead = count - 1 - place if reverse else place
    gathered = jax.tree.map(lambda a: lax.all_gather(a, axis), part)
    state = jax.tree.map(lambda a, e: jnp.zeros_like(a) + jnp.asarray(e, a.dtype), part, identity)

    def one(turn, state):
        source = count - 1 - turn if reverse else turn
        return combine(
            state, jax.tree.map(lambda a: lax.dynamic_index_in_dim(a, source, 0, False), gathered)
        )

    return lax.fori_loop(0, ahead, one, state)


def padded_2(block, sides, width):
    for axis, dim in sides:
        count = lax.axis_size(axis)
        forward = [(i, i + 1) for i in range(count - 1)]
        backward = [(target, source) for source, target in forward]
        low = lax.ppermute(
            lax.slice_in_dim(block, block.shape[dim] - width, None, axis=dim), axis, forward
        )
        high = lax.ppermute(lax.slice_in_dim(block, 0, width, axis=dim), axis, backward)
        block = jnp.concatenate([low, block, high], axis=dim)
    return block


def time_embed(steps):
    half = TEMB // 2
    freq = jnp.exp(-math.log(10000.0) * jnp.arange(half, dtype=jnp.float32) / half)
    angle = steps.astype(jnp.float32)[..., None] * freq
    return jnp.concatenate([jnp.sin(angle), jnp.cos(angle)], axis=-1)


def silu_grad(values):
    sigma = jax.nn.sigmoid(values)
    return sigma * (1.0 + values * (1.0 - sigma))


def tap_masks(rows, cols, slot):
    half = slot // 2
    row_pos = lax.axis_index("rows") * rows + jnp.arange(rows)
    col_pos = lax.axis_index("cols") * cols + jnp.arange(cols)
    row_ok = [
        (row_pos + offset + half) // slot == (row_pos + half) // slot for offset in (-1, 0, 1)
    ]
    col_ok = [
        (col_pos + offset + half) // slot == (col_pos + half) // slot for offset in (-1, 0, 1)
    ]
    return [
        (row_ok[tap // 3][:, None] & col_ok[tap % 3][None, :]).astype(jnp.bfloat16)
        for tap in range(9)
    ]


def slot_level(rows, cols, slot, size):
    half = slot // 2
    labels = jnp.arange(SLOTS)
    row_pos = lax.axis_index("rows") * rows + jnp.arange(rows)
    col_pos = lax.axis_index("cols") * cols + jnp.arange(cols)
    row_map = (((row_pos + half) // slot)[:, None] == labels[None, :]).astype(jnp.float32)
    col_map = (((col_pos + half) // slot)[:, None] == labels[None, :]).astype(jnp.float32)
    every = (jnp.arange(size) + half) // slot
    side = jnp.sum((every[:, None] == labels[None, :]).astype(jnp.float32), axis=0)
    return (row_map, col_map, side[:, None] * side[None, :])


def to_slots(values, level):
    return jnp.einsum("nhwk,ha,wb->nabk", values, level[0], level[1], precision=HIGH)


def to_pixels(table, level):
    return jnp.einsum("nabk,ha,wb->nhwk", table, level[0], level[1], precision=HIGH)


def add_pair(earlier, later):
    return (earlier[0] + later[0], earlier[1] + later[1])


def slot_total(tables):
    empty = (jnp.zeros_like(tables[0]), jnp.zeros_like(tables[1]))
    before = entering(tables, ("rows", "cols"), add_pair, empty, False)
    after = entering(tables, ("rows", "cols"), add_pair, empty, True)
    return (before[0] + tables[0] + after[0], before[1] + tables[1] + after[1])


def pad_rim(values):
    return padded_2(values, (("rows", 1), ("cols", 2)), 1)


def tap_patch(padded, masks, tap, stride):
    rows = padded.shape[1] - 2
    cols = padded.shape[2] - 2
    row_off, col_off = (tap // 3, tap % 3)
    patch = padded[:, row_off : row_off + rows : stride, col_off : col_off + cols : stride, :]
    return patch * masks[tap][::stride, ::stride][None, :, :, None]


def conv_taps(padded, weight, masks, stride):
    total = None
    for tap in range(9):
        term = jnp.einsum(
            "nhwc,cd->nhwd",
            tap_patch(padded, masks, tap, stride),
            weight[tap],
            preferred_element_type=jnp.float32,
        )
        total = term if total is None else total + term
    return total


def conv_weight_grad(padded, grad_out, masks, stride):
    return jnp.stack(
        [
            jnp.einsum(
                "nhwc,nhwd->cd",
                tap_patch(padded, masks, tap, stride),
                grad_out,
                preferred_element_type=jnp.float32,
            )
            for tap in range(9)
        ]
    )


def conv_input_grad(grad_out, weight, masks, stride):
    spread = grad_out
    if stride == 2:
        canvases, rows, cols, width = grad_out.shape
        spread = jnp.stack([grad_out, jnp.zeros_like(grad_out)], axis=2).reshape(
            canvases, 2 * rows, cols, width
        )
        spread = jnp.stack([spread, jnp.zeros_like(spread)], axis=3).reshape(
            canvases, 2 * rows, 2 * cols, width
        )
    flipped = jnp.swapaxes(weight[::-1], 1, 2)
    padded = padded_2(spread, (("rows", 1), ("cols", 2)), 1)
    return conv_taps(padded, flipped, masks, 1)


def norm_forward(values, gain, bias, scale, shift, level):
    count_n, rows, cols, width = values.shape
    grouped = values.reshape(count_n, rows, cols, GROUPS, width // GROUPS)
    total, squares = slot_total(
        (
            to_slots(jnp.sum(grouped, axis=4), level),
            to_slots(jnp.sum(grouped * grouped, axis=4), level),
        )
    )
    count = level[2][None, :, :, None] * (width // GROUPS)
    mean = total / count
    var = squares / count - mean * mean
    inverse = lax.rsqrt(var + EPS_NORM)
    mean_pix = to_pixels(mean, level)
    inv_pix = to_pixels(inverse, level)
    hat = ((grouped - mean_pix[..., None]) * inv_pix[..., None]).reshape(values.shape)
    normed = hat * gain + bias
    if scale is None:
        return (normed, (hat, inv_pix, normed, None))
    factor = 1.0 + to_pixels(scale, level)
    return (normed * factor + to_pixels(shift, level), (hat, inv_pix, normed, factor))


def norm_backward(grad_out, kept, gain, level):
    hat, inv_pix, normed, factor = kept
    count_n, rows, cols, width = hat.shape
    if factor is None:
        film_grad = None
        grad_normed = grad_out
    else:
        film_grad = jnp.concatenate(
            [to_slots(grad_out * normed, level), to_slots(grad_out, level)], axis=-1
        )
        grad_normed = grad_out * factor
    grad_gain = jnp.sum(grad_normed * hat, axis=(0, 1, 2))
    grad_bias = jnp.sum(grad_normed, axis=(0, 1, 2))
    shape = (count_n, rows, cols, GROUPS, width // GROUPS)
    grad_hat = (grad_normed * gain).reshape(shape)
    grouped_hat = hat.reshape(shape)
    first, second = slot_total(
        (
            to_slots(jnp.sum(grad_hat, axis=4), level),
            to_slots(jnp.sum(grad_hat * grouped_hat, axis=4), level),
        )
    )
    count = level[2][None, :, :, None] * (width // GROUPS)
    mean_one = to_pixels(first / count, level)[..., None]
    mean_two = to_pixels(second / count, level)[..., None]
    grad_in = inv_pix[..., None] * (grad_hat - mean_one - grouped_hat * mean_two)
    return (grad_in.reshape(hat.shape), grad_gain, grad_bias, film_grad)


def block_forward(hidden, weights, gains, film, level, masks):
    pre_one, saved_one = norm_forward(hidden, gains[0], gains[1], None, None, level)
    rim_one = pad_rim(jax.nn.silu(pre_one).astype(jnp.bfloat16))
    conv_one = conv_taps(rim_one, weights[0], masks, 1)
    pre_two, saved_two = norm_forward(conv_one, gains[2], gains[3], film[0], film[1], level)
    rim_two = pad_rim(jax.nn.silu(pre_two).astype(jnp.bfloat16))
    out = hidden + conv_taps(rim_two, weights[1], masks, 1)
    return (out, (pre_one, saved_one, rim_one, pre_two, saved_two, rim_two))


def block_backward(grad_out, weights, gains, kept, level, masks):
    pre_one, saved_one, rim_one, pre_two, saved_two, rim_two = kept
    grad_two = grad_out.astype(jnp.bfloat16)
    weight_two = conv_weight_grad(rim_two, grad_two, masks, 1)
    grad_pre_two = conv_input_grad(grad_two, weights[1], masks, 1) * silu_grad(pre_two)
    grad_conv, gain_two, bias_two, film_grad = norm_backward(
        grad_pre_two, saved_two, gains[2], level
    )
    grad_one = grad_conv.astype(jnp.bfloat16)
    weight_one = conv_weight_grad(rim_one, grad_one, masks, 1)
    grad_pre_one = conv_input_grad(grad_one, weights[0], masks, 1) * silu_grad(pre_one)
    grad_in, gain_one, bias_one, _ = norm_backward(grad_pre_one, saved_one, gains[0], level)
    return (
        grad_out + grad_in,
        (weight_one, weight_two),
        (gain_one, bias_one, gain_two, bias_two),
        film_grad,
    )


def per_device(
    image_pair,
    noise_target,
    timesteps,
    text_pooled,
    slot_live,
    edgeconv_weight,
    edgeconv_first,
    edgeconv_second,
    convlow_weight,
    convlow_first,
    convlow_second,
    convhigh_weight,
    convhigh_first,
    convhigh_second,
    downconv_weight,
    downconv_first,
    downconv_second,
    upconv_weight,
    upconv_first,
    upconv_second,
    condproj_weight,
    condproj_first,
    condproj_second,
    filmproj_weight,
    filmproj_first,
    filmproj_second,
    normparams_weight,
    normparams_first,
    normparams_second,
):
    canvases, rows_one, cols_one = image_pair.shape[:3]
    size_full = rows_one * lax.axis_size("rows")
    level_full = slot_level(rows_one, cols_one, SLOT, size_full)
    level_half = slot_level(rows_one // 2, cols_one // 2, SLOT // 2, size_full // 2)
    by_rows = (
        lax.all_gather(convlow_weight.astype(jnp.bfloat16), "rows", axis=2, tiled=True),
        lax.all_gather(convhigh_weight.astype(jnp.bfloat16), "rows", axis=2, tiled=True),
        lax.all_gather(downconv_weight.astype(jnp.bfloat16), "rows", axis=1, tiled=True),
        lax.all_gather(upconv_weight.astype(jnp.bfloat16), "rows", axis=1, tiled=True),
        lax.all_gather(filmproj_weight.astype(jnp.bfloat16), "rows", axis=0, tiled=True),
    )
    low_convs, high_convs, down_conv, up_conv, film_full = (
        lax.all_gather(by_rows[0], "cols", axis=3, tiled=True),
        lax.all_gather(by_rows[1], "cols", axis=3, tiled=True),
        lax.all_gather(by_rows[2], "cols", axis=2, tiled=True),
        lax.all_gather(by_rows[3], "cols", axis=2, tiled=True),
        lax.all_gather(by_rows[4], "cols", axis=1, tiled=True),
    )
    joined = jnp.concatenate([time_embed(timesteps).astype(jnp.bfloat16), text_pooled], axis=-1)
    cond_full = lax.all_gather(
        condproj_weight.astype(jnp.bfloat16), ("rows", "cols"), axis=1, tiled=True
    )
    pre_cond = jnp.einsum("nabk,kf->nabf", joined, cond_full, preferred_element_type=jnp.float32)
    cond_low = jax.nn.silu(pre_cond).astype(jnp.bfloat16)
    film_all = jnp.einsum("nabk,kf->nabf", cond_low, film_full, preferred_element_type=jnp.float32)
    offsets = [0, C1, 2 * C1, 3 * C1, 4 * C1, 4 * C1 + C2, 4 * C1 + 2 * C2, 5 * C1 + 2 * C2]

    def norm_part(index, which):
        return normparams_weight[which, offsets[index] : offsets[index + 1]]

    def block_gains(index):
        return (
            norm_part(2 * index, 0),
            norm_part(2 * index, 1),
            norm_part(2 * index + 1, 0),
            norm_part(2 * index + 1, 1),
        )

    def block_film(index):
        base = (0, 2 * C1, 4 * C1)[index]
        width = (C1, C1, C2)[index]
        return (film_all[..., base : base + width], film_all[..., base + width : base + 2 * width])

    masks_one = tap_masks(rows_one, cols_one, SLOT)
    masks_two = tap_masks(rows_one // 2, cols_one // 2, SLOT // 2)
    edge_low = edgeconv_weight.astype(jnp.bfloat16)
    inconv_low = jnp.swapaxes(edge_low[:, :, 0:6], 1, 2)
    head_low = edge_low[:, :, 6:9]
    rim_in = pad_rim(image_pair)
    hidden = conv_taps(rim_in, inconv_low, masks_one, 1)
    kept_blocks = []
    for index in range(2):
        hidden, kept = block_forward(
            hidden,
            (low_convs[2 * index], low_convs[2 * index + 1]),
            block_gains(index),
            block_film(index),
            level_full,
            masks_one,
        )
        kept_blocks.append(kept)
    rim_skip = pad_rim(hidden.astype(jnp.bfloat16))
    deep, kept_deep = block_forward(
        conv_taps(rim_skip, down_conv, masks_one, 2),
        (high_convs[0], high_convs[1]),
        block_gains(2),
        block_film(2),
        level_half,
        masks_two,
    )
    upsampled = jnp.repeat(jnp.repeat(deep.astype(jnp.bfloat16), 2, axis=1), 2, axis=2)
    rim_up = pad_rim(upsampled)
    merged = conv_taps(rim_up, up_conv, masks_one, 1) + hidden
    pre_head, kept_head = norm_forward(
        merged, norm_part(6, 0), norm_part(6, 1), None, None, level_full
    )
    rim_head = pad_rim(jax.nn.silu(pre_head).astype(jnp.bfloat16))
    pred = conv_taps(rim_head, head_low, masks_one, 1)
    live_slots = slot_live.astype(jnp.float32)
    live = to_pixels(live_slots[..., None], level_full)
    count = 3.0 * jnp.sum(live_slots * level_full[2][None, :, :])
    diff = pred - noise_target
    loss_local = jnp.sum(live * diff * diff)
    grad_pred = (2.0 * live * diff / count).astype(jnp.bfloat16)
    grad_head = conv_weight_grad(rim_head, grad_pred, masks_one, 1)
    grad_act = conv_input_grad(grad_pred, head_low, masks_one, 1) * silu_grad(pre_head)
    grad_merged, head_gain, head_bias, _ = norm_backward(
        grad_act, kept_head, norm_part(6, 0), level_full
    )
    merged_low = grad_merged.astype(jnp.bfloat16)
    grad_upconv = conv_weight_grad(rim_up, merged_low, masks_one, 1)
    grad_up = conv_input_grad(merged_low, up_conv, masks_one, 1)
    grad_deep = grad_up.reshape(canvases, rows_one // 2, 2, cols_one // 2, 2, C2).sum(axis=(2, 4))
    grad_down, deep_convs, deep_norms, deep_film = block_backward(
        grad_deep, (high_convs[0], high_convs[1]), block_gains(2), kept_deep, level_half, masks_two
    )
    down_low = grad_down.astype(jnp.bfloat16)
    grad_downconv = conv_weight_grad(rim_skip, down_low, masks_one, 2)
    grad_hidden = grad_merged + conv_input_grad(down_low, down_conv, masks_one, 2)
    block_convs = [None, None]
    block_norms = [None, None]
    block_films = [None, None]
    for index in (1, 0):
        grad_hidden, block_convs[index], block_norms[index], block_films[index] = block_backward(
            grad_hidden,
            (low_convs[2 * index], low_convs[2 * index + 1]),
            block_gains(index),
            kept_blocks[index],
            level_full,
            masks_one,
        )
    hidden_low = grad_hidden.astype(jnp.bfloat16)
    grad_inconv = conv_weight_grad(rim_in, hidden_low, masks_one, 1)
    image_grad = conv_input_grad(hidden_low, inconv_low, masks_one, 1) * count
    all_norms = block_norms + [deep_norms]
    gain_vector = jnp.concatenate([part[k] for part in all_norms for k in (0, 2)] + [head_gain])
    bias_vector = jnp.concatenate([part[k] for part in all_norms for k in (1, 3)] + [head_bias])
    film_grads = jnp.concatenate([block_films[0], block_films[1], deep_film], axis=-1)
    edge_local = jnp.concatenate([jnp.swapaxes(grad_inconv, 1, 2), grad_head], axis=2)
    film_sum, edge_sum, norm_sum, loss_sum = lax.psum(
        (film_grads, edge_local, jnp.stack([gain_vector, bias_vector]), loss_local),
        ("rows", "cols"),
    )
    grad_film_full = jnp.einsum(
        "nabk,nabf->kf", cond_low.astype(jnp.float32), film_sum, precision=HIGH
    )
    grad_cond = jnp.einsum(
        "nabf,kf->nabk", film_sum, film_full.astype(jnp.float32), precision=HIGH
    ) * silu_grad(pre_cond)
    grad_cond_full = jnp.einsum(
        "nabk,nabf->kf", joined.astype(jnp.float32), grad_cond, precision=HIGH
    )
    film_rows, film_cols = filmproj_weight.shape
    film_own = lax.dynamic_slice_in_dim(
        grad_film_full, lax.axis_index("rows") * film_rows, film_rows, 0
    )
    film_own = lax.dynamic_slice_in_dim(film_own, lax.axis_index("cols") * film_cols, film_cols, 1)
    cond_cols = condproj_weight.shape[1]
    cond_own = lax.dynamic_slice_in_dim(
        grad_cond_full, lax.axis_index(("rows", "cols")) * cond_cols, cond_cols, 1
    )
    by_cols = (
        lax.psum_scatter(
            jnp.stack(
                [block_convs[0][0], block_convs[0][1], block_convs[1][0], block_convs[1][1]]
            ).astype(jnp.bfloat16),
            "cols",
            scatter_dimension=3,
            tiled=True,
        ).astype(jnp.float32),
        lax.psum_scatter(
            jnp.stack([deep_convs[0], deep_convs[1]]).astype(jnp.bfloat16),
            "cols",
            scatter_dimension=3,
            tiled=True,
        ).astype(jnp.float32),
        lax.psum_scatter(
            grad_downconv.astype(jnp.bfloat16), "cols", scatter_dimension=2, tiled=True
        ).astype(jnp.float32),
        lax.psum_scatter(
            grad_upconv.astype(jnp.bfloat16), "cols", scatter_dimension=2, tiled=True
        ).astype(jnp.float32),
    )
    lowconv_own, highconv_own, downconv_own, upconv_own = (
        lax.psum_scatter(
            by_cols[0].astype(jnp.bfloat16), "rows", scatter_dimension=2, tiled=True
        ).astype(jnp.float32),
        lax.psum_scatter(
            by_cols[1].astype(jnp.bfloat16), "rows", scatter_dimension=2, tiled=True
        ).astype(jnp.float32),
        lax.psum_scatter(
            by_cols[2].astype(jnp.bfloat16), "rows", scatter_dimension=1, tiled=True
        ).astype(jnp.float32),
        lax.psum_scatter(
            by_cols[3].astype(jnp.bfloat16), "rows", scatter_dimension=1, tiled=True
        ).astype(jnp.float32),
    )
    weights = (
        edgeconv_weight,
        convlow_weight,
        convhigh_weight,
        downconv_weight,
        upconv_weight,
        condproj_weight,
        filmproj_weight,
        normparams_weight,
    )
    firsts = (
        edgeconv_first,
        convlow_first,
        convhigh_first,
        downconv_first,
        upconv_first,
        condproj_first,
        filmproj_first,
        normparams_first,
    )
    seconds = (
        edgeconv_second,
        convlow_second,
        convhigh_second,
        downconv_second,
        upconv_second,
        condproj_second,
        filmproj_second,
        normparams_second,
    )
    grads = (
        edge_sum,
        lowconv_own,
        highconv_own,
        downconv_own,
        upconv_own,
        cond_own,
        film_own,
        norm_sum,
    )
    sharded = (1, 2, 3, 4, 5, 6)
    stacked = (1, 2)
    owned_sq = sum((jnp.sum(grads[k] * grads[k]) for k in sharded))
    shared_sq = sum((jnp.sum(grads[k] * grads[k]) for k in range(8) if k not in sharded))
    clip_norm = jnp.sqrt(lax.psum(owned_sq, ("rows", "cols")) + shared_sq)
    factor = jnp.minimum(1.0, CLIP_AT / clip_norm)
    clipped, moments, updates = ([], [], [])
    for k in range(8):
        grad = grads[k] * factor
        first_new = BETA_ONE * firsts[k] + (1.0 - BETA_ONE) * grad
        second_new = BETA_TWO * seconds[k] + (1.0 - BETA_TWO) * grad * grad
        first_hat = first_new / (1.0 - BETA_ONE**STEP)
        second_hat = second_new / (1.0 - BETA_TWO**STEP)
        clipped.append(grad)
        moments.append(second_new)
        updates.append(first_hat / (jnp.sqrt(second_hat) + EPS_ADAM) + DECAY * weights[k])

    def matrix_squares(values, k):
        if k in stacked:
            return jnp.sum(values * values, axis=tuple(range(1, values.ndim)))
        return jnp.sum(values * values).reshape(1)

    weight_sq, update_sq = lax.psum(
        (
            jnp.concatenate([matrix_squares(weights[k], k) for k in sharded]),
            jnp.concatenate([matrix_squares(updates[k], k) for k in sharded]),
        ),
        ("rows", "cols"),
    )
    ratios = jnp.sqrt(weight_sq) / jnp.sqrt(update_sq)
    position = 0
    results = []
    for k in range(8):
        if k in sharded:
            span = weights[k].shape[0] if k in stacked else 1
            ratio = ratios[position : position + span]
            position += span
            ratio = (
                ratio.reshape((span,) + (1,) * (weights[k].ndim - 1)) if k in stacked else ratio[0]
            )
        elif k == 0:
            part = (jnp.arange(9) < 6)[None, None, :]
            other = jnp.logical_not(part)
            weight_sq_two = weights[k] * weights[k]
            update_sq_two = updates[k] * updates[k]
            ratio_in = jnp.sqrt(jnp.sum(jnp.where(part, weight_sq_two, 0.0))) / jnp.sqrt(
                jnp.sum(jnp.where(part, update_sq_two, 0.0))
            )
            ratio_out = jnp.sqrt(jnp.sum(jnp.where(other, weight_sq_two, 0.0))) / jnp.sqrt(
                jnp.sum(jnp.where(other, update_sq_two, 0.0))
            )
            ratio = jnp.where(part, ratio_in, ratio_out)
        else:
            ratio = jnp.sqrt(jnp.sum(weights[k] * weights[k])) / jnp.sqrt(
                jnp.sum(updates[k] * updates[k])
            )
        results.extend([clipped[k], moments[k], weights[k] - RATE * ratio * updates[k]])
    return (
        results[0],
        results[1],
        results[2],
        results[3],
        results[4],
        results[5],
        results[6],
        results[7],
        results[8],
        results[9],
        results[10],
        results[11],
        results[12],
        results[13],
        results[14],
        results[15],
        results[16],
        results[17],
        results[18],
        results[19],
        results[20],
        results[21],
        results[22],
        results[23],
        loss_sum,
        count,
        clip_norm,
        image_grad,
    )


F32 = jnp.float32
BF = jnp.bfloat16
MESH = pl.DeviceIdType.MESH
NORM_AT = (0, 128, 256, 384, 512, 768, 1024, 1152)
FILM_AT = {1: 0, 3: 256, 5: 512}
ROW_OF = (0, 1, -1, 2)
COL_OF = (-1, 0, 1, 2)
N_EXCHANGE = 20


def phase_tables():
    by_cell = np.zeros((9, 4, 4, 9), np.float32)
    by_tile = np.zeros((4, 4, 4, 9), np.float32)
    for out in range(4):
        cp_out, rp_out = out // 2, out % 2
        for cell in range(9):
            for inp in range(4):
                a = 2 * (cell // 3 - 1) + inp % 2 - rp_out + 1
                b = 2 * (cell % 3 - 1) + inp // 2 - cp_out + 1
                if 0 <= a <= 2 and 0 <= b <= 2:
                    by_cell[cell, inp, out, 3 * a + b] = 1.0
        for g in range(4):
            for r in range(4):
                a = ROW_OF[r] - rp_out + 1
                b = COL_OF[g] - cp_out + 1
                if 0 <= a <= 2 and 0 <= b <= 2:
                    by_tile[g, r, out, 3 * a + b] = 1.0
    return by_cell, by_tile


def unet_kernel(
    img_ref,
    tgt_ref,
    small_ref,
    film_ref,
    norm_ref,
    low_ref,
    high_ref,
    down_ref,
    up_ref,
    wi_ref,
    wit_ref,
    wh_ref,
    wht_ref,
    dlow_ref,
    dhigh_ref,
    ddown_ref,
    dup_ref,
    dwi_ref,
    dwh_ref,
    fgrad_ref,
    ngrad_ref,
    loss_ref,
    imgrad_ref,
    full_ref,
    half_ref,
    work_ref,
    grad_ref,
    wide_ref,
    thin_ref,
    act_ref,
    acth_ref,
    turn_ref,
    wc_ref,
    wr_ref,
    wu_ref,
    wut_ref,
    wd_ref,
    coef_ref,
    rows_ref,
    patch_ref,
    ext_ref,
    send_ref,
    recv_ref,
    send_sem,
    recv_sem,
):
    rr = lax.axis_index("rows")
    cc = lax.axis_index("cols")
    core = lax.rem(cc, 2)
    partner = cc + 1 - 2 * core
    halo = rr >= 2
    split = jnp.logical_and(lax.rem(rr, 2) == 1, cc >= 2)

    def flag(cond):
        return jnp.where(cond, 1.0, 0.0).astype(F32)

    f_halo = flag(halo)
    f_core1 = flag(core == 1)
    f_core0 = 1.0 - f_core1
    f_top = f_halo * f_core1
    f_bot = f_halo * f_core0
    f_split = flag(split)
    f_joined = 1.0 - f_split

    place = lax.broadcasted_iota(jnp.int32, (32, 256), 0)
    lo_mask = jnp.where(place == 0, 0.0, jnp.where(place == 16, f_joined, 1.0))
    hi_mask = jnp.where(place == 31, 0.0, jnp.where(place == 15, f_joined, 1.0))

    barrier = pltpu.get_barrier_semaphore()
    pl.semaphore_signal(barrier, inc=1, device_id={"cols": partner}, device_id_type=MESH)
    pl.semaphore_wait(barrier, 1)

    def before(x):
        return pltpu.roll(x, 1, 0) * lo_mask

    def after(x):
        return pltpu.roll(x, 31, 0) * hi_mask

    def at(i):
        return pl.ds(pl.multiple_of(i * 32, 32), 32)

    def loop(body, init=0, count=16):
        return lax.fori_loop(0, count, body, init)

    def dot(a, b):
        return jnp.dot(a, b, preferred_element_type=F32)

    def dot_nt(a, b):
        return lax.dot_general(a, b, (((1,), (1,)), ((), ())), preferred_element_type=F32)

    def sigmoid(z):
        return 0.5 * jnp.tanh(0.5 * z) + 0.5

    def double(v):
        return jnp.concatenate([v, v], axis=1)


    def copy_of(e):
        return pltpu.make_async_remote_copy(
            src_ref=send_ref.at[e],
            dst_ref=recv_ref.at[e],
            send_sem=send_sem.at[e],
            recv_sem=recv_sem.at[e],
            device_id={"cols": partner},
            device_id_type=MESH,
        )

    def send(e, row, stats=None):
        send_ref[e, 0:32, :] = row
        send_ref[e, 32:40, :] = jnp.zeros((8, 256), F32) if stats is None else stats
        copy_of(e).start()

    def arrive(e):
        copy_of(e).wait()

    def edge_full(ref):
        low = f_core0 * ref[0, 480:512, 128:256] + f_core1 * ref[0, 0:32, 0:128]
        high = f_core0 * ref[1, 480:512, 128:256] + f_core1 * ref[1, 0:32, 0:128]
        return jnp.concatenate([low, high], axis=1)

    def edge_cell(ref):
        return f_core0 * ref[480:512, :] + f_core1 * ref[0:32, :]

    def edge(ref, planes):
        return edge_full(ref) if planes == 2 else edge_cell(ref.at[0])


    def halves(x):
        return x[0:8] + x[8:16], x[16:24] + x[24:32]

    def gathered(sums, planes):
        rows = []
        for s in sums:
            row = jnp.sum(s, axis=0, keepdims=True)
            rows.append(double(row[:, 0:128] + row[:, 128:256]) if planes == 2 else row)
        return jnp.concatenate(rows + [jnp.zeros((4, 256), F32)], axis=0)

    zero8 = jnp.zeros((8, 256), F32)

    def stats_of(x_ref, planes):
        def body(i, carry):
            s_l, s_r, q_l, q_r = carry
            for p in range(planes):
                x = x_ref[p, at(i), :]
                a, b = halves(x)
                c, d = halves(x * x)
                s_l, s_r, q_l, q_r = s_l + a, s_r + b, q_l + c, q_r + d
            return s_l, s_r, q_l, q_r

        return gathered(loop(body, (zero8,) * 4), planes)

    def over_slot(block, planes):
        swapped = jnp.concatenate(
            [block[1:2], block[0:1], block[3:4], block[2:3], block[4:8]], axis=0
        )
        x = block + f_joined * swapped
        lane = lax.broadcasted_iota(jnp.int32, (8, 256), 1)
        step = 1
        while step < (4 if planes == 2 else 8):
            up = pltpu.roll(x, 256 - step, 1)
            down = pltpu.roll(x, step, 1)
            x = x + jnp.where(lax.rem(lane, 2 * step) < step, up, down)
            step *= 2
        size = 16.0 if planes == 2 else 8.0
        count = (16.0 + 16.0 * f_halo) * (16.0 + 16.0 * f_joined) * size
        return x / count

    def spread(two):
        return jnp.concatenate(
            [
                jnp.broadcast_to(two[0:1], (16, 256)),
                jnp.broadcast_to(two[1:2], (16, 256)),
            ],
            axis=0,
        )

    def norm_row(k, which):
        width = NORM_AT[k + 1] - NORM_AT[k] if k < 6 else 128
        row = norm_ref[which : which + 1, NORM_AT[k] : NORM_AT[k] + width]
        return double(row) if width == 128 else row

    def film_rows(k, which):
        if k not in FILM_AT:
            return jnp.zeros((2, 256), F32)
        width = 256 if k == 5 else 128
        base = FILM_AT[k] + which * width
        two = film_ref[0:2, base : base + width]
        return double(two) if width == 128 else two

    def norm_ready(k, stats, e, planes):
        total = over_slot(stats + f_halo * recv_ref[e, 32:40, :], planes)
        mean = total[0:2]
        var = total[2:4] - mean * mean
        inverse = lax.rsqrt(var + EPS_NORM)
        gain, bias = norm_row(k, 0), norm_row(k, 1)
        factor = 1.0 + film_rows(k, 0)
        slope = inverse * gain * factor
        coef_ref[k, 0] = spread(slope)
        coef_ref[k, 1] = spread((bias - mean * inverse * gain) * factor + film_rows(k, 1))
        coef_ref[k, 2] = spread(mean)
        coef_ref[k, 3] = spread(inverse)
        rows_ref[k, 0:2, :] = mean
        rows_ref[k, 2:4, :] = inverse

    def activated(x, k):
        z = x * coef_ref[k, 0] + coef_ref[k, 1]
        return z * sigmoid(z)


    def put_wide(i, even, odd):
        for t, g in enumerate((before(odd), even, odd, after(even))):
            b = g.astype(BF)
            wide_ref[at(i + 1), 512 * t : 512 * t + 256] = b
            wide_ref[at(i + 2), 512 * t + 256 : 512 * t + 384] = b[:, 128:256]
            wide_ref[at(i), 512 * t + 384 : 512 * t + 512] = b[:, 0:128]

    def put_wide_edge(row):
        even, odd = row[:, 0:128], row[:, 128:256]
        lo, hi = lo_mask[:, 0:128], hi_mask[:, 0:128]
        for t, g in enumerate((pltpu.roll(odd, 1, 0) * lo, even, odd, pltpu.roll(even, 31, 0) * hi)):
            wide_ref[32:64, 512 * t + 256 : 512 * t + 384] = (g * f_top).astype(BF)
            wide_ref[512:544, 512 * t + 384 : 512 * t + 512] = (g * f_bot).astype(BF)

    def put_thin(i, x):
        for t, g in enumerate((before(x), x, after(x))):
            thin_ref[at(i + 1), 256 * t : 256 * t + 256] = g.astype(BF)

    def put_thin_edge(row):
        for t, g in enumerate((before(row), row, after(row))):
            thin_ref[0:32, 256 * t : 256 * t + 256] = (g * f_top).astype(BF)
            thin_ref[544:576, 256 * t : 256 * t + 256] = (g * f_bot).astype(BF)

    def keep_wide(slot):
        act_ref[slot, 0] = wide_ref[32:544, 512:768]
        act_ref[slot, 1] = wide_ref[32:544, 1024:1280]

    def keep_thin(slot):
        acth_ref[slot] = thin_ref[32:544, 256:512]

    def turn_wide(slot):
        turn_ref[0:256, :] = act_ref[slot, 0].T
        turn_ref[256:512, :] = act_ref[slot, 1].T


    def load_wc(index):
        for b in range(3):
            for r in range(4):
                for rp in range(2):
                    a = ROW_OF[r] - rp + 1
                    if 0 <= a <= 2:
                        wc_ref[
                            b * 512 + r * 128 : b * 512 + r * 128 + 128, rp * 128 : rp * 128 + 128
                        ] = low_ref[index, 3 * a + b]

    def load_wr(index):
        for b in range(3):
            for r in range(4):
                for rp in range(2):
                    a = ROW_OF[r] - rp + 1
                    if 0 <= a <= 2:
                        wr_ref[
                            rp * 128 : rp * 128 + 128, b * 512 + r * 128 : b * 512 + r * 128 + 128
                        ] = low_ref[index, 8 - 3 * a - b]

    def taps_of(parity, d):
        if parity == 0:
            return {-1: (0,), 0: (1, 2)}.get(d, ())
        return {0: (0, 1), 1: (2,)}.get(d, ())

    def load_up():
        for cp in range(2):
            for rp in range(2):
                for di in (-1, 0, 1):
                    for dj in (-1, 0, 1):
                        taps = [3 * a + b for a in taps_of(rp, di) for b in taps_of(cp, dj)]
                        if not taps:
                            continue
                        total = up_ref[taps[0]].astype(F32)
                        for t in taps[1:]:
                            total = total + up_ref[t].astype(F32)
                        low = total.astype(BF)
                        at_k = (dj + 1 - cp) * 256
                        wu_ref[cp, di + 1, at_k : at_k + 256, rp * 128 : rp * 128 + 128] = low
                        row = ROW_OF.index(rp - 2 * di)
                        col = COL_OF.index(cp - 2 * dj)
                        wut_ref[:, col * 512 + row * 128 : col * 512 + row * 128 + 128] = low

    def load_down():
        for b in range(3):
            for r in range(3):
                a = ROW_OF[r] + 1
                wd_ref[b * 512 + r * 128 : b * 512 + r * 128 + 128, :] = down_ref[3 * a + b]


    def conv_low(out, weight_nt=False):
        for cp in range(2):
            left = wide_ref[32:544, cp * 512 : cp * 512 + 1536]
            out(cp, dot_nt(left, wr_ref[...]) if weight_nt else dot(left, wc_ref[...]))

    def conv_high(index):
        total = None
        for a in range(3):
            term = dot(
                thin_ref[32 * a : 32 * a + 512, :],
                high_ref[index, 3 * a : 3 * a + 3].reshape(768, 256),
            )
            total = term if total is None else total + term
        return total

    def conv_high_back(index):
        total = None
        for a in range(3):
            for b in range(3):
                term = dot_nt(
                    thin_ref[32 * a : 32 * a + 512, b * 256 : b * 256 + 256],
                    high_ref[index, 8 - 3 * a - b],
                )
                total = term if total is None else total + term
        return total

    def grad_low(index, slot):
        turn_wide(slot)
        for b in range(3):
            block = dot(turn_ref[0:256, :], wide_ref[32:544, b * 512 : b * 512 + 512]) + dot(
                turn_ref[256:512, :], wide_ref[32:544, b * 512 + 512 : b * 512 + 1024]
            )
            for a in range(3):
                first = ROW_OF.index(a - 1) * 128
                second = ROW_OF.index(a) * 128
                dlow_ref[index, 8 - 3 * a - b] = (
                    block[0:128, first : first + 128] + block[128:256, second : second + 128]
                ).astype(dlow_ref.dtype)

    def grad_high(index, slot):
        turn_ref[0:256, :] = acth_ref[slot].T
        for a in range(3):
            block = dot(turn_ref[0:256, :], thin_ref[32 * a : 32 * a + 512, :])
            for b in range(3):
                dhigh_ref[index, 8 - 3 * a - b] = block[:, b * 256 : b * 256 + 256].astype(
                    dhigh_ref.dtype
                )


    def put_patch(slot, source, row, lanes):
        ext_ref[0:32, :] = row * f_top
        ext_ref[544:576, :] = row * f_bot

        def fill(i, carry):
            ext_ref[at(i + 1), :] = source[at(i), :]
            return carry

        loop(fill)

        def body(i, carry):
            total = None
            for di in (-1, 0, 1):
                x = ext_ref[at(i + 1 + di), :]
                for dj, g in enumerate((before(x), x, after(x))):
                    shift = ((di + 1) * 3 + dj) * lanes
                    term = pltpu.roll(g, shift, 1) if shift else g
                    total = term if total is None else total + term
            patch_ref[slot, at(i), :] = total.astype(BF)
            return carry

        loop(body)


    def norm_back_start(k, x_ref, planes):
        def body(i, carry):
            s_l, s_r, q_l, q_r = carry
            for p in range(planes):
                x = x_ref[p, at(i), :]
                z = x * coef_ref[k, 0] + coef_ref[k, 1]
                s = sigmoid(z)
                d = work_ref[p, at(i), :] * (s * (1.0 + z * (1.0 - s)))
                work_ref[p, at(i), :] = d
                a, b = halves(d)
                c, e = halves(d * ((x - coef_ref[k, 2]) * coef_ref[k, 3]))
                s_l, s_r, q_l, q_r = s_l + a, s_r + b, q_l + c, q_r + e
            return s_l, s_r, q_l, q_r

        return gathered(loop(body, (zero8,) * 4), planes)

    def norm_back_ready(k, stats, e, planes):
        gain, bias = norm_row(k, 0), norm_row(k, 1)
        factor = 1.0 + film_rows(k, 0)
        width = 128 if planes == 2 else 256
        one, two = stats[0:2], stats[2:4]
        dgain, dbias = factor * two, factor * one
        o = NORM_AT[k]
        ngrad_ref[0:1, o : o + width] = (dgain[0:1] + dgain[1:2])[:, 0:width]
        ngrad_ref[1:2, o : o + width] = (dbias[0:1] + dbias[1:2])[:, 0:width]
        if k in FILM_AT:
            f = FILM_AT[k]
            fgrad_ref[0:2, f : f + width] = (gain * two + bias * one)[:, 0:width]
            fgrad_ref[0:2, f + width : f + 2 * width] = one[:, 0:width]
        both = stats + f_halo * recv_ref[e, 32:40, :]
        kk = gain * factor
        scaled = jnp.concatenate([kk * both[0:2], kk * both[2:4], both[4:8]], axis=0)
        total = over_slot(scaled, planes)
        mean, inverse = rows_ref[k, 0:2, :], rows_ref[k, 2:4, :]
        second = -inverse * inverse * total[2:4]
        third = -inverse * total[0:2] - mean * second
        coef_ref[k, 4] = spread(inverse * kk)
        coef_ref[k, 5] = spread(second)
        coef_ref[k, 6] = spread(third)

    def back_value(k, d, x):
        return d * coef_ref[k, 4] + x * coef_ref[k, 5] + coef_ref[k, 6]


    def zero(i, carry):
        wc_ref[at(i), :] = jnp.zeros((32, 256), BF)
        return carry

    loop(zero, count=48)
    wr_ref[...] = jnp.zeros(wr_ref.shape, BF)
    for cp in range(2):
        for di in range(3):
            wu_ref[cp, di] = jnp.zeros((512, 256), BF)
    for b in range(3):
        wd_ref[b * 512 + 384 : b * 512 + 512, :] = jnp.zeros((128, 256), BF)

    send(0, edge_cell(img_ref))
    load_wc(0)
    load_up()
    load_down()
    arrive(0)
    put_patch(0, img_ref, recv_ref[0, 0:32, :], 24)
    for cp in range(2):
        full_ref[0, cp] = dot(patch_ref[0], wi_ref[cp])

    def fwd_norm_full(k, source, e):
        stats = stats_of(source, 2)
        send(e, edge_full(source), stats)
        return stats

    def fwd_apply_full(k, source, stats, e):
        arrive(e)
        norm_ready(k, stats, e, 2)

        def body(i, carry):
            put_wide(
                i,
                activated(source[0, at(i), :], k),
                activated(source[1, at(i), :], k),
            )
            return carry

        loop(body)
        put_wide_edge(activated(recv_ref[e, 0:32, :], k))

    for index in range(2):
        h = full_ref.at[2 * index]
        mid = full_ref.at[2 * index + 1]
        out = full_ref.at[2 * index + 2]
        k = 2 * index
        stats = fwd_norm_full(k, h, 1 + k)
        if index:
            load_wc(2)
        fwd_apply_full(k, h, stats, 1 + k)
        keep_wide(k)

        def put_mid(cp, value, mid=mid):
            mid[cp] = value

        conv_low(put_mid)
        stats = fwd_norm_full(k + 1, mid, 2 + k)
        load_wc(2 * index + 1)
        fwd_apply_full(k + 1, mid, stats, 2 + k)
        keep_wide(k + 1)

        def put_out(cp, value, h=h, out=out):
            out[cp] = h[cp] + value

        conv_low(put_out)

    skip = full_ref.at[4]
    send(5, edge_full(skip))

    def skip_body(i, carry):
        put_wide(i, skip[0, at(i), :], skip[1, at(i), :])
        return carry

    loop(skip_body)
    arrive(5)
    put_wide_edge(recv_ref[5, 0:32, :])
    keep_wide(4)
    half_ref[0, 0] = dot(wide_ref[32:544, 0:1536], wd_ref[...])

    def fwd_half(k, source, e):
        stats = stats_of(source, 1)
        send(e, edge_cell(source.at[0]), stats)
        arrive(e)
        norm_ready(k, stats, e, 1)

        def body(i, carry):
            put_thin(i, activated(source[0, at(i), :], k))
            return carry

        loop(body)
        put_thin_edge(activated(recv_ref[e, 0:32, :], k))

    fwd_half(4, half_ref.at[0], 6)
    keep_thin(0)
    half_ref[1, 0] = conv_high(0)
    fwd_half(5, half_ref.at[1], 7)
    keep_thin(1)
    half_ref[2, 0] = half_ref[0, 0] + conv_high(1)
    deep = half_ref.at[2]
    send(8, edge_cell(deep.at[0]))

    def deep_body(i, carry):
        put_thin(i, deep[0, at(i), :])
        return carry

    loop(deep_body)
    arrive(8)
    put_thin_edge(recv_ref[8, 0:32, :])
    keep_thin(2)
    merged = full_ref.at[5]
    for cp in range(2):
        total = skip[cp]
        for di in range(3):
            total = total + dot(
                thin_ref[32 * di : 32 * di + 512, cp * 256 : cp * 256 + 512], wu_ref[cp, di]
            )
        merged[cp] = total

    stats = fwd_norm_full(6, merged, 9)
    fwd_apply_full(6, merged, stats, 9)
    keep_wide(5)
    work_ref[0] = jnp.concatenate(
        [dot(wide_ref[32:544, :], wh_ref[...]), jnp.zeros((512, 128), F32)], axis=1
    )

    live = spread(small_ref[0:2, :])
    weight = small_ref[2:3, :]

    def loss_body(i, carry):
        diff = work_ref[0, at(i), :] - tgt_ref[at(i), :]
        half = live * diff
        work_ref[0, at(i), :] = (half * weight).astype(BF).astype(F32)
        return carry + half * diff

    lost = loop(loss_body, jnp.zeros((32, 256), F32))
    loss_ref[...] = jnp.sum(lost.reshape(4, 8, 256), axis=0)


    send(10, edge_cell(work_ref.at[0]))
    arrive(10)
    put_patch(1, work_ref.at[0], recv_ref[10, 0:32, :], 12)
    for cp in range(2):
        work_ref[cp] = dot(patch_ref[1], wht_ref[cp])
    stats = norm_back_start(6, merged, 2)
    send(11, edge_full(work_ref), stats)
    turn_ref[0:256, :] = patch_ref[1].T
    for cp in range(2):
        dwh_ref[cp] = dot(turn_ref[0:256, :], act_ref[5, cp])
    arrive(11)
    norm_back_ready(6, stats, 11, 2)

    def head_body(i, carry):
        pair = []
        for p in range(2):
            g = back_value(6, work_ref[p, at(i), :], merged[p, at(i), :])
            grad_ref[p, at(i), :] = g
            pair.append(g)
        put_wide(i, pair[0], pair[1])
        return carry

    loop(head_body)
    put_wide_edge(back_value(6, recv_ref[11, 0:32, :], recv_ref[9, 0:32, :]))

    hgrad = half_ref.at[3]
    hgrad[0] = dot_nt(wide_ref[32:544, :], wut_ref[...])
    send(12, edge_cell(hgrad.at[0]))
    turn_ref[0:256, :] = acth_ref[2].T
    for b in range(3):
        cols = {0: (3, 2), 1: (1, 2), 2: (1, 0)}[b]
        block = dot(turn_ref[0:256, :], wide_ref[32:544, cols[0] * 512 : cols[0] * 512 + 512]) + dot(
            turn_ref[0:256, :], wide_ref[32:544, cols[1] * 512 : cols[1] * 512 + 512]
        )
        for a in range(3):
            one, two = {0: (3, 1), 1: (0, 1), 2: (0, 2)}[a]
            dup_ref[3 * a + b] = (
                block[:, one * 128 : one * 128 + 128] + block[:, two * 128 : two * 128 + 128]
            ).astype(dup_ref.dtype)

    def deep_grad(i, carry):
        put_thin(i, hgrad[0, at(i), :])
        return carry

    loop(deep_grad)
    arrive(12)
    put_thin_edge(recv_ref[12, 0:32, :])
    work_ref[0] = conv_high_back(1)
    stats = norm_back_start(5, half_ref.at[1], 1)
    send(13, edge_cell(work_ref.at[0]), stats)
    grad_high(1, 1)
    arrive(13)
    norm_back_ready(5, stats, 13, 1)

    def mid_grad(i, carry):
        put_thin(i, back_value(5, work_ref[0, at(i), :], half_ref[1, 0, at(i), :]))
        return carry

    loop(mid_grad)
    put_thin_edge(back_value(5, recv_ref[13, 0:32, :], recv_ref[7, 0:32, :]))
    work_ref[0] = conv_high_back(0)
    stats = norm_back_start(4, half_ref.at[0], 1)
    send(14, edge_cell(work_ref.at[0]), stats)
    grad_high(0, 0)
    arrive(14)
    norm_back_ready(4, stats, 14, 1)

    def first_grad(i, carry):
        put_thin(
            i, hgrad[0, at(i), :] + back_value(4, work_ref[0, at(i), :], half_ref[0, 0, at(i), :])
        )
        return carry

    loop(first_grad)
    put_thin_edge(
        recv_ref[12, 0:32, :] + back_value(4, recv_ref[14, 0:32, :], recv_ref[6, 0:32, :])
    )

    for cp in range(2):
        for rp in range(2):
            total = None
            for di in range(1 + rp):
                for dj in range(1 + cp):
                    a = 0 if di else 1 + rp
                    b = 0 if dj else 1 + cp
                    term = dot_nt(
                        thin_ref[32 * (1 + di) : 32 * (1 + di) + 512, (1 + dj) * 256 : (2 + dj) * 256],
                        down_ref[3 * a + b],
                    )
                    total = term if total is None else total + term
            grad_ref[cp, :, rp * 128 : rp * 128 + 128] = (
                grad_ref[cp, :, rp * 128 : rp * 128 + 128] + total
            )
    send(15, edge_full(grad_ref))
    turn_wide(4)
    for cp in range(2):
        for rp in range(2):
            for di in range(1 + rp):
                for dj in range(1 + cp):
                    a = 0 if di else 1 + rp
                    b = 0 if dj else 1 + cp
                    at_row = cp * 256 + rp * 128
                    ddown_ref[3 * a + b] = dot(
                        turn_ref[at_row : at_row + 128, :],
                        thin_ref[32 * (1 + di) : 32 * (1 + di) + 512, (1 + dj) * 256 : (2 + dj) * 256],
                    ).astype(ddown_ref.dtype)

    def put_work(cp, value):
        work_ref[cp] = value

    edge_grad = None
    for index in (1, 0):
        h = full_ref.at[2 * index]
        mid = full_ref.at[2 * index + 1]
        k = 2 * index
        e = 16 if index else 18
        load_wr(k + 1)
        if index:

            def out_grad(i, carry):
                put_wide(i, grad_ref[0, at(i), :], grad_ref[1, at(i), :])
                return carry

            loop(out_grad)
            arrive(15)
            edge_grad = recv_ref[15, 0:32, :]
            put_wide_edge(edge_grad)
        conv_low(put_work, True)
        stats = norm_back_start(k + 1, mid, 2)
        send(e, edge_full(work_ref), stats)
        grad_low(k + 1, k + 1)
        load_wr(k)
        arrive(e)
        norm_back_ready(k + 1, stats, e, 2)

        def mid_body(i, carry, mid=mid, k=k):
            put_wide(
                i,
                back_value(k + 1, work_ref[0, at(i), :], mid[0, at(i), :]),
                back_value(k + 1, work_ref[1, at(i), :], mid[1, at(i), :]),
            )
            return carry

        loop(mid_body)
        put_wide_edge(back_value(k + 1, recv_ref[e, 0:32, :], recv_ref[k + 2, 0:32, :]))
        conv_low(put_work, True)
        stats = norm_back_start(k, h, 2)
        send(e + 1, edge_full(work_ref), stats)
        grad_low(k, k)
        arrive(e + 1)
        norm_back_ready(k, stats, e + 1, 2)

        def in_body(i, carry, h=h, k=k):
            pair = []
            for p in range(2):
                g = grad_ref[p, at(i), :] + back_value(k, work_ref[p, at(i), :], h[p, at(i), :])
                grad_ref[p, at(i), :] = g
                pair.append(g)
            put_wide(i, pair[0], pair[1])
            return carry

        loop(in_body)
        edge_grad = edge_grad + back_value(k, recv_ref[e + 1, 0:32, :], recv_ref[k + 1, 0:32, :])
        put_wide_edge(edge_grad)

    imgrad_ref[...] = dot(wide_ref[32:544, :], wit_ref[...])
    turn_ref[0:256, :] = patch_ref[0].T
    for cp in range(2):
        dwi_ref[cp] = dot(turn_ref[0:256, :], wide_ref[32:544, 512 + cp * 512 : 768 + cp * 512])


def unet(*operands):
    outs = (
        jax.ShapeDtypeStruct((4, 9, 128, 128), BF),
        jax.ShapeDtypeStruct((2, 9, 256, 256), BF),
        jax.ShapeDtypeStruct((9, 128, 256), BF),
        jax.ShapeDtypeStruct((9, 256, 128), BF),
        jax.ShapeDtypeStruct((2, 256, 256), F32),
        jax.ShapeDtypeStruct((2, 256, 256), F32),
        jax.ShapeDtypeStruct((2, 1024), F32),
        jax.ShapeDtypeStruct((2, 1152), F32),
        jax.ShapeDtypeStruct((8, 256), F32),
        jax.ShapeDtypeStruct((512, 128), F32),
    )
    vmem = pl.BlockSpec(memory_space=pltpu.VMEM)
    return pl.pallas_call(
        unet_kernel,
        out_shape=outs,
        in_specs=[vmem] * len(operands),
        out_specs=[vmem] * len(outs),
        scratch_shapes=[
            pltpu.VMEM((6, 2, 512, 256), F32),
            pltpu.VMEM((4, 1, 512, 256), F32),
            pltpu.VMEM((2, 512, 256), F32),
            pltpu.VMEM((2, 512, 256), F32),
            pltpu.VMEM((576, 2048), BF),
            pltpu.VMEM((576, 768), BF),
            pltpu.VMEM((6, 2, 512, 256), BF),
            pltpu.VMEM((3, 512, 256), BF),
            pltpu.VMEM((512, 512), BF),
            pltpu.VMEM((1536, 256), BF),
            pltpu.VMEM((256, 1536), BF),
            pltpu.VMEM((2, 3, 512, 256), BF),
            pltpu.VMEM((256, 2048), BF),
            pltpu.VMEM((1536, 256), BF),
            pltpu.VMEM((7, 7, 32, 256), F32),
            pltpu.VMEM((7, 8, 256), F32),
            pltpu.VMEM((2, 512, 256), BF),
            pltpu.VMEM((576, 256), F32),
            pltpu.VMEM((N_EXCHANGE, 40, 256), F32),
            pltpu.VMEM((N_EXCHANGE, 40, 256), F32),
            pltpu.SemaphoreType.DMA((N_EXCHANGE,)),
            pltpu.SemaphoreType.DMA((N_EXCHANGE,)),
        ],
        compiler_params=pltpu.CompilerParams(
            collective_id=1, has_side_effects=True, vmem_limit_bytes=58 * 1024 * 1024
        ),
        name="unet",
    )(*operands)


def strip_moves():
    left, right = [], []
    for r in range(8):
        for c in range(4):
            pair = ((r + 1) // 2) % 4
            core = (r + 1) % 2
            target = (pair * 2 + c // 2) * 4 + (c % 2) * 2 + core
            right.append((r * 4 + c, target))
            left.append((r * 4 + (c + 1) % 4, target))
    return left, right


def cells_of(block):
    rows, cols, width = block.shape
    x = block.reshape(rows // 2, 2, cols // 2, 2, width)
    return jnp.transpose(x, (0, 2, 3, 1, 4)).reshape(rows // 2, cols // 2, 4 * width)


def pixels_of(cells):
    rows, cols, width = cells.shape
    x = cells.reshape(rows, cols, 2, 2, width // 4)
    return jnp.transpose(x, (0, 3, 1, 2, 4)).reshape(2 * rows, 2 * cols, width // 4)


BOTH = ("rows", "cols")


def flip_t(w):
    return jnp.swapaxes(w[::-1], 1, 2)


def per_device_strips(
    image_pair,
    noise_target,
    timesteps,
    text_pooled,
    slot_live,
    *params,
):
    weights, firsts, seconds = params[0::3], params[1::3], params[2::3]
    edge_w, low_w, high_w, down_w, up_w, cond_w, film_w, norm_w = weights
    rr, cc = lax.axis_index("rows"), lax.axis_index("cols")
    by_cell, by_tile = phase_tables()
    moves_left, moves_right = strip_moves()

    block = jnp.concatenate(
        [cells_of(image_pair[0].astype(F32)), cells_of(noise_target[0])], axis=-1
    )
    left = lax.ppermute(block[:, 16:], BOTH, moves_right)
    right = lax.ppermute(block[:, :16], BOTH, moves_left)
    strip = jnp.concatenate([left, right], axis=1).reshape(512, 36)
    img = jnp.pad(strip[:, 0:24], ((0, 0), (0, 232)))
    tgt = jnp.pad(strip[:, 24:36], ((0, 0), (0, 244)))

    pair, core = rr // 2, lax.rem(cc, 2)
    col = lax.rem(rr, 2) * 2 + cc // 2
    slot_row = jnp.where(pair == 0, 4 * (1 - core), pair)
    slot_left = slot_row * 5 + col + 1
    slot_right = slot_row * 5 + jnp.where(col == 3, 0, col + 1)
    slots = jnp.stack([slot_left, slot_right])

    shards = [low_w, high_w, down_w, up_w]
    flat = [w.astype(BF).reshape(-1, 128) for w in shards]
    sizes = [f.shape[0] for f in flat]
    every = lax.all_gather(jnp.concatenate(flat, axis=0), BOTH, axis=0, tiled=False)
    starts = np.cumsum([0] + sizes)

    def whole(k, shape):
        part = every[:, starts[k] : starts[k + 1]].reshape((8, 4) + shape)
        n = len(shape)
        order = tuple(range(2, n)) + (0, n, 1, n + 1)
        x = jnp.transpose(part, order)
        return x.reshape(shape[:-2] + (8 * shape[-2], 4 * shape[-1]))

    low = whole(0, low_w.shape)
    high = whole(1, high_w.shape)
    down = whole(2, down_w.shape)
    up = whole(3, up_w.shape)

    joined = jnp.concatenate([time_embed(timesteps).astype(BF), text_pooled], axis=-1)[0].reshape(25, -1)
    pre_own = jnp.dot(joined, cond_w.astype(BF), preferred_element_type=F32)
    pre = lax.all_gather(pre_own, BOTH, axis=1, tiled=True)
    cond = jax.nn.silu(pre).astype(BF)
    film_rows, film_cols = film_w.shape
    cond_own = lax.dynamic_slice_in_dim(cond, rr * film_rows, film_rows, 1)
    film_low = film_w.astype(BF)
    film_part = jnp.dot(cond_own, film_low, preferred_element_type=F32)
    film = lax.all_gather(lax.psum(film_part, "rows"), "cols", axis=1, tiled=True)
    own_film = jnp.take(film, slots, axis=0)

    live_slots = slot_live[0].astype(F32)
    side = np.array([32, 64, 64, 64, 32], np.float32)
    count = 3.0 * jnp.sum(live_slots * (side[:, None] * side[None, :]))
    own_live = jnp.take(live_slots.reshape(25), slots)
    small = jnp.concatenate([own_live, (2.0 / count)[None], jnp.zeros((5,), F32)])
    small = jnp.broadcast_to(small[:, None], (8, 256))

    edge_low = edge_w.astype(BF)
    inconv = jnp.swapaxes(edge_low[:, :, 0:6], 1, 2)
    head = edge_low[:, :, 6:9]
    cell_tab = by_cell.astype(jnp.bfloat16)
    tile_tab = by_tile.astype(jnp.bfloat16)

    def by_cells(w):
        x = jnp.einsum("oqpt,tcd->oqcpd", cell_tab, w)
        x = x.reshape(-1, 2, 256)
        return jnp.transpose(jnp.pad(x, ((0, 256 - x.shape[0]), (0, 0), (0, 0))), (1, 0, 2))

    def by_tiles(w):
        x = jnp.einsum("grpt,tcd->grcpd", tile_tab, w).reshape(2048, -1)
        return jnp.pad(x, ((0, 0), (0, 128 - x.shape[1])))

    outs = unet(
        img,
        tgt,
        small,
        own_film,
        norm_w,
        low,
        high,
        down,
        up,
        by_cells(inconv),
        by_tiles(flip_t(inconv)),
        by_tiles(head),
        by_cells(flip_t(head)),
    )
    dlow, dhigh, ddown, dup, dwi, dwh, fgrad, ngrad, lost, imgrad = outs

    back = (imgrad[:, 0:24] * (count)).reshape(16, 32, 24)
    back_right = lax.ppermute(back[:, :16], BOTH, [(t, s) for s, t in moves_right])
    back_left = lax.ppermute(back[:, 16:], BOTH, [(t, s) for s, t in moves_left])
    image_grad = pixels_of(jnp.concatenate([back_left, back_right], axis=1))[None]

    def fold(x, width):
        x = jnp.transpose(x, (1, 0, 2))[: 36 * width].reshape(9, 4, width, 4, 128)
        return jnp.einsum("oqpt,oqcpd->tcd", by_cell, x, precision=HIGH)

    grad_in = fold(dwi, 6)
    grad_head = fold(dwh, 3)[::-1]
    edge_local = jnp.concatenate([jnp.swapaxes(grad_in, 1, 2), jnp.swapaxes(grad_head, 1, 2)], axis=2)
    spot = (jnp.arange(25)[:, None] == slots[None, :]).astype(F32)
    film_local = jnp.dot(spot, fgrad, precision=HIGH)
    pieces = [film_local.reshape(-1), edge_local.reshape(-1), ngrad.reshape(-1), jnp.sum(lost).reshape(1)]
    lens = [p.shape[0] for p in pieces]
    total = lax.psum(jnp.concatenate(pieces), BOTH)
    ends = np.cumsum([0] + lens)
    film_sum = total[ends[0] : ends[1]].reshape(25, 1024)
    edge_sum = total[ends[1] : ends[2]].reshape(9, 128, 9)
    norm_sum = total[ends[2] : ends[3]].reshape(2, 1152)
    loss_sum = total[ends[3]]

    film_mine = lax.dynamic_slice_in_dim(film_sum, cc * film_cols, film_cols, 1)
    film_own = lax.dot_general(
        cond_own.astype(F32), film_mine, (((0,), (0,)), ((), ())), precision=HIGH
    )
    gc_part = lax.dot_general(
        film_mine, film_low.astype(F32), (((1,), (1,)), ((), ())), precision=HIGH
    )
    gc = lax.psum_scatter(gc_part, "cols", scatter_dimension=1, tiled=True) * silu_grad(pre_own)
    cond_grad = lax.dot_general(joined.astype(F32), gc, (((0,), (0,)), ((), ())), precision=HIGH)

    def dealt(g, shape):
        n = len(shape)
        lead = shape[:-2]
        x = g.reshape(lead + (8, shape[-2], 4, shape[-1]))
        m = len(lead)
        x = jnp.transpose(x, (m, m + 2) + tuple(range(m)) + (m + 1, m + 3))
        return x.reshape(32, -1, 128)

    packed = jnp.concatenate(
        [dealt(g, w.shape) for g, w in zip((dlow, dhigh, ddown, dup), shards)], axis=1
    )
    mine = lax.psum_scatter(packed, BOTH, scatter_dimension=0, tiled=False).astype(F32)
    own = [mine[starts[k] : starts[k + 1]].reshape(w.shape) for k, w in enumerate(shards)]
    grads = (edge_sum, own[0], own[1], own[2], own[3], cond_grad, film_own, norm_sum)
    results, clip_norm = lamb(weights, firsts, seconds, grads)
    return tuple(results) + (loss_sum, count, clip_norm, image_grad)


def lamb(weights, firsts, seconds, grads):
    sharded = (1, 2, 3, 4, 5, 6)
    stacked = (1, 2)
    owned_sq = sum((jnp.sum(grads[k] * grads[k]) for k in sharded))
    shared_sq = sum((jnp.sum(grads[k] * grads[k]) for k in range(8) if k not in sharded))
    clip_norm = jnp.sqrt(lax.psum(owned_sq, BOTH) + shared_sq)
    factor = jnp.minimum(1.0, CLIP_AT / clip_norm)
    clipped, moments, updates = ([], [], [])
    for k in range(8):
        grad = grads[k] * factor
        first_new = BETA_ONE * firsts[k] + (1.0 - BETA_ONE) * grad
        second_new = BETA_TWO * seconds[k] + (1.0 - BETA_TWO) * grad * grad
        first_hat = first_new / (1.0 - BETA_ONE**STEP)
        second_hat = second_new / (1.0 - BETA_TWO**STEP)
        clipped.append(grad)
        moments.append(second_new)
        updates.append(first_hat / (jnp.sqrt(second_hat) + EPS_ADAM) + DECAY * weights[k])

    def matrix_squares(values, k):
        if k in stacked:
            return jnp.sum(values * values, axis=tuple(range(1, values.ndim)))
        return jnp.sum(values * values).reshape(1)

    sums = lax.psum(
        jnp.stack(
            [
                jnp.concatenate([matrix_squares(weights[k], k) for k in sharded]),
                jnp.concatenate([matrix_squares(updates[k], k) for k in sharded]),
            ]
        ),
        BOTH,
    )
    ratios = jnp.sqrt(sums[0]) / jnp.sqrt(sums[1])
    position = 0
    results = []
    for k in range(8):
        if k in sharded:
            span = weights[k].shape[0] if k in stacked else 1
            ratio = ratios[position : position + span]
            position += span
            ratio = (
                ratio.reshape((span,) + (1,) * (weights[k].ndim - 1)) if k in stacked else ratio[0]
            )
        elif k == 0:
            part = (jnp.arange(9) < 6)[None, None, :]
            other = jnp.logical_not(part)
            weight_sq_two = weights[k] * weights[k]
            update_sq_two = updates[k] * updates[k]
            ratio_in = jnp.sqrt(jnp.sum(jnp.where(part, weight_sq_two, 0.0))) / jnp.sqrt(
                jnp.sum(jnp.where(part, update_sq_two, 0.0))
            )
            ratio_out = jnp.sqrt(jnp.sum(jnp.where(other, weight_sq_two, 0.0))) / jnp.sqrt(
                jnp.sum(jnp.where(other, update_sq_two, 0.0))
            )
            ratio = jnp.where(part, ratio_in, ratio_out)
        else:
            ratio = jnp.sqrt(jnp.sum(weights[k] * weights[k])) / jnp.sqrt(
                jnp.sum(updates[k] * updates[k])
            )
        results.extend([clipped[k], moments[k], weights[k] - RATE * ratio * updates[k]])
    return results, clip_norm


def solution(mesh):
    strips = mesh.shape["rows"] == 8 and mesh.shape["cols"] == 4
    placed = (
        P(None, "rows", "cols", None),
        P(None, "rows", "cols", None),
        P(),
        P(),
        P(),
        P(),
        P(),
        P(),
        P(None, None, "rows", "cols"),
        P(None, None, "rows", "cols"),
        P(None, None, "rows", "cols"),
        P(None, None, "rows", "cols"),
        P(None, None, "rows", "cols"),
        P(None, None, "rows", "cols"),
        P(None, "rows", "cols"),
        P(None, "rows", "cols"),
        P(None, "rows", "cols"),
        P(None, "rows", "cols"),
        P(None, "rows", "cols"),
        P(None, "rows", "cols"),
        P(None, ("rows", "cols")),
        P(None, ("rows", "cols")),
        P(None, ("rows", "cols")),
        P("rows", "cols"),
        P("rows", "cols"),
        P("rows", "cols"),
        P(),
        P(),
        P(),
    )
    return jax.shard_map(
        per_device_strips if strips else per_device,
        mesh=mesh,
        in_specs=placed,
        out_specs=(
            P(),
            P(),
            P(),
            P(None, None, "rows", "cols"),
            P(None, None, "rows", "cols"),
            P(None, None, "rows", "cols"),
            P(None, None, "rows", "cols"),
            P(None, None, "rows", "cols"),
            P(None, None, "rows", "cols"),
            P(None, "rows", "cols"),
            P(None, "rows", "cols"),
            P(None, "rows", "cols"),
            P(None, "rows", "cols"),
            P(None, "rows", "cols"),
            P(None, "rows", "cols"),
            P(None, ("rows", "cols")),
            P(None, ("rows", "cols")),
            P(None, ("rows", "cols")),
            P("rows", "cols"),
            P("rows", "cols"),
            P("rows", "cols"),
            P(),
            P(),
            P(),
            P(),
            P(),
            P(),
            P(None, "rows", "cols", None),
        ),
        check_vma=False,
    )
```

```python
import math

import jax
import jax.numpy as jnp
import numpy as np
from jax import lax
from jax.experimental import pallas as pl
from jax.experimental.pallas import tpu as pltpu
from jax.sharding import PartitionSpec as P

SLOT = 64
SLOTS = 5
C1 = 128
C2 = 256
GROUPS = 32
TEMB = 128
STEP = 10


HIGH = lax.Precision.HIGHEST
EPS_NORM = 1e-05
CLIP_AT = 0.05
RATE = 0.5
BETA_ONE = 0.9
BETA_TWO = 0.999
EPS_ADAM = 1e-06
DECAY = 0.01


def entering(part, axis, combine, identity, reverse):
    count = lax.axis_size(axis)
    place = lax.axis_index(axis)
    ahead = count - 1 - place if reverse else place
    gathered = jax.tree.map(lambda a: lax.all_gather(a, axis), part)
    state = jax.tree.map(lambda a, e: jnp.zeros_like(a) + jnp.asarray(e, a.dtype), part, identity)

    def one(turn, state):
        source = count - 1 - turn if reverse else turn
        return combine(
            state, jax.tree.map(lambda a: lax.dynamic_index_in_dim(a, source, 0, False), gathered)
        )

    return lax.fori_loop(0, ahead, one, state)


def padded_2(block, sides, width):
    for axis, dim in sides:
        count = lax.axis_size(axis)
        forward = [(i, i + 1) for i in range(count - 1)]
        backward = [(target, source) for source, target in forward]
        low = lax.ppermute(
            lax.slice_in_dim(block, block.shape[dim] - width, None, axis=dim), axis, forward
        )
        high = lax.ppermute(lax.slice_in_dim(block, 0, width, axis=dim), axis, backward)
        block = jnp.concatenate([low, block, high], axis=dim)
    return block


def time_embed(steps):
    half = TEMB // 2
    freq = jnp.exp(-math.log(10000.0) * jnp.arange(half, dtype=jnp.float32) / half)
    angle = steps.astype(jnp.float32)[..., None] * freq
    return jnp.concatenate([jnp.sin(angle), jnp.cos(angle)], axis=-1)


def silu_grad(values):
    sigma = jax.nn.sigmoid(values)
    return sigma * (1.0 + values * (1.0 - sigma))


def tap_masks(rows, cols, slot):
    half = slot // 2
    row_pos = lax.axis_index("rows") * rows + jnp.arange(rows)
    col_pos = lax.axis_index("cols") * cols + jnp.arange(cols)
    row_ok = [
        (row_pos + offset + half) // slot == (row_pos + half) // slot for offset in (-1, 0, 1)
    ]
    col_ok = [
        (col_pos + offset + half) // slot == (col_pos + half) // slot for offset in (-1, 0, 1)
    ]
    return [
        (row_ok[tap // 3][:, None] & col_ok[tap % 3][None, :]).astype(jnp.bfloat16)
        for tap in range(9)
    ]


def slot_level(rows, cols, slot, size):
    half = slot // 2
    labels = jnp.arange(SLOTS)
    row_pos = lax.axis_index("rows") * rows + jnp.arange(rows)
    col_pos = lax.axis_index("cols") * cols + jnp.arange(cols)
    row_map = (((row_pos + half) // slot)[:, None] == labels[None, :]).astype(jnp.float32)
    col_map = (((col_pos + half) // slot)[:, None] == labels[None, :]).astype(jnp.float32)
    every = (jnp.arange(size) + half) // slot
    side = jnp.sum((every[:, None] == labels[None, :]).astype(jnp.float32), axis=0)
    return (row_map, col_map, side[:, None] * side[None, :])


def to_slots(values, level):
    return jnp.einsum("nhwk,ha,wb->nabk", values, level[0], level[1], precision=HIGH)


def to_pixels(table, level):
    return jnp.einsum("nabk,ha,wb->nhwk", table, level[0], level[1], precision=HIGH)


def add_pair(earlier, later):
    return (earlier[0] + later[0], earlier[1] + later[1])


def slot_total(tables):
    empty = (jnp.zeros_like(tables[0]), jnp.zeros_like(tables[1]))
    before = entering(tables, ("rows", "cols"), add_pair, empty, False)
    after = entering(tables, ("rows", "cols"), add_pair, empty, True)
    return (before[0] + tables[0] + after[0], before[1] + tables[1] + after[1])


def pad_rim(values):
    return padded_2(values, (("rows", 1), ("cols", 2)), 1)


def tap_patch(padded, masks, tap, stride):
    rows = padded.shape[1] - 2
    cols = padded.shape[2] - 2
    row_off, col_off = (tap // 3, tap % 3)
    patch = padded[:, row_off : row_off + rows : stride, col_off : col_off + cols : stride, :]
    return patch * masks[tap][::stride, ::stride][None, :, :, None]


def conv_taps(padded, weight, masks, stride):
    total = None
    for tap in range(9):
        term = jnp.einsum(
            "nhwc,cd->nhwd",
            tap_patch(padded, masks, tap, stride),
            weight[tap],
            preferred_element_type=jnp.float32,
        )
        total = term if total is None else total + term
    return total


def conv_weight_grad(padded, grad_out, masks, stride):
    return jnp.stack(
        [
            jnp.einsum(
                "nhwc,nhwd->cd",
                tap_patch(padded, masks, tap, stride),
                grad_out,
                preferred_element_type=jnp.float32,
            )
            for tap in range(9)
        ]
    )


def conv_input_grad(grad_out, weight, masks, stride):
    spread = grad_out
    if stride == 2:
        canvases, rows, cols, width = grad_out.shape
        spread = jnp.stack([grad_out, jnp.zeros_like(grad_out)], axis=2).reshape(
            canvases, 2 * rows, cols, width
        )
        spread = jnp.stack([spread, jnp.zeros_like(spread)], axis=3).reshape(
            canvases, 2 * rows, 2 * cols, width
        )
    flipped = jnp.swapaxes(weight[::-1], 1, 2)
    padded = padded_2(spread, (("rows", 1), ("cols", 2)), 1)
    return conv_taps(padded, flipped, masks, 1)


def norm_forward(values, gain, bias, scale, shift, level):
    count_n, rows, cols, width = values.shape
    grouped = values.reshape(count_n, rows, cols, GROUPS, width // GROUPS)
    total, squares = slot_total(
        (
            to_slots(jnp.sum(grouped, axis=4), level),
            to_slots(jnp.sum(grouped * grouped, axis=4), level),
        )
    )
    count = level[2][None, :, :, None] * (width // GROUPS)
    mean = total / count
    var = squares / count - mean * mean
    inverse = lax.rsqrt(var + EPS_NORM)
    mean_pix = to_pixels(mean, level)
    inv_pix = to_pixels(inverse, level)
    hat = ((grouped - mean_pix[..., None]) * inv_pix[..., None]).reshape(values.shape)
    normed = hat * gain + bias
    if scale is None:
        return (normed, (hat, inv_pix, normed, None))
    factor = 1.0 + to_pixels(scale, level)
    return (normed * factor + to_pixels(shift, level), (hat, inv_pix, normed, factor))


def norm_backward(grad_out, kept, gain, level):
    hat, inv_pix, normed, factor = kept
    count_n, rows, cols, width = hat.shape
    if factor is None:
        film_grad = None
        grad_normed = grad_out
    else:
        film_grad = jnp.concatenate(
            [to_slots(grad_out * normed, level), to_slots(grad_out, level)], axis=-1
        )
        grad_normed = grad_out * factor
    grad_gain = jnp.sum(grad_normed * hat, axis=(0, 1, 2))
    grad_bias = jnp.sum(grad_normed, axis=(0, 1, 2))
    shape = (count_n, rows, cols, GROUPS, width // GROUPS)
    grad_hat = (grad_normed * gain).reshape(shape)
    grouped_hat = hat.reshape(shape)
    first, second = slot_total(
        (
            to_slots(jnp.sum(grad_hat, axis=4), level),
            to_slots(jnp.sum(grad_hat * grouped_hat, axis=4), level),
        )
    )
    count = level[2][None, :, :, None] * (width // GROUPS)
    mean_one = to_pixels(first / count, level)[..., None]
    mean_two = to_pixels(second / count, level)[..., None]
    grad_in = inv_pix[..., None] * (grad_hat - mean_one - grouped_hat * mean_two)
    return (grad_in.reshape(hat.shape), grad_gain, grad_bias, film_grad)


def block_forward(hidden, weights, gains, film, level, masks):
    pre_one, saved_one = norm_forward(hidden, gains[0], gains[1], None, None, level)
    rim_one = pad_rim(jax.nn.silu(pre_one).astype(jnp.bfloat16))
    conv_one = conv_taps(rim_one, weights[0], masks, 1)
    pre_two, saved_two = norm_forward(conv_one, gains[2], gains[3], film[0], film[1], level)
    rim_two = pad_rim(jax.nn.silu(pre_two).astype(jnp.bfloat16))
    out = hidden + conv_taps(rim_two, weights[1], masks, 1)
    return (out, (pre_one, saved_one, rim_one, pre_two, saved_two, rim_two))


def block_backward(grad_out, weights, gains, kept, level, masks):
    pre_one, saved_one, rim_one, pre_two, saved_two, rim_two = kept
    grad_two = grad_out.astype(jnp.bfloat16)
    weight_two = conv_weight_grad(rim_two, grad_two, masks, 1)
    grad_pre_two = conv_input_grad(grad_two, weights[1], masks, 1) * silu_grad(pre_two)
    grad_conv, gain_two, bias_two, film_grad = norm_backward(
        grad_pre_two, saved_two, gains[2], level
    )
    grad_one = grad_conv.astype(jnp.bfloat16)
    weight_one = conv_weight_grad(rim_one, grad_one, masks, 1)
    grad_pre_one = conv_input_grad(grad_one, weights[0], masks, 1) * silu_grad(pre_one)
    grad_in, gain_one, bias_one, _ = norm_backward(grad_pre_one, saved_one, gains[0], level)
    return (
        grad_out + grad_in,
        (weight_one, weight_two),
        (gain_one, bias_one, gain_two, bias_two),
        film_grad,
    )


def per_device(
    image_pair,
    noise_target,
    timesteps,
    text_pooled,
    slot_live,
    edgeconv_weight,
    edgeconv_first,
    edgeconv_second,
    convlow_weight,
    convlow_first,
    convlow_second,
    convhigh_weight,
    convhigh_first,
    convhigh_second,
    downconv_weight,
    downconv_first,
    downconv_second,
    upconv_weight,
    upconv_first,
    upconv_second,
    condproj_weight,
    condproj_first,
    condproj_second,
    filmproj_weight,
    filmproj_first,
    filmproj_second,
    normparams_weight,
    normparams_first,
    normparams_second,
):
    canvases, rows_one, cols_one = image_pair.shape[:3]
    size_full = rows_one * lax.axis_size("rows")
    level_full = slot_level(rows_one, cols_one, SLOT, size_full)
    level_half = slot_level(rows_one // 2, cols_one // 2, SLOT // 2, size_full // 2)
    by_rows = (
        lax.all_gather(convlow_weight.astype(jnp.bfloat16), "rows", axis=2, tiled=True),
        lax.all_gather(convhigh_weight.astype(jnp.bfloat16), "rows", axis=2, tiled=True),
        lax.all_gather(downconv_weight.astype(jnp.bfloat16), "rows", axis=1, tiled=True),
        lax.all_gather(upconv_weight.astype(jnp.bfloat16), "rows", axis=1, tiled=True),
        lax.all_gather(filmproj_weight.astype(jnp.bfloat16), "rows", axis=0, tiled=True),
    )
    low_convs, high_convs, down_conv, up_conv, film_full = (
        lax.all_gather(by_rows[0], "cols", axis=3, tiled=True),
        lax.all_gather(by_rows[1], "cols", axis=3, tiled=True),
        lax.all_gather(by_rows[2], "cols", axis=2, tiled=True),
        lax.all_gather(by_rows[3], "cols", axis=2, tiled=True),
        lax.all_gather(by_rows[4], "cols", axis=1, tiled=True),
    )
    joined = jnp.concatenate([time_embed(timesteps).astype(jnp.bfloat16), text_pooled], axis=-1)
    cond_full = lax.all_gather(
        condproj_weight.astype(jnp.bfloat16), ("rows", "cols"), axis=1, tiled=True
    )
    pre_cond = jnp.einsum("nabk,kf->nabf", joined, cond_full, preferred_element_type=jnp.float32)
    cond_low = jax.nn.silu(pre_cond).astype(jnp.bfloat16)
    film_all = jnp.einsum("nabk,kf->nabf", cond_low, film_full, preferred_element_type=jnp.float32)
    offsets = [0, C1, 2 * C1, 3 * C1, 4 * C1, 4 * C1 + C2, 4 * C1 + 2 * C2, 5 * C1 + 2 * C2]

    def norm_part(index, which):
        return normparams_weight[which, offsets[index] : offsets[index + 1]]

    def block_gains(index):
        return (
            norm_part(2 * index, 0),
            norm_part(2 * index, 1),
            norm_part(2 * index + 1, 0),
            norm_part(2 * index + 1, 1),
        )

    def block_film(index):
        base = (0, 2 * C1, 4 * C1)[index]
        width = (C1, C1, C2)[index]
        return (film_all[..., base : base + width], film_all[..., base + width : base + 2 * width])

    masks_one = tap_masks(rows_one, cols_one, SLOT)
    masks_two = tap_masks(rows_one // 2, cols_one // 2, SLOT // 2)
    edge_low = edgeconv_weight.astype(jnp.bfloat16)
    inconv_low = jnp.swapaxes(edge_low[:, :, 0:6], 1, 2)
    head_low = edge_low[:, :, 6:9]
    rim_in = pad_rim(image_pair)
    hidden = conv_taps(rim_in, inconv_low, masks_one, 1)
    kept_blocks = []
    for index in range(2):
        hidden, kept = block_forward(
            hidden,
            (low_convs[2 * index], low_convs[2 * index + 1]),
            block_gains(index),
            block_film(index),
            level_full,
            masks_one,
        )
        kept_blocks.append(kept)
    rim_skip = pad_rim(hidden.astype(jnp.bfloat16))
    deep, kept_deep = block_forward(
        conv_taps(rim_skip, down_conv, masks_one, 2),
        (high_convs[0], high_convs[1]),
        block_gains(2),
        block_film(2),
        level_half,
        masks_two,
    )
    upsampled = jnp.repeat(jnp.repeat(deep.astype(jnp.bfloat16), 2, axis=1), 2, axis=2)
    rim_up = pad_rim(upsampled)
    merged = conv_taps(rim_up, up_conv, masks_one, 1) + hidden
    pre_head, kept_head = norm_forward(
        merged, norm_part(6, 0), norm_part(6, 1), None, None, level_full
    )
    rim_head = pad_rim(jax.nn.silu(pre_head).astype(jnp.bfloat16))
    pred = conv_taps(rim_head, head_low, masks_one, 1)
    live_slots = slot_live.astype(jnp.float32)
    live = to_pixels(live_slots[..., None], level_full)
    count = 3.0 * jnp.sum(live_slots * level_full[2][None, :, :])
    diff = pred - noise_target
    loss_local = jnp.sum(live * diff * diff)
    grad_pred = (2.0 * live * diff / count).astype(jnp.bfloat16)
    grad_head = conv_weight_grad(rim_head, grad_pred, masks_one, 1)
    grad_act = conv_input_grad(grad_pred, head_low, masks_one, 1) * silu_grad(pre_head)
    grad_merged, head_gain, head_bias, _ = norm_backward(
        grad_act, kept_head, norm_part(6, 0), level_full
    )
    merged_low = grad_merged.astype(jnp.bfloat16)
    grad_upconv = conv_weight_grad(rim_up, merged_low, masks_one, 1)
    grad_up = conv_input_grad(merged_low, up_conv, masks_one, 1)
    grad_deep = grad_up.reshape(canvases, rows_one // 2, 2, cols_one // 2, 2, C2).sum(axis=(2, 4))
    grad_down, deep_convs, deep_norms, deep_film = block_backward(
        grad_deep, (high_convs[0], high_convs[1]), block_gains(2), kept_deep, level_half, masks_two
    )
    down_low = grad_down.astype(jnp.bfloat16)
    grad_downconv = conv_weight_grad(rim_skip, down_low, masks_one, 2)
    grad_hidden = grad_merged + conv_input_grad(down_low, down_conv, masks_one, 2)
    block_convs = [None, None]
    block_norms = [None, None]
    block_films = [None, None]
    for index in (1, 0):
        grad_hidden, block_convs[index], block_norms[index], block_films[index] = block_backward(
            grad_hidden,
            (low_convs[2 * index], low_convs[2 * index + 1]),
            block_gains(index),
            kept_blocks[index],
            level_full,
            masks_one,
        )
    hidden_low = grad_hidden.astype(jnp.bfloat16)
    grad_inconv = conv_weight_grad(rim_in, hidden_low, masks_one, 1)
    image_grad = conv_input_grad(hidden_low, inconv_low, masks_one, 1) * count
    all_norms = block_norms + [deep_norms]
    gain_vector = jnp.concatenate([part[k] for part in all_norms for k in (0, 2)] + [head_gain])
    bias_vector = jnp.concatenate([part[k] for part in all_norms for k in (1, 3)] + [head_bias])
    film_grads = jnp.concatenate([block_films[0], block_films[1], deep_film], axis=-1)
    edge_local = jnp.concatenate([jnp.swapaxes(grad_inconv, 1, 2), grad_head], axis=2)
    film_sum, edge_sum, norm_sum, loss_sum = lax.psum(
        (film_grads, edge_local, jnp.stack([gain_vector, bias_vector]), loss_local),
        ("rows", "cols"),
    )
    grad_film_full = jnp.einsum(
        "nabk,nabf->kf", cond_low.astype(jnp.float32), film_sum, precision=HIGH
    )
    grad_cond = jnp.einsum(
        "nabf,kf->nabk", film_sum, film_full.astype(jnp.float32), precision=HIGH
    ) * silu_grad(pre_cond)
    grad_cond_full = jnp.einsum(
        "nabk,nabf->kf", joined.astype(jnp.float32), grad_cond, precision=HIGH
    )
    film_rows, film_cols = filmproj_weight.shape
    film_own = lax.dynamic_slice_in_dim(
        grad_film_full, lax.axis_index("rows") * film_rows, film_rows, 0
    )
    film_own = lax.dynamic_slice_in_dim(film_own, lax.axis_index("cols") * film_cols, film_cols, 1)
    cond_cols = condproj_weight.shape[1]
    cond_own = lax.dynamic_slice_in_dim(
        grad_cond_full, lax.axis_index(("rows", "cols")) * cond_cols, cond_cols, 1
    )
    by_cols = (
        lax.psum_scatter(
            jnp.stack(
                [block_convs[0][0], block_convs[0][1], block_convs[1][0], block_convs[1][1]]
            ).astype(jnp.bfloat16),
            "cols",
            scatter_dimension=3,
            tiled=True,
        ).astype(jnp.float32),
        lax.psum_scatter(
            jnp.stack([deep_convs[0], deep_convs[1]]).astype(jnp.bfloat16),
            "cols",
            scatter_dimension=3,
            tiled=True,
        ).astype(jnp.float32),
        lax.psum_scatter(
            grad_downconv.astype(jnp.bfloat16), "cols", scatter_dimension=2, tiled=True
        ).astype(jnp.float32),
        lax.psum_scatter(
            grad_upconv.astype(jnp.bfloat16), "cols", scatter_dimension=2, tiled=True
        ).astype(jnp.float32),
    )
    lowconv_own, highconv_own, downconv_own, upconv_own = (
        lax.psum_scatter(
            by_cols[0].astype(jnp.bfloat16), "rows", scatter_dimension=2, tiled=True
        ).astype(jnp.float32),
        lax.psum_scatter(
            by_cols[1].astype(jnp.bfloat16), "rows", scatter_dimension=2, tiled=True
        ).astype(jnp.float32),
        lax.psum_scatter(
            by_cols[2].astype(jnp.bfloat16), "rows", scatter_dimension=1, tiled=True
        ).astype(jnp.float32),
        lax.psum_scatter(
            by_cols[3].astype(jnp.bfloat16), "rows", scatter_dimension=1, tiled=True
        ).astype(jnp.float32),
    )
    weights = (
        edgeconv_weight,
        convlow_weight,
        convhigh_weight,
        downconv_weight,
        upconv_weight,
        condproj_weight,
        filmproj_weight,
        normparams_weight,
    )
    firsts = (
        edgeconv_first,
        convlow_first,
        convhigh_first,
        downconv_first,
        upconv_first,
        condproj_first,
        filmproj_first,
        normparams_first,
    )
    seconds = (
        edgeconv_second,
        convlow_second,
        convhigh_second,
        downconv_second,
        upconv_second,
        condproj_second,
        filmproj_second,
        normparams_second,
    )
    grads = (
        edge_sum,
        lowconv_own,
        highconv_own,
        downconv_own,
        upconv_own,
        cond_own,
        film_own,
        norm_sum,
    )
    sharded = (1, 2, 3, 4, 5, 6)
    stacked = (1, 2)
    owned_sq = sum((jnp.sum(grads[k] * grads[k]) for k in sharded))
    shared_sq = sum((jnp.sum(grads[k] * grads[k]) for k in range(8) if k not in sharded))
    clip_norm = jnp.sqrt(lax.psum(owned_sq, ("rows", "cols")) + shared_sq)
    factor = jnp.minimum(1.0, CLIP_AT / clip_norm)
    clipped, moments, updates = ([], [], [])
    for k in range(8):
        grad = grads[k] * factor
        first_new = BETA_ONE * firsts[k] + (1.0 - BETA_ONE) * grad
        second_new = BETA_TWO * seconds[k] + (1.0 - BETA_TWO) * grad * grad
        first_hat = first_new / (1.0 - BETA_ONE**STEP)
        second_hat = second_new / (1.0 - BETA_TWO**STEP)
        clipped.append(grad)
        moments.append(second_new)
        updates.append(first_hat / (jnp.sqrt(second_hat) + EPS_ADAM) + DECAY * weights[k])

    def matrix_squares(values, k):
        if k in stacked:
            return jnp.sum(values * values, axis=tuple(range(1, values.ndim)))
        return jnp.sum(values * values).reshape(1)

    weight_sq, update_sq = lax.psum(
        (
            jnp.concatenate([matrix_squares(weights[k], k) for k in sharded]),
            jnp.concatenate([matrix_squares(updates[k], k) for k in sharded]),
        ),
        ("rows", "cols"),
    )
    ratios = jnp.sqrt(weight_sq) / jnp.sqrt(update_sq)
    position = 0
    results = []
    for k in range(8):
        if k in sharded:
            span = weights[k].shape[0] if k in stacked else 1
            ratio = ratios[position : position + span]
            position += span
            ratio = (
                ratio.reshape((span,) + (1,) * (weights[k].ndim - 1)) if k in stacked else ratio[0]
            )
        elif k == 0:
            part = (jnp.arange(9) < 6)[None, None, :]
            other = jnp.logical_not(part)
            weight_sq_two = weights[k] * weights[k]
            update_sq_two = updates[k] * updates[k]
            ratio_in = jnp.sqrt(jnp.sum(jnp.where(part, weight_sq_two, 0.0))) / jnp.sqrt(
                jnp.sum(jnp.where(part, update_sq_two, 0.0))
            )
            ratio_out = jnp.sqrt(jnp.sum(jnp.where(other, weight_sq_two, 0.0))) / jnp.sqrt(
                jnp.sum(jnp.where(other, update_sq_two, 0.0))
            )
            ratio = jnp.where(part, ratio_in, ratio_out)
        else:
            ratio = jnp.sqrt(jnp.sum(weights[k] * weights[k])) / jnp.sqrt(
                jnp.sum(updates[k] * updates[k])
            )
        results.extend([clipped[k], moments[k], weights[k] - RATE * ratio * updates[k]])
    return (
        results[0],
        results[1],
        results[2],
        results[3],
        results[4],
        results[5],
        results[6],
        results[7],
        results[8],
        results[9],
        results[10],
        results[11],
        results[12],
        results[13],
        results[14],
        results[15],
        results[16],
        results[17],
        results[18],
        results[19],
        results[20],
        results[21],
        results[22],
        results[23],
        loss_sum,
        count,
        clip_norm,
        image_grad,
    )


F32 = jnp.float32
BF = jnp.bfloat16
MESH = pl.DeviceIdType.MESH
NORM_AT = (0, 128, 256, 384, 512, 768, 1024, 1152)
FILM_AT = {1: 0, 3: 256, 5: 512}
ROW_OF = (0, 1, -1, 2)
COL_OF = (-1, 0, 1, 2)
N_EXCHANGE = 20


def phase_tables():
    by_cell = np.zeros((9, 4, 4, 9), np.float32)
    by_tile = np.zeros((4, 4, 4, 9), np.float32)
    for out in range(4):
        cp_out, rp_out = out // 2, out % 2
        for cell in range(9):
            for inp in range(4):
                a = 2 * (cell // 3 - 1) + inp % 2 - rp_out + 1
                b = 2 * (cell % 3 - 1) + inp // 2 - cp_out + 1
                if 0 <= a <= 2 and 0 <= b <= 2:
                    by_cell[cell, inp, out, 3 * a + b] = 1.0
        for g in range(4):
            for r in range(4):
                a = ROW_OF[r] - rp_out + 1
                b = COL_OF[g] - cp_out + 1
                if 0 <= a <= 2 and 0 <= b <= 2:
                    by_tile[g, r, out, 3 * a + b] = 1.0
    return by_cell, by_tile


def unet_kernel(
    strip_ref,
    small_ref,
    film_ref,
    norm_ref,
    low_ref,
    high_ref,
    down_ref,
    up_ref,
    wi_ref,
    wit_ref,
    wh_ref,
    wht_ref,
    dlow_ref,
    dhigh_ref,
    ddown_ref,
    dup_ref,
    part_ref,
    fgrad_ref,
    imgrad_ref,
    img_ref,
    tgt_ref,
    dwi_ref,
    dwh_ref,
    ngrad_ref,
    full_ref,
    half_ref,
    work_ref,
    grad_ref,
    wide_ref,
    thin_ref,
    act_ref,
    acth_ref,
    turn_ref,
    wc_ref,
    wr_ref,
    wu_ref,
    wut_ref,
    wd_ref,
    coef_ref,
    rows_ref,
    patch_ref,
    ext_ref,
    send_ref,
    recv_ref,
    send_sem,
    recv_sem,
):
    rr = lax.axis_index("rows")
    cc = lax.axis_index("cols")
    core = lax.rem(cc, 2)
    partner = cc + 1 - 2 * core
    halo = rr >= 2
    split = jnp.logical_and(lax.rem(rr, 2) == 1, cc >= 2)

    def flag(cond):
        return jnp.where(cond, 1.0, 0.0).astype(F32)

    f_halo = flag(halo)
    f_core1 = flag(core == 1)
    f_core0 = 1.0 - f_core1
    f_top = f_halo * f_core1
    f_bot = f_halo * f_core0
    f_split = flag(split)
    f_joined = 1.0 - f_split

    place = lax.broadcasted_iota(jnp.int32, (32, 256), 0)
    lo_mask = jnp.where(place == 0, 0.0, jnp.where(place == 16, f_joined, 1.0))
    hi_mask = jnp.where(place == 31, 0.0, jnp.where(place == 15, f_joined, 1.0))

    barrier = pltpu.get_barrier_semaphore()
    pl.semaphore_signal(barrier, inc=1, device_id={"cols": partner}, device_id_type=MESH)
    pl.semaphore_wait(barrier, 1)

    def before(x):
        return pltpu.roll(x, 1, 0) * lo_mask

    def after(x):
        return pltpu.roll(x, 31, 0) * hi_mask

    def at(i):
        return pl.ds(pl.multiple_of(i * 32, 32), 32)

    def loop(body, init=0, count=16):
        return lax.fori_loop(0, count, body, init)

    def dot(a, b):
        return jnp.dot(a, b, preferred_element_type=F32)

    def dot_nt(a, b):
        return lax.dot_general(a, b, (((1,), (1,)), ((), ())), preferred_element_type=F32)

    def sigmoid(z):
        return 0.5 * jnp.tanh(0.5 * z) + 0.5

    def double(v):
        return jnp.concatenate([v, v], axis=1)


    def copy_of(e):
        return pltpu.make_async_remote_copy(
            src_ref=send_ref.at[e],
            dst_ref=recv_ref.at[e],
            send_sem=send_sem.at[e],
            recv_sem=recv_sem.at[e],
            device_id={"cols": partner},
            device_id_type=MESH,
        )

    def send(e, row, stats=None):
        send_ref[e, 0:32, :] = row
        send_ref[e, 32:40, :] = jnp.zeros((8, 256), F32) if stats is None else stats
        copy_of(e).start()

    def arrive(e):
        copy_of(e).wait()

    def edge_full(ref):
        low = f_core0 * ref[0, 480:512, 128:256] + f_core1 * ref[0, 0:32, 0:128]
        high = f_core0 * ref[1, 480:512, 128:256] + f_core1 * ref[1, 0:32, 0:128]
        return jnp.concatenate([low, high], axis=1)

    def edge_cell(ref):
        return f_core0 * ref[480:512, :] + f_core1 * ref[0:32, :]

    def edge(ref, planes):
        return edge_full(ref) if planes == 2 else edge_cell(ref.at[0])


    def halves(x):
        return x[0:8] + x[8:16], x[16:24] + x[24:32]

    def gathered(sums, planes):
        rows = []
        for s in sums:
            row = jnp.sum(s, axis=0, keepdims=True)
            rows.append(double(row[:, 0:128] + row[:, 128:256]) if planes == 2 else row)
        return jnp.concatenate(rows + [jnp.zeros((4, 256), F32)], axis=0)

    zero8 = jnp.zeros((8, 256), F32)

    def stats_of(x_ref, planes):
        def body(i, carry):
            s_l, s_r, q_l, q_r = carry
            for p in range(planes):
                x = x_ref[p, at(i), :]
                a, b = halves(x)
                c, d = halves(x * x)
                s_l, s_r, q_l, q_r = s_l + a, s_r + b, q_l + c, q_r + d
            return s_l, s_r, q_l, q_r

        return gathered(loop(body, (zero8,) * 4), planes)

    def over_slot(block, planes):
        swapped = jnp.concatenate(
            [block[1:2], block[0:1], block[3:4], block[2:3], block[4:8]], axis=0
        )
        x = block + f_joined * swapped
        lane = lax.broadcasted_iota(jnp.int32, (8, 256), 1)
        step = 1
        while step < (4 if planes == 2 else 8):
            up = pltpu.roll(x, 256 - step, 1)
            down = pltpu.roll(x, step, 1)
            x = x + jnp.where(lax.rem(lane, 2 * step) < step, up, down)
            step *= 2
        size = 16.0 if planes == 2 else 8.0
        count = (16.0 + 16.0 * f_halo) * (16.0 + 16.0 * f_joined) * size
        return x / count

    def spread(two):
        return jnp.concatenate(
            [
                jnp.broadcast_to(two[0:1], (16, 256)),
                jnp.broadcast_to(two[1:2], (16, 256)),
            ],
            axis=0,
        )

    def norm_row(k, which):
        width = NORM_AT[k + 1] - NORM_AT[k] if k < 6 else 128
        row = norm_ref[which : which + 1, NORM_AT[k] : NORM_AT[k] + width]
        return double(row) if width == 128 else row

    def film_rows(k, which):
        if k not in FILM_AT:
            return jnp.zeros((2, 256), F32)
        width = 256 if k == 5 else 128
        base = FILM_AT[k] + which * width
        two = film_ref[0:2, base : base + width]
        return double(two) if width == 128 else two

    def norm_ready(k, stats, e, planes):
        total = over_slot(stats + f_halo * recv_ref[e, 32:40, :], planes)
        mean = total[0:2]
        var = total[2:4] - mean * mean
        inverse = lax.rsqrt(var + EPS_NORM)
        gain, bias = norm_row(k, 0), norm_row(k, 1)
        factor = 1.0 + film_rows(k, 0)
        slope = inverse * gain * factor
        coef_ref[k, 0] = spread(slope)
        coef_ref[k, 1] = spread((bias - mean * inverse * gain) * factor + film_rows(k, 1))
        coef_ref[k, 2] = spread(mean)
        coef_ref[k, 3] = spread(inverse)
        rows_ref[k, 0:2, :] = mean
        rows_ref[k, 2:4, :] = inverse

    def activated(x, k):
        z = x * coef_ref[k, 0] + coef_ref[k, 1]
        return z * sigmoid(z)


    def put_wide(i, even, odd):
        for t, g in enumerate((before(odd), even, odd, after(even))):
            b = g.astype(BF)
            wide_ref[at(i + 1), 512 * t : 512 * t + 256] = b
            wide_ref[at(i + 2), 512 * t + 256 : 512 * t + 384] = b[:, 128:256]
            wide_ref[at(i), 512 * t + 384 : 512 * t + 512] = b[:, 0:128]

    def put_wide_edge(row):
        even, odd = row[:, 0:128], row[:, 128:256]
        lo, hi = lo_mask[:, 0:128], hi_mask[:, 0:128]
        for t, g in enumerate((pltpu.roll(odd, 1, 0) * lo, even, odd, pltpu.roll(even, 31, 0) * hi)):
            wide_ref[32:64, 512 * t + 256 : 512 * t + 384] = (g * f_top).astype(BF)
            wide_ref[512:544, 512 * t + 384 : 512 * t + 512] = (g * f_bot).astype(BF)

    def put_thin(i, x):
        for t, g in enumerate((before(x), x, after(x))):
            thin_ref[at(i + 1), 256 * t : 256 * t + 256] = g.astype(BF)

    def put_thin_edge(row):
        for t, g in enumerate((before(row), row, after(row))):
            thin_ref[0:32, 256 * t : 256 * t + 256] = (g * f_top).astype(BF)
            thin_ref[544:576, 256 * t : 256 * t + 256] = (g * f_bot).astype(BF)

    def keep_wide(slot):
        act_ref[slot, 0] = wide_ref[32:544, 512:768]
        act_ref[slot, 1] = wide_ref[32:544, 1024:1280]

    def keep_thin(slot):
        acth_ref[slot] = thin_ref[32:544, 256:512]

    def turn_wide(slot):
        turn_ref[0:256, :] = act_ref[slot, 0].T
        turn_ref[256:512, :] = act_ref[slot, 1].T


    def load_wc(index):
        for b in range(3):
            for r in range(4):
                for rp in range(2):
                    a = ROW_OF[r] - rp + 1
                    if 0 <= a <= 2:
                        wc_ref[
                            b * 512 + r * 128 : b * 512 + r * 128 + 128, rp * 128 : rp * 128 + 128
                        ] = low_ref[index, 3 * a + b]

    def load_wr(index):
        for b in range(3):
            for r in range(4):
                for rp in range(2):
                    a = ROW_OF[r] - rp + 1
                    if 0 <= a <= 2:
                        wr_ref[
                            rp * 128 : rp * 128 + 128, b * 512 + r * 128 : b * 512 + r * 128 + 128
                        ] = low_ref[index, 8 - 3 * a - b]

    def taps_of(parity, d):
        if parity == 0:
            return {-1: (0,), 0: (1, 2)}.get(d, ())
        return {0: (0, 1), 1: (2,)}.get(d, ())

    def load_up():
        for cp in range(2):
            for rp in range(2):
                for di in (-1, 0, 1):
                    for dj in (-1, 0, 1):
                        taps = [3 * a + b for a in taps_of(rp, di) for b in taps_of(cp, dj)]
                        if not taps:
                            continue
                        total = up_ref[taps[0]].astype(F32)
                        for t in taps[1:]:
                            total = total + up_ref[t].astype(F32)
                        low = total.astype(BF)
                        at_k = (dj + 1 - cp) * 256
                        wu_ref[cp, di + 1, at_k : at_k + 256, rp * 128 : rp * 128 + 128] = low
                        row = ROW_OF.index(rp - 2 * di)
                        col = COL_OF.index(cp - 2 * dj)
                        wut_ref[:, col * 512 + row * 128 : col * 512 + row * 128 + 128] = low

    def load_down():
        for b in range(3):
            for r in range(3):
                a = ROW_OF[r] + 1
                wd_ref[b * 512 + r * 128 : b * 512 + r * 128 + 128, :] = down_ref[3 * a + b]


    def conv_low(out, weight_nt=False):
        for cp in range(2):
            left = wide_ref[32:544, cp * 512 : cp * 512 + 1536]
            out(cp, dot_nt(left, wr_ref[...]) if weight_nt else dot(left, wc_ref[...]))

    def conv_high(index):
        total = None
        for a in range(3):
            term = dot(
                thin_ref[32 * a : 32 * a + 512, :],
                high_ref[index, 3 * a : 3 * a + 3].reshape(768, 256),
            )
            total = term if total is None else total + term
        return total

    def conv_high_back(index):
        total = None
        for a in range(3):
            for b in range(3):
                term = dot_nt(
                    thin_ref[32 * a : 32 * a + 512, b * 256 : b * 256 + 256],
                    high_ref[index, 8 - 3 * a - b],
                )
                total = term if total is None else total + term
        return total

    def grad_low(index, slot):
        turn_wide(slot)
        for b in range(3):
            block = dot(turn_ref[0:256, :], wide_ref[32:544, b * 512 : b * 512 + 512]) + dot(
                turn_ref[256:512, :], wide_ref[32:544, b * 512 + 512 : b * 512 + 1024]
            )
            for a in range(3):
                first = ROW_OF.index(a - 1) * 128
                second = ROW_OF.index(a) * 128
                dlow_ref[index, 8 - 3 * a - b] = (
                    block[0:128, first : first + 128] + block[128:256, second : second + 128]
                ).astype(dlow_ref.dtype)

    def grad_high(index, slot):
        turn_ref[0:256, :] = acth_ref[slot].T
        for a in range(3):
            block = dot(turn_ref[0:256, :], thin_ref[32 * a : 32 * a + 512, :])
            for b in range(3):
                dhigh_ref[index, 8 - 3 * a - b] = block[:, b * 256 : b * 256 + 256].astype(
                    dhigh_ref.dtype
                )


    def put_patch(slot, source, row, lanes):
        ext_ref[0:32, :] = row * f_top
        ext_ref[544:576, :] = row * f_bot

        def fill(i, carry):
            ext_ref[at(i + 1), :] = source[at(i), :]
            return carry

        loop(fill)

        def body(i, carry):
            total = None
            for di in (-1, 0, 1):
                x = ext_ref[at(i + 1 + di), :]
                for dj, g in enumerate((before(x), x, after(x))):
                    shift = ((di + 1) * 3 + dj) * lanes
                    term = pltpu.roll(g, shift, 1) if shift else g
                    total = term if total is None else total + term
            patch_ref[slot, at(i), :] = total.astype(BF)
            return carry

        loop(body)


    def norm_back_start(k, x_ref, planes):
        def body(i, carry):
            s_l, s_r, q_l, q_r = carry
            for p in range(planes):
                x = x_ref[p, at(i), :]
                z = x * coef_ref[k, 0] + coef_ref[k, 1]
                s = sigmoid(z)
                d = work_ref[p, at(i), :] * (s * (1.0 + z * (1.0 - s)))
                work_ref[p, at(i), :] = d
                a, b = halves(d)
                c, e = halves(d * ((x - coef_ref[k, 2]) * coef_ref[k, 3]))
                s_l, s_r, q_l, q_r = s_l + a, s_r + b, q_l + c, q_r + e
            return s_l, s_r, q_l, q_r

        return gathered(loop(body, (zero8,) * 4), planes)

    def norm_back_ready(k, stats, e, planes):
        gain, bias = norm_row(k, 0), norm_row(k, 1)
        factor = 1.0 + film_rows(k, 0)
        width = 128 if planes == 2 else 256
        one, two = stats[0:2], stats[2:4]
        dgain, dbias = factor * two, factor * one
        o = NORM_AT[k]
        ngrad_ref[0:1, o : o + width] = (dgain[0:1] + dgain[1:2])[:, 0:width]
        ngrad_ref[1:2, o : o + width] = (dbias[0:1] + dbias[1:2])[:, 0:width]
        if k in FILM_AT:
            f = FILM_AT[k]
            fgrad_ref[0:2, f : f + width] = (gain * two + bias * one)[:, 0:width]
            fgrad_ref[0:2, f + width : f + 2 * width] = one[:, 0:width]
        both = stats + f_halo * recv_ref[e, 32:40, :]
        kk = gain * factor
        scaled = jnp.concatenate([kk * both[0:2], kk * both[2:4], both[4:8]], axis=0)
        total = over_slot(scaled, planes)
        mean, inverse = rows_ref[k, 0:2, :], rows_ref[k, 2:4, :]
        second = -inverse * inverse * total[2:4]
        third = -inverse * total[0:2] - mean * second
        coef_ref[k, 4] = spread(inverse * kk)
        coef_ref[k, 5] = spread(second)
        coef_ref[k, 6] = spread(third)

    def back_value(k, d, x):
        return d * coef_ref[k, 4] + x * coef_ref[k, 5] + coef_ref[k, 6]


    def zero(i, carry):
        wc_ref[at(i), :] = jnp.zeros((32, 256), BF)
        return carry

    loop(zero, count=48)
    wr_ref[...] = jnp.zeros(wr_ref.shape, BF)
    for cp in range(2):
        for di in range(3):
            wu_ref[cp, di] = jnp.zeros((512, 256), BF)
    for b in range(3):
        wd_ref[b * 512 + 384 : b * 512 + 512, :] = jnp.zeros((128, 256), BF)

    lane = lax.broadcasted_iota(jnp.int32, (32, 128), 1)
    none = jnp.zeros((32, 128), F32)

    def open_strip(i, carry):
        half = pl.ds(pl.multiple_of(i * 16, 16), 16)
        x = jnp.concatenate([strip_ref[0, half, :], strip_ref[1, half, :]], axis=0)
        img_ref[at(i), :] = jnp.concatenate([jnp.where(lane < 24, x, 0.0), none], axis=1)
        x = jnp.where(lane < 12, pltpu.roll(x, 104, 1), 0.0)
        tgt_ref[at(i), :] = jnp.concatenate([x, none], axis=1)
        return carry

    loop(open_strip)
    send(0, edge_cell(img_ref))
    load_wc(0)
    load_up()
    load_down()
    arrive(0)
    put_patch(0, img_ref, recv_ref[0, 0:32, :], 24)
    for cp in range(2):
        full_ref[0, cp] = dot(patch_ref[0], wi_ref[cp])

    def fwd_norm_full(k, source, e):
        stats = stats_of(source, 2)
        send(e, edge_full(source), stats)
        return stats

    def fwd_apply_full(k, source, stats, e):
        arrive(e)
        norm_ready(k, stats, e, 2)

        def body(i, carry):
            put_wide(
                i,
                activated(source[0, at(i), :], k),
                activated(source[1, at(i), :], k),
            )
            return carry

        loop(body)
        put_wide_edge(activated(recv_ref[e, 0:32, :], k))

    for index in range(2):
        h = full_ref.at[2 * index]
        mid = full_ref.at[2 * index + 1]
        out = full_ref.at[2 * index + 2]
        k = 2 * index
        stats = fwd_norm_full(k, h, 1 + k)
        if index:
            load_wc(2)
        fwd_apply_full(k, h, stats, 1 + k)
        keep_wide(k)

        def put_mid(cp, value, mid=mid):
            mid[cp] = value

        conv_low(put_mid)
        stats = fwd_norm_full(k + 1, mid, 2 + k)
        load_wc(2 * index + 1)
        fwd_apply_full(k + 1, mid, stats, 2 + k)
        keep_wide(k + 1)

        def put_out(cp, value, h=h, out=out):
            out[cp] = h[cp] + value

        conv_low(put_out)

    skip = full_ref.at[4]
    send(5, edge_full(skip))

    def skip_body(i, carry):
        put_wide(i, skip[0, at(i), :], skip[1, at(i), :])
        return carry

    loop(skip_body)
    arrive(5)
    put_wide_edge(recv_ref[5, 0:32, :])
    keep_wide(4)
    half_ref[0, 0] = dot(wide_ref[32:544, 0:1536], wd_ref[...])

    def fwd_half(k, source, e):
        stats = stats_of(source, 1)
        send(e, edge_cell(source.at[0]), stats)
        arrive(e)
        norm_ready(k, stats, e, 1)

        def body(i, carry):
            put_thin(i, activated(source[0, at(i), :], k))
            return carry

        loop(body)
        put_thin_edge(activated(recv_ref[e, 0:32, :], k))

    fwd_half(4, half_ref.at[0], 6)
    keep_thin(0)
    half_ref[1, 0] = conv_high(0)
    fwd_half(5, half_ref.at[1], 7)
    keep_thin(1)
    half_ref[2, 0] = half_ref[0, 0] + conv_high(1)
    deep = half_ref.at[2]
    send(8, edge_cell(deep.at[0]))

    def deep_body(i, carry):
        put_thin(i, deep[0, at(i), :])
        return carry

    loop(deep_body)
    arrive(8)
    put_thin_edge(recv_ref[8, 0:32, :])
    keep_thin(2)
    merged = full_ref.at[5]
    for cp in range(2):
        total = skip[cp]
        for di in range(3):
            total = total + dot(
                thin_ref[32 * di : 32 * di + 512, cp * 256 : cp * 256 + 512], wu_ref[cp, di]
            )
        merged[cp] = total

    stats = fwd_norm_full(6, merged, 9)
    fwd_apply_full(6, merged, stats, 9)
    keep_wide(5)
    work_ref[0] = jnp.concatenate(
        [dot(wide_ref[32:544, :], wh_ref[...]), jnp.zeros((512, 128), F32)], axis=1
    )

    live = spread(small_ref[0:2, :])
    weight = small_ref[2:3, :]

    def loss_body(i, carry):
        diff = work_ref[0, at(i), :] - tgt_ref[at(i), :]
        half = live * diff
        work_ref[0, at(i), :] = (half * weight).astype(BF).astype(F32)
        return carry + half * diff

    lost = loop(loss_body, jnp.zeros((32, 256), F32))
    lost = jnp.sum(lost, axis=0, keepdims=True)
    part_ref[...] = jnp.zeros(part_ref.shape, F32)
    part_ref[99:100, :] = lost[:, 0:128] + lost[:, 128:256]
    fgrad_ref[...] = jnp.zeros(fgrad_ref.shape, F32)


    send(10, edge_cell(work_ref.at[0]))
    arrive(10)
    put_patch(1, work_ref.at[0], recv_ref[10, 0:32, :], 12)
    for cp in range(2):
        work_ref[cp] = dot(patch_ref[1], wht_ref[cp])
    stats = norm_back_start(6, merged, 2)
    send(11, edge_full(work_ref), stats)
    turn_ref[0:256, :] = patch_ref[1].T
    for cp in range(2):
        dwh_ref[cp] = dot(turn_ref[0:256, :], act_ref[5, cp])
    arrive(11)
    norm_back_ready(6, stats, 11, 2)

    def head_body(i, carry):
        pair = []
        for p in range(2):
            g = back_value(6, work_ref[p, at(i), :], merged[p, at(i), :])
            grad_ref[p, at(i), :] = g
            pair.append(g)
        put_wide(i, pair[0], pair[1])
        return carry

    loop(head_body)
    put_wide_edge(back_value(6, recv_ref[11, 0:32, :], recv_ref[9, 0:32, :]))

    hgrad = half_ref.at[3]
    hgrad[0] = dot_nt(wide_ref[32:544, :], wut_ref[...])
    send(12, edge_cell(hgrad.at[0]))
    turn_ref[0:256, :] = acth_ref[2].T
    for b in range(3):
        cols = {0: (3, 2), 1: (1, 2), 2: (1, 0)}[b]
        block = dot(turn_ref[0:256, :], wide_ref[32:544, cols[0] * 512 : cols[0] * 512 + 512]) + dot(
            turn_ref[0:256, :], wide_ref[32:544, cols[1] * 512 : cols[1] * 512 + 512]
        )
        for a in range(3):
            one, two = {0: (3, 1), 1: (0, 1), 2: (0, 2)}[a]
            dup_ref[3 * a + b] = (
                block[:, one * 128 : one * 128 + 128] + block[:, two * 128 : two * 128 + 128]
            ).astype(dup_ref.dtype)

    def deep_grad(i, carry):
        put_thin(i, hgrad[0, at(i), :])
        return carry

    loop(deep_grad)
    arrive(12)
    put_thin_edge(recv_ref[12, 0:32, :])
    work_ref[0] = conv_high_back(1)
    stats = norm_back_start(5, half_ref.at[1], 1)
    send(13, edge_cell(work_ref.at[0]), stats)
    grad_high(1, 1)
    arrive(13)
    norm_back_ready(5, stats, 13, 1)

    def mid_grad(i, carry):
        put_thin(i, back_value(5, work_ref[0, at(i), :], half_ref[1, 0, at(i), :]))
        return carry

    loop(mid_grad)
    put_thin_edge(back_value(5, recv_ref[13, 0:32, :], recv_ref[7, 0:32, :]))
    work_ref[0] = conv_high_back(0)
    stats = norm_back_start(4, half_ref.at[0], 1)
    send(14, edge_cell(work_ref.at[0]), stats)
    grad_high(0, 0)
    arrive(14)
    norm_back_ready(4, stats, 14, 1)

    def first_grad(i, carry):
        put_thin(
            i, hgrad[0, at(i), :] + back_value(4, work_ref[0, at(i), :], half_ref[0, 0, at(i), :])
        )
        return carry

    loop(first_grad)
    put_thin_edge(
        recv_ref[12, 0:32, :] + back_value(4, recv_ref[14, 0:32, :], recv_ref[6, 0:32, :])
    )

    for cp in range(2):
        for rp in range(2):
            total = None
            for di in range(1 + rp):
                for dj in range(1 + cp):
                    a = 0 if di else 1 + rp
                    b = 0 if dj else 1 + cp
                    term = dot_nt(
                        thin_ref[32 * (1 + di) : 32 * (1 + di) + 512, (1 + dj) * 256 : (2 + dj) * 256],
                        down_ref[3 * a + b],
                    )
                    total = term if total is None else total + term
            grad_ref[cp, :, rp * 128 : rp * 128 + 128] = (
                grad_ref[cp, :, rp * 128 : rp * 128 + 128] + total
            )
    send(15, edge_full(grad_ref))
    turn_wide(4)
    for cp in range(2):
        for rp in range(2):
            for di in range(1 + rp):
                for dj in range(1 + cp):
                    a = 0 if di else 1 + rp
                    b = 0 if dj else 1 + cp
                    at_row = cp * 256 + rp * 128
                    ddown_ref[3 * a + b] = dot(
                        turn_ref[at_row : at_row + 128, :],
                        thin_ref[32 * (1 + di) : 32 * (1 + di) + 512, (1 + dj) * 256 : (2 + dj) * 256],
                    ).astype(ddown_ref.dtype)

    def put_work(cp, value):
        work_ref[cp] = value

    edge_grad = None
    for index in (1, 0):
        h = full_ref.at[2 * index]
        mid = full_ref.at[2 * index + 1]
        k = 2 * index
        e = 16 if index else 18
        load_wr(k + 1)
        if index:

            def out_grad(i, carry):
                put_wide(i, grad_ref[0, at(i), :], grad_ref[1, at(i), :])
                return carry

            loop(out_grad)
            arrive(15)
            edge_grad = recv_ref[15, 0:32, :]
            put_wide_edge(edge_grad)
        conv_low(put_work, True)
        stats = norm_back_start(k + 1, mid, 2)
        send(e, edge_full(work_ref), stats)
        grad_low(k + 1, k + 1)
        load_wr(k)
        arrive(e)
        norm_back_ready(k + 1, stats, e, 2)

        def mid_body(i, carry, mid=mid, k=k):
            put_wide(
                i,
                back_value(k + 1, work_ref[0, at(i), :], mid[0, at(i), :]),
                back_value(k + 1, work_ref[1, at(i), :], mid[1, at(i), :]),
            )
            return carry

        loop(mid_body)
        put_wide_edge(back_value(k + 1, recv_ref[e, 0:32, :], recv_ref[k + 2, 0:32, :]))
        conv_low(put_work, True)
        stats = norm_back_start(k, h, 2)
        send(e + 1, edge_full(work_ref), stats)
        grad_low(k, k)
        arrive(e + 1)
        norm_back_ready(k, stats, e + 1, 2)

        def in_body(i, carry, h=h, k=k):
            pair = []
            for p in range(2):
                g = grad_ref[p, at(i), :] + back_value(k, work_ref[p, at(i), :], h[p, at(i), :])
                grad_ref[p, at(i), :] = g
                pair.append(g)
            put_wide(i, pair[0], pair[1])
            return carry

        loop(in_body)
        edge_grad = edge_grad + back_value(k, recv_ref[e + 1, 0:32, :], recv_ref[k + 1, 0:32, :])
        put_wide_edge(edge_grad)

    imgrad_ref[...] = dot(wide_ref[32:544, :], wit_ref[...]) * small_ref[3:4, 0:128]
    turn_ref[0:256, :] = patch_ref[0].T
    for cp in range(2):
        dwi_ref[cp] = dot(turn_ref[0:256, :], wide_ref[32:544, 512 + cp * 512 : 768 + cp * 512])

    for a in range(3):
        for b in range(3):
            first, last = None, None
            for cp in range(2):
                for rp in range(2):
                    rho, gamma = rp + a - 1, cp + b - 1
                    cell = (rho // 2 + 1) * 3 + gamma // 2 + 1
                    phase = (gamma % 2) * 2 + rho % 2
                    row = cell * 24 + phase * 6
                    term = dwi_ref[cp, row : row + 6, rp * 128 : rp * 128 + 128]
                    first = term if first is None else first + term
                    row = cell * 12 + phase * 3
                    term = dwh_ref[cp, row : row + 3, rp * 128 : rp * 128 + 128]
                    last = term if last is None else last + term
            t = 3 * a + b
            part_ref[9 * t : 9 * t + 6, :] = first
            part_ref[9 * (8 - t) + 6 : 9 * (8 - t) + 9, :] = last
    for which in range(2):
        for j in range(9):
            row = 81 + 9 * which + j
            part_ref[row : row + 1, :] = ngrad_ref[which : which + 1, 128 * j : 128 * j + 128]


def unet(*operands):
    outs = (
        jax.ShapeDtypeStruct((4, 9, 128, 128), BF),
        jax.ShapeDtypeStruct((2, 9, 256, 256), BF),
        jax.ShapeDtypeStruct((9, 128, 256), BF),
        jax.ShapeDtypeStruct((9, 256, 128), BF),
        jax.ShapeDtypeStruct((256, 128), F32),
        jax.ShapeDtypeStruct((8, 1024), F32),
        jax.ShapeDtypeStruct((512, 128), F32),
    )
    vmem = pl.BlockSpec(memory_space=pltpu.VMEM)
    return pl.pallas_call(
        unet_kernel,
        out_shape=outs,
        in_specs=[vmem] * len(operands),
        out_specs=[vmem] * len(outs),
        scratch_shapes=[
            pltpu.VMEM((512, 256), F32),
            pltpu.VMEM((512, 256), F32),
            pltpu.VMEM((2, 256, 256), F32),
            pltpu.VMEM((2, 256, 256), F32),
            pltpu.VMEM((2, 1152), F32),
            pltpu.VMEM((6, 2, 512, 256), F32),
            pltpu.VMEM((4, 1, 512, 256), F32),
            pltpu.VMEM((2, 512, 256), F32),
            pltpu.VMEM((2, 512, 256), F32),
            pltpu.VMEM((576, 2048), BF),
            pltpu.VMEM((576, 768), BF),
            pltpu.VMEM((6, 2, 512, 256), BF),
            pltpu.VMEM((3, 512, 256), BF),
            pltpu.VMEM((512, 512), BF),
            pltpu.VMEM((1536, 256), BF),
            pltpu.VMEM((256, 1536), BF),
            pltpu.VMEM((2, 3, 512, 256), BF),
            pltpu.VMEM((256, 2048), BF),
            pltpu.VMEM((1536, 256), BF),
            pltpu.VMEM((7, 7, 32, 256), F32),
            pltpu.VMEM((7, 8, 256), F32),
            pltpu.VMEM((2, 512, 256), BF),
            pltpu.VMEM((576, 256), F32),
            pltpu.VMEM((N_EXCHANGE, 40, 256), F32),
            pltpu.VMEM((N_EXCHANGE, 40, 256), F32),
            pltpu.SemaphoreType.DMA((N_EXCHANGE,)),
            pltpu.SemaphoreType.DMA((N_EXCHANGE,)),
        ],
        compiler_params=pltpu.CompilerParams(
            collective_id=1, has_side_effects=True, vmem_limit_bytes=58 * 1024 * 1024
        ),
        name="unet",
    )(*operands)


def cells_of(block):
    rows, cols, width = block.shape
    x = block.reshape(rows // 2, 2, cols // 2, 2, width)
    return jnp.transpose(x, (0, 2, 3, 1, 4)).reshape(rows // 2, cols // 2, 4 * width)


def pixels_of(cells):
    rows, cols, width = cells.shape
    x = cells.reshape(rows, cols, 2, 2, width // 4)
    return jnp.transpose(x, (0, 3, 1, 2, 4)).reshape(2 * rows, 2 * cols, width // 4)


def place_of():
    rr, cc = lax.axis_index("rows"), lax.axis_index("cols")
    return rr, cc, rr // 2, lax.rem(rr, 2), cc // 2, lax.rem(cc, 2)


def device_at(z, y, x, k):
    return {"rows": z * 2 + y, "cols": x * 2 + k}


def device_no(d):
    return {"rows": d // 4, "cols": lax.rem(d, 4)}


def meet_all(me, count=32):
    barrier = pltpu.get_barrier_semaphore()

    def hello(d, carry):
        @pl.when(d != me)
        def _():
            pl.semaphore_signal(barrier, inc=1, device_id=device_no(d), device_id_type=MESH)

        return carry

    lax.fori_loop(0, count, hello, 0)
    pl.semaphore_wait(barrier, count - 1)


def strip_at(r, c):
    pair = lax.rem((r + 1) // 2, 4)
    return (pair * 2 + c // 2) * 4 + lax.rem(c, 2) * 2 + lax.rem(r + 1, 2)


def strip_of(d):
    rr, cc = d // 4, lax.rem(d, 4)
    pair, core = rr // 2, lax.rem(cc, 2)
    r = jnp.where(pair == 0, 7 * (1 - core), 2 * pair - 1 + core)
    return r, lax.rem(rr, 2) * 2 + cc // 2


def slots_of(d):
    r, c = strip_of(d)
    row = (r + 1) // 2
    return row * 5 + c + 1, row * 5 + lax.rem(c + 1, 4)


def lane_tables():
    low = np.zeros((512, 512), np.float32)
    high = np.zeros((512, 512), np.float32)
    rest = np.zeros((512, 512), np.float32)
    for lane in range(512):
        c, q = lane // 128, lane % 128
        low[lane, (q // 32) * 128 + c * 32 + q % 32] = 1.0
        high[lane, (q // 64) * 256 + c * 64 + q % 64] = 1.0
        to = c * 64 + q if q < 64 else (256 if q < 96 else 384) + c * 32 + q % 32
        rest[lane, to] = 1.0
    return np.stack([low, high, rest])


def place_lanes(x, at, width=128):
    n = x.shape[1]
    one = (
        lax.broadcasted_iota(jnp.int32, (n, width), 0) + at
        == lax.broadcasted_iota(jnp.int32, (n, width), 1)
    )
    return jnp.dot(x, jnp.where(one, 1.0, 0.0).astype(x.dtype), preferred_element_type=F32)


LOW_ROWS, HIGH_ROWS, ALL_ROWS = 144, 432, 576
Z_ORDER = (0, 1, -1, 2, -2, 3, -3)


def gather_kernel(
    low_ref,
    high_ref,
    down_ref,
    up_ref,
    cond_ref,
    film_ref,
    joined_ref,
    block_ref,
    lanes_ref,
    low_out,
    high_out,
    down_out,
    up_out,
    strip_out,
    film_out,
    pre_out,
    cond_out,
    all_ref,
    strip_ref,
    cbuf_ref,
    csend_ref,
    part_ref,
    fsend_ref,
    frecv_ref,
    send_sem,
    recv_sem,
    strip_send,
    strip_recv,
    cond_send,
    cond_recv,
    film_send,
    film_recv,
):
    rr, cc, z, y, x, k = place_of()
    me = rr * 4 + cc

    own = all_ref.at[z, y, x, k]
    total = None
    for j in range(4):
        term = place_lanes(low_ref[j].reshape(144, 32).astype(BF), 32 * j)
        total = term if total is None else total + term
    own[0:144, :] = total.astype(BF)
    own[144:432, :] = (
        place_lanes(high_ref[0].reshape(288, 64).astype(BF), 0)
        + place_lanes(high_ref[1].reshape(288, 64).astype(BF), 64)
    ).astype(BF)
    own[432:576, :] = (
        place_lanes(down_ref[...].reshape(144, 64).astype(BF), 0)
        + place_lanes(up_ref[:, 0:16, :].reshape(144, 32).astype(BF), 64)
        + place_lanes(up_ref[:, 16:32, :].reshape(144, 32).astype(BF), 96)
    ).astype(BF)

    meet_all(me)

    def shard(kind, zs, ys, xs, ks, device):
        return pltpu.make_async_remote_copy(
            src_ref=all_ref.at[zs, ys, xs, ks],
            dst_ref=all_ref.at[zs, ys, xs, ks],
            send_sem=send_sem.at[kind, zs, ys, xs],
            recv_sem=recv_sem.at[zs, ys, xs, ks],
            device_id=device,
            device_id_type=MESH,
        )

    def to_up(zs):
        return shard(0, zs, y, x, k, device_at(z + 1, y, x, k))

    def to_down(zs):
        return shard(1, zs, y, x, k, device_at(z - 1, y, x, k))

    def to_x(zs, ys):
        return shard(2, zs, ys, x, k, device_at(z, y, 1 - x, k))

    def to_y(zs, xs):
        return shard(3, zs, y, xs, k, device_at(z, 1 - y, x, k))

    def to_core(zs, ys, xs):
        return shard(4, zs, ys, xs, k, device_at(z, y, x, 1 - k))

    def each_shard(act, wait, after_own):
        for dz in Z_ORDER:
            zs = z + dz
            if dz == 1:
                after_own()

            @pl.when(jnp.logical_and(zs >= 0, zs <= 3))
            def _(zs=zs, dz=dz):
                if dz:
                    wait(zs, y, x)
                if dz <= 0:

                    @pl.when(z < 3)
                    def _():
                        act(to_up(zs))

                if dz >= 0:

                    @pl.when(z > 0)
                    def _():
                        act(to_down(zs))

                act(to_x(zs, y))
                act(to_y(zs, x))
                act(to_core(zs, y, x))

        for dz in Z_ORDER:
            zs = z + dz

            @pl.when(jnp.logical_and(zs >= 0, zs <= 3))
            def _(zs=zs):
                wait(zs, y, 1 - x)

                @pl.when(lax.rem(zs, 2) == 0)
                def _():
                    act(to_y(zs, 1 - x))

                act(to_core(zs, y, 1 - x))
                wait(zs, 1 - y, x)

                @pl.when(lax.rem(zs, 2) == 1)
                def _():
                    act(to_x(zs, 1 - y))

                act(to_core(zs, 1 - y, x))

        for dz in Z_ORDER:
            zs = z + dz

            @pl.when(jnp.logical_and(zs >= 0, zs <= 3))
            def _(zs=zs):
                wait(zs, 1 - y, 1 - x)
                act(to_core(zs, 1 - y, 1 - x))

    to_left = strip_at(rr, cc)
    to_right = strip_at(rr, lax.rem(cc + 3, 4))

    def strip_copy(side, device):
        return pltpu.make_async_remote_copy(
            src_ref=block_ref.at[1 - side],
            dst_ref=strip_ref.at[side],
            send_sem=strip_send.at[side],
            recv_sem=strip_recv.at[side],
            device_id=device_no(device),
            device_id_type=MESH,
        )

    strip_copy(0, to_left).start()

    @pl.when(to_right != me)
    def _():
        strip_copy(1, to_right).start()

    pre = lax.dot_general(
        joined_ref[...],
        cond_ref[...].astype(BF),
        (((1,), (1,)), ((), ())),
        preferred_element_type=F32,
    )
    pre_out[...] = pre
    csend_ref[...] = jnp.concatenate([pre, jnp.zeros((32, 112), F32)], axis=1)

    def cond_copy(c):
        return pltpu.make_async_remote_copy(
            src_ref=csend_ref,
            dst_ref=cbuf_ref.at[cc],
            send_sem=cond_send.at[c],
            recv_sem=cond_recv.at[cc],
            device_id={"rows": rr, "cols": c},
            device_id_type=MESH,
        )

    def cond_arrives(c):
        return pltpu.make_async_remote_copy(
            src_ref=csend_ref,
            dst_ref=cbuf_ref.at[c],
            send_sem=cond_send.at[c],
            recv_sem=cond_recv.at[c],
            device_id={"rows": rr, "cols": c},
            device_id_type=MESH,
        )

    for c in range(4):

        @pl.when(cc != c)
        def _(c=c):
            cond_copy(c).start()

    cbuf_ref[cc] = csend_ref[...]

    def arrived(zs, ys, xs, ks=None):
        ks = k if ks is None else ks
        pltpu.make_async_remote_copy(
            src_ref=all_ref.at[zs, ys, xs, ks],
            dst_ref=all_ref.at[zs, ys, xs, ks],
            send_sem=send_sem.at[0, zs, ys, xs],
            recv_sem=recv_sem.at[zs, ys, xs, ks],
            device_id=device_at(z, y, x, 1 - k),
            device_id_type=MESH,
        ).wait_recv()

    def film_step():
        for c in range(4):

            @pl.when(cc != c)
            def _(c=c):
                cond_arrives(c).wait_recv()

        whole = cbuf_ref[0]
        for c in range(1, 4):
            whole = whole + pltpu.roll(cbuf_ref[c], 16 * c, 1)
        whole = whole[:, 0:64]
        cond = (whole * (0.5 * jnp.tanh(0.5 * whole) + 0.5)).astype(BF)
        cond_out[...] = cond.astype(F32)
        part_ref[...] = jnp.dot(cond, film_ref[...].astype(BF), preferred_element_type=F32)

        def deal(d, carry):
            s_l, s_r = slots_of(d)
            fsend_ref[d, 0:1, :] = part_ref[pl.ds(s_l, 1), :]
            fsend_ref[d, 1:2, :] = part_ref[pl.ds(s_r, 1), :]

            @pl.when(d != me)
            def _():
                film_copy(d).start()

            return carry

        fsend_ref[...] = jnp.zeros(fsend_ref.shape, F32)
        lax.fori_loop(0, 32, deal, 0)
        frecv_ref[me] = fsend_ref[me]

    def film_copy(d):
        return pltpu.make_async_remote_copy(
            src_ref=fsend_ref.at[d],
            dst_ref=frecv_ref.at[me],
            send_sem=film_send.at[d],
            recv_sem=film_recv.at[me],
            device_id=device_no(d),
            device_id_type=MESH,
        )

    def film_arrives(d):
        return pltpu.make_async_remote_copy(
            src_ref=fsend_ref.at[d],
            dst_ref=frecv_ref.at[d],
            send_sem=film_send.at[d],
            recv_sem=film_recv.at[d],
            device_id=device_no(d),
            device_id_type=MESH,
        )

    each_shard(lambda copy: copy.start(), arrived, film_step)

    for zs in range(4):
        for ys in range(2):
            for xs in range(2):
                arrived(zs, ys, xs, 1 - k)

    def row(r, carry):
        zr, yr = r // 2, lax.rem(r, 2)

        def joined(lo, hi):
            return jnp.concatenate(
                [all_ref[zr, yr, c // 2, c % 2, lo:hi, :] for c in range(4)], axis=1
            )

        low = jnp.dot(joined(0, 144), lanes_ref[0], preferred_element_type=F32).astype(BF)
        at16 = pl.ds(pl.multiple_of(r * 16, 16), 16)
        at32 = pl.ds(pl.multiple_of(r * 32, 32), 32)
        for j in range(4):
            low_out[j, :, at16, :] = low[:, j * 128 : j * 128 + 128].reshape(9, 16, 128)
        high = jnp.dot(joined(144, 432), lanes_ref[1], preferred_element_type=F32).astype(BF)
        for j in range(2):
            high_out[j, :, at32, :] = high[:, j * 256 : j * 256 + 256].reshape(9, 32, 256)
        rest = jnp.dot(joined(432, 576), lanes_ref[2], preferred_element_type=F32).astype(BF)
        down_out[:, at16, :] = rest[:, 0:256].reshape(9, 16, 256)
        up_out[:, at32, :] = jnp.concatenate(
            [rest[:, 256:384].reshape(9, 16, 128), rest[:, 384:512].reshape(9, 16, 128)], axis=1
        )
        return carry

    lax.fori_loop(0, 8, row, 0)

    strip_copy(0, to_left).wait()

    @pl.when(to_right != me)
    def _():
        strip_copy(1, to_right).wait()

    @pl.when(to_right == me)
    def _():
        strip_ref[1] = block_ref[0]

    strip_out[...] = strip_ref[...]

    def film_wait(d, carry):
        @pl.when(d != me)
        def _():
            film_arrives(d).wait_recv()

        return carry

    lax.fori_loop(0, 32, film_wait, 0)
    for c in range(4):
        total = frecv_ref[c]
        for r in range(1, 8):
            total = total + frecv_ref[4 * r + c]
        film_out[:, c * 256 : c * 256 + 256] = total

    def film_sent(d, carry):
        @pl.when(d != me)
        def _():
            film_copy(d).wait_send()

        return carry

    lax.fori_loop(0, 32, film_sent, 0)
    for c in range(4):

        @pl.when(cc != c)
        def _(c=c):
            cond_copy(c).wait_send()

    each_shard(lambda copy: copy.wait_send(), lambda *a: None, lambda: None)


def gather(*operands):
    outs = (
        jax.ShapeDtypeStruct((4, 9, 128, 128), BF),
        jax.ShapeDtypeStruct((2, 9, 256, 256), BF),
        jax.ShapeDtypeStruct((9, 128, 256), BF),
        jax.ShapeDtypeStruct((9, 256, 128), BF),
        jax.ShapeDtypeStruct((2, 256, 128), F32),
        jax.ShapeDtypeStruct((8, 1024), F32),
        jax.ShapeDtypeStruct((32, 16), F32),
        jax.ShapeDtypeStruct((32, 64), F32),
    )
    vmem = pl.BlockSpec(memory_space=pltpu.VMEM)
    dma = pltpu.SemaphoreType.DMA
    return pl.pallas_call(
        gather_kernel,
        out_shape=outs,
        in_specs=[vmem] * len(operands),
        out_specs=[vmem] * len(outs),
        scratch_shapes=[
            pltpu.VMEM((4, 2, 2, 2, ALL_ROWS, 128), BF),
            pltpu.VMEM((2, 256, 128), F32),
            pltpu.VMEM((4, 32, 128), F32),
            pltpu.VMEM((32, 128), F32),
            pltpu.VMEM((32, 256), F32),
            pltpu.VMEM((32, 8, 256), F32),
            pltpu.VMEM((32, 8, 256), F32),
            dma((5, 4, 2, 2)),
            dma((4, 2, 2, 2)),
            dma((2,)),
            dma((2,)),
            dma((4,)),
            dma((4,)),
            dma((32,)),
            dma((32,)),
        ],
        compiler_params=pltpu.CompilerParams(
            collective_id=2, has_side_effects=True, vmem_limit_bytes=40 * 1024 * 1024
        ),
        name="gather",
    )(*operands)


PART_ROWS = 256
NORM_ROW = 81
LOSS_ROW = 99


def lane_value(pairs):
    lane = lax.broadcasted_iota(jnp.int32, (8, 128), 1)
    total = jnp.zeros((8, 128), F32)
    for at, value in pairs:
        total = total + jnp.where(lane == at, value, 0.0)
    return total


def square_sum(x):
    x = x * x
    while x.ndim > 2:
        x = jnp.sum(x, axis=0)
    return jnp.sum(jnp.sum(x, axis=0, keepdims=True), axis=1, keepdims=True)


def finish_kernel(*refs):
    (
        dlow_ref,
        dhigh_ref,
        ddown_ref,
        dup_ref,
        part_ref,
        fgrad_ref,
        imgrad_ref,
        lanes_ref,
        joined_ref,
        pre_ref,
        cond_ref,
    ) = refs[:11]
    params = refs[11:35]
    outs = refs[35:59]
    loss_out, clip_out, back_out = refs[59:62]
    (
        sb_ref,
        rb_ref,
        rx_ref,
        ry_ref,
        rz_ref,
        m1_ref,
        r1_ref,
        m2_ref,
        r2_ref,
        m3_ref,
        r3_ref,
        gcs_ref,
        gcr_ref,
        film_ref,
        total_ref,
        back_ref,
        core_send,
        core_recv,
        x_send,
        x_recv,
        y_send,
        y_recv,
        z_send,
        z_recv,
        m_send,
        m_recv,
        gc_send,
        gc_recv,
        back_send,
        back_recv,
    ) = refs[62:]
    weights, firsts, seconds = params[0::3], params[1::3], params[2::3]
    rr, cc, z, y, x, k = place_of()
    me = rr * 4 + cc
    meet_all(me)

    def message(n, src, dst, d, source):
        return pltpu.make_async_remote_copy(
            src_ref=src,
            dst_ref=dst.at[source],
            send_sem=m_send.at[n, d],
            recv_sem=m_recv.at[n, source],
            device_id=device_no(d),
            device_id_type=MESH,
        )

    def others(body):
        def one(d, carry):
            @pl.when(d != me)
            def _():
                body(d)

            return carry

        lax.fori_loop(0, 32, one, 0)

    def fill(d, carry):
        c = lax.rem(d, 4)
        m1_ref[d, 0:2, 0:256] = fgrad_ref[0:2, pl.ds(pl.multiple_of(c * 256, 256), 256)]
        m1_ref[d, :, 256:384] = part_ref[pl.ds(pl.multiple_of(d * 8, 8), 8), :]

        @pl.when(d != me)
        def _():
            message(0, m1_ref.at[d], r1_ref, d, me).start()

        return carry

    m1_ref[...] = jnp.zeros(m1_ref.shape, F32)
    lax.fori_loop(0, 32, fill, 0)
    r1_ref[me] = m1_ref[me]

    s_r, s_c = strip_of(me)
    home_left = s_r * 4 + s_c
    home_right = s_r * 4 + lax.rem(s_c + 1, 4)

    def back_copy(side, device):
        return pltpu.make_async_remote_copy(
            src_ref=imgrad_ref.at[:, 16 * side : 16 * side + 16, :],
            dst_ref=back_ref.at[1 - side],
            send_sem=back_send.at[side],
            recv_sem=back_recv.at[side],
            device_id=device_no(device),
            device_id_type=MESH,
        )

    back_copy(0, home_left).start()

    @pl.when(home_right != me)
    def _():
        back_copy(1, home_right).start()

    def back_lanes(v, which):
        return lax.dot_general(
            v, lanes_ref[which], (((1,), (1,)), ((), ())), preferred_element_type=F32
        ).astype(BF)

    def row(r, carry):
        zr, yr = r // 2, lax.rem(r, 2)
        at16 = pl.ds(pl.multiple_of(r * 16, 16), 16)
        at32 = pl.ds(pl.multiple_of(r * 32, 32), 32)
        b16 = pl.ds(pl.multiple_of(r * 32 + 16, 16), 16)
        a16 = pl.ds(pl.multiple_of(r * 32, 16), 16)
        low = back_lanes(
            jnp.concatenate([dlow_ref[j, :, at16, :].reshape(144, 128) for j in range(4)], axis=1), 0
        )
        high = back_lanes(
            jnp.concatenate([dhigh_ref[j, :, at32, :].reshape(288, 256) for j in range(2)], axis=1), 1
        )
        rest = back_lanes(
            jnp.concatenate(
                [
                    ddown_ref[:, at16, :].reshape(144, 256),
                    dup_ref[:, a16, :].reshape(144, 128),
                    dup_ref[:, b16, :].reshape(144, 128),
                ],
                axis=1,
            ),
            2,
        )
        for c in range(4):
            to = sb_ref.at[zr, yr, c // 2, c % 2]
            to[0:144, :] = low[:, c * 128 : c * 128 + 128]
            to[144:432, :] = high[:, c * 128 : c * 128 + 128]
            to[432:576, :] = rest[:, c * 128 : c * 128 + 128]
        return carry

    def core_copy(zs):
        return pltpu.make_async_remote_copy(
            src_ref=sb_ref.at[zs, :, :, 1 - k],
            dst_ref=rb_ref.at[zs],
            send_sem=core_send.at[zs],
            recv_sem=core_recv.at[zs],
            device_id=device_at(z, y, x, 1 - k),
            device_id_type=MESH,
        )

    for zs in range(4):
        lax.fori_loop(2 * zs, 2 * zs + 2, row, 0)
        core_copy(zs).start()

    def add(to, a, b):
        to[...] = (a[...].astype(F32) + b[...].astype(F32)).astype(BF)

    def first_copy(zs):
        by_x = zs % 2 == 0
        return pltpu.make_async_remote_copy(
            src_ref=rb_ref.at[zs, :, 1 - x] if by_x else rb_ref.at[zs, 1 - y],
            dst_ref=rx_ref.at[zs],
            send_sem=x_send.at[zs],
            recv_sem=x_recv.at[zs],
            device_id=device_at(z, y, 1 - x, k) if by_x else device_at(z, 1 - y, x, k),
            device_id_type=MESH,
        )

    def second_copy(zs):
        by_x = zs % 2 == 1
        return pltpu.make_async_remote_copy(
            src_ref=rb_ref.at[zs, y, 1 - x] if by_x else rb_ref.at[zs, 1 - y, x],
            dst_ref=ry_ref.at[zs],
            send_sem=y_send.at[zs],
            recv_sem=y_recv.at[zs],
            device_id=device_at(z, y, 1 - x, k) if by_x else device_at(z, 1 - y, x, k),
            device_id_type=MESH,
        )

    for zs in range(4):
        core_copy(zs).wait_recv()
        for ys in range(2):
            for xs in range(2):
                to = rb_ref.at[zs, ys, xs]
                add(to, to, sb_ref.at[zs, ys, xs, k])
        first_copy(zs).start()

    others(lambda d: message(0, m1_ref.at[d], r1_ref, d, d).wait_recv())
    film_ref[...] = jnp.zeros(film_ref.shape, F32)

    def collect(d, total):
        s_l, s_rt = slots_of(d)
        film_ref[pl.ds(s_l, 1), :] = film_ref[pl.ds(s_l, 1), :] + r1_ref[d, 0:1, 0:256]
        film_ref[pl.ds(s_rt, 1), :] = film_ref[pl.ds(s_rt, 1), :] + r1_ref[d, 1:2, 0:256]
        return total + r1_ref[d, :, 256:384]

    m2_ref[0:8, :] = lax.fori_loop(0, 32, collect, jnp.zeros((8, 128), F32))
    film_mine = film_ref[...]
    film_w = weights[6][...].astype(BF).astype(F32)
    gc_part = lax.dot_general(
        film_mine, film_w, (((1,), (1,)), ((), ())), precision=HIGH, preferred_element_type=F32
    )
    wide = jnp.concatenate([gc_part, jnp.zeros((32, 64), F32)], axis=1)
    for c in range(4):
        gcs_ref[c] = pltpu.roll(wide, 128 - 16 * c, 1) if c else wide

    def gc_copy(c, source):
        return pltpu.make_async_remote_copy(
            src_ref=gcs_ref.at[c],
            dst_ref=gcr_ref.at[source],
            send_sem=gc_send.at[c],
            recv_sem=gc_recv.at[source],
            device_id={"rows": rr, "cols": c},
            device_id_type=MESH,
        )

    for c in range(4):

        @pl.when(cc != c)
        def _(c=c):
            gc_copy(c, cc).start()

        @pl.when(cc == c)
        def _(c=c):
            gcr_ref[c] = gcs_ref[c]

    grads = [None] * 8
    grads[6] = lax.dot_general(
        cond_ref[...], film_mine, (((0,), (0,)), ((), ())), precision=HIGH, preferred_element_type=F32
    )

    for zs in range(4):
        first_copy(zs).wait_recv()
        for other in range(2):
            to = rb_ref.at[zs, other, x] if zs % 2 == 0 else rb_ref.at[zs, y, other]
            add(to, to, rx_ref.at[zs, other])
        second_copy(zs).start()

    for c in range(4):

        @pl.when(cc != c)
        def _(c=c):
            gc_copy(c, c).wait_recv()

    pre = pre_ref[...]
    gc = gcr_ref[0] + gcr_ref[1] + gcr_ref[2] + gcr_ref[3]
    gc = gc[:, 0:16] * silu_grad_tanh(pre)
    grads[5] = lax.dot_general(
        gc,
        joined_ref[...].astype(F32),
        (((0,), (0,)), ((), ())),
        precision=HIGH,
        preferred_element_type=F32,
    )

    def z_copy(zs):
        return pltpu.make_async_remote_copy(
            src_ref=rb_ref.at[zs, y, x],
            dst_ref=rz_ref.at[z],
            send_sem=z_send.at[zs],
            recv_sem=z_recv.at[z],
            device_id=device_at(zs, y, x, k),
            device_id_type=MESH,
        )

    def z_arrives(zs):
        return pltpu.make_async_remote_copy(
            src_ref=rb_ref.at[zs, y, x],
            dst_ref=rz_ref.at[zs],
            send_sem=z_send.at[zs],
            recv_sem=z_recv.at[zs],
            device_id=device_at(zs, y, x, k),
            device_id_type=MESH,
        )

    for zs in range(4):
        second_copy(zs).wait_recv()
        to = rb_ref.at[zs, y, x]
        add(to, to, ry_ref.at[zs])

        @pl.when(zs != z)
        def _(zs=zs):
            z_copy(zs).start()

        @pl.when(zs == z)
        def _(zs=zs):
            rz_ref[zs] = rb_ref[zs, y, x]

    for zs in range(4):

        @pl.when(zs != z)
        def _(zs=zs):
            z_arrives(zs).wait_recv()

    own = rz_ref[0].astype(F32)
    for zs in range(1, 4):
        own = own + rz_ref[zs].astype(F32)
    grads[1] = jnp.stack([own[0:144, 32 * j : 32 * j + 32].reshape(9, 16, 32) for j in range(4)])
    grads[2] = jnp.stack([own[144:432, 64 * j : 64 * j + 64].reshape(9, 32, 64) for j in range(2)])
    grads[3] = own[432:576, 0:64].reshape(9, 16, 64)
    grads[4] = jnp.concatenate(
        [own[432:576, 64:96].reshape(9, 16, 32), own[432:576, 96:128].reshape(9, 16, 32)], axis=1
    )

    owned = square_sum(own)
    for n in (5, 6):
        owned = owned + square_sum(grads[n])
    m2_ref[8:16, :] = jnp.broadcast_to(owned, (8, 128))
    others(lambda d: message(1, m2_ref, r2_ref, d, me).start())
    r2_ref[me] = m2_ref[...]
    others(lambda d: message(1, m2_ref, r2_ref, d, d).wait_recv())

    def take(d, total):
        total_ref[pl.ds(pl.multiple_of(d * 8, 8), 8), :] = r2_ref[d, 0:8, :]
        return total + r2_ref[d, 8:16, :]

    squares = lax.fori_loop(0, 32, take, jnp.zeros((8, 128), F32))
    shared = square_sum(total_ref[0:LOSS_ROW, :])
    clip = jnp.sqrt(squares[0:1, 0:1] + shared)
    factor = jnp.minimum(1.0, CLIP_AT / clip)
    clip_out[...] = jnp.broadcast_to(clip, (1, 128))
    loss_out[...] = jnp.broadcast_to(
        jnp.sum(total_ref[LOSS_ROW : LOSS_ROW + 1, :], axis=1, keepdims=True), (1, 128)
    )
    grads[0] = jnp.stack([total_ref[9 * t : 9 * t + 9, :] for t in range(9)])
    grads[7] = jnp.concatenate(
        [
            jnp.concatenate(
                [total_ref[NORM_ROW + 9 * n + j : NORM_ROW + 9 * n + j + 1, :] for j in range(9)],
                axis=1,
            )
            for n in range(2)
        ],
        axis=0,
    )

    updates = []
    pairs = []
    spot = 0
    for n in range(8):
        grad = grads[n] * factor.reshape((1,) * grads[n].ndim)
        first_new = BETA_ONE * firsts[n][...] + (1.0 - BETA_ONE) * grad
        second_new = BETA_TWO * seconds[n][...] + (1.0 - BETA_TWO) * grad * grad
        first_hat = first_new / (1.0 - BETA_ONE**STEP)
        second_hat = second_new / (1.0 - BETA_TWO**STEP)
        update = first_hat / (jnp.sqrt(second_hat) + EPS_ADAM) + DECAY * weights[n][...]
        outs[3 * n][...] = grad
        outs[3 * n + 1][...] = second_new
        outs[3 * n + 2][...] = update
        if n in (1, 2):
            for j in range(update.shape[0]):
                pairs.append((spot, square_sum(weights[n][j])))
                pairs.append((64 + spot, square_sum(update[j])))
                spot += 1
        elif 2 < n < 7:
            pairs.append((spot, square_sum(weights[n][...])))
            pairs.append((64 + spot, square_sum(update)))
            spot += 1

    m3_ref[...] = lane_value(pairs)
    others(lambda d: message(2, m3_ref, r3_ref, d, me).start())
    r3_ref[me] = m3_ref[...]

    def step(n, ratio, at=None):
        ratio = ratio * RATE
        if at is None:
            weight, out = weights[n][...], outs[3 * n + 2]
            out[...] = weight - ratio.reshape((1,) * weight.ndim) * out[...]
        else:
            weight, out = weights[n][at], outs[3 * n + 2]
            out[at] = weight - ratio.reshape((1,) * weight.ndim) * out[at]

    def root_ratio(a, b):
        return jnp.sqrt(a) / jnp.sqrt(b)

    step(7, root_ratio(square_sum(weights[7][...]), square_sum(outs[23][...])))
    edge_w, edge_u = weights[0][...], outs[2][...]
    for lo, hi in ((0, 6), (6, 9)):
        ratio = root_ratio(square_sum(edge_w[:, lo:hi, :]), square_sum(edge_u[:, lo:hi, :])) * RATE
        outs[2][:, lo:hi, :] = edge_w[:, lo:hi, :] - ratio.reshape(1, 1, 1) * edge_u[:, lo:hi, :]

    others(lambda d: message(2, m3_ref, r3_ref, d, d).wait_recv())
    sums = lax.fori_loop(0, 32, lambda d, t: t + r3_ref[d], jnp.zeros((8, 128), F32))
    spot = 0
    for n in range(1, 7):
        for j in range(weights[n].shape[0] if n in (1, 2) else 1):
            ratio = root_ratio(sums[0:1, spot : spot + 1], sums[0:1, 64 + spot : 65 + spot])
            step(n, ratio, j if n in (1, 2) else None)
            spot += 1

    back_copy(0, home_left).wait()

    @pl.when(home_right != me)
    def _():
        back_copy(1, home_right).wait()

    @pl.when(home_right == me)
    def _():
        back_ref[0] = imgrad_ref[:, 16:32, :]

    back_out[...] = back_ref[...]

    others(lambda d: message(0, m1_ref.at[d], r1_ref, d, me).wait_send())
    others(lambda d: message(1, m2_ref, r2_ref, d, me).wait_send())
    others(lambda d: message(2, m3_ref, r3_ref, d, me).wait_send())
    for c in range(4):

        @pl.when(cc != c)
        def _(c=c):
            gc_copy(c, cc).wait_send()

    for zs in range(4):
        core_copy(zs).wait_send()
        first_copy(zs).wait_send()
        second_copy(zs).wait_send()

        @pl.when(zs != z)
        def _(zs=zs):
            z_copy(zs).wait_send()


def silu_grad_tanh(v):
    s = 0.5 * jnp.tanh(0.5 * v) + 0.5
    return s * (1.0 + v * (1.0 - s))


def finish(*operands):
    outs = []
    for n in range(8):
        outs += [jax.ShapeDtypeStruct(operands[11 + 3 * n].shape, F32)] * 3
    outs += [
        jax.ShapeDtypeStruct((1, 128), F32),
        jax.ShapeDtypeStruct((1, 128), F32),
        jax.ShapeDtypeStruct((2, 16, 16, 128), F32),
    ]
    vmem = pl.BlockSpec(memory_space=pltpu.VMEM)
    dma = pltpu.SemaphoreType.DMA
    return pl.pallas_call(
        finish_kernel,
        out_shape=tuple(outs),
        in_specs=[vmem] * len(operands),
        out_specs=[vmem] * len(outs),
        scratch_shapes=[
            pltpu.VMEM((4, 2, 2, 2, ALL_ROWS, 128), BF),
            pltpu.VMEM((4, 2, 2, ALL_ROWS, 128), BF),
            pltpu.VMEM((4, 2, ALL_ROWS, 128), BF),
            pltpu.VMEM((4, ALL_ROWS, 128), BF),
            pltpu.VMEM((4, ALL_ROWS, 128), BF),
            pltpu.VMEM((32, 8, 384), F32),
            pltpu.VMEM((32, 8, 384), F32),
            pltpu.VMEM((16, 128), F32),
            pltpu.VMEM((32, 16, 128), F32),
            pltpu.VMEM((8, 128), F32),
            pltpu.VMEM((32, 8, 128), F32),
            pltpu.VMEM((4, 32, 128), F32),
            pltpu.VMEM((4, 32, 128), F32),
            pltpu.VMEM((32, 256), F32),
            pltpu.VMEM((256, 128), F32),
            pltpu.VMEM((2, 16, 16, 128), F32),
            dma((4,)),
            dma((4,)),
            dma((4,)),
            dma((4,)),
            dma((4,)),
            dma((4,)),
            dma((4,)),
            dma((4,)),
            dma((3, 32)),
            dma((3, 32)),
            dma((4,)),
            dma((4,)),
            dma((2,)),
            dma((2,)),
        ],
        compiler_params=pltpu.CompilerParams(
            collective_id=3, has_side_effects=True, vmem_limit_bytes=56 * 1024 * 1024
        ),
        name="finish",
    )(*operands)


def per_device_strips(
    image_pair,
    noise_target,
    timesteps,
    text_pooled,
    slot_live,
    *params,
):
    edge_w, low_w, high_w, down_w, up_w, cond_w, film_w, norm_w = params[0::3]
    me = lax.axis_index("rows") * 4 + lax.axis_index("cols")
    by_cell, by_tile = phase_tables()
    lanes = jnp.asarray(lane_tables(), BF)

    block = jnp.concatenate(
        [cells_of(image_pair[0].astype(F32)), cells_of(noise_target[0])], axis=-1
    )
    block = jnp.pad(block, ((0, 0), (0, 0), (0, 92)))
    block = jnp.stack([block[:, 0:16], block[:, 16:32]]).reshape(2, 256, 128)
    joined = jnp.concatenate([time_embed(timesteps).astype(BF), text_pooled], axis=-1)[0]
    joined = jnp.pad(joined.reshape(25, -1), ((0, 7), (0, 0)))
    low, high, down, up, strip, own_film, pre, cond = gather(
        low_w, high_w, down_w, up_w, cond_w.T, film_w, joined, block, lanes
    )

    live_slots = slot_live[0].astype(F32)
    side = np.array([32, 64, 64, 64, 32], np.float32)
    count = 3.0 * jnp.sum(live_slots * (side[:, None] * side[None, :]))
    slots = jnp.stack(slots_of(me))
    own_live = jnp.take(live_slots.reshape(25), slots)
    small = jnp.concatenate([own_live, (2.0 / count)[None], count[None], jnp.zeros((4,), F32)])
    small = jnp.broadcast_to(small[:, None], (8, 256))

    edge_low = edge_w.astype(BF)
    inconv = jnp.swapaxes(edge_low[:, :, 0:6], 1, 2)
    head = edge_low[:, :, 6:9]
    cell_tab = by_cell.astype(jnp.bfloat16)
    tile_tab = by_tile.astype(jnp.bfloat16)

    def by_cells(w):
        x = jnp.einsum("oqpt,tcd->oqcpd", cell_tab, w)
        x = x.reshape(-1, 2, 256)
        return jnp.transpose(jnp.pad(x, ((0, 256 - x.shape[0]), (0, 0), (0, 0))), (1, 0, 2))

    def by_tiles(w):
        x = jnp.einsum("grpt,tcd->grcpd", tile_tab, w).reshape(2048, -1)
        return jnp.pad(x, ((0, 0), (0, 128 - x.shape[1])))

    def flip_t(w):
        return jnp.swapaxes(w[::-1], 1, 2)

    dlow, dhigh, ddown, dup, part, fgrad, imgrad = unet(
        strip,
        small,
        own_film,
        norm_w,
        low,
        high,
        down,
        up,
        by_cells(inconv),
        by_tiles(flip_t(inconv)),
        by_tiles(head),
        by_cells(flip_t(head)),
    )

    def view(n, a):
        return jnp.swapaxes(a, 1, 2) if n == 0 else a.T if n == 5 else a

    state = [view(n // 3, a) for n, a in enumerate(params)]
    results = finish(
        dlow, dhigh, ddown, dup, part, fgrad, imgrad.reshape(16, 32, 128), lanes, joined, pre, cond, *state
    )
    new = [view(n // 3, a) for n, a in enumerate(results[:24])]
    loss, clip, back = results[24:]
    back = jnp.concatenate([back[0], back[1]], axis=1)[:, :, 0:24]
    return tuple(new) + (loss[0, 0], count, clip[0, 0], pixels_of(back)[None])


def solution(mesh):
    strips = mesh.shape["rows"] == 8 and mesh.shape["cols"] == 4
    placed = (
        P(None, "rows", "cols", None),
        P(None, "rows", "cols", None),
        P(),
        P(),
        P(),
        P(),
        P(),
        P(),
        P(None, None, "rows", "cols"),
        P(None, None, "rows", "cols"),
        P(None, None, "rows", "cols"),
        P(None, None, "rows", "cols"),
        P(None, None, "rows", "cols"),
        P(None, None, "rows", "cols"),
        P(None, "rows", "cols"),
        P(None, "rows", "cols"),
        P(None, "rows", "cols"),
        P(None, "rows", "cols"),
        P(None, "rows", "cols"),
        P(None, "rows", "cols"),
        P(None, ("rows", "cols")),
        P(None, ("rows", "cols")),
        P(None, ("rows", "cols")),
        P("rows", "cols"),
        P("rows", "cols"),
        P("rows", "cols"),
        P(),
        P(),
        P(),
    )
    return jax.shard_map(
        per_device_strips if strips else per_device,
        mesh=mesh,
        in_specs=placed,
        out_specs=(
            P(),
            P(),
            P(),
            P(None, None, "rows", "cols"),
            P(None, None, "rows", "cols"),
            P(None, None, "rows", "cols"),
            P(None, None, "rows", "cols"),
            P(None, None, "rows", "cols"),
            P(None, None, "rows", "cols"),
            P(None, "rows", "cols"),
            P(None, "rows", "cols"),
            P(None, "rows", "cols"),
            P(None, "rows", "cols"),
            P(None, "rows", "cols"),
            P(None, "rows", "cols"),
            P(None, ("rows", "cols")),
            P(None, ("rows", "cols")),
            P(None, ("rows", "cols")),
            P("rows", "cols"),
            P("rows", "cols"),
            P("rows", "cols"),
            P(),
            P(),
            P(),
            P(),
            P(),
            P(),
            P(None, "rows", "cols", None),
        ),
        check_vma=False,
    )
```

```python
import math

import jax
import jax.numpy as jnp
import numpy as np
from jax import lax
from jax.experimental import pallas as pl
from jax.experimental.pallas import tpu as pltpu
from jax.sharding import PartitionSpec as P

SLOT = 64
SLOTS = 5
C1 = 128
C2 = 256
GROUPS = 32
TEMB = 128
STEP = 10


HIGH = lax.Precision.HIGHEST
EPS_NORM = 1e-05
CLIP_AT = 0.05
RATE = 0.5
BETA_ONE = 0.9
BETA_TWO = 0.999
EPS_ADAM = 1e-06
DECAY = 0.01


def entering(part, axis, combine, identity, reverse):
    count = lax.axis_size(axis)
    place = lax.axis_index(axis)
    ahead = count - 1 - place if reverse else place
    gathered = jax.tree.map(lambda a: lax.all_gather(a, axis), part)
    state = jax.tree.map(lambda a, e: jnp.zeros_like(a) + jnp.asarray(e, a.dtype), part, identity)

    def one(turn, state):
        source = count - 1 - turn if reverse else turn
        return combine(
            state, jax.tree.map(lambda a: lax.dynamic_index_in_dim(a, source, 0, False), gathered)
        )

    return lax.fori_loop(0, ahead, one, state)


def padded_2(block, sides, width):
    for axis, dim in sides:
        count = lax.axis_size(axis)
        forward = [(i, i + 1) for i in range(count - 1)]
        backward = [(target, source) for source, target in forward]
        low = lax.ppermute(
            lax.slice_in_dim(block, block.shape[dim] - width, None, axis=dim), axis, forward
        )
        high = lax.ppermute(lax.slice_in_dim(block, 0, width, axis=dim), axis, backward)
        block = jnp.concatenate([low, block, high], axis=dim)
    return block


def time_embed(steps):
    half = TEMB // 2
    freq = jnp.exp(-math.log(10000.0) * jnp.arange(half, dtype=jnp.float32) / half)
    angle = steps.astype(jnp.float32)[..., None] * freq
    return jnp.concatenate([jnp.sin(angle), jnp.cos(angle)], axis=-1)


def silu_grad(values):
    sigma = jax.nn.sigmoid(values)
    return sigma * (1.0 + values * (1.0 - sigma))


def tap_masks(rows, cols, slot):
    half = slot // 2
    row_pos = lax.axis_index("rows") * rows + jnp.arange(rows)
    col_pos = lax.axis_index("cols") * cols + jnp.arange(cols)
    row_ok = [
        (row_pos + offset + half) // slot == (row_pos + half) // slot for offset in (-1, 0, 1)
    ]
    col_ok = [
        (col_pos + offset + half) // slot == (col_pos + half) // slot for offset in (-1, 0, 1)
    ]
    return [
        (row_ok[tap // 3][:, None] & col_ok[tap % 3][None, :]).astype(jnp.bfloat16)
        for tap in range(9)
    ]


def slot_level(rows, cols, slot, size):
    half = slot // 2
    labels = jnp.arange(SLOTS)
    row_pos = lax.axis_index("rows") * rows + jnp.arange(rows)
    col_pos = lax.axis_index("cols") * cols + jnp.arange(cols)
    row_map = (((row_pos + half) // slot)[:, None] == labels[None, :]).astype(jnp.float32)
    col_map = (((col_pos + half) // slot)[:, None] == labels[None, :]).astype(jnp.float32)
    every = (jnp.arange(size) + half) // slot
    side = jnp.sum((every[:, None] == labels[None, :]).astype(jnp.float32), axis=0)
    return (row_map, col_map, side[:, None] * side[None, :])


def to_slots(values, level):
    return jnp.einsum("nhwk,ha,wb->nabk", values, level[0], level[1], precision=HIGH)


def to_pixels(table, level):
    return jnp.einsum("nabk,ha,wb->nhwk", table, level[0], level[1], precision=HIGH)


def add_pair(earlier, later):
    return (earlier[0] + later[0], earlier[1] + later[1])


def slot_total(tables):
    empty = (jnp.zeros_like(tables[0]), jnp.zeros_like(tables[1]))
    before = entering(tables, ("rows", "cols"), add_pair, empty, False)
    after = entering(tables, ("rows", "cols"), add_pair, empty, True)
    return (before[0] + tables[0] + after[0], before[1] + tables[1] + after[1])


def pad_rim(values):
    return padded_2(values, (("rows", 1), ("cols", 2)), 1)


def tap_patch(padded, masks, tap, stride):
    rows = padded.shape[1] - 2
    cols = padded.shape[2] - 2
    row_off, col_off = (tap // 3, tap % 3)
    patch = padded[:, row_off : row_off + rows : stride, col_off : col_off + cols : stride, :]
    return patch * masks[tap][::stride, ::stride][None, :, :, None]


def conv_taps(padded, weight, masks, stride):
    total = None
    for tap in range(9):
        term = jnp.einsum(
            "nhwc,cd->nhwd",
            tap_patch(padded, masks, tap, stride),
            weight[tap],
            preferred_element_type=jnp.float32,
        )
        total = term if total is None else total + term
    return total


def conv_weight_grad(padded, grad_out, masks, stride):
    return jnp.stack(
        [
            jnp.einsum(
                "nhwc,nhwd->cd",
                tap_patch(padded, masks, tap, stride),
                grad_out,
                preferred_element_type=jnp.float32,
            )
            for tap in range(9)
        ]
    )


def conv_input_grad(grad_out, weight, masks, stride):
    spread = grad_out
    if stride == 2:
        canvases, rows, cols, width = grad_out.shape
        spread = jnp.stack([grad_out, jnp.zeros_like(grad_out)], axis=2).reshape(
            canvases, 2 * rows, cols, width
        )
        spread = jnp.stack([spread, jnp.zeros_like(spread)], axis=3).reshape(
            canvases, 2 * rows, 2 * cols, width
        )
    flipped = jnp.swapaxes(weight[::-1], 1, 2)
    padded = padded_2(spread, (("rows", 1), ("cols", 2)), 1)
    return conv_taps(padded, flipped, masks, 1)


def norm_forward(values, gain, bias, scale, shift, level):
    count_n, rows, cols, width = values.shape
    grouped = values.reshape(count_n, rows, cols, GROUPS, width // GROUPS)
    total, squares = slot_total(
        (
            to_slots(jnp.sum(grouped, axis=4), level),
            to_slots(jnp.sum(grouped * grouped, axis=4), level),
        )
    )
    count = level[2][None, :, :, None] * (width // GROUPS)
    mean = total / count
    var = squares / count - mean * mean
    inverse = lax.rsqrt(var + EPS_NORM)
    mean_pix = to_pixels(mean, level)
    inv_pix = to_pixels(inverse, level)
    hat = ((grouped - mean_pix[..., None]) * inv_pix[..., None]).reshape(values.shape)
    normed = hat * gain + bias
    if scale is None:
        return (normed, (hat, inv_pix, normed, None))
    factor = 1.0 + to_pixels(scale, level)
    return (normed * factor + to_pixels(shift, level), (hat, inv_pix, normed, factor))


def norm_backward(grad_out, kept, gain, level):
    hat, inv_pix, normed, factor = kept
    count_n, rows, cols, width = hat.shape
    if factor is None:
        film_grad = None
        grad_normed = grad_out
    else:
        film_grad = jnp.concatenate(
            [to_slots(grad_out * normed, level), to_slots(grad_out, level)], axis=-1
        )
        grad_normed = grad_out * factor
    grad_gain = jnp.sum(grad_normed * hat, axis=(0, 1, 2))
    grad_bias = jnp.sum(grad_normed, axis=(0, 1, 2))
    shape = (count_n, rows, cols, GROUPS, width // GROUPS)
    grad_hat = (grad_normed * gain).reshape(shape)
    grouped_hat = hat.reshape(shape)
    first, second = slot_total(
        (
            to_slots(jnp.sum(grad_hat, axis=4), level),
            to_slots(jnp.sum(grad_hat * grouped_hat, axis=4), level),
        )
    )
    count = level[2][None, :, :, None] * (width // GROUPS)
    mean_one = to_pixels(first / count, level)[..., None]
    mean_two = to_pixels(second / count, level)[..., None]
    grad_in = inv_pix[..., None] * (grad_hat - mean_one - grouped_hat * mean_two)
    return (grad_in.reshape(hat.shape), grad_gain, grad_bias, film_grad)


def block_forward(hidden, weights, gains, film, level, masks):
    pre_one, saved_one = norm_forward(hidden, gains[0], gains[1], None, None, level)
    rim_one = pad_rim(jax.nn.silu(pre_one).astype(jnp.bfloat16))
    conv_one = conv_taps(rim_one, weights[0], masks, 1)
    pre_two, saved_two = norm_forward(conv_one, gains[2], gains[3], film[0], film[1], level)
    rim_two = pad_rim(jax.nn.silu(pre_two).astype(jnp.bfloat16))
    out = hidden + conv_taps(rim_two, weights[1], masks, 1)
    return (out, (pre_one, saved_one, rim_one, pre_two, saved_two, rim_two))


def block_backward(grad_out, weights, gains, kept, level, masks):
    pre_one, saved_one, rim_one, pre_two, saved_two, rim_two = kept
    grad_two = grad_out.astype(jnp.bfloat16)
    weight_two = conv_weight_grad(rim_two, grad_two, masks, 1)
    grad_pre_two = conv_input_grad(grad_two, weights[1], masks, 1) * silu_grad(pre_two)
    grad_conv, gain_two, bias_two, film_grad = norm_backward(
        grad_pre_two, saved_two, gains[2], level
    )
    grad_one = grad_conv.astype(jnp.bfloat16)
    weight_one = conv_weight_grad(rim_one, grad_one, masks, 1)
    grad_pre_one = conv_input_grad(grad_one, weights[0], masks, 1) * silu_grad(pre_one)
    grad_in, gain_one, bias_one, _ = norm_backward(grad_pre_one, saved_one, gains[0], level)
    return (
        grad_out + grad_in,
        (weight_one, weight_two),
        (gain_one, bias_one, gain_two, bias_two),
        film_grad,
    )


def per_device(
    image_pair,
    noise_target,
    timesteps,
    text_pooled,
    slot_live,
    edgeconv_weight,
    edgeconv_first,
    edgeconv_second,
    convlow_weight,
    convlow_first,
    convlow_second,
    convhigh_weight,
    convhigh_first,
    convhigh_second,
    downconv_weight,
    downconv_first,
    downconv_second,
    upconv_weight,
    upconv_first,
    upconv_second,
    condproj_weight,
    condproj_first,
    condproj_second,
    filmproj_weight,
    filmproj_first,
    filmproj_second,
    normparams_weight,
    normparams_first,
    normparams_second,
):
    canvases, rows_one, cols_one = image_pair.shape[:3]
    size_full = rows_one * lax.axis_size("rows")
    level_full = slot_level(rows_one, cols_one, SLOT, size_full)
    level_half = slot_level(rows_one // 2, cols_one // 2, SLOT // 2, size_full // 2)
    by_rows = (
        lax.all_gather(convlow_weight.astype(jnp.bfloat16), "rows", axis=2, tiled=True),
        lax.all_gather(convhigh_weight.astype(jnp.bfloat16), "rows", axis=2, tiled=True),
        lax.all_gather(downconv_weight.astype(jnp.bfloat16), "rows", axis=1, tiled=True),
        lax.all_gather(upconv_weight.astype(jnp.bfloat16), "rows", axis=1, tiled=True),
        lax.all_gather(filmproj_weight.astype(jnp.bfloat16), "rows", axis=0, tiled=True),
    )
    low_convs, high_convs, down_conv, up_conv, film_full = (
        lax.all_gather(by_rows[0], "cols", axis=3, tiled=True),
        lax.all_gather(by_rows[1], "cols", axis=3, tiled=True),
        lax.all_gather(by_rows[2], "cols", axis=2, tiled=True),
        lax.all_gather(by_rows[3], "cols", axis=2, tiled=True),
        lax.all_gather(by_rows[4], "cols", axis=1, tiled=True),
    )
    joined = jnp.concatenate([time_embed(timesteps).astype(jnp.bfloat16), text_pooled], axis=-1)
    cond_full = lax.all_gather(
        condproj_weight.astype(jnp.bfloat16), ("rows", "cols"), axis=1, tiled=True
    )
    pre_cond = jnp.einsum("nabk,kf->nabf", joined, cond_full, preferred_element_type=jnp.float32)
    cond_low = jax.nn.silu(pre_cond).astype(jnp.bfloat16)
    film_all = jnp.einsum("nabk,kf->nabf", cond_low, film_full, preferred_element_type=jnp.float32)
    offsets = [0, C1, 2 * C1, 3 * C1, 4 * C1, 4 * C1 + C2, 4 * C1 + 2 * C2, 5 * C1 + 2 * C2]

    def norm_part(index, which):
        return normparams_weight[which, offsets[index] : offsets[index + 1]]

    def block_gains(index):
        return (
            norm_part(2 * index, 0),
            norm_part(2 * index, 1),
            norm_part(2 * index + 1, 0),
            norm_part(2 * index + 1, 1),
        )

    def block_film(index):
        base = (0, 2 * C1, 4 * C1)[index]
        width = (C1, C1, C2)[index]
        return (film_all[..., base : base + width], film_all[..., base + width : base + 2 * width])

    masks_one = tap_masks(rows_one, cols_one, SLOT)
    masks_two = tap_masks(rows_one // 2, cols_one // 2, SLOT // 2)
    edge_low = edgeconv_weight.astype(jnp.bfloat16)
    inconv_low = jnp.swapaxes(edge_low[:, :, 0:6], 1, 2)
    head_low = edge_low[:, :, 6:9]
    rim_in = pad_rim(image_pair)
    hidden = conv_taps(rim_in, inconv_low, masks_one, 1)
    kept_blocks = []
    for index in range(2):
        hidden, kept = block_forward(
            hidden,
            (low_convs[2 * index], low_convs[2 * index + 1]),
            block_gains(index),
            block_film(index),
            level_full,
            masks_one,
        )
        kept_blocks.append(kept)
    rim_skip = pad_rim(hidden.astype(jnp.bfloat16))
    deep, kept_deep = block_forward(
        conv_taps(rim_skip, down_conv, masks_one, 2),
        (high_convs[0], high_convs[1]),
        block_gains(2),
        block_film(2),
        level_half,
        masks_two,
    )
    upsampled = jnp.repeat(jnp.repeat(deep.astype(jnp.bfloat16), 2, axis=1), 2, axis=2)
    rim_up = pad_rim(upsampled)
    merged = conv_taps(rim_up, up_conv, masks_one, 1) + hidden
    pre_head, kept_head = norm_forward(
        merged, norm_part(6, 0), norm_part(6, 1), None, None, level_full
    )
    rim_head = pad_rim(jax.nn.silu(pre_head).astype(jnp.bfloat16))
    pred = conv_taps(rim_head, head_low, masks_one, 1)
    live_slots = slot_live.astype(jnp.float32)
    live = to_pixels(live_slots[..., None], level_full)
    count = 3.0 * jnp.sum(live_slots * level_full[2][None, :, :])
    diff = pred - noise_target
    loss_local = jnp.sum(live * diff * diff)
    grad_pred = (2.0 * live * diff / count).astype(jnp.bfloat16)
    grad_head = conv_weight_grad(rim_head, grad_pred, masks_one, 1)
    grad_act = conv_input_grad(grad_pred, head_low, masks_one, 1) * silu_grad(pre_head)
    grad_merged, head_gain, head_bias, _ = norm_backward(
        grad_act, kept_head, norm_part(6, 0), level_full
    )
    merged_low = grad_merged.astype(jnp.bfloat16)
    grad_upconv = conv_weight_grad(rim_up, merged_low, masks_one, 1)
    grad_up = conv_input_grad(merged_low, up_conv, masks_one, 1)
    grad_deep = grad_up.reshape(canvases, rows_one // 2, 2, cols_one // 2, 2, C2).sum(axis=(2, 4))
    grad_down, deep_convs, deep_norms, deep_film = block_backward(
        grad_deep, (high_convs[0], high_convs[1]), block_gains(2), kept_deep, level_half, masks_two
    )
    down_low = grad_down.astype(jnp.bfloat16)
    grad_downconv = conv_weight_grad(rim_skip, down_low, masks_one, 2)
    grad_hidden = grad_merged + conv_input_grad(down_low, down_conv, masks_one, 2)
    block_convs = [None, None]
    block_norms = [None, None]
    block_films = [None, None]
    for index in (1, 0):
        grad_hidden, block_convs[index], block_norms[index], block_films[index] = block_backward(
            grad_hidden,
            (low_convs[2 * index], low_convs[2 * index + 1]),
            block_gains(index),
            kept_blocks[index],
            level_full,
            masks_one,
        )
    hidden_low = grad_hidden.astype(jnp.bfloat16)
    grad_inconv = conv_weight_grad(rim_in, hidden_low, masks_one, 1)
    image_grad = conv_input_grad(hidden_low, inconv_low, masks_one, 1) * count
    all_norms = block_norms + [deep_norms]
    gain_vector = jnp.concatenate([part[k] for part in all_norms for k in (0, 2)] + [head_gain])
    bias_vector = jnp.concatenate([part[k] for part in all_norms for k in (1, 3)] + [head_bias])
    film_grads = jnp.concatenate([block_films[0], block_films[1], deep_film], axis=-1)
    edge_local = jnp.concatenate([jnp.swapaxes(grad_inconv, 1, 2), grad_head], axis=2)
    film_sum, edge_sum, norm_sum, loss_sum = lax.psum(
        (film_grads, edge_local, jnp.stack([gain_vector, bias_vector]), loss_local),
        ("rows", "cols"),
    )
    grad_film_full = jnp.einsum(
        "nabk,nabf->kf", cond_low.astype(jnp.float32), film_sum, precision=HIGH
    )
    grad_cond = jnp.einsum(
        "nabf,kf->nabk", film_sum, film_full.astype(jnp.float32), precision=HIGH
    ) * silu_grad(pre_cond)
    grad_cond_full = jnp.einsum(
        "nabk,nabf->kf", joined.astype(jnp.float32), grad_cond, precision=HIGH
    )
    film_rows, film_cols = filmproj_weight.shape
    film_own = lax.dynamic_slice_in_dim(
        grad_film_full, lax.axis_index("rows") * film_rows, film_rows, 0
    )
    film_own = lax.dynamic_slice_in_dim(film_own, lax.axis_index("cols") * film_cols, film_cols, 1)
    cond_cols = condproj_weight.shape[1]
    cond_own = lax.dynamic_slice_in_dim(
        grad_cond_full, lax.axis_index(("rows", "cols")) * cond_cols, cond_cols, 1
    )
    by_cols = (
        lax.psum_scatter(
            jnp.stack(
                [block_convs[0][0], block_convs[0][1], block_convs[1][0], block_convs[1][1]]
            ).astype(jnp.bfloat16),
            "cols",
            scatter_dimension=3,
            tiled=True,
        ).astype(jnp.float32),
        lax.psum_scatter(
            jnp.stack([deep_convs[0], deep_convs[1]]).astype(jnp.bfloat16),
            "cols",
            scatter_dimension=3,
            tiled=True,
        ).astype(jnp.float32),
        lax.psum_scatter(
            grad_downconv.astype(jnp.bfloat16), "cols", scatter_dimension=2, tiled=True
        ).astype(jnp.float32),
        lax.psum_scatter(
            grad_upconv.astype(jnp.bfloat16), "cols", scatter_dimension=2, tiled=True
        ).astype(jnp.float32),
    )
    lowconv_own, highconv_own, downconv_own, upconv_own = (
        lax.psum_scatter(
            by_cols[0].astype(jnp.bfloat16), "rows", scatter_dimension=2, tiled=True
        ).astype(jnp.float32),
        lax.psum_scatter(
            by_cols[1].astype(jnp.bfloat16), "rows", scatter_dimension=2, tiled=True
        ).astype(jnp.float32),
        lax.psum_scatter(
            by_cols[2].astype(jnp.bfloat16), "rows", scatter_dimension=1, tiled=True
        ).astype(jnp.float32),
        lax.psum_scatter(
            by_cols[3].astype(jnp.bfloat16), "rows", scatter_dimension=1, tiled=True
        ).astype(jnp.float32),
    )
    weights = (
        edgeconv_weight,
        convlow_weight,
        convhigh_weight,
        downconv_weight,
        upconv_weight,
        condproj_weight,
        filmproj_weight,
        normparams_weight,
    )
    firsts = (
        edgeconv_first,
        convlow_first,
        convhigh_first,
        downconv_first,
        upconv_first,
        condproj_first,
        filmproj_first,
        normparams_first,
    )
    seconds = (
        edgeconv_second,
        convlow_second,
        convhigh_second,
        downconv_second,
        upconv_second,
        condproj_second,
        filmproj_second,
        normparams_second,
    )
    grads = (
        edge_sum,
        lowconv_own,
        highconv_own,
        downconv_own,
        upconv_own,
        cond_own,
        film_own,
        norm_sum,
    )
    sharded = (1, 2, 3, 4, 5, 6)
    stacked = (1, 2)
    owned_sq = sum((jnp.sum(grads[k] * grads[k]) for k in sharded))
    shared_sq = sum((jnp.sum(grads[k] * grads[k]) for k in range(8) if k not in sharded))
    clip_norm = jnp.sqrt(lax.psum(owned_sq, ("rows", "cols")) + shared_sq)
    factor = jnp.minimum(1.0, CLIP_AT / clip_norm)
    clipped, moments, updates = ([], [], [])
    for k in range(8):
        grad = grads[k] * factor
        first_new = BETA_ONE * firsts[k] + (1.0 - BETA_ONE) * grad
        second_new = BETA_TWO * seconds[k] + (1.0 - BETA_TWO) * grad * grad
        first_hat = first_new / (1.0 - BETA_ONE**STEP)
        second_hat = second_new / (1.0 - BETA_TWO**STEP)
        clipped.append(grad)
        moments.append(second_new)
        updates.append(first_hat / (jnp.sqrt(second_hat) + EPS_ADAM) + DECAY * weights[k])

    def matrix_squares(values, k):
        if k in stacked:
            return jnp.sum(values * values, axis=tuple(range(1, values.ndim)))
        return jnp.sum(values * values).reshape(1)

    weight_sq, update_sq = lax.psum(
        (
            jnp.concatenate([matrix_squares(weights[k], k) for k in sharded]),
            jnp.concatenate([matrix_squares(updates[k], k) for k in sharded]),
        ),
        ("rows", "cols"),
    )
    ratios = jnp.sqrt(weight_sq) / jnp.sqrt(update_sq)
    position = 0
    results = []
    for k in range(8):
        if k in sharded:
            span = weights[k].shape[0] if k in stacked else 1
            ratio = ratios[position : position + span]
            position += span
            ratio = (
                ratio.reshape((span,) + (1,) * (weights[k].ndim - 1)) if k in stacked else ratio[0]
            )
        elif k == 0:
            part = (jnp.arange(9) < 6)[None, None, :]
            other = jnp.logical_not(part)
            weight_sq_two = weights[k] * weights[k]
            update_sq_two = updates[k] * updates[k]
            ratio_in = jnp.sqrt(jnp.sum(jnp.where(part, weight_sq_two, 0.0))) / jnp.sqrt(
                jnp.sum(jnp.where(part, update_sq_two, 0.0))
            )
            ratio_out = jnp.sqrt(jnp.sum(jnp.where(other, weight_sq_two, 0.0))) / jnp.sqrt(
                jnp.sum(jnp.where(other, update_sq_two, 0.0))
            )
            ratio = jnp.where(part, ratio_in, ratio_out)
        else:
            ratio = jnp.sqrt(jnp.sum(weights[k] * weights[k])) / jnp.sqrt(
                jnp.sum(updates[k] * updates[k])
            )
        results.extend([clipped[k], moments[k], weights[k] - RATE * ratio * updates[k]])
    return (
        results[0],
        results[1],
        results[2],
        results[3],
        results[4],
        results[5],
        results[6],
        results[7],
        results[8],
        results[9],
        results[10],
        results[11],
        results[12],
        results[13],
        results[14],
        results[15],
        results[16],
        results[17],
        results[18],
        results[19],
        results[20],
        results[21],
        results[22],
        results[23],
        loss_sum,
        count,
        clip_norm,
        image_grad,
    )


F32 = jnp.float32
BF = jnp.bfloat16
MESH = pl.DeviceIdType.MESH
NORM_AT = (0, 128, 256, 384, 512, 768, 1024, 1152)
FILM_AT = {1: 0, 3: 256, 5: 512}
ROW_OF = (0, 1, -1, 2)
COL_OF = (-1, 0, 1, 2)
N_EXCHANGE = 20


def place_of():
    rr, cc = lax.axis_index("rows"), lax.axis_index("cols")
    return rr, cc, rr // 2, lax.rem(rr, 2), cc // 2, lax.rem(cc, 2)


def device_at(z, y, x, k):
    return {"rows": z * 2 + y, "cols": x * 2 + k}


def device_no(d):
    return {"rows": d // 4, "cols": lax.rem(d, 4)}


def meet_all(me, count=32):
    barrier = pltpu.get_barrier_semaphore()

    def hello(d, carry):
        @pl.when(d != me)
        def _():
            pl.semaphore_signal(barrier, inc=1, device_id=device_no(d), device_id_type=MESH)

        return carry

    lax.fori_loop(0, count, hello, 0)
    pl.semaphore_wait(barrier, count - 1)


def strip_at(r, c):
    pair = lax.rem((r + 1) // 2, 4)
    return (pair * 2 + c // 2) * 4 + lax.rem(c, 2) * 2 + lax.rem(r + 1, 2)


def strip_of(d):
    rr, cc = d // 4, lax.rem(d, 4)
    pair, core = rr // 2, lax.rem(cc, 2)
    r = jnp.where(pair == 0, 7 * (1 - core), 2 * pair - 1 + core)
    return r, lax.rem(rr, 2) * 2 + cc // 2


def slots_of(d):
    r, c = strip_of(d)
    row = (r + 1) // 2
    return row * 5 + c + 1, row * 5 + lax.rem(c + 1, 4)


def lane_tables():
    low = np.zeros((512, 512), np.float32)
    high = np.zeros((512, 512), np.float32)
    rest = np.zeros((512, 512), np.float32)
    for lane in range(512):
        c, q = lane // 128, lane % 128
        low[lane, (q // 32) * 128 + c * 32 + q % 32] = 1.0
        high[lane, (q // 64) * 256 + c * 64 + q % 64] = 1.0
        to = c * 64 + q if q < 64 else (256 if q < 96 else 384) + c * 32 + q % 32
        rest[lane, to] = 1.0
    return np.stack([low, rest, high])


def place_lanes(x, at, width=128):
    n = x.shape[1]
    one = (
        lax.broadcasted_iota(jnp.int32, (n, width), 0) + at
        == lax.broadcasted_iota(jnp.int32, (n, width), 1)
    )
    return jnp.dot(x, jnp.where(one, 1.0, 0.0).astype(x.dtype), preferred_element_type=F32)


ALL_ROWS = 576
LOW, REST, HIGH_PART = range(3)
ROWS_OF = ((0, 144), (144, 288), (288, 576))
Z_ORDER = (0, 1, -1, 2, -2, 3, -3)


NORM_ROW = 81
LOSS_ROW = 99


def lane_value(pairs):
    lane = lax.broadcasted_iota(jnp.int32, (8, 128), 1)
    total = jnp.zeros((8, 128), F32)
    for at, value in pairs:
        total = total + jnp.where(lane == at, value, 0.0)
    return total


def square_sum(x):
    x = x * x
    while x.ndim > 2:
        x = jnp.sum(x, axis=0)
    return jnp.sum(jnp.sum(x, axis=0, keepdims=True), axis=1, keepdims=True)


def silu_grad_tanh(v):
    s = 0.5 * jnp.tanh(0.5 * v) + 0.5
    return s * (1.0 + v * (1.0 - s))


def step_kernel(*refs):
    live_ref, temb_ref, text_ref, block_ref, lanes_ref = refs[:5]
    params, outs = refs[5:29], refs[29:53]
    loss_out, count_out, clip_out, back_out = refs[53:57]
    (
        low_ref,
        high_ref,
        down_ref,
        up_ref,
        full_ref,
        half_ref,
        work_ref,
        grad_ref,
        wide_ref,
        thin_ref,
        act_ref,
        acth_ref,
        turn_ref,
        wc_ref,
        wr_ref,
        wu_ref,
        wut_ref,
        wd_ref,
        coef_ref,
        rows_ref,
        patch_ref,
        ext_ref,
        send_ref,
        recv_ref,
        img_ref,
        tgt_ref,
        dwi_ref,
        dwh_ref,
        ngrad_ref,
        fgrad_ref,
        part_ref,
        imgrad_ref,
        wi_ref,
        wht_ref,
        wit_ref,
        wh_ref,
        tmp_ref,
        all_ref,
        strip_ref,
        cbuf_ref,
        csend_ref,
        cpart_ref,
        fsend_ref,
        frecv_ref,
        film_ref,
        joined_ref,
        condv_ref,
        rb_ref,
        rx_ref,
        ry_ref,
        rz_ref,
        own_ref,
        m1_ref,
        r1_ref,
        m2_ref,
        r2_ref,
        m3_ref,
        r3_ref,
        gcs_ref,
        gcr_ref,
        fsum_ref,
        total_ref,
        back_ref,
        send_sem,
        recv_sem,
        g_send,
        g_recv,
        strip_send,
        strip_recv,
        cond_send,
        cond_recv,
        film_send,
        film_recv,
        core_send,
        core_recv,
        x_send,
        x_recv,
        y_send,
        y_recv,
        z_send,
        z_recv,
        m_send,
        m_recv,
        gc_send,
        gc_recv,
        back_send,
        back_recv,
    ) = refs[57:]
    weights, firsts, seconds = params[0::3], params[1::3], params[2::3]
    edge_ref, norm_ref = weights[0], weights[7]
    dlow_ref, dhigh_ref, ddown_ref, dup_ref = low_ref, high_ref, down_ref, up_ref
    sb_ref = all_ref
    rr, cc, z, y, x, co = place_of()
    me = rr * 4 + cc
    core = co
    partner = 1 - co + 2 * x
    halo = rr >= 2
    split = jnp.logical_and(lax.rem(rr, 2) == 1, cc >= 2)

    def flag(cond):
        return jnp.where(cond, 1.0, 0.0).astype(F32)

    f_halo = flag(halo)
    f_core1 = flag(core == 1)
    f_core0 = 1.0 - f_core1
    f_top = f_halo * f_core1
    f_bot = f_halo * f_core0
    f_split = flag(split)
    f_joined = 1.0 - f_split

    place = lax.broadcasted_iota(jnp.int32, (32, 256), 0)
    lo_mask = jnp.where(place == 0, 0.0, jnp.where(place == 16, f_joined, 1.0))
    hi_mask = jnp.where(place == 31, 0.0, jnp.where(place == 15, f_joined, 1.0))

    def before(x):
        return pltpu.roll(x, 1, 0) * lo_mask

    def after(x):
        return pltpu.roll(x, 31, 0) * hi_mask

    def at(i):
        return pl.ds(pl.multiple_of(i * 32, 32), 32)

    def loop(body, init=0, count=16):
        return lax.fori_loop(0, count, body, init)

    def dot(a, b):
        return jnp.dot(a, b, preferred_element_type=F32)

    def dot_nt(a, b):
        return lax.dot_general(a, b, (((1,), (1,)), ((), ())), preferred_element_type=F32)

    def sigmoid(z):
        return 0.5 * jnp.tanh(0.5 * z) + 0.5

    def double(v):
        return jnp.concatenate([v, v], axis=1)


    def copy_of(e):
        return pltpu.make_async_remote_copy(
            src_ref=send_ref.at[e],
            dst_ref=recv_ref.at[e],
            send_sem=send_sem.at[e],
            recv_sem=recv_sem.at[e],
            device_id={"cols": partner},
            device_id_type=MESH,
        )

    def send(e, row, stats=None):
        send_ref[e, 0:32, :] = row
        send_ref[e, 32:40, :] = jnp.zeros((8, 256), F32) if stats is None else stats
        copy_of(e).start()

    def arrive(e):
        copy_of(e).wait()

    def edge_full(ref):
        low = f_core0 * ref[0, 480:512, 128:256] + f_core1 * ref[0, 0:32, 0:128]
        high = f_core0 * ref[1, 480:512, 128:256] + f_core1 * ref[1, 0:32, 0:128]
        return jnp.concatenate([low, high], axis=1)

    def edge_cell(ref):
        return f_core0 * ref[480:512, :] + f_core1 * ref[0:32, :]

    def edge(ref, planes):
        return edge_full(ref) if planes == 2 else edge_cell(ref.at[0])


    def halves(x):
        return x[0:8] + x[8:16], x[16:24] + x[24:32]

    def gathered(sums, planes):
        rows = []
        for s in sums:
            row = jnp.sum(s, axis=0, keepdims=True)
            rows.append(double(row[:, 0:128] + row[:, 128:256]) if planes == 2 else row)
        return jnp.concatenate(rows + [jnp.zeros((4, 256), F32)], axis=0)

    zero8 = jnp.zeros((8, 256), F32)

    def stats_of(x_ref, planes):
        def body(i, carry):
            s_l, s_r, q_l, q_r = carry
            for p in range(planes):
                x = x_ref[p, at(i), :]
                a, b = halves(x)
                c, d = halves(x * x)
                s_l, s_r, q_l, q_r = s_l + a, s_r + b, q_l + c, q_r + d
            return s_l, s_r, q_l, q_r

        return gathered(loop(body, (zero8,) * 4), planes)

    def over_slot(block, planes):
        swapped = jnp.concatenate(
            [block[1:2], block[0:1], block[3:4], block[2:3], block[4:8]], axis=0
        )
        x = block + f_joined * swapped
        lane = lax.broadcasted_iota(jnp.int32, (8, 256), 1)
        step = 1
        while step < (4 if planes == 2 else 8):
            up = pltpu.roll(x, 256 - step, 1)
            down = pltpu.roll(x, step, 1)
            x = x + jnp.where(lax.rem(lane, 2 * step) < step, up, down)
            step *= 2
        size = 16.0 if planes == 2 else 8.0
        count = (16.0 + 16.0 * f_halo) * (16.0 + 16.0 * f_joined) * size
        return x / count

    def spread(two):
        return jnp.concatenate(
            [
                jnp.broadcast_to(two[0:1], (16, 256)),
                jnp.broadcast_to(two[1:2], (16, 256)),
            ],
            axis=0,
        )

    def norm_row(k, which):
        width = NORM_AT[k + 1] - NORM_AT[k] if k < 6 else 128
        row = norm_ref[which : which + 1, NORM_AT[k] : NORM_AT[k] + width]
        return double(row) if width == 128 else row

    def film_rows(k, which):
        if k not in FILM_AT:
            return jnp.zeros((2, 256), F32)
        width = 256 if k == 5 else 128
        base = FILM_AT[k] + which * width
        two = film_ref[0:2, base : base + width]
        return double(two) if width == 128 else two

    def norm_ready(k, stats, e, planes):
        total = over_slot(stats + f_halo * recv_ref[e, 32:40, :], planes)
        mean = total[0:2]
        var = total[2:4] - mean * mean
        inverse = lax.rsqrt(var + EPS_NORM)
        gain, bias = norm_row(k, 0), norm_row(k, 1)
        factor = 1.0 + film_rows(k, 0)
        slope = inverse * gain * factor
        coef_ref[k, 0] = spread(slope)
        coef_ref[k, 1] = spread((bias - mean * inverse * gain) * factor + film_rows(k, 1))
        coef_ref[k, 2] = spread(mean)
        coef_ref[k, 3] = spread(inverse)
        rows_ref[k, 0:2, :] = mean
        rows_ref[k, 2:4, :] = inverse

    def activated(x, k):
        z = x * coef_ref[k, 0] + coef_ref[k, 1]
        return z * sigmoid(z)


    def put_wide(i, even, odd):
        for t, g in enumerate((before(odd), even, odd, after(even))):
            b = g.astype(BF)
            wide_ref[at(i + 1), 512 * t : 512 * t + 256] = b
            wide_ref[at(i + 2), 512 * t + 256 : 512 * t + 384] = b[:, 128:256]
            wide_ref[at(i), 512 * t + 384 : 512 * t + 512] = b[:, 0:128]

    def put_wide_edge(row):
        even, odd = row[:, 0:128], row[:, 128:256]
        lo, hi = lo_mask[:, 0:128], hi_mask[:, 0:128]
        for t, g in enumerate((pltpu.roll(odd, 1, 0) * lo, even, odd, pltpu.roll(even, 31, 0) * hi)):
            wide_ref[32:64, 512 * t + 256 : 512 * t + 384] = (g * f_top).astype(BF)
            wide_ref[512:544, 512 * t + 384 : 512 * t + 512] = (g * f_bot).astype(BF)

    def put_thin(i, x):
        for t, g in enumerate((before(x), x, after(x))):
            thin_ref[at(i + 1), 256 * t : 256 * t + 256] = g.astype(BF)

    def put_thin_edge(row):
        for t, g in enumerate((before(row), row, after(row))):
            thin_ref[0:32, 256 * t : 256 * t + 256] = (g * f_top).astype(BF)
            thin_ref[544:576, 256 * t : 256 * t + 256] = (g * f_bot).astype(BF)

    def keep_wide(slot):
        act_ref[slot, 0] = wide_ref[32:544, 512:768]
        act_ref[slot, 1] = wide_ref[32:544, 1024:1280]

    def keep_thin(slot):
        acth_ref[slot] = thin_ref[32:544, 256:512]

    def turn_wide(slot):
        turn_ref[0:256, :] = act_ref[slot, 0].T
        turn_ref[256:512, :] = act_ref[slot, 1].T


    def load_wc(index):
        for b in range(3):
            for r in range(4):
                for rp in range(2):
                    a = ROW_OF[r] - rp + 1
                    if 0 <= a <= 2:
                        wc_ref[
                            b * 512 + r * 128 : b * 512 + r * 128 + 128, rp * 128 : rp * 128 + 128
                        ] = low_ref[index, 3 * a + b]

    def load_wr(index):
        for b in range(3):
            for r in range(4):
                for rp in range(2):
                    a = ROW_OF[r] - rp + 1
                    if 0 <= a <= 2:
                        wr_ref[
                            rp * 128 : rp * 128 + 128, b * 512 + r * 128 : b * 512 + r * 128 + 128
                        ] = low_ref[index, 8 - 3 * a - b]

    def taps_of(parity, d):
        if parity == 0:
            return {-1: (0,), 0: (1, 2)}.get(d, ())
        return {0: (0, 1), 1: (2,)}.get(d, ())

    def load_up():
        for cp in range(2):
            for rp in range(2):
                for di in (-1, 0, 1):
                    for dj in (-1, 0, 1):
                        taps = [3 * a + b for a in taps_of(rp, di) for b in taps_of(cp, dj)]
                        if not taps:
                            continue
                        total = up_ref[taps[0]].astype(F32)
                        for t in taps[1:]:
                            total = total + up_ref[t].astype(F32)
                        low = total.astype(BF)
                        at_k = (dj + 1 - cp) * 256
                        wu_ref[cp, di + 1, at_k : at_k + 256, rp * 128 : rp * 128 + 128] = low
                        row = ROW_OF.index(rp - 2 * di)
                        col = COL_OF.index(cp - 2 * dj)
                        wut_ref[:, col * 512 + row * 128 : col * 512 + row * 128 + 128] = low

    def load_down():
        for b in range(3):
            for r in range(3):
                a = ROW_OF[r] + 1
                wd_ref[b * 512 + r * 128 : b * 512 + r * 128 + 128, :] = down_ref[3 * a + b]


    def conv_low(out, weight_nt=False):
        for cp in range(2):
            left = wide_ref[32:544, cp * 512 : cp * 512 + 1536]
            out(cp, dot_nt(left, wr_ref[...]) if weight_nt else dot(left, wc_ref[...]))

    def conv_high(index):
        total = None
        for a in range(3):
            term = dot(
                thin_ref[32 * a : 32 * a + 512, :],
                high_ref[index, 3 * a : 3 * a + 3].reshape(768, 256),
            )
            total = term if total is None else total + term
        return total

    def conv_high_back(index):
        total = None
        for a in range(3):
            for b in range(3):
                term = dot_nt(
                    thin_ref[32 * a : 32 * a + 512, b * 256 : b * 256 + 256],
                    high_ref[index, 8 - 3 * a - b],
                )
                total = term if total is None else total + term
        return total

    def grad_low(index, slot):
        turn_wide(slot)
        for b in range(3):
            block = dot(turn_ref[0:256, :], wide_ref[32:544, b * 512 : b * 512 + 512]) + dot(
                turn_ref[256:512, :], wide_ref[32:544, b * 512 + 512 : b * 512 + 1024]
            )
            for a in range(3):
                first = ROW_OF.index(a - 1) * 128
                second = ROW_OF.index(a) * 128
                dlow_ref[index, 8 - 3 * a - b] = (
                    block[0:128, first : first + 128] + block[128:256, second : second + 128]
                ).astype(dlow_ref.dtype)

    def grad_high(index, slot):
        turn_ref[0:256, :] = acth_ref[slot].T
        for a in range(3):
            block = dot(turn_ref[0:256, :], thin_ref[32 * a : 32 * a + 512, :])
            for b in range(3):
                dhigh_ref[index, 8 - 3 * a - b] = block[:, b * 256 : b * 256 + 256].astype(
                    dhigh_ref.dtype
                )


    def put_patch(slot, source, row, lanes):
        ext_ref[0:32, :] = row * f_top
        ext_ref[544:576, :] = row * f_bot

        def fill(i, carry):
            ext_ref[at(i + 1), :] = source[at(i), :]
            return carry

        loop(fill)

        def body(i, carry):
            total = None
            for di in (-1, 0, 1):
                x = ext_ref[at(i + 1 + di), :]
                for dj, g in enumerate((before(x), x, after(x))):
                    shift = ((di + 1) * 3 + dj) * lanes
                    term = pltpu.roll(g, shift, 1) if shift else g
                    total = term if total is None else total + term
            patch_ref[slot, at(i), :] = total.astype(BF)
            return carry

        loop(body)


    def norm_back_start(k, x_ref, planes):
        def body(i, carry):
            s_l, s_r, q_l, q_r = carry
            for p in range(planes):
                x = x_ref[p, at(i), :]
                z = x * coef_ref[k, 0] + coef_ref[k, 1]
                s = sigmoid(z)
                d = work_ref[p, at(i), :] * (s * (1.0 + z * (1.0 - s)))
                work_ref[p, at(i), :] = d
                a, b = halves(d)
                c, e = halves(d * ((x - coef_ref[k, 2]) * coef_ref[k, 3]))
                s_l, s_r, q_l, q_r = s_l + a, s_r + b, q_l + c, q_r + e
            return s_l, s_r, q_l, q_r

        return gathered(loop(body, (zero8,) * 4), planes)

    def norm_back_ready(k, stats, e, planes):
        gain, bias = norm_row(k, 0), norm_row(k, 1)
        factor = 1.0 + film_rows(k, 0)
        width = 128 if planes == 2 else 256
        one, two = stats[0:2], stats[2:4]
        dgain, dbias = factor * two, factor * one
        o = NORM_AT[k]
        ngrad_ref[0:1, o : o + width] = (dgain[0:1] + dgain[1:2])[:, 0:width]
        ngrad_ref[1:2, o : o + width] = (dbias[0:1] + dbias[1:2])[:, 0:width]
        if k in FILM_AT:
            f = FILM_AT[k]
            fgrad_ref[0:2, f : f + width] = (gain * two + bias * one)[:, 0:width]
            fgrad_ref[0:2, f + width : f + 2 * width] = one[:, 0:width]
        both = stats + f_halo * recv_ref[e, 32:40, :]
        kk = gain * factor
        scaled = jnp.concatenate([kk * both[0:2], kk * both[2:4], both[4:8]], axis=0)
        total = over_slot(scaled, planes)
        mean, inverse = rows_ref[k, 0:2, :], rows_ref[k, 2:4, :]
        second = -inverse * inverse * total[2:4]
        third = -inverse * total[0:2] - mean * second
        coef_ref[k, 4] = spread(inverse * kk)
        coef_ref[k, 5] = spread(second)
        coef_ref[k, 6] = spread(third)

    def back_value(k, d, x):
        return d * coef_ref[k, 4] + x * coef_ref[k, 5] + coef_ref[k, 6]


    def shard(kind, part, zs, ys, xs, ks, device):
        rows = slice(*ROWS_OF[part])
        return pltpu.make_async_remote_copy(
            src_ref=all_ref.at[zs, ys, xs, ks, rows],
            dst_ref=all_ref.at[zs, ys, xs, ks, rows],
            send_sem=g_send.at[part, kind, zs, ys, xs],
            recv_sem=g_recv.at[part, zs, ys, xs, ks],
            device_id=device,
            device_id_type=MESH,
        )

    def to_up(part, zs):
        return shard(0, part, zs, y, x, co, device_at(z + 1, y, x, co))

    def to_down(part, zs):
        return shard(1, part, zs, y, x, co, device_at(z - 1, y, x, co))

    def to_x(part, zs, ys):
        return shard(2, part, zs, ys, x, co, device_at(z, y, 1 - x, co))

    def to_y(part, zs, xs):
        return shard(3, part, zs, y, xs, co, device_at(z, 1 - y, x, co))

    def to_core(part, zs, ys, xs):
        return shard(4, part, zs, ys, xs, co, device_at(z, y, x, 1 - co))

    def arrived(part, zs, ys, xs, ks=co):
        shard(4, part, zs, ys, xs, ks, device_at(z, y, x, 1 - co)).wait_recv()

    def start(copy):
        copy.start()

    def in_line(dz, act):
        zs = z + dz

        @pl.when(jnp.logical_and(zs >= 0, zs <= 3))
        def _():
            act(zs)

    def gather_z(part, dzs, act=start, wait=arrived):
        for dz in dzs:

            def one(zs, dz=dz):
                if dz:
                    wait(part, zs, y, x)
                if dz <= 0:

                    @pl.when(z < 3)
                    def _():
                        act(to_up(part, zs))

                if dz >= 0:

                    @pl.when(z > 0)
                    def _():
                        act(to_down(part, zs))

                act(to_x(part, zs, y))
                act(to_y(part, zs, x))
                act(to_core(part, zs, y, x))

            in_line(dz, one)

    def gather_xy(part, act=start, wait=arrived):
        for dz in Z_ORDER:

            def one(zs):
                wait(part, zs, y, 1 - x)

                @pl.when(lax.rem(zs, 2) == 0)
                def _():
                    act(to_y(part, zs, 1 - x))

                act(to_core(part, zs, y, 1 - x))
                wait(part, zs, 1 - y, x)

                @pl.when(lax.rem(zs, 2) == 1)
                def _():
                    act(to_x(part, zs, 1 - y))

                act(to_core(part, zs, 1 - y, x))

            in_line(dz, one)

    def gather_last(part, act=start, wait=arrived):
        for dz in Z_ORDER:

            def one(zs):
                wait(part, zs, 1 - y, 1 - x)
                act(to_core(part, zs, 1 - y, 1 - x))

            in_line(dz, one)

    def gather_sent(part):
        def sent(copy):
            copy.wait_send()

        def none(*a):
            return None

        gather_z(part, Z_ORDER, sent, none)
        gather_xy(part, sent, none)
        gather_last(part, sent, none)

    def row_places(r):
        def rows(at_row, size):
            return pl.ds(pl.multiple_of(at_row, 16), size)

        return rows(r * 16, 16), rows(r * 32, 32), rows(r * 32, 16), rows(r * 32 + 16, 16)

    def gather_place(part):
        for zs in range(4):
            for ys in range(2):
                for xs in range(2):
                    arrived(part, zs, ys, xs, 1 - co)
        rows = slice(*ROWS_OF[part])

        def row(r, carry):
            zr, yr = r // 2, lax.rem(r, 2)
            at16, at32, a16, b16 = row_places(r)
            packed = jnp.concatenate(
                [all_ref[zr, yr, c // 2, c % 2, rows, :] for c in range(4)], axis=1
            )
            v = jnp.dot(packed, lanes_ref[part], preferred_element_type=F32).astype(BF)
            if part == LOW:
                for j in range(4):
                    low_ref[j, :, at16, :] = v[:, j * 128 : j * 128 + 128].reshape(9, 16, 128)
            elif part == HIGH_PART:
                for j in range(2):
                    high_ref[j, :, at32, :] = v[:, j * 256 : j * 256 + 256].reshape(9, 32, 256)
            else:
                down_ref[:, at16, :] = v[:, 0:256].reshape(9, 16, 256)
                up_ref[:, a16, :] = v[:, 256:384].reshape(9, 16, 128)
                up_ref[:, b16, :] = v[:, 384:512].reshape(9, 16, 128)
            return carry

        lax.fori_loop(0, 8, row, 0)

    def pack_own(part):
        rows = slice(*ROWS_OF[part])
        own = all_ref.at[z, y, x, co]
        if part == LOW:
            total = None
            for j in range(4):
                term = place_lanes(weights[1][j].reshape(144, 32).astype(BF), 32 * j)
                total = term if total is None else total + term
        elif part == HIGH_PART:
            total = place_lanes(weights[2][0].reshape(288, 64).astype(BF), 0) + place_lanes(
                weights[2][1].reshape(288, 64).astype(BF), 64
            )
        else:
            total = (
                place_lanes(weights[3][...].reshape(144, 64).astype(BF), 0)
                + place_lanes(weights[4][:, 0:16, :].reshape(144, 32).astype(BF), 64)
                + place_lanes(weights[4][:, 16:32, :].reshape(144, 32).astype(BF), 96)
            )
        own[rows, :] = total.astype(BF)

    to_left = strip_at(rr, cc)
    to_right = strip_at(rr, lax.rem(cc + 3, 4))

    def strip_copy(side, device):
        return pltpu.make_async_remote_copy(
            src_ref=block_ref.at[1 - side],
            dst_ref=strip_ref.at[side],
            send_sem=strip_send.at[side],
            recv_sem=strip_recv.at[side],
            device_id=device_no(device),
            device_id_type=MESH,
        )


    def others(body):
        def one(d, carry):
            @pl.when(d != me)
            def _():
                body(d)

            return carry

        lax.fori_loop(0, 32, one, 0)

    def row_mates(body):
        for c in range(4):

            @pl.when(cc != c)
            def _(c=c):
                body(c)

    def cond_copy(c, source):
        return pltpu.make_async_remote_copy(
            src_ref=csend_ref,
            dst_ref=cbuf_ref.at[source],
            send_sem=cond_send.at[c],
            recv_sem=cond_recv.at[source],
            device_id={"rows": rr, "cols": c},
            device_id_type=MESH,
        )

    def film_copy(d, source):
        return pltpu.make_async_remote_copy(
            src_ref=fsend_ref.at[d],
            dst_ref=frecv_ref.at[source],
            send_sem=film_send.at[d],
            recv_sem=film_recv.at[source],
            device_id=device_no(d),
            device_id_type=MESH,
        )

    def cond_start():
        joined_ref[24:32, :] = jnp.zeros((8, joined_ref.shape[1]), F32)
        for a in range(5):
            joined_ref[5 * a : 5 * a + 5, 0:128] = temb_ref[a].astype(F32)
            joined_ref[5 * a : 5 * a + 5, 128:] = text_ref[a].astype(F32)
        own = dot_nt(joined_ref[...].astype(BF), weights[5][...].astype(BF))
        csend_ref[...] = jnp.concatenate([own, jnp.zeros((32, 112), F32)], axis=1)
        row_mates(lambda c: cond_copy(c, cc).start())
        cbuf_ref[cc] = csend_ref[...]

    def film_start():
        row_mates(lambda c: cond_copy(c, c).wait_recv())
        whole = cbuf_ref[0]
        for c in range(1, 4):
            whole = whole + pltpu.roll(cbuf_ref[c], 16 * c, 1)
        whole = whole[:, 0:64]
        cond = (whole * sigmoid(whole)).astype(BF)
        condv_ref[...] = cond.astype(F32)
        cpart_ref[...] = dot(cond, weights[6][...].astype(BF))
        fsend_ref[...] = jnp.zeros(fsend_ref.shape, F32)

        def deal(d, carry):
            s_l, s_r = slots_of(d)
            fsend_ref[d, 0:1, :] = cpart_ref[pl.ds(s_l, 1), :]
            fsend_ref[d, 1:2, :] = cpart_ref[pl.ds(s_r, 1), :]

            @pl.when(d != me)
            def _():
                film_copy(d, me).start()

            return carry

        lax.fori_loop(0, 32, deal, 0)
        frecv_ref[me] = fsend_ref[me]

    def film_ready():
        others(lambda d: film_copy(d, d).wait_recv())
        for c in range(4):
            total = frecv_ref[c]
            for r in range(1, 8):
                total = total + frecv_ref[4 * r + c]
            film_ref[:, c * 256 : c * 256 + 256] = total


    def edge_terms():
        for a in range(3):
            for b in range(3):
                for cp in range(2):
                    for rp in range(2):
                        rho, gamma = rp + a - 1, cp + b - 1
                        cell = (rho // 2 + 1) * 3 + gamma // 2 + 1
                        phase = (gamma % 2) * 2 + rho % 2
                        tile = COL_OF.index(gamma) * 512 + ROW_OF.index(rho) * 128
                        yield 3 * a + b, cp, rp, cell, phase, tile

    def load_edges():
        dwi_ref[...] = jnp.zeros(dwi_ref.shape, F32)
        dwh_ref[...] = jnp.zeros(dwh_ref.shape, F32)
        for t, cp, rp, cell, phase, _ in edge_terms():
            lanes = slice(rp * 128, rp * 128 + 128)
            row = cell * 24 + phase * 6
            dwi_ref[cp, row : row + 6, lanes] = edge_ref[t, 0:6, :]
            row = cell * 12 + phase * 3
            dwh_ref[cp, row : row + 3, lanes] = edge_ref[8 - t, 6:9, :]
        wi_ref[...] = dwi_ref[...].astype(BF)
        wht_ref[...] = dwh_ref[...].astype(BF)
        for ref, taps, lo, size in ((wh_ref, 1, 6, 3), (wit_ref, -1, 0, 6)):
            ref[...] = jnp.zeros(ref.shape, BF)
            tmp_ref[...] = jnp.zeros(tmp_ref.shape, F32)
            for t, cp, rp, _, _, tile in edge_terms():
                row = (cp * 2 + rp) * size
                tap = t if taps > 0 else 8 - t
                tmp_ref[row : row + size, tile : tile + 128] = edge_ref[tap, lo : lo + size, :]
            ref[0:32, :] = tmp_ref[...].astype(BF)


    def add(to, b):
        to[...] = (to[...].astype(F32) + b[...].astype(F32)).astype(BF)

    def deal_pack(part, r_lo, r_hi):
        rows = slice(*ROWS_OF[part])

        def row(r, carry):
            zr, yr = r // 2, lax.rem(r, 2)
            at16, at32, a16, b16 = row_places(r)
            if part == LOW:
                pieces = [dlow_ref[j, :, at16, :].reshape(144, 128) for j in range(4)]
            elif part == HIGH_PART:
                pieces = [dhigh_ref[j, :, at32, :].reshape(288, 256) for j in range(2)]
            else:
                pieces = [
                    ddown_ref[:, at16, :].reshape(144, 256),
                    dup_ref[:, a16, :].reshape(144, 128),
                    dup_ref[:, b16, :].reshape(144, 128),
                ]
            v = dot_nt(jnp.concatenate(pieces, axis=1), lanes_ref[part]).astype(BF)
            for c in range(4):
                sb_ref[zr, yr, c // 2, c % 2, rows, :] = v[:, c * 128 : c * 128 + 128]
            return carry

        lax.fori_loop(r_lo, r_hi, row, 0)

    def core_copy(part, zs):
        rows = slice(*ROWS_OF[part])
        return pltpu.make_async_remote_copy(
            src_ref=sb_ref.at[zs, :, :, 1 - co, rows],
            dst_ref=rb_ref.at[zs, :, :, rows],
            send_sem=core_send.at[part, zs],
            recv_sem=core_recv.at[part, zs],
            device_id=device_at(z, y, x, 1 - co),
            device_id_type=MESH,
        )

    def first_copy(part, zs):
        rows = slice(*ROWS_OF[part])
        by_x = zs % 2 == 0
        return pltpu.make_async_remote_copy(
            src_ref=rb_ref.at[zs, :, 1 - x, rows] if by_x else rb_ref.at[zs, 1 - y, :, rows],
            dst_ref=rx_ref.at[zs, :, rows],
            send_sem=x_send.at[part, zs],
            recv_sem=x_recv.at[part, zs],
            device_id=device_at(z, y, 1 - x, co) if by_x else device_at(z, 1 - y, x, co),
            device_id_type=MESH,
        )

    def second_copy(part, zs):
        rows = slice(*ROWS_OF[part])
        by_x = zs % 2 == 1
        return pltpu.make_async_remote_copy(
            src_ref=rb_ref.at[zs, y, 1 - x, rows] if by_x else rb_ref.at[zs, 1 - y, x, rows],
            dst_ref=ry_ref.at[zs, rows],
            send_sem=y_send.at[part, zs],
            recv_sem=y_recv.at[part, zs],
            device_id=device_at(z, y, 1 - x, co) if by_x else device_at(z, 1 - y, x, co),
            device_id_type=MESH,
        )

    def z_copy(part, zs, source):
        rows = slice(*ROWS_OF[part])
        return pltpu.make_async_remote_copy(
            src_ref=rb_ref.at[zs, y, x, rows],
            dst_ref=rz_ref.at[source, rows],
            send_sem=z_send.at[part, zs],
            recv_sem=z_recv.at[part, source],
            device_id=device_at(zs, y, x, co),
            device_id_type=MESH,
        )

    def deal_core(part):
        for zs in range(4):
            deal_pack(part, 2 * zs, 2 * zs + 2)
            core_copy(part, zs).start()

    def deal_first(part):
        rows = slice(*ROWS_OF[part])
        for zs in range(4):
            core_copy(part, zs).wait_recv()
            for ys in range(2):
                for xs in range(2):
                    add(rb_ref.at[zs, ys, xs, rows], sb_ref.at[zs, ys, xs, co, rows])
            first_copy(part, zs).start()

    def deal_second(part):
        rows = slice(*ROWS_OF[part])
        for zs in range(4):
            first_copy(part, zs).wait_recv()
            for other in range(2):
                to = rb_ref.at[zs, other, x, rows] if zs % 2 == 0 else rb_ref.at[zs, y, other, rows]
                add(to, rx_ref.at[zs, other, rows])
            second_copy(part, zs).start()

    def deal_z(part):
        rows = slice(*ROWS_OF[part])
        for zs in range(4):
            second_copy(part, zs).wait_recv()
            add(rb_ref.at[zs, y, x, rows], ry_ref.at[zs, rows])

            @pl.when(zs != z)
            def _(zs=zs):
                z_copy(part, zs, z).start()

            @pl.when(zs == z)
            def _(zs=zs):
                rz_ref[zs, rows, :] = rb_ref[zs, y, x, rows, :]

    def deal_end(part):
        rows = slice(*ROWS_OF[part])
        for zs in range(4):

            @pl.when(zs != z)
            def _(zs=zs):
                z_copy(part, zs, zs).wait_recv()

        own = rz_ref[0, rows, :].astype(F32)
        for zs in range(1, 4):
            own = own + rz_ref[zs, rows, :].astype(F32)
        own_ref[rows, :] = own

    def deal_sent(part):
        for zs in range(4):
            core_copy(part, zs).wait_send()
            first_copy(part, zs).wait_send()
            second_copy(part, zs).wait_send()

            @pl.when(zs != z)
            def _(zs=zs):
                z_copy(part, zs, z).wait_send()


    pack_own(LOW)
    meet_all(me)
    gather_z(LOW, (0,))
    strip_copy(0, to_left).start()

    @pl.when(to_right != me)
    def _():
        strip_copy(1, to_right).start()

    cond_start()
    gather_z(LOW, (1, -1))
    pack_own(REST)
    pack_own(HIGH_PART)
    gather_z(LOW, (2, -2))
    gather_z(LOW, (3, -3))
    gather_xy(LOW)
    gather_z(REST, (0,))
    gather_z(HIGH_PART, (0,))
    load_edges()
    film_start()
    gather_last(LOW)

    live_all = live_ref[...].astype(F32)
    slot_r = lax.broadcasted_iota(jnp.int32, (5, 5), 0)
    slot_c = lax.broadcasted_iota(jnp.int32, (5, 5), 1)

    def side(s):
        return jnp.where(jnp.logical_or(s == 0, s == 4), 32.0, 64.0)

    def all_sum(v):
        return jnp.sum(jnp.sum(v, axis=0, keepdims=True), axis=1, keepdims=True)

    count = 3.0 * all_sum(live_all * side(slot_r) * side(slot_c))
    count_out[...] = jnp.broadcast_to(count, (1, 128))
    my_l, my_r = slots_of(me)
    slot_id = slot_r * 5 + slot_c
    live_l = all_sum(jnp.where(slot_id == my_l, live_all, 0.0))
    live_r = all_sum(jnp.where(slot_id == my_r, live_all, 0.0))

    def zero(i, carry):
        wc_ref[at(i), :] = jnp.zeros((32, 256), BF)
        return carry

    loop(zero, count=48)
    wr_ref[...] = jnp.zeros(wr_ref.shape, BF)
    for cp in range(2):
        for di in range(3):
            wu_ref[cp, di] = jnp.zeros((512, 256), BF)
    for b in range(3):
        wd_ref[b * 512 + 384 : b * 512 + 512, :] = jnp.zeros((128, 256), BF)


    strip_copy(0, to_left).wait()

    @pl.when(to_right != me)
    def _():
        strip_copy(1, to_right).wait()

    @pl.when(to_right == me)
    def _():
        strip_ref[1] = block_ref[0]


    lane = lax.broadcasted_iota(jnp.int32, (32, 128), 1)
    none = jnp.zeros((32, 128), F32)

    def open_strip(i, carry):
        half = pl.ds(pl.multiple_of(i * 16, 16), 16)
        x = jnp.concatenate([strip_ref[0, half, :], strip_ref[1, half, :]], axis=0)
        img_ref[at(i), :] = jnp.concatenate([jnp.where(lane < 24, x, 0.0), none], axis=1)
        x = jnp.where(lane < 12, pltpu.roll(x, 104, 1), 0.0)
        tgt_ref[at(i), :] = jnp.concatenate([x, none], axis=1)
        return carry

    loop(open_strip)
    send(0, edge_cell(img_ref))
    arrive(0)
    put_patch(0, img_ref, recv_ref[0, 0:32, :], 24)
    for cp in range(2):
        full_ref[0, cp] = dot(patch_ref[0], wi_ref[cp])

    def fwd_norm_full(k, source, e):
        stats = stats_of(source, 2)
        send(e, edge_full(source), stats)
        return stats

    def fwd_apply_full(k, source, stats, e):
        arrive(e)
        norm_ready(k, stats, e, 2)

        def body(i, carry):
            put_wide(
                i,
                activated(source[0, at(i), :], k),
                activated(source[1, at(i), :], k),
            )
            return carry

        loop(body)
        put_wide_edge(activated(recv_ref[e, 0:32, :], k))

    for index in range(2):
        h = full_ref.at[2 * index]
        mid = full_ref.at[2 * index + 1]
        out = full_ref.at[2 * index + 2]
        k = 2 * index
        stats = fwd_norm_full(k, h, 1 + k)
        if index:
            gather_xy(REST)
            gather_xy(HIGH_PART)
            load_wc(2)
        else:
            gather_place(LOW)
            load_wc(0)
        fwd_apply_full(k, h, stats, 1 + k)
        keep_wide(k)

        def put_mid(cp, value, mid=mid):
            mid[cp] = value

        conv_low(put_mid)
        if not index:
            gather_z(REST, (1, -1))
            gather_z(HIGH_PART, (1, -1))
        stats = fwd_norm_full(k + 1, mid, 2 + k)
        load_wc(2 * index + 1)
        if index:
            gather_last(REST)
            gather_last(HIGH_PART)
        else:
            gather_z(REST, (2, -2))
            gather_z(HIGH_PART, (2, -2))
            film_ready()
        fwd_apply_full(k + 1, mid, stats, 2 + k)
        keep_wide(k + 1)

        def put_out(cp, value, h=h, out=out):
            out[cp] = h[cp] + value

        conv_low(put_out)
        if not index:
            gather_z(REST, (3, -3))
            gather_z(HIGH_PART, (3, -3))

    skip = full_ref.at[4]
    send(5, edge_full(skip))
    gather_place(REST)
    load_down()

    def skip_body(i, carry):
        put_wide(i, skip[0, at(i), :], skip[1, at(i), :])
        return carry

    loop(skip_body)
    arrive(5)
    put_wide_edge(recv_ref[5, 0:32, :])
    keep_wide(4)
    half_ref[0, 0] = dot(wide_ref[32:544, 0:1536], wd_ref[...])

    def fwd_half(k, source, e):
        stats = stats_of(source, 1)
        send(e, edge_cell(source.at[0]), stats)
        arrive(e)
        norm_ready(k, stats, e, 1)

        def body(i, carry):
            put_thin(i, activated(source[0, at(i), :], k))
            return carry

        loop(body)
        put_thin_edge(activated(recv_ref[e, 0:32, :], k))

    fwd_half(4, half_ref.at[0], 6)
    keep_thin(0)
    gather_place(HIGH_PART)
    half_ref[1, 0] = conv_high(0)
    fwd_half(5, half_ref.at[1], 7)
    keep_thin(1)
    half_ref[2, 0] = half_ref[0, 0] + conv_high(1)
    deep = half_ref.at[2]
    send(8, edge_cell(deep.at[0]))
    load_up()

    def deep_body(i, carry):
        put_thin(i, deep[0, at(i), :])
        return carry

    loop(deep_body)
    arrive(8)
    put_thin_edge(recv_ref[8, 0:32, :])
    keep_thin(2)
    merged = full_ref.at[5]
    for cp in range(2):
        total = skip[cp]
        for di in range(3):
            total = total + dot(
                thin_ref[32 * di : 32 * di + 512, cp * 256 : cp * 256 + 512], wu_ref[cp, di]
            )
        merged[cp] = total

    stats = fwd_norm_full(6, merged, 9)
    fwd_apply_full(6, merged, stats, 9)
    keep_wide(5)
    work_ref[0] = jnp.concatenate(
        [dot_nt(wide_ref[32:544, :], wh_ref[...]), jnp.zeros((512, 128), F32)], axis=1
    )

    live = spread(jnp.broadcast_to(jnp.concatenate([live_l, live_r], axis=0), (2, 256)))
    weight = 2.0 / count

    def loss_body(i, carry):
        diff = work_ref[0, at(i), :] - tgt_ref[at(i), :]
        half = live * diff
        work_ref[0, at(i), :] = (half * weight).astype(BF).astype(F32)
        return carry + half * diff

    lost = loop(loss_body, jnp.zeros((32, 256), F32))
    lost = jnp.sum(lost, axis=0, keepdims=True)
    part_ref[...] = jnp.zeros(part_ref.shape, F32)
    part_ref[99:100, :] = lost[:, 0:128] + lost[:, 128:256]
    fgrad_ref[...] = jnp.zeros(fgrad_ref.shape, F32)


    send(10, edge_cell(work_ref.at[0]))
    arrive(10)
    put_patch(1, work_ref.at[0], recv_ref[10, 0:32, :], 12)
    for cp in range(2):
        work_ref[cp] = dot(patch_ref[1], wht_ref[cp])
    stats = norm_back_start(6, merged, 2)
    send(11, edge_full(work_ref), stats)
    turn_ref[0:256, :] = patch_ref[1].T
    for cp in range(2):
        dwh_ref[cp] = dot(turn_ref[0:256, :], act_ref[5, cp])
    arrive(11)
    norm_back_ready(6, stats, 11, 2)

    def head_body(i, carry):
        pair = []
        for p in range(2):
            g = back_value(6, work_ref[p, at(i), :], merged[p, at(i), :])
            grad_ref[p, at(i), :] = g
            pair.append(g)
        put_wide(i, pair[0], pair[1])
        return carry

    loop(head_body)
    put_wide_edge(back_value(6, recv_ref[11, 0:32, :], recv_ref[9, 0:32, :]))

    hgrad = half_ref.at[3]
    hgrad[0] = dot_nt(wide_ref[32:544, :], wut_ref[...])
    send(12, edge_cell(hgrad.at[0]))
    turn_ref[0:256, :] = acth_ref[2].T
    for b in range(3):
        cols = {0: (3, 2), 1: (1, 2), 2: (1, 0)}[b]
        block = dot(turn_ref[0:256, :], wide_ref[32:544, cols[0] * 512 : cols[0] * 512 + 512]) + dot(
            turn_ref[0:256, :], wide_ref[32:544, cols[1] * 512 : cols[1] * 512 + 512]
        )
        for a in range(3):
            one, two = {0: (3, 1), 1: (0, 1), 2: (0, 2)}[a]
            dup_ref[3 * a + b] = (
                block[:, one * 128 : one * 128 + 128] + block[:, two * 128 : two * 128 + 128]
            ).astype(dup_ref.dtype)

    def deep_grad(i, carry):
        put_thin(i, hgrad[0, at(i), :])
        return carry

    loop(deep_grad)
    arrive(12)
    put_thin_edge(recv_ref[12, 0:32, :])
    work_ref[0] = conv_high_back(1)
    stats = norm_back_start(5, half_ref.at[1], 1)
    send(13, edge_cell(work_ref.at[0]), stats)
    grad_high(1, 1)
    arrive(13)
    norm_back_ready(5, stats, 13, 1)

    def mid_grad(i, carry):
        put_thin(i, back_value(5, work_ref[0, at(i), :], half_ref[1, 0, at(i), :]))
        return carry

    loop(mid_grad)
    put_thin_edge(back_value(5, recv_ref[13, 0:32, :], recv_ref[7, 0:32, :]))
    work_ref[0] = conv_high_back(0)
    stats = norm_back_start(4, half_ref.at[0], 1)
    send(14, edge_cell(work_ref.at[0]), stats)
    grad_high(0, 0)
    arrive(14)
    norm_back_ready(4, stats, 14, 1)

    def first_grad(i, carry):
        put_thin(
            i, hgrad[0, at(i), :] + back_value(4, work_ref[0, at(i), :], half_ref[0, 0, at(i), :])
        )
        return carry

    loop(first_grad)
    put_thin_edge(
        recv_ref[12, 0:32, :] + back_value(4, recv_ref[14, 0:32, :], recv_ref[6, 0:32, :])
    )

    for part in range(3):
        gather_sent(part)
    deal_core(HIGH_PART)

    for cp in range(2):
        for rp in range(2):
            total = None
            for di in range(1 + rp):
                for dj in range(1 + cp):
                    a = 0 if di else 1 + rp
                    b = 0 if dj else 1 + cp
                    term = dot_nt(
                        thin_ref[32 * (1 + di) : 32 * (1 + di) + 512, (1 + dj) * 256 : (2 + dj) * 256],
                        down_ref[3 * a + b],
                    )
                    total = term if total is None else total + term
            grad_ref[cp, :, rp * 128 : rp * 128 + 128] = (
                grad_ref[cp, :, rp * 128 : rp * 128 + 128] + total
            )
    send(15, edge_full(grad_ref))
    turn_wide(4)
    for cp in range(2):
        for rp in range(2):
            for di in range(1 + rp):
                for dj in range(1 + cp):
                    a = 0 if di else 1 + rp
                    b = 0 if dj else 1 + cp
                    at_row = cp * 256 + rp * 128
                    ddown_ref[3 * a + b] = dot(
                        turn_ref[at_row : at_row + 128, :],
                        thin_ref[32 * (1 + di) : 32 * (1 + di) + 512, (1 + dj) * 256 : (2 + dj) * 256],
                    ).astype(ddown_ref.dtype)

    deal_first(HIGH_PART)
    deal_core(REST)

    def put_work(cp, value):
        work_ref[cp] = value

    edge_grad = None
    for index in (1, 0):
        h = full_ref.at[2 * index]
        mid = full_ref.at[2 * index + 1]
        k = 2 * index
        e = 16 if index else 18
        load_wr(k + 1)
        if index:

            def out_grad(i, carry):
                put_wide(i, grad_ref[0, at(i), :], grad_ref[1, at(i), :])
                return carry

            loop(out_grad)
            arrive(15)
            edge_grad = recv_ref[15, 0:32, :]
            put_wide_edge(edge_grad)
        conv_low(put_work, True)
        stats = norm_back_start(k + 1, mid, 2)
        send(e, edge_full(work_ref), stats)
        grad_low(k + 1, k + 1)
        if index:
            deal_second(HIGH_PART)
            deal_first(REST)
        else:
            deal_end(HIGH_PART)
            deal_z(REST)
        load_wr(k)
        arrive(e)
        norm_back_ready(k + 1, stats, e, 2)

        def mid_body(i, carry, mid=mid, k=k):
            put_wide(
                i,
                back_value(k + 1, work_ref[0, at(i), :], mid[0, at(i), :]),
                back_value(k + 1, work_ref[1, at(i), :], mid[1, at(i), :]),
            )
            return carry

        loop(mid_body)
        put_wide_edge(back_value(k + 1, recv_ref[e, 0:32, :], recv_ref[k + 2, 0:32, :]))
        conv_low(put_work, True)
        stats = norm_back_start(k, h, 2)
        send(e + 1, edge_full(work_ref), stats)
        grad_low(k, k)
        if index:
            deal_z(HIGH_PART)
            deal_second(REST)
        else:
            deal_end(REST)
            deal_core(LOW)
        arrive(e + 1)
        norm_back_ready(k, stats, e + 1, 2)

        def in_body(i, carry, h=h, k=k):
            pair = []
            for p in range(2):
                g = grad_ref[p, at(i), :] + back_value(k, work_ref[p, at(i), :], h[p, at(i), :])
                grad_ref[p, at(i), :] = g
                pair.append(g)
            put_wide(i, pair[0], pair[1])
            return carry

        loop(in_body)
        edge_grad = edge_grad + back_value(k, recv_ref[e + 1, 0:32, :], recv_ref[k + 1, 0:32, :])
        put_wide_edge(edge_grad)

    deal_first(LOW)
    turn_ref[0:256, :] = patch_ref[0].T
    for cp in range(2):
        dwi_ref[cp] = dot(turn_ref[0:256, :], wide_ref[32:544, 512 + cp * 512 : 768 + cp * 512])

    for a in range(3):
        for b in range(3):
            first, last = None, None
            for cp in range(2):
                for rp in range(2):
                    rho, gamma = rp + a - 1, cp + b - 1
                    cell = (rho // 2 + 1) * 3 + gamma // 2 + 1
                    phase = (gamma % 2) * 2 + rho % 2
                    row = cell * 24 + phase * 6
                    term = dwi_ref[cp, row : row + 6, rp * 128 : rp * 128 + 128]
                    first = term if first is None else first + term
                    row = cell * 12 + phase * 3
                    term = dwh_ref[cp, row : row + 3, rp * 128 : rp * 128 + 128]
                    last = term if last is None else last + term
            t = 3 * a + b
            part_ref[9 * t : 9 * t + 6, :] = first
            part_ref[9 * (8 - t) + 6 : 9 * (8 - t) + 9, :] = last
    for which in range(2):
        for j in range(9):
            row = 81 + 9 * which + j
            part_ref[row : row + 1, :] = ngrad_ref[which : which + 1, 128 * j : 128 * j + 128]


    def message(n, src, dst, d, source):
        return pltpu.make_async_remote_copy(
            src_ref=src,
            dst_ref=dst.at[source],
            send_sem=m_send.at[n, d],
            recv_sem=m_recv.at[n, source],
            device_id=device_no(d),
            device_id_type=MESH,
        )

    def fill(d, carry):
        c = lax.rem(d, 4)
        m1_ref[d, 0:2, 0:256] = fgrad_ref[0:2, pl.ds(pl.multiple_of(c * 256, 256), 256)]
        m1_ref[d, :, 256:384] = part_ref[pl.ds(pl.multiple_of(d * 8, 8), 8), :]

        @pl.when(d != me)
        def _():
            message(0, m1_ref.at[d], r1_ref, d, me).start()

        return carry

    m1_ref[...] = jnp.zeros(m1_ref.shape, F32)
    lax.fori_loop(0, 32, fill, 0)
    r1_ref[me] = m1_ref[me]

    deal_second(LOW)
    imgrad = dot_nt(wide_ref[32:544, :], wit_ref[...]) * count
    imgrad_ref[...] = imgrad.reshape(16, 32, 128)

    s_r, s_c = strip_of(me)
    home_left = s_r * 4 + s_c
    home_right = s_r * 4 + lax.rem(s_c + 1, 4)

    def back_copy(side, device):
        return pltpu.make_async_remote_copy(
            src_ref=imgrad_ref.at[:, 16 * side : 16 * side + 16, :],
            dst_ref=back_ref.at[1 - side],
            send_sem=back_send.at[side],
            recv_sem=back_recv.at[side],
            device_id=device_no(device),
            device_id_type=MESH,
        )

    back_copy(0, home_left).start()

    @pl.when(home_right != me)
    def _():
        back_copy(1, home_right).start()

    others(lambda d: message(0, m1_ref.at[d], r1_ref, d, d).wait_recv())
    fsum_ref[...] = jnp.zeros(fsum_ref.shape, F32)

    def collect(d, total):
        s_l, s_rt = slots_of(d)
        fsum_ref[pl.ds(s_l, 1), :] = fsum_ref[pl.ds(s_l, 1), :] + r1_ref[d, 0:1, 0:256]
        fsum_ref[pl.ds(s_rt, 1), :] = fsum_ref[pl.ds(s_rt, 1), :] + r1_ref[d, 1:2, 0:256]
        return total + r1_ref[d, :, 256:384]

    m2_ref[0:8, :] = lax.fori_loop(0, 32, collect, jnp.zeros((8, 128), F32))
    film_mine = fsum_ref[...]
    film_w = weights[6][...].astype(BF).astype(F32)
    gc_part = lax.dot_general(
        film_mine, film_w, (((1,), (1,)), ((), ())), precision=HIGH, preferred_element_type=F32
    )
    wide = jnp.concatenate([gc_part, jnp.zeros((32, 64), F32)], axis=1)
    for c in range(4):
        gcs_ref[c] = pltpu.roll(wide, 128 - 16 * c, 1) if c else wide

    def gc_copy(c, source):
        return pltpu.make_async_remote_copy(
            src_ref=gcs_ref.at[c],
            dst_ref=gcr_ref.at[source],
            send_sem=gc_send.at[c],
            recv_sem=gc_recv.at[source],
            device_id={"rows": rr, "cols": c},
            device_id_type=MESH,
        )

    for c in range(4):

        @pl.when(cc != c)
        def _(c=c):
            gc_copy(c, cc).start()

        @pl.when(cc == c)
        def _(c=c):
            gcr_ref[c] = gcs_ref[c]

    grads = [None] * 8
    grads[6] = lax.dot_general(
        condv_ref[...], film_mine, (((0,), (0,)), ((), ())), precision=HIGH, preferred_element_type=F32
    )

    deal_z(LOW)

    for c in range(4):

        @pl.when(cc != c)
        def _(c=c):
            gc_copy(c, c).wait_recv()

    pre = csend_ref[:, 0:16]
    gc = gcr_ref[0] + gcr_ref[1] + gcr_ref[2] + gcr_ref[3]
    gc = gc[:, 0:16] * silu_grad_tanh(pre)
    grads[5] = lax.dot_general(
        gc,
        joined_ref[...],
        (((0,), (0,)), ((), ())),
        precision=HIGH,
        preferred_element_type=F32,
    )

    deal_end(LOW)
    own = own_ref[...]
    grads[1] = jnp.stack([own[0:144, 32 * j : 32 * j + 32].reshape(9, 16, 32) for j in range(4)])
    grads[2] = jnp.stack([own[288:576, 64 * j : 64 * j + 64].reshape(9, 32, 64) for j in range(2)])
    grads[3] = own[144:288, 0:64].reshape(9, 16, 64)
    grads[4] = jnp.concatenate(
        [own[144:288, 64:96].reshape(9, 16, 32), own[144:288, 96:128].reshape(9, 16, 32)], axis=1
    )

    owned = square_sum(own)
    for n in (5, 6):
        owned = owned + square_sum(grads[n])
    m2_ref[8:16, :] = jnp.broadcast_to(owned, (8, 128))
    others(lambda d: message(1, m2_ref, r2_ref, d, me).start())
    r2_ref[me] = m2_ref[...]
    others(lambda d: message(1, m2_ref, r2_ref, d, d).wait_recv())

    def take(d, total):
        total_ref[pl.ds(pl.multiple_of(d * 8, 8), 8), :] = r2_ref[d, 0:8, :]
        return total + r2_ref[d, 8:16, :]

    squares = lax.fori_loop(0, 32, take, jnp.zeros((8, 128), F32))
    shared = square_sum(total_ref[0:LOSS_ROW, :])
    clip = jnp.sqrt(squares[0:1, 0:1] + shared)
    factor = jnp.minimum(1.0, CLIP_AT / clip)
    clip_out[...] = jnp.broadcast_to(clip, (1, 128))
    loss_out[...] = jnp.broadcast_to(
        jnp.sum(total_ref[LOSS_ROW : LOSS_ROW + 1, :], axis=1, keepdims=True), (1, 128)
    )
    grads[0] = jnp.stack([total_ref[9 * t : 9 * t + 9, :] for t in range(9)])
    grads[7] = jnp.concatenate(
        [
            jnp.concatenate(
                [total_ref[NORM_ROW + 9 * n + j : NORM_ROW + 9 * n + j + 1, :] for j in range(9)],
                axis=1,
            )
            for n in range(2)
        ],
        axis=0,
    )

    updates = []
    pairs = []
    spot = 0
    for n in range(8):
        grad = grads[n] * factor.reshape((1,) * grads[n].ndim)
        first_new = BETA_ONE * firsts[n][...] + (1.0 - BETA_ONE) * grad
        second_new = BETA_TWO * seconds[n][...] + (1.0 - BETA_TWO) * grad * grad
        first_hat = first_new / (1.0 - BETA_ONE**STEP)
        second_hat = second_new / (1.0 - BETA_TWO**STEP)
        update = first_hat / (jnp.sqrt(second_hat) + EPS_ADAM) + DECAY * weights[n][...]
        outs[3 * n][...] = grad
        outs[3 * n + 1][...] = second_new
        outs[3 * n + 2][...] = update
        if n in (1, 2):
            for j in range(update.shape[0]):
                pairs.append((spot, square_sum(weights[n][j])))
                pairs.append((64 + spot, square_sum(update[j])))
                spot += 1
        elif 2 < n < 7:
            pairs.append((spot, square_sum(weights[n][...])))
            pairs.append((64 + spot, square_sum(update)))
            spot += 1

    m3_ref[...] = lane_value(pairs)
    others(lambda d: message(2, m3_ref, r3_ref, d, me).start())
    r3_ref[me] = m3_ref[...]

    def step(n, ratio, at=None):
        ratio = ratio * RATE
        if at is None:
            weight, out = weights[n][...], outs[3 * n + 2]
            out[...] = weight - ratio.reshape((1,) * weight.ndim) * out[...]
        else:
            weight, out = weights[n][at], outs[3 * n + 2]
            out[at] = weight - ratio.reshape((1,) * weight.ndim) * out[at]

    def root_ratio(a, b):
        return jnp.sqrt(a) / jnp.sqrt(b)

    step(7, root_ratio(square_sum(weights[7][...]), square_sum(outs[23][...])))
    edge_w, edge_u = weights[0][...], outs[2][...]
    for lo, hi in ((0, 6), (6, 9)):
        ratio = root_ratio(square_sum(edge_w[:, lo:hi, :]), square_sum(edge_u[:, lo:hi, :])) * RATE
        outs[2][:, lo:hi, :] = edge_w[:, lo:hi, :] - ratio.reshape(1, 1, 1) * edge_u[:, lo:hi, :]

    others(lambda d: message(2, m3_ref, r3_ref, d, d).wait_recv())
    sums = lax.fori_loop(0, 32, lambda d, t: t + r3_ref[d], jnp.zeros((8, 128), F32))
    spot = 0
    for n in range(1, 7):
        for j in range(weights[n].shape[0] if n in (1, 2) else 1):
            ratio = root_ratio(sums[0:1, spot : spot + 1], sums[0:1, 64 + spot : 65 + spot])
            step(n, ratio, j if n in (1, 2) else None)
            spot += 1

    back_copy(0, home_left).wait()

    @pl.when(home_right != me)
    def _():
        back_copy(1, home_right).wait()

    @pl.when(home_right == me)
    def _():
        back_ref[0] = imgrad_ref[:, 16:32, :]

    back_out[...] = back_ref[...]

    for part in range(3):
        deal_sent(part)
    others(lambda d: film_copy(d, me).wait_send())
    row_mates(lambda c: cond_copy(c, cc).wait_send())
    row_mates(lambda c: gc_copy(c, cc).wait_send())
    for n, src in ((1, m2_ref), (2, m3_ref)):
        others(lambda d, n=n, src=src: message(n, src, r2_ref if n == 1 else r3_ref, d, me).wait_send())
    others(lambda d: message(0, m1_ref.at[d], r1_ref, d, me).wait_send())


def step(*operands):
    outs = []
    for n in range(8):
        outs += [jax.ShapeDtypeStruct(operands[5 + 3 * n].shape, F32)] * 3
    outs += [jax.ShapeDtypeStruct((1, 128), F32)] * 3
    outs += [jax.ShapeDtypeStruct((2, 16, 16, 128), F32)]
    vmem = pl.BlockSpec(memory_space=pltpu.VMEM)
    dma = pltpu.SemaphoreType.DMA

    def half(*shape):
        return pltpu.VMEM(shape, BF)

    def full(*shape):
        return pltpu.VMEM(shape, F32)

    return pl.pallas_call(
        step_kernel,
        out_shape=tuple(outs),
        in_specs=[vmem] * len(operands),
        out_specs=[vmem] * len(outs),
        scratch_shapes=[
            half(4, 9, 128, 128),
            half(2, 9, 256, 256),
            half(9, 128, 256),
            half(9, 256, 128),
            full(6, 2, 512, 256),
            full(4, 1, 512, 256),
            full(2, 512, 256),
            full(2, 512, 256),
            half(576, 2048),
            half(576, 768),
            half(6, 2, 512, 256),
            half(3, 512, 256),
            half(512, 512),
            half(1536, 256),
            half(256, 1536),
            half(2, 3, 512, 256),
            half(256, 2048),
            half(1536, 256),
            full(7, 7, 32, 256),
            full(7, 8, 256),
            half(2, 512, 256),
            full(576, 256),
            full(N_EXCHANGE, 40, 256),
            full(N_EXCHANGE, 40, 256),
            full(512, 256),
            full(512, 256),
            full(2, 256, 256),
            full(2, 256, 256),
            full(2, 1152),
            full(8, 1024),
            full(256, 128),
            full(16, 32, 128),
            half(2, 256, 256),
            half(2, 256, 256),
            half(128, 2048),
            half(128, 2048),
            full(32, 2048),
            half(4, 2, 2, 2, ALL_ROWS, 128),
            full(2, 256, 128),
            full(4, 32, 128),
            full(32, 128),
            full(32, 256),
            full(32, 8, 256),
            full(32, 8, 256),
            full(8, 1024),
            full(32, 4224),
            full(32, 64),
            half(4, 2, 2, ALL_ROWS, 128),
            half(4, 2, ALL_ROWS, 128),
            half(4, ALL_ROWS, 128),
            half(4, ALL_ROWS, 128),
            full(ALL_ROWS, 128),
            full(32, 8, 384),
            full(32, 8, 384),
            full(16, 128),
            full(32, 16, 128),
            full(8, 128),
            full(32, 8, 128),
            full(4, 32, 128),
            full(4, 32, 128),
            full(32, 256),
            full(256, 128),
            full(2, 16, 16, 128),
            dma((N_EXCHANGE,)),
            dma((N_EXCHANGE,)),
            dma((3, 5, 4, 2, 2)),
            dma((3, 4, 2, 2, 2)),
            dma((2,)),
            dma((2,)),
            dma((4,)),
            dma((4,)),
            dma((32,)),
            dma((32,)),
            dma((3, 4)),
            dma((3, 4)),
            dma((3, 4)),
            dma((3, 4)),
            dma((3, 4)),
            dma((3, 4)),
            dma((3, 4)),
            dma((3, 4)),
            dma((3, 32)),
            dma((3, 32)),
            dma((4,)),
            dma((4,)),
            dma((2,)),
            dma((2,)),
        ],
        compiler_params=pltpu.CompilerParams(
            collective_id=1, has_side_effects=True, vmem_limit_bytes=62 * 1024 * 1024
        ),
        name="step",
    )(*operands)


def per_device_strips(
    image_pair,
    noise_target,
    timesteps,
    text_pooled,
    slot_live,
    *params,
):
    block = jnp.concatenate(
        [cells_of(image_pair[0].astype(F32)), cells_of(noise_target[0])], axis=-1
    )
    block = jnp.pad(block, ((0, 0), (0, 0), (0, 92)))
    block = jnp.stack([block[:, 0:16], block[:, 16:32]]).reshape(2, 256, 128)
    lanes = jnp.asarray(lane_tables(), BF)

    def view(n, a):
        return jnp.swapaxes(a, 1, 2) if n == 0 else a.T if n == 5 else a

    state = [view(n // 3, a) for n, a in enumerate(params)]
    results = step(
        slot_live[0], time_embed(timesteps)[0].astype(BF), text_pooled[0], block, lanes, *state
    )
    new = [view(n // 3, a) for n, a in enumerate(results[:24])]
    loss, count, clip, back = results[24:]
    back = jnp.concatenate([back[0], back[1]], axis=1)[:, :, 0:24]
    return tuple(new) + (loss[0, 0], count[0, 0], clip[0, 0], pixels_of(back)[None])


def cells_of(block):
    rows, cols, width = block.shape
    x = block.reshape(rows // 2, 2, cols // 2, 2, width)
    return jnp.transpose(x, (0, 2, 3, 1, 4)).reshape(rows // 2, cols // 2, 4 * width)


def pixels_of(cells):
    rows, cols, width = cells.shape
    x = cells.reshape(rows, cols, 2, 2, width // 4)
    return jnp.transpose(x, (0, 3, 1, 2, 4)).reshape(2 * rows, 2 * cols, width // 4)


def solution(mesh):
    strips = mesh.shape["rows"] == 8 and mesh.shape["cols"] == 4
    placed = (
        P(None, "rows", "cols", None),
        P(None, "rows", "cols", None),
        P(),
        P(),
        P(),
        P(),
        P(),
        P(),
        P(None, None, "rows", "cols"),
        P(None, None, "rows", "cols"),
        P(None, None, "rows", "cols"),
        P(None, None, "rows", "cols"),
        P(None, None, "rows", "cols"),
        P(None, None, "rows", "cols"),
        P(None, "rows", "cols"),
        P(None, "rows", "cols"),
        P(None, "rows", "cols"),
        P(None, "rows", "cols"),
        P(None, "rows", "cols"),
        P(None, "rows", "cols"),
        P(None, ("rows", "cols")),
        P(None, ("rows", "cols")),
        P(None, ("rows", "cols")),
        P("rows", "cols"),
        P("rows", "cols"),
        P("rows", "cols"),
        P(),
        P(),
        P(),
    )
    return jax.shard_map(
        per_device_strips if strips else per_device,
        mesh=mesh,
        in_specs=placed,
        out_specs=(
            P(),
            P(),
            P(),
            P(None, None, "rows", "cols"),
            P(None, None, "rows", "cols"),
            P(None, None, "rows", "cols"),
            P(None, None, "rows", "cols"),
            P(None, None, "rows", "cols"),
            P(None, None, "rows", "cols"),
            P(None, "rows", "cols"),
            P(None, "rows", "cols"),
            P(None, "rows", "cols"),
            P(None, "rows", "cols"),
            P(None, "rows", "cols"),
            P(None, "rows", "cols"),
            P(None, ("rows", "cols")),
            P(None, ("rows", "cols")),
            P(None, ("rows", "cols")),
            P("rows", "cols"),
            P("rows", "cols"),
            P("rows", "cols"),
            P(),
            P(),
            P(),
            P(),
            P(),
            P(),
            P(None, "rows", "cols", None),
        ),
        check_vma=False,
    )
```

```python
import math

import jax
import jax.numpy as jnp
import numpy as np
from jax import lax
from jax.experimental import pallas as pl
from jax.experimental.pallas import tpu as pltpu
from jax.sharding import PartitionSpec as P

SLOT = 64
SLOTS = 5
C1 = 128
C2 = 256
GROUPS = 32
TEMB = 128
STEP = 10


HIGH = lax.Precision.HIGHEST
EPS_NORM = 1e-05
CLIP_AT = 0.05
RATE = 0.5
BETA_ONE = 0.9
BETA_TWO = 0.999
EPS_ADAM = 1e-06
DECAY = 0.01


def entering(part, axis, combine, identity, reverse):
    count = lax.axis_size(axis)
    place = lax.axis_index(axis)
    ahead = count - 1 - place if reverse else place
    gathered = jax.tree.map(lambda a: lax.all_gather(a, axis), part)
    state = jax.tree.map(lambda a, e: jnp.zeros_like(a) + jnp.asarray(e, a.dtype), part, identity)

    def one(turn, state):
        source = count - 1 - turn if reverse else turn
        return combine(
            state, jax.tree.map(lambda a: lax.dynamic_index_in_dim(a, source, 0, False), gathered)
        )

    return lax.fori_loop(0, ahead, one, state)


def padded_2(block, sides, width):
    for axis, dim in sides:
        count = lax.axis_size(axis)
        forward = [(i, i + 1) for i in range(count - 1)]
        backward = [(target, source) for source, target in forward]
        low = lax.ppermute(
            lax.slice_in_dim(block, block.shape[dim] - width, None, axis=dim), axis, forward
        )
        high = lax.ppermute(lax.slice_in_dim(block, 0, width, axis=dim), axis, backward)
        block = jnp.concatenate([low, block, high], axis=dim)
    return block


def time_embed(steps):
    half = TEMB // 2
    freq = jnp.exp(-math.log(10000.0) * jnp.arange(half, dtype=jnp.float32) / half)
    angle = steps.astype(jnp.float32)[..., None] * freq
    return jnp.concatenate([jnp.sin(angle), jnp.cos(angle)], axis=-1)


def silu_grad(values):
    sigma = jax.nn.sigmoid(values)
    return sigma * (1.0 + values * (1.0 - sigma))


def tap_masks(rows, cols, slot):
    half = slot // 2
    row_pos = lax.axis_index("rows") * rows + jnp.arange(rows)
    col_pos = lax.axis_index("cols") * cols + jnp.arange(cols)
    row_ok = [
        (row_pos + offset + half) // slot == (row_pos + half) // slot for offset in (-1, 0, 1)
    ]
    col_ok = [
        (col_pos + offset + half) // slot == (col_pos + half) // slot for offset in (-1, 0, 1)
    ]
    return [
        (row_ok[tap // 3][:, None] & col_ok[tap % 3][None, :]).astype(jnp.bfloat16)
        for tap in range(9)
    ]


def slot_level(rows, cols, slot, size):
    half = slot // 2
    labels = jnp.arange(SLOTS)
    row_pos = lax.axis_index("rows") * rows + jnp.arange(rows)
    col_pos = lax.axis_index("cols") * cols + jnp.arange(cols)
    row_map = (((row_pos + half) // slot)[:, None] == labels[None, :]).astype(jnp.float32)
    col_map = (((col_pos + half) // slot)[:, None] == labels[None, :]).astype(jnp.float32)
    every = (jnp.arange(size) + half) // slot
    side = jnp.sum((every[:, None] == labels[None, :]).astype(jnp.float32), axis=0)
    return (row_map, col_map, side[:, None] * side[None, :])


def to_slots(values, level):
    return jnp.einsum("nhwk,ha,wb->nabk", values, level[0], level[1], precision=HIGH)


def to_pixels(table, level):
    return jnp.einsum("nabk,ha,wb->nhwk", table, level[0], level[1], precision=HIGH)


def add_pair(earlier, later):
    return (earlier[0] + later[0], earlier[1] + later[1])


def slot_total(tables):
    empty = (jnp.zeros_like(tables[0]), jnp.zeros_like(tables[1]))
    before = entering(tables, ("rows", "cols"), add_pair, empty, False)
    after = entering(tables, ("rows", "cols"), add_pair, empty, True)
    return (before[0] + tables[0] + after[0], before[1] + tables[1] + after[1])


def pad_rim(values):
    return padded_2(values, (("rows", 1), ("cols", 2)), 1)


def tap_patch(padded, masks, tap, stride):
    rows = padded.shape[1] - 2
    cols = padded.shape[2] - 2
    row_off, col_off = (tap // 3, tap % 3)
    patch = padded[:, row_off : row_off + rows : stride, col_off : col_off + cols : stride, :]
    return patch * masks[tap][::stride, ::stride][None, :, :, None]


def conv_taps(padded, weight, masks, stride):
    total = None
    for tap in range(9):
        term = jnp.einsum(
            "nhwc,cd->nhwd",
            tap_patch(padded, masks, tap, stride),
            weight[tap],
            preferred_element_type=jnp.float32,
        )
        total = term if total is None else total + term
    return total


def conv_weight_grad(padded, grad_out, masks, stride):
    return jnp.stack(
        [
            jnp.einsum(
                "nhwc,nhwd->cd",
                tap_patch(padded, masks, tap, stride),
                grad_out,
                preferred_element_type=jnp.float32,
            )
            for tap in range(9)
        ]
    )


def conv_input_grad(grad_out, weight, masks, stride):
    spread = grad_out
    if stride == 2:
        canvases, rows, cols, width = grad_out.shape
        spread = jnp.stack([grad_out, jnp.zeros_like(grad_out)], axis=2).reshape(
            canvases, 2 * rows, cols, width
        )
        spread = jnp.stack([spread, jnp.zeros_like(spread)], axis=3).reshape(
            canvases, 2 * rows, 2 * cols, width
        )
    flipped = jnp.swapaxes(weight[::-1], 1, 2)
    padded = padded_2(spread, (("rows", 1), ("cols", 2)), 1)
    return conv_taps(padded, flipped, masks, 1)


def norm_forward(values, gain, bias, scale, shift, level):
    count_n, rows, cols, width = values.shape
    grouped = values.reshape(count_n, rows, cols, GROUPS, width // GROUPS)
    total, squares = slot_total(
        (
            to_slots(jnp.sum(grouped, axis=4), level),
            to_slots(jnp.sum(grouped * grouped, axis=4), level),
        )
    )
    count = level[2][None, :, :, None] * (width // GROUPS)
    mean = total / count
    var = squares / count - mean * mean
    inverse = lax.rsqrt(var + EPS_NORM)
    mean_pix = to_pixels(mean, level)
    inv_pix = to_pixels(inverse, level)
    hat = ((grouped - mean_pix[..., None]) * inv_pix[..., None]).reshape(values.shape)
    normed = hat * gain + bias
    if scale is None:
        return (normed, (hat, inv_pix, normed, None))
    factor = 1.0 + to_pixels(scale, level)
    return (normed * factor + to_pixels(shift, level), (hat, inv_pix, normed, factor))


def norm_backward(grad_out, kept, gain, level):
    hat, inv_pix, normed, factor = kept
    count_n, rows, cols, width = hat.shape
    if factor is None:
        film_grad = None
        grad_normed = grad_out
    else:
        film_grad = jnp.concatenate(
            [to_slots(grad_out * normed, level), to_slots(grad_out, level)], axis=-1
        )
        grad_normed = grad_out * factor
    grad_gain = jnp.sum(grad_normed * hat, axis=(0, 1, 2))
    grad_bias = jnp.sum(grad_normed, axis=(0, 1, 2))
    shape = (count_n, rows, cols, GROUPS, width // GROUPS)
    grad_hat = (grad_normed * gain).reshape(shape)
    grouped_hat = hat.reshape(shape)
    first, second = slot_total(
        (
            to_slots(jnp.sum(grad_hat, axis=4), level),
            to_slots(jnp.sum(grad_hat * grouped_hat, axis=4), level),
        )
    )
    count = level[2][None, :, :, None] * (width // GROUPS)
    mean_one = to_pixels(first / count, level)[..., None]
    mean_two = to_pixels(second / count, level)[..., None]
    grad_in = inv_pix[..., None] * (grad_hat - mean_one - grouped_hat * mean_two)
    return (grad_in.reshape(hat.shape), grad_gain, grad_bias, film_grad)


def block_forward(hidden, weights, gains, film, level, masks):
    pre_one, saved_one = norm_forward(hidden, gains[0], gains[1], None, None, level)
    rim_one = pad_rim(jax.nn.silu(pre_one).astype(jnp.bfloat16))
    conv_one = conv_taps(rim_one, weights[0], masks, 1)
    pre_two, saved_two = norm_forward(conv_one, gains[2], gains[3], film[0], film[1], level)
    rim_two = pad_rim(jax.nn.silu(pre_two).astype(jnp.bfloat16))
    out = hidden + conv_taps(rim_two, weights[1], masks, 1)
    return (out, (pre_one, saved_one, rim_one, pre_two, saved_two, rim_two))


def block_backward(grad_out, weights, gains, kept, level, masks):
    pre_one, saved_one, rim_one, pre_two, saved_two, rim_two = kept
    grad_two = grad_out.astype(jnp.bfloat16)
    weight_two = conv_weight_grad(rim_two, grad_two, masks, 1)
    grad_pre_two = conv_input_grad(grad_two, weights[1], masks, 1) * silu_grad(pre_two)
    grad_conv, gain_two, bias_two, film_grad = norm_backward(
        grad_pre_two, saved_two, gains[2], level
    )
    grad_one = grad_conv.astype(jnp.bfloat16)
    weight_one = conv_weight_grad(rim_one, grad_one, masks, 1)
    grad_pre_one = conv_input_grad(grad_one, weights[0], masks, 1) * silu_grad(pre_one)
    grad_in, gain_one, bias_one, _ = norm_backward(grad_pre_one, saved_one, gains[0], level)
    return (
        grad_out + grad_in,
        (weight_one, weight_two),
        (gain_one, bias_one, gain_two, bias_two),
        film_grad,
    )


def per_device(
    image_pair,
    noise_target,
    timesteps,
    text_pooled,
    slot_live,
    edgeconv_weight,
    edgeconv_first,
    edgeconv_second,
    convlow_weight,
    convlow_first,
    convlow_second,
    convhigh_weight,
    convhigh_first,
    convhigh_second,
    downconv_weight,
    downconv_first,
    downconv_second,
    upconv_weight,
    upconv_first,
    upconv_second,
    condproj_weight,
    condproj_first,
    condproj_second,
    filmproj_weight,
    filmproj_first,
    filmproj_second,
    normparams_weight,
    normparams_first,
    normparams_second,
):
    canvases, rows_one, cols_one = image_pair.shape[:3]
    size_full = rows_one * lax.axis_size("rows")
    level_full = slot_level(rows_one, cols_one, SLOT, size_full)
    level_half = slot_level(rows_one // 2, cols_one // 2, SLOT // 2, size_full // 2)
    by_rows = (
        lax.all_gather(convlow_weight.astype(jnp.bfloat16), "rows", axis=2, tiled=True),
        lax.all_gather(convhigh_weight.astype(jnp.bfloat16), "rows", axis=2, tiled=True),
        lax.all_gather(downconv_weight.astype(jnp.bfloat16), "rows", axis=1, tiled=True),
        lax.all_gather(upconv_weight.astype(jnp.bfloat16), "rows", axis=1, tiled=True),
        lax.all_gather(filmproj_weight.astype(jnp.bfloat16), "rows", axis=0, tiled=True),
    )
    low_convs, high_convs, down_conv, up_conv, film_full = (
        lax.all_gather(by_rows[0], "cols", axis=3, tiled=True),
        lax.all_gather(by_rows[1], "cols", axis=3, tiled=True),
        lax.all_gather(by_rows[2], "cols", axis=2, tiled=True),
        lax.all_gather(by_rows[3], "cols", axis=2, tiled=True),
        lax.all_gather(by_rows[4], "cols", axis=1, tiled=True),
    )
    joined = jnp.concatenate([time_embed(timesteps).astype(jnp.bfloat16), text_pooled], axis=-1)
    cond_full = lax.all_gather(
        condproj_weight.astype(jnp.bfloat16), ("rows", "cols"), axis=1, tiled=True
    )
    pre_cond = jnp.einsum("nabk,kf->nabf", joined, cond_full, preferred_element_type=jnp.float32)
    cond_low = jax.nn.silu(pre_cond).astype(jnp.bfloat16)
    film_all = jnp.einsum("nabk,kf->nabf", cond_low, film_full, preferred_element_type=jnp.float32)
    offsets = [0, C1, 2 * C1, 3 * C1, 4 * C1, 4 * C1 + C2, 4 * C1 + 2 * C2, 5 * C1 + 2 * C2]

    def norm_part(index, which):
        return normparams_weight[which, offsets[index] : offsets[index + 1]]

    def block_gains(index):
        return (
            norm_part(2 * index, 0),
            norm_part(2 * index, 1),
            norm_part(2 * index + 1, 0),
            norm_part(2 * index + 1, 1),
        )

    def block_film(index):
        base = (0, 2 * C1, 4 * C1)[index]
        width = (C1, C1, C2)[index]
        return (film_all[..., base : base + width], film_all[..., base + width : base + 2 * width])

    masks_one = tap_masks(rows_one, cols_one, SLOT)
    masks_two = tap_masks(rows_one // 2, cols_one // 2, SLOT // 2)
    edge_low = edgeconv_weight.astype(jnp.bfloat16)
    inconv_low = jnp.swapaxes(edge_low[:, :, 0:6], 1, 2)
    head_low = edge_low[:, :, 6:9]
    rim_in = pad_rim(image_pair)
    hidden = conv_taps(rim_in, inconv_low, masks_one, 1)
    kept_blocks = []
    for index in range(2):
        hidden, kept = block_forward(
            hidden,
            (low_convs[2 * index], low_convs[2 * index + 1]),
            block_gains(index),
            block_film(index),
            level_full,
            masks_one,
        )
        kept_blocks.append(kept)
    rim_skip = pad_rim(hidden.astype(jnp.bfloat16))
    deep, kept_deep = block_forward(
        conv_taps(rim_skip, down_conv, masks_one, 2),
        (high_convs[0], high_convs[1]),
        block_gains(2),
        block_film(2),
        level_half,
        masks_two,
    )
    upsampled = jnp.repeat(jnp.repeat(deep.astype(jnp.bfloat16), 2, axis=1), 2, axis=2)
    rim_up = pad_rim(upsampled)
    merged = conv_taps(rim_up, up_conv, masks_one, 1) + hidden
    pre_head, kept_head = norm_forward(
        merged, norm_part(6, 0), norm_part(6, 1), None, None, level_full
    )
    rim_head = pad_rim(jax.nn.silu(pre_head).astype(jnp.bfloat16))
    pred = conv_taps(rim_head, head_low, masks_one, 1)
    live_slots = slot_live.astype(jnp.float32)
    live = to_pixels(live_slots[..., None], level_full)
    count = 3.0 * jnp.sum(live_slots * level_full[2][None, :, :])
    diff = pred - noise_target
    loss_local = jnp.sum(live * diff * diff)
    grad_pred = (2.0 * live * diff / count).astype(jnp.bfloat16)
    grad_head = conv_weight_grad(rim_head, grad_pred, masks_one, 1)
    grad_act = conv_input_grad(grad_pred, head_low, masks_one, 1) * silu_grad(pre_head)
    grad_merged, head_gain, head_bias, _ = norm_backward(
        grad_act, kept_head, norm_part(6, 0), level_full
    )
    merged_low = grad_merged.astype(jnp.bfloat16)
    grad_upconv = conv_weight_grad(rim_up, merged_low, masks_one, 1)
    grad_up = conv_input_grad(merged_low, up_conv, masks_one, 1)
    grad_deep = grad_up.reshape(canvases, rows_one // 2, 2, cols_one // 2, 2, C2).sum(axis=(2, 4))
    grad_down, deep_convs, deep_norms, deep_film = block_backward(
        grad_deep, (high_convs[0], high_convs[1]), block_gains(2), kept_deep, level_half, masks_two
    )
    down_low = grad_down.astype(jnp.bfloat16)
    grad_downconv = conv_weight_grad(rim_skip, down_low, masks_one, 2)
    grad_hidden = grad_merged + conv_input_grad(down_low, down_conv, masks_one, 2)
    block_convs = [None, None]
    block_norms = [None, None]
    block_films = [None, None]
    for index in (1, 0):
        grad_hidden, block_convs[index], block_norms[index], block_films[index] = block_backward(
            grad_hidden,
            (low_convs[2 * index], low_convs[2 * index + 1]),
            block_gains(index),
            kept_blocks[index],
            level_full,
            masks_one,
        )
    hidden_low = grad_hidden.astype(jnp.bfloat16)
    grad_inconv = conv_weight_grad(rim_in, hidden_low, masks_one, 1)
    image_grad = conv_input_grad(hidden_low, inconv_low, masks_one, 1) * count
    all_norms = block_norms + [deep_norms]
    gain_vector = jnp.concatenate([part[k] for part in all_norms for k in (0, 2)] + [head_gain])
    bias_vector = jnp.concatenate([part[k] for part in all_norms for k in (1, 3)] + [head_bias])
    film_grads = jnp.concatenate([block_films[0], block_films[1], deep_film], axis=-1)
    edge_local = jnp.concatenate([jnp.swapaxes(grad_inconv, 1, 2), grad_head], axis=2)
    film_sum, edge_sum, norm_sum, loss_sum = lax.psum(
        (film_grads, edge_local, jnp.stack([gain_vector, bias_vector]), loss_local),
        ("rows", "cols"),
    )
    grad_film_full = jnp.einsum(
        "nabk,nabf->kf", cond_low.astype(jnp.float32), film_sum, precision=HIGH
    )
    grad_cond = jnp.einsum(
        "nabf,kf->nabk", film_sum, film_full.astype(jnp.float32), precision=HIGH
    ) * silu_grad(pre_cond)
    grad_cond_full = jnp.einsum(
        "nabk,nabf->kf", joined.astype(jnp.float32), grad_cond, precision=HIGH
    )
    film_rows, film_cols = filmproj_weight.shape
    film_own = lax.dynamic_slice_in_dim(
        grad_film_full, lax.axis_index("rows") * film_rows, film_rows, 0
    )
    film_own = lax.dynamic_slice_in_dim(film_own, lax.axis_index("cols") * film_cols, film_cols, 1)
    cond_cols = condproj_weight.shape[1]
    cond_own = lax.dynamic_slice_in_dim(
        grad_cond_full, lax.axis_index(("rows", "cols")) * cond_cols, cond_cols, 1
    )
    by_cols = (
        lax.psum_scatter(
            jnp.stack(
                [block_convs[0][0], block_convs[0][1], block_convs[1][0], block_convs[1][1]]
            ).astype(jnp.bfloat16),
            "cols",
            scatter_dimension=3,
            tiled=True,
        ).astype(jnp.float32),
        lax.psum_scatter(
            jnp.stack([deep_convs[0], deep_convs[1]]).astype(jnp.bfloat16),
            "cols",
            scatter_dimension=3,
            tiled=True,
        ).astype(jnp.float32),
        lax.psum_scatter(
            grad_downconv.astype(jnp.bfloat16), "cols", scatter_dimension=2, tiled=True
        ).astype(jnp.float32),
        lax.psum_scatter(
            grad_upconv.astype(jnp.bfloat16), "cols", scatter_dimension=2, tiled=True
        ).astype(jnp.float32),
    )
    lowconv_own, highconv_own, downconv_own, upconv_own = (
        lax.psum_scatter(
            by_cols[0].astype(jnp.bfloat16), "rows", scatter_dimension=2, tiled=True
        ).astype(jnp.float32),
        lax.psum_scatter(
            by_cols[1].astype(jnp.bfloat16), "rows", scatter_dimension=2, tiled=True
        ).astype(jnp.float32),
        lax.psum_scatter(
            by_cols[2].astype(jnp.bfloat16), "rows", scatter_dimension=1, tiled=True
        ).astype(jnp.float32),
        lax.psum_scatter(
            by_cols[3].astype(jnp.bfloat16), "rows", scatter_dimension=1, tiled=True
        ).astype(jnp.float32),
    )
    weights = (
        edgeconv_weight,
        convlow_weight,
        convhigh_weight,
        downconv_weight,
        upconv_weight,
        condproj_weight,
        filmproj_weight,
        normparams_weight,
    )
    firsts = (
        edgeconv_first,
        convlow_first,
        convhigh_first,
        downconv_first,
        upconv_first,
        condproj_first,
        filmproj_first,
        normparams_first,
    )
    seconds = (
        edgeconv_second,
        convlow_second,
        convhigh_second,
        downconv_second,
        upconv_second,
        condproj_second,
        filmproj_second,
        normparams_second,
    )
    grads = (
        edge_sum,
        lowconv_own,
        highconv_own,
        downconv_own,
        upconv_own,
        cond_own,
        film_own,
        norm_sum,
    )
    sharded = (1, 2, 3, 4, 5, 6)
    stacked = (1, 2)
    owned_sq = sum((jnp.sum(grads[k] * grads[k]) for k in sharded))
    shared_sq = sum((jnp.sum(grads[k] * grads[k]) for k in range(8) if k not in sharded))
    clip_norm = jnp.sqrt(lax.psum(owned_sq, ("rows", "cols")) + shared_sq)
    factor = jnp.minimum(1.0, CLIP_AT / clip_norm)
    clipped, moments, updates = ([], [], [])
    for k in range(8):
        grad = grads[k] * factor
        first_new = BETA_ONE * firsts[k] + (1.0 - BETA_ONE) * grad
        second_new = BETA_TWO * seconds[k] + (1.0 - BETA_TWO) * grad * grad
        first_hat = first_new / (1.0 - BETA_ONE**STEP)
        second_hat = second_new / (1.0 - BETA_TWO**STEP)
        clipped.append(grad)
        moments.append(second_new)
        updates.append(first_hat / (jnp.sqrt(second_hat) + EPS_ADAM) + DECAY * weights[k])

    def matrix_squares(values, k):
        if k in stacked:
            return jnp.sum(values * values, axis=tuple(range(1, values.ndim)))
        return jnp.sum(values * values).reshape(1)

    weight_sq, update_sq = lax.psum(
        (
            jnp.concatenate([matrix_squares(weights[k], k) for k in sharded]),
            jnp.concatenate([matrix_squares(updates[k], k) for k in sharded]),
        ),
        ("rows", "cols"),
    )
    ratios = jnp.sqrt(weight_sq) / jnp.sqrt(update_sq)
    position = 0
    results = []
    for k in range(8):
        if k in sharded:
            span = weights[k].shape[0] if k in stacked else 1
            ratio = ratios[position : position + span]
            position += span
            ratio = (
                ratio.reshape((span,) + (1,) * (weights[k].ndim - 1)) if k in stacked else ratio[0]
            )
        elif k == 0:
            part = (jnp.arange(9) < 6)[None, None, :]
            other = jnp.logical_not(part)
            weight_sq_two = weights[k] * weights[k]
            update_sq_two = updates[k] * updates[k]
            ratio_in = jnp.sqrt(jnp.sum(jnp.where(part, weight_sq_two, 0.0))) / jnp.sqrt(
                jnp.sum(jnp.where(part, update_sq_two, 0.0))
            )
            ratio_out = jnp.sqrt(jnp.sum(jnp.where(other, weight_sq_two, 0.0))) / jnp.sqrt(
                jnp.sum(jnp.where(other, update_sq_two, 0.0))
            )
            ratio = jnp.where(part, ratio_in, ratio_out)
        else:
            ratio = jnp.sqrt(jnp.sum(weights[k] * weights[k])) / jnp.sqrt(
                jnp.sum(updates[k] * updates[k])
            )
        results.extend([clipped[k], moments[k], weights[k] - RATE * ratio * updates[k]])
    return (
        results[0],
        results[1],
        results[2],
        results[3],
        results[4],
        results[5],
        results[6],
        results[7],
        results[8],
        results[9],
        results[10],
        results[11],
        results[12],
        results[13],
        results[14],
        results[15],
        results[16],
        results[17],
        results[18],
        results[19],
        results[20],
        results[21],
        results[22],
        results[23],
        loss_sum,
        count,
        clip_norm,
        image_grad,
    )


F32 = jnp.float32
BF = jnp.bfloat16
MESH = pl.DeviceIdType.MESH
NORM_AT = (0, 128, 256, 384, 512, 768, 1024, 1152)
FILM_AT = {1: 0, 3: 256, 5: 512}
ROW_OF = (0, 1, -1, 2)
COL_OF = (-1, 0, 1, 2)
N_EXCHANGE = 20


def place_of():
    rr, cc = lax.axis_index("rows"), lax.axis_index("cols")
    return rr, cc, rr // 2, lax.rem(rr, 2), cc // 2, lax.rem(cc, 2)


def device_at(z, y, x, k):
    return {"rows": z * 2 + y, "cols": x * 2 + k}


def device_no(d):
    return {"rows": d // 4, "cols": lax.rem(d, 4)}


def meet_all(me, count=32):
    barrier = pltpu.get_barrier_semaphore()

    def hello(d, carry):
        @pl.when(d != me)
        def _():
            pl.semaphore_signal(barrier, inc=1, device_id=device_no(d), device_id_type=MESH)

        return carry

    lax.fori_loop(0, count, hello, 0)
    pl.semaphore_wait(barrier, count - 1)


def strip_at(r, c):
    pair = lax.rem((r + 1) // 2, 4)
    return (pair * 2 + c // 2) * 4 + lax.rem(c, 2) * 2 + lax.rem(r + 1, 2)


def strip_of(d):
    rr, cc = d // 4, lax.rem(d, 4)
    pair, core = rr // 2, lax.rem(cc, 2)
    r = jnp.where(pair == 0, 7 * (1 - core), 2 * pair - 1 + core)
    return r, lax.rem(rr, 2) * 2 + cc // 2


def slots_of(d):
    r, c = strip_of(d)
    row = (r + 1) // 2
    return row * 5 + c + 1, row * 5 + lax.rem(c + 1, 4)


def lane_tables():
    low = np.zeros((512, 512), np.float32)
    high = np.zeros((512, 512), np.float32)
    rest = np.zeros((512, 512), np.float32)
    for lane in range(512):
        c, q = lane // 128, lane % 128
        low[lane, (q // 32) * 128 + c * 32 + q % 32] = 1.0
        high[lane, (q // 64) * 256 + c * 64 + q % 64] = 1.0
        to = c * 64 + q if q < 64 else (256 if q < 96 else 384) + c * 32 + q % 32
        rest[lane, to] = 1.0
    return np.stack([low, rest, high])


def place_lanes(x, at, width=128):
    n = x.shape[1]
    one = (
        lax.broadcasted_iota(jnp.int32, (n, width), 0) + at
        == lax.broadcasted_iota(jnp.int32, (n, width), 1)
    )
    return jnp.dot(x, jnp.where(one, 1.0, 0.0).astype(x.dtype), preferred_element_type=F32)


ALL_ROWS = 576
LOW, REST, HIGH_PART = range(3)
ROWS_OF = ((0, 144), (144, 288), (288, 576))
BIG = 1
GATHER_ROWS = ((0, 144), (144, 576))
Z_ORDER = (0, 1, -1, 2, -2, 3, -3)


NORM_ROW = 81
LOSS_ROW = 99


def lane_value(pairs):
    lane = lax.broadcasted_iota(jnp.int32, (8, 128), 1)
    total = jnp.zeros((8, 128), F32)
    for at, value in pairs:
        total = total + jnp.where(lane == at, value, 0.0)
    return total


def square_sum(x):
    x = x * x
    while x.ndim > 2:
        x = jnp.sum(x, axis=0)
    return jnp.sum(jnp.sum(x, axis=0, keepdims=True), axis=1, keepdims=True)


def silu_grad_tanh(v):
    s = 0.5 * jnp.tanh(0.5 * v) + 0.5
    return s * (1.0 + v * (1.0 - s))


def lamb_update(weight, first, second, grad):
    first_new = BETA_ONE * first + (1.0 - BETA_ONE) * grad
    second_new = BETA_TWO * second + (1.0 - BETA_TWO) * grad * grad
    first_hat = first_new / (1.0 - BETA_ONE**STEP)
    second_hat = second_new / (1.0 - BETA_TWO**STEP)
    return second_new, first_hat / (jnp.sqrt(second_hat) + EPS_ADAM) + DECAY * weight


LAST_ORDER = (5, 1, 2, 4, 3, 6, 0, 7)


def last_kernel(*refs):
    scalars_ref, back_ref = refs[:2]
    far, outs, (loss_out, count_out, clip_out, image_out) = refs[2:34], refs[34:58], refs[58:62]
    near, made = refs[62:94], refs[94:118]
    pixel_ref, load_sem, store_sem = refs[118:]

    def load(n, kind):
        at = 4 * n + kind
        return pltpu.make_async_copy(far[at], near[at], load_sem.at[at])

    for n in LAST_ORDER:
        for kind in range(4):
            load(n, kind).start()

    column = lax.broadcasted_iota(jnp.int32, (64, 128), 1)
    row_no = lax.broadcasted_iota(jnp.int32, (64, 128), 0)
    pixel = jnp.bitwise_and(column, 63)
    pick = jnp.where(pixel == 2 * (row_no - 16) + lax.shift_right_logical(column, 6), 1.0, 0.0)
    for i in range(16):
        for side in range(2):
            pixel_ref[24 * i : 24 * i + 24, 32 * side : 32 * side + 32] = back_ref[
                side, :, 32 * i : 32 * i + 32
            ]
    wide = jnp.dot(pixel_ref[...], pick, precision=HIGH, preferred_element_type=F32)
    row_no = lax.broadcasted_iota(jnp.int32, (192, 384), 0)
    h = jnp.bitwise_and(row_no, 31)
    source = (
        lax.shift_right_logical(h, 1) * 24
        + jnp.bitwise_and(h, 1) * 6
        + lax.shift_right_logical(row_no, 5)
    )
    at_row = lax.broadcasted_iota(jnp.int32, (192, 384), 1)
    total = None
    for cp in range(2):
        pick = jnp.where(at_row == source + 12 * cp, 1.0, 0.0)
        term = jnp.dot(
            pick, wide[:, 64 * cp : 64 * cp + 64], precision=HIGH, preferred_element_type=F32
        )
        total = term if total is None else total + term
    image_out[...] = total.reshape(6, 32, 64)

    scalars = scalars_ref[...]
    factor = scalars[8:9, 0:1]
    for n, out in ((9, loss_out), (10, count_out), (11, clip_out)):
        out[...] = scalars[n : n + 1, 0:1]

    def root_ratio(a, b):
        return RATE * jnp.sqrt(a) / jnp.sqrt(b)

    def like(ratio, v):
        return ratio.reshape((1,) * v.ndim)

    spot_of = (None, 0, 4, 6, 7, 8, 9, None)
    stores = []
    for n in LAST_ORDER:
        for kind in range(4):
            load(n, kind).wait()
        grad_ref, weight_ref, first_ref, second_ref = near[4 * n : 4 * n + 4]
        grad_out, moment_out, new_out = made[3 * n : 3 * n + 3]
        weight = weight_ref[...]
        grad = grad_ref[...] * like(factor, weight)
        second_new, update = lamb_update(weight, first_ref[...], second_ref[...], grad)
        grad_out[...] = grad
        moment_out[...] = second_new
        if n == 0:
            for lo, hi in ((0, 6), (6, 9)):
                w, u = weight[:, lo:hi, :], update[:, lo:hi, :]
                new_out[:, lo:hi, :] = w - like(root_ratio(square_sum(w), square_sum(u)), w) * u
        elif n == 7:
            new_out[...] = weight - root_ratio(square_sum(weight), square_sum(update)) * update
        else:
            for j in range(weight.shape[0] if n < 3 else 1):
                s = spot_of[n] + j
                ratio = root_ratio(scalars[0:1, s : s + 1], scalars[0:1, 64 + s : 65 + s])
                if n < 3:
                    new_out[j] = weight[j] - like(ratio, weight[j]) * update[j]
                else:
                    new_out[...] = weight - like(ratio, weight) * update
        for kind in range(3):
            at = 3 * n + kind
            copy = pltpu.make_async_copy(made[at], outs[at], store_sem.at[at])
            copy.start()
            stores.append(copy)
    for copy in stores:
        copy.wait()


def last(scalars, back, grads, state):
    def shape(a):
        return jax.ShapeDtypeStruct(a.shape, F32)

    far = []
    for n in range(8):
        far += [grads[n], *state[3 * n : 3 * n + 3]]
    outs = [shape(a) for a in state]
    small = [jax.ShapeDtypeStruct((1, 1), F32)] * 3 + [jax.ShapeDtypeStruct((6, 32, 64), F32)]
    vmem = pl.BlockSpec(memory_space=pltpu.VMEM)
    away = pl.BlockSpec(memory_space=pltpu.HBM)
    return pl.pallas_call(
        last_kernel,
        out_shape=tuple(outs + small),
        in_specs=[vmem] * 2 + [away] * 32,
        out_specs=[away] * 24 + [vmem] * 4,
        scratch_shapes=[pltpu.VMEM(a.shape, F32) for a in far]
        + [pltpu.VMEM(a.shape, F32) for a in state]
        + [
            pltpu.VMEM((384, 64), F32),
            pltpu.SemaphoreType.DMA((32,)),
            pltpu.SemaphoreType.DMA((24,)),
        ],
        compiler_params=pltpu.CompilerParams(vmem_limit_bytes=60 * 1024 * 1024),
        name="last",
    )(scalars, back, *far)


def step_kernel(*refs):
    live_ref, temb_ref, image_ref, target_ref = refs[:4]
    far, outs = refs[4:30], refs[30:38]
    scalars_out, back_out = refs[38:40]
    near = refs[40:66]
    (
        low_ref,
        high_ref,
        down_ref,
        up_ref,
        full_ref,
        half_ref,
        work_ref,
        grad_ref,
        wide_ref,
        thin_ref,
        act_ref,
        acth_ref,
        turn_ref,
        wc_ref,
        wr_ref,
        wu_ref,
        wut_ref,
        wd_ref,
        coef_ref,
        rows_ref,
        patch_ref,
        ext_ref,
        send_ref,
        recv_ref,
        img_ref,
        tgt_ref,
        dwi_ref,
        dwh_ref,
        ngrad_ref,
        fgrad_ref,
        part_ref,
    part4_ref,
        imgrad_ref,
        wi_ref,
        wht_ref,
        wit_ref,
        wh_ref,
        tmp_ref,
        all_ref,
        block_ref,
        strips_ref,
        planes_ref,
        cbuf_ref,
        csend_ref,
        cpart_ref,
        fsend_ref,
        frecv_ref,
        film_ref,
        joined_ref,
        condv_ref,
        rb_ref,
        rx_ref,
        ry_ref,
        rz_ref,
        own_ref,
        m1_ref,
        r1_ref,
        m2_ref,
        r2_ref,
        m3_ref,
        r3_ref,
        gcs_ref,
        gcr_ref,
        fsum_ref,
        total_ref,
        back_ref,
        send_sem,
        recv_sem,
        load_sem,
        g_send,
        g_recv,
        strip_send,
        strip_recv,
        cond_send,
        cond_recv,
        film_send,
        film_recv,
        core_send,
        core_recv,
        x_send,
        x_recv,
        y_send,
        y_recv,
        z_send,
        z_recv,
        m_send,
        m_recv,
        gc_send,
        gc_recv,
        back_send,
        back_recv,
    ) = refs[66:]
    lanes_ref, text_ref = near[:2]
    weights, firsts, seconds = near[2::3], near[3::3], near[4::3]
    edge_ref, norm_ref = weights[0], weights[7]
    dlow_ref, dhigh_ref, ddown_ref, dup_ref = low_ref, high_ref, down_ref, up_ref
    sb_ref = all_ref
    rr, cc, z, y, x, co = place_of()
    me = rr * 4 + cc
    core = co
    partner = 1 - co + 2 * x
    halo = rr >= 2
    split = jnp.logical_and(lax.rem(rr, 2) == 1, cc >= 2)

    def flag(cond):
        return jnp.where(cond, 1.0, 0.0).astype(F32)

    f_halo = flag(halo)
    f_core1 = flag(core == 1)
    f_core0 = 1.0 - f_core1
    f_top = f_halo * f_core1
    f_bot = f_halo * f_core0
    f_split = flag(split)
    f_joined = 1.0 - f_split

    place = lax.broadcasted_iota(jnp.int32, (32, 256), 0)
    lo_mask = jnp.where(place == 0, 0.0, jnp.where(place == 16, f_joined, 1.0))
    hi_mask = jnp.where(place == 31, 0.0, jnp.where(place == 15, f_joined, 1.0))

    def before(x):
        return pltpu.roll(x, 1, 0) * lo_mask

    def after(x):
        return pltpu.roll(x, 31, 0) * hi_mask

    def at(i):
        return pl.ds(pl.multiple_of(i * 32, 32), 32)

    def loop(body, init=0, count=16):
        return lax.fori_loop(0, count, body, init, unroll=16)

    def dot(a, b):
        return jnp.dot(a, b, preferred_element_type=F32)

    def dot_nt(a, b):
        return lax.dot_general(a, b, (((1,), (1,)), ((), ())), preferred_element_type=F32)

    def sigmoid(z):
        return 0.5 * jnp.tanh(0.5 * z) + 0.5

    def double(v):
        return jnp.concatenate([v, v], axis=1)


    def copy_of(e):
        return pltpu.make_async_remote_copy(
            src_ref=send_ref.at[e],
            dst_ref=recv_ref.at[e],
            send_sem=send_sem.at[e],
            recv_sem=recv_sem.at[e],
            device_id={"cols": partner},
            device_id_type=MESH,
        )

    def send(e, row, stats=None):
        send_ref[e, 0:32, :] = row
        send_ref[e, 32:40, :] = jnp.zeros((8, 256), F32) if stats is None else stats
        copy_of(e).start()

    def arrive(e):
        copy_of(e).wait()

    def edge_full(ref):
        low = f_core0 * ref[0, 480:512, 128:256] + f_core1 * ref[0, 0:32, 0:128]
        high = f_core0 * ref[1, 480:512, 128:256] + f_core1 * ref[1, 0:32, 0:128]
        return jnp.concatenate([low, high], axis=1)

    def edge_cell(ref):
        return f_core0 * ref[480:512, :] + f_core1 * ref[0:32, :]

    def edge(ref, planes):
        return edge_full(ref) if planes == 2 else edge_cell(ref.at[0])


    def halves(x):
        return x[0:8] + x[8:16], x[16:24] + x[24:32]

    def gathered(sums, planes):
        rows = []
        for s in sums:
            row = jnp.sum(s, axis=0, keepdims=True)
            rows.append(double(row[:, 0:128] + row[:, 128:256]) if planes == 2 else row)
        return jnp.concatenate(rows + [jnp.zeros((4, 256), F32)], axis=0)

    zero8 = jnp.zeros((8, 256), F32)

    def stats_of(x_ref, planes):
        def body(i, carry):
            s_l, s_r, q_l, q_r = carry
            for p in range(planes):
                x = x_ref[p, at(i), :]
                a, b = halves(x)
                c, d = halves(x * x)
                s_l, s_r, q_l, q_r = s_l + a, s_r + b, q_l + c, q_r + d
            return s_l, s_r, q_l, q_r

        return gathered(loop(body, (zero8,) * 4), planes)

    def over_slot(block, planes):
        swapped = jnp.concatenate(
            [block[1:2], block[0:1], block[3:4], block[2:3], block[4:8]], axis=0
        )
        x = block + f_joined * swapped
        lane = lax.broadcasted_iota(jnp.int32, (8, 256), 1)
        step = 1
        while step < (4 if planes == 2 else 8):
            up = pltpu.roll(x, 256 - step, 1)
            down = pltpu.roll(x, step, 1)
            x = x + jnp.where(lax.rem(lane, 2 * step) < step, up, down)
            step *= 2
        size = 16.0 if planes == 2 else 8.0
        count = (16.0 + 16.0 * f_halo) * (16.0 + 16.0 * f_joined) * size
        return x / count

    def spread(two):
        return jnp.concatenate(
            [
                jnp.broadcast_to(two[0:1], (16, 256)),
                jnp.broadcast_to(two[1:2], (16, 256)),
            ],
            axis=0,
        )

    def norm_row(k, which):
        width = NORM_AT[k + 1] - NORM_AT[k] if k < 6 else 128
        row = norm_ref[which : which + 1, NORM_AT[k] : NORM_AT[k] + width]
        return double(row) if width == 128 else row

    def film_rows(k, which):
        if k not in FILM_AT:
            return jnp.zeros((2, 256), F32)
        width = 256 if k == 5 else 128
        base = FILM_AT[k] + which * width
        two = film_ref[0:2, base : base + width]
        return double(two) if width == 128 else two

    def norm_ready(k, stats, e, planes):
        total = over_slot(stats + f_halo * recv_ref[e, 32:40, :], planes)
        mean = total[0:2]
        var = total[2:4] - mean * mean
        inverse = lax.rsqrt(var + EPS_NORM)
        gain, bias = norm_row(k, 0), norm_row(k, 1)
        factor = 1.0 + film_rows(k, 0)
        slope = inverse * gain * factor
        coef_ref[k, 0] = spread(slope)
        coef_ref[k, 1] = spread((bias - mean * inverse * gain) * factor + film_rows(k, 1))
        coef_ref[k, 2] = spread(mean)
        coef_ref[k, 3] = spread(inverse)
        rows_ref[k, 0:2, :] = mean
        rows_ref[k, 2:4, :] = inverse

    def activated(x, k):
        z = x * coef_ref[k, 0] + coef_ref[k, 1]
        return z * sigmoid(z)


    def put_wide(i, even, odd):
        for t, g in enumerate((before(odd), even, odd, after(even))):
            b = g.astype(BF)
            wide_ref[at(i + 1), 512 * t : 512 * t + 256] = b
            wide_ref[at(i + 2), 512 * t + 256 : 512 * t + 384] = b[:, 128:256]
            wide_ref[at(i), 512 * t + 384 : 512 * t + 512] = b[:, 0:128]

    def put_wide_edge(row):
        even, odd = row[:, 0:128], row[:, 128:256]
        lo, hi = lo_mask[:, 0:128], hi_mask[:, 0:128]
        for t, g in enumerate((pltpu.roll(odd, 1, 0) * lo, even, odd, pltpu.roll(even, 31, 0) * hi)):
            wide_ref[32:64, 512 * t + 256 : 512 * t + 384] = (g * f_top).astype(BF)
            wide_ref[512:544, 512 * t + 384 : 512 * t + 512] = (g * f_bot).astype(BF)

    def put_thin(i, x):
        for t, g in enumerate((before(x), x, after(x))):
            thin_ref[at(i + 1), 256 * t : 256 * t + 256] = g.astype(BF)

    def put_thin_edge(row):
        for t, g in enumerate((before(row), row, after(row))):
            thin_ref[0:32, 256 * t : 256 * t + 256] = (g * f_top).astype(BF)
            thin_ref[544:576, 256 * t : 256 * t + 256] = (g * f_bot).astype(BF)

    def keep_wide(slot):
        act_ref[slot, 0] = wide_ref[32:544, 512:768]
        act_ref[slot, 1] = wide_ref[32:544, 1024:1280]

    def keep_thin(slot):
        acth_ref[slot] = thin_ref[32:544, 256:512]

    def turn_wide(slot):
        turn_ref[0:256, :] = act_ref[slot, 0].T
        turn_ref[256:512, :] = act_ref[slot, 1].T


    def load_wc(index):
        for b in range(3):
            for r in range(4):
                for rp in range(2):
                    a = ROW_OF[r] - rp + 1
                    if 0 <= a <= 2:
                        wc_ref[
                            b * 512 + r * 128 : b * 512 + r * 128 + 128, rp * 128 : rp * 128 + 128
                        ] = low_ref[index, 3 * a + b]

    def load_wr(index):
        for b in range(3):
            for r in range(4):
                for rp in range(2):
                    a = ROW_OF[r] - rp + 1
                    if 0 <= a <= 2:
                        wr_ref[
                            rp * 128 : rp * 128 + 128, b * 512 + r * 128 : b * 512 + r * 128 + 128
                        ] = low_ref[index, 8 - 3 * a - b]

    def taps_of(parity, d):
        if parity == 0:
            return {-1: (0,), 0: (1, 2)}.get(d, ())
        return {0: (0, 1), 1: (2,)}.get(d, ())

    def load_up():
        for cp in range(2):
            for rp in range(2):
                for di in (-1, 0, 1):
                    for dj in (-1, 0, 1):
                        taps = [3 * a + b for a in taps_of(rp, di) for b in taps_of(cp, dj)]
                        if not taps:
                            continue
                        total = up_ref[taps[0]].astype(F32)
                        for t in taps[1:]:
                            total = total + up_ref[t].astype(F32)
                        low = total.astype(BF)
                        at_k = (dj + 1 - cp) * 256
                        wu_ref[cp, di + 1, at_k : at_k + 256, rp * 128 : rp * 128 + 128] = low
                        row = ROW_OF.index(rp - 2 * di)
                        col = COL_OF.index(cp - 2 * dj)
                        wut_ref[:, col * 512 + row * 128 : col * 512 + row * 128 + 128] = low

    def load_down():
        for b in range(3):
            for r in range(3):
                a = ROW_OF[r] + 1
                wd_ref[b * 512 + r * 128 : b * 512 + r * 128 + 128, :] = down_ref[3 * a + b]


    def conv_low(out, weight_nt=False):
        for cp in range(2):
            left = wide_ref[32:544, cp * 512 : cp * 512 + 1536]
            out(cp, dot_nt(left, wr_ref[...]) if weight_nt else dot(left, wc_ref[...]))

    def conv_high(index):
        total = None
        for a in range(3):
            term = dot(
                thin_ref[32 * a : 32 * a + 512, :],
                high_ref[index, 3 * a : 3 * a + 3].reshape(768, 256),
            )
            total = term if total is None else total + term
        return total

    def conv_high_back(index):
        total = None
        for a in range(3):
            for b in range(3):
                term = dot_nt(
                    thin_ref[32 * a : 32 * a + 512, b * 256 : b * 256 + 256],
                    high_ref[index, 8 - 3 * a - b],
                )
                total = term if total is None else total + term
        return total

    def grad_low(index, slot):
        turn_wide(slot)
        for b in range(3):
            block = dot(turn_ref[0:256, :], wide_ref[32:544, b * 512 : b * 512 + 512]) + dot(
                turn_ref[256:512, :], wide_ref[32:544, b * 512 + 512 : b * 512 + 1024]
            )
            for a in range(3):
                first = ROW_OF.index(a - 1) * 128
                second = ROW_OF.index(a) * 128
                dlow_ref[index, 8 - 3 * a - b] = (
                    block[0:128, first : first + 128] + block[128:256, second : second + 128]
                ).astype(dlow_ref.dtype)

    def grad_high(index, slot):
        turn_ref[0:256, :] = acth_ref[slot].T
        for a in range(3):
            block = dot(turn_ref[0:256, :], thin_ref[32 * a : 32 * a + 512, :])
            for b in range(3):
                dhigh_ref[index, 8 - 3 * a - b] = block[:, b * 256 : b * 256 + 256].astype(
                    dhigh_ref.dtype
                )


    def put_patch(slot, source, row, lanes):
        ext_ref[0:32, :] = row * f_top
        ext_ref[544:576, :] = row * f_bot

        def fill(i, carry):
            ext_ref[at(i + 1), :] = source[at(i), :]
            return carry

        loop(fill)

        def body(i, carry):
            total = None
            for di in (-1, 0, 1):
                x = ext_ref[at(i + 1 + di), :]
                for dj, g in enumerate((before(x), x, after(x))):
                    shift = ((di + 1) * 3 + dj) * lanes
                    term = pltpu.roll(g, shift, 1) if shift else g
                    total = term if total is None else total + term
            patch_ref[slot, at(i), :] = total.astype(BF)
            return carry

        loop(body)


    def norm_back_start(k, x_ref, planes):
        def body(i, carry):
            s_l, s_r, q_l, q_r = carry
            for p in range(planes):
                x = x_ref[p, at(i), :]
                z = x * coef_ref[k, 0] + coef_ref[k, 1]
                s = sigmoid(z)
                d = work_ref[p, at(i), :] * (s * (1.0 + z * (1.0 - s)))
                work_ref[p, at(i), :] = d
                a, b = halves(d)
                c, e = halves(d * ((x - coef_ref[k, 2]) * coef_ref[k, 3]))
                s_l, s_r, q_l, q_r = s_l + a, s_r + b, q_l + c, q_r + e
            return s_l, s_r, q_l, q_r

        return gathered(loop(body, (zero8,) * 4), planes)

    def norm_back_ready(k, stats, e, planes):
        gain, bias = norm_row(k, 0), norm_row(k, 1)
        factor = 1.0 + film_rows(k, 0)
        width = 128 if planes == 2 else 256
        one, two = stats[0:2], stats[2:4]
        dgain, dbias = factor * two, factor * one
        o = NORM_AT[k]
        ngrad_ref[0:1, o : o + width] = (dgain[0:1] + dgain[1:2])[:, 0:width]
        ngrad_ref[1:2, o : o + width] = (dbias[0:1] + dbias[1:2])[:, 0:width]
        if k in FILM_AT:
            f = FILM_AT[k]
            fgrad_ref[0:2, f : f + width] = (gain * two + bias * one)[:, 0:width]
            fgrad_ref[0:2, f + width : f + 2 * width] = one[:, 0:width]
        both = stats + f_halo * recv_ref[e, 32:40, :]
        kk = gain * factor
        scaled = jnp.concatenate([kk * both[0:2], kk * both[2:4], both[4:8]], axis=0)
        total = over_slot(scaled, planes)
        mean, inverse = rows_ref[k, 0:2, :], rows_ref[k, 2:4, :]
        second = -inverse * inverse * total[2:4]
        third = -inverse * total[0:2] - mean * second
        coef_ref[k, 4] = spread(inverse * kk)
        coef_ref[k, 5] = spread(second)
        coef_ref[k, 6] = spread(third)

    def back_value(k, d, x):
        return d * coef_ref[k, 4] + x * coef_ref[k, 5] + coef_ref[k, 6]


    def shard(kind, part, zs, ys, xs, ks, device):
        rows = slice(*GATHER_ROWS[part])
        return pltpu.make_async_remote_copy(
            src_ref=all_ref.at[zs, ys, xs, ks, rows],
            dst_ref=all_ref.at[zs, ys, xs, ks, rows],
            send_sem=g_send.at[part, kind, zs, ys, xs],
            recv_sem=g_recv.at[part, zs, ys, xs, ks],
            device_id=device,
            device_id_type=MESH,
        )

    def to_z(part, zd):
        return shard(zd, part, z, y, x, co, device_at(zd, y, x, co))

    def to_x(part, zs, ys):
        return shard(4, part, zs, ys, x, co, device_at(z, y, 1 - x, co))

    def to_y(part, zs, xs):
        return shard(5, part, zs, y, xs, co, device_at(z, 1 - y, x, co))

    def to_core(part, zs, ys, xs):
        return shard(6, part, zs, ys, xs, co, device_at(z, y, x, 1 - co))

    def arrived(part, zs, ys, xs, ks=co):
        shard(6, part, zs, ys, xs, ks, device_at(z, y, x, 1 - co)).wait_recv()

    def start(copy):
        copy.start()

    def in_line(dz, act):
        zs = z + dz

        @pl.when(jnp.logical_and(zs >= 0, zs <= 3))
        def _():
            act(zs)

    def gather_far(part, act=start):
        for zd in range(4):

            @pl.when(zd != z)
            def _(zd=zd):
                act(to_z(part, zd))

    def gather_near(part, act=start):
        act(to_x(part, z, y))
        act(to_y(part, z, x))
        act(to_core(part, z, y, x))

    def gather_z(part, act=start, wait=arrived):
        for dz in Z_ORDER[1:]:

            def one(zs):
                wait(part, zs, y, x)
                act(to_x(part, zs, y))
                act(to_y(part, zs, x))
                act(to_core(part, zs, y, x))

            in_line(dz, one)

    def gather_xy(part, act=start, wait=arrived):
        for dz in Z_ORDER:

            def one(zs):
                wait(part, zs, y, 1 - x)

                @pl.when(lax.rem(zs, 2) == 0)
                def _():
                    act(to_y(part, zs, 1 - x))

                act(to_core(part, zs, y, 1 - x))
                wait(part, zs, 1 - y, x)

                @pl.when(lax.rem(zs, 2) == 1)
                def _():
                    act(to_x(part, zs, 1 - y))

                act(to_core(part, zs, 1 - y, x))

            in_line(dz, one)

    def gather_last(part, act=start, wait=arrived):
        for dz in Z_ORDER:

            def one(zs):
                wait(part, zs, 1 - y, 1 - x)
                act(to_core(part, zs, 1 - y, 1 - x))

            in_line(dz, one)

    def gather_core(part):
        for zs in range(4):
            for ys in range(2):
                for xs in range(2):
                    arrived(part, zs, ys, xs, 1 - co)

    def gather_sent(part):
        def sent(copy):
            copy.wait_send()

        def none(*a):
            return None

        gather_far(part, sent)
        gather_near(part, sent)
        gather_z(part, sent, none)
        gather_xy(part, sent, none)
        gather_last(part, sent, none)

    def row_places(r):
        def rows(at_row, size):
            return pl.ds(pl.multiple_of(at_row, 16), size)

        return rows(r * 16, 16), rows(r * 32, 32), rows(r * 32, 16), rows(r * 32 + 16, 16)

    def gather_place(part):
        rows = slice(*ROWS_OF[part])

        def row(r, carry):
            zr, yr = r // 2, lax.rem(r, 2)
            at16, at32, a16, b16 = row_places(r)
            packed = jnp.concatenate(
                [all_ref[zr, yr, c // 2, c % 2, rows, :] for c in range(4)], axis=1
            )
            v = jnp.dot(packed, lanes_ref[part], preferred_element_type=F32).astype(BF)
            if part == LOW:
                for j in range(4):
                    low_ref[j, :, at16, :] = v[:, j * 128 : j * 128 + 128].reshape(9, 16, 128)
            elif part == HIGH_PART:
                for j in range(2):
                    high_ref[j, :, at32, :] = v[:, j * 256 : j * 256 + 256].reshape(9, 32, 256)
            else:
                down_ref[:, at16, :] = v[:, 0:256].reshape(9, 16, 256)
                up_ref[:, a16, :] = v[:, 256:384].reshape(9, 16, 128)
                up_ref[:, b16, :] = v[:, 384:512].reshape(9, 16, 128)
            return carry

        lax.fori_loop(0, 8, row, 0)

    def pack_own(part):
        rows = slice(*ROWS_OF[part])
        own = all_ref.at[z, y, x, co]
        if part == LOW:
            total = None
            for j in range(4):
                term = place_lanes(weights[1][j].reshape(144, 32).astype(BF), 32 * j)
                total = term if total is None else total + term
        elif part == HIGH_PART:
            total = place_lanes(weights[2][0].reshape(288, 64).astype(BF), 0) + place_lanes(
                weights[2][1].reshape(288, 64).astype(BF), 64
            )
        else:
            total = (
                place_lanes(weights[3][...].reshape(144, 64).astype(BF), 0)
                + place_lanes(weights[4][:, 0:16, :].reshape(144, 32).astype(BF), 64)
                + place_lanes(weights[4][:, 16:32, :].reshape(144, 32).astype(BF), 96)
            )
        own[rows, :] = total.astype(BF)

    to_left = strip_at(rr, cc)
    to_right = strip_at(rr, lax.rem(cc + 3, 4))

    def strip_copies(side, device):
        return [
            pltpu.make_async_remote_copy(
                src_ref=block_ref.at[1 - side],
                dst_ref=strips_ref.at[side],
                send_sem=strip_send.at[side],
                recv_sem=strip_recv.at[side],
                device_id=device_no(device),
                device_id_type=MESH,
            )
        ]

    def pack_block():
        planes_ref[0:192, :] = image_ref[...].astype(F32).reshape(192, 64)
        planes_ref[192:288, :] = target_ref[...].reshape(96, 64)
        for g in range(4):
            for h in range(2):
                block_ref[h, :, 32 * g : 32 * g + 32] = planes_ref[
                    72 * g : 72 * g + 72, 32 * h : 32 * h + 32
                ]

    loads = [
        pltpu.make_async_copy(a, b, load_sem.at[n]) for n, (a, b) in enumerate(zip(far, near))
    ]
    for n in (5, 11, 14, 8, 1, 17, 0, 2, 20, 23):
        loads[n].start()
    for n in range(26):
        if n > 1 and n % 3 != 2:
            loads[n].start()


    def others(body):
        def one(d, carry):
            @pl.when(d != me)
            def _():
                body(d)

            return carry

        lax.fori_loop(0, 32, one, 0)

    def row_mates(body):
        for c in range(4):

            @pl.when(cc != c)
            def _(c=c):
                body(c)

    def cond_copy(c, source):
        return pltpu.make_async_remote_copy(
            src_ref=csend_ref,
            dst_ref=cbuf_ref.at[source],
            send_sem=cond_send.at[c],
            recv_sem=cond_recv.at[source],
            device_id={"rows": rr, "cols": c},
            device_id_type=MESH,
        )

    def film_copy(d, source):
        return pltpu.make_async_remote_copy(
            src_ref=fsend_ref.at[d],
            dst_ref=frecv_ref.at[source],
            send_sem=film_send.at[d],
            recv_sem=film_recv.at[source],
            device_id=device_no(d),
            device_id_type=MESH,
        )

    def cond_start():
        joined_ref[24:32, :] = jnp.zeros((8, joined_ref.shape[1]), F32)
        for a in range(5):
            joined_ref[5 * a : 5 * a + 5, 0:128] = temb_ref[a].astype(F32)
            joined_ref[5 * a : 5 * a + 5, 128:] = text_ref[a].astype(F32)
        own = dot_nt(joined_ref[...].astype(BF), weights[5][...].astype(BF))
        csend_ref[...] = jnp.concatenate([own, jnp.zeros((32, 112), F32)], axis=1)
        row_mates(lambda c: cond_copy(c, cc).start())
        cbuf_ref[cc] = csend_ref[...]

    def film_start():
        row_mates(lambda c: cond_copy(c, c).wait_recv())
        whole = cbuf_ref[0]
        for c in range(1, 4):
            whole = whole + pltpu.roll(cbuf_ref[c], 16 * c, 1)
        whole = whole[:, 0:64]
        cond = (whole * sigmoid(whole)).astype(BF)
        condv_ref[...] = cond.astype(F32)
        cpart_ref[...] = dot(cond, weights[6][...].astype(BF))

        def deal(d, carry):
            s_l, s_r = slots_of(d)
            for n, slot in enumerate((s_l, s_r)):
                line = cpart_ref[pl.ds(slot, 1), :]
                fsend_ref[d, 2 * n : 2 * n + 1, :] = line[:, 0:128]
                fsend_ref[d, 2 * n + 1 : 2 * n + 2, :] = line[:, 128:256]

            @pl.when(d != me)
            def _():
                film_copy(d, me).start()

            return carry

        lax.fori_loop(0, 32, deal, 0)
        frecv_ref[me] = fsend_ref[me]

    def film_ready():
        others(lambda d: film_copy(d, d).wait_recv())
        for c in range(4):
            total = frecv_ref[c]
            for r in range(1, 8):
                total = total + frecv_ref[4 * r + c]
            for n in range(4):
                at_lane = c * 256 + n % 2 * 128
                film_ref[n // 2 : n // 2 + 1, at_lane : at_lane + 128] = total[n : n + 1]


    def edge_terms():
        for a in range(3):
            for b in range(3):
                for cp in range(2):
                    for rp in range(2):
                        rho, gamma = rp + a - 1, cp + b - 1
                        cell = (rho // 2 + 1) * 3 + gamma // 2 + 1
                        phase = (gamma % 2) * 2 + rho % 2
                        tile = COL_OF.index(gamma) * 512 + ROW_OF.index(rho) * 128
                        yield 3 * a + b, cp, rp, cell, phase, tile

    def load_edges():
        dwi_ref[...] = jnp.zeros(dwi_ref.shape, F32)
        dwh_ref[...] = jnp.zeros(dwh_ref.shape, F32)
        for t, cp, rp, cell, phase, _ in edge_terms():
            lanes = slice(rp * 128, rp * 128 + 128)
            row = cell * 24 + phase * 6
            dwi_ref[cp, row : row + 6, lanes] = edge_ref[t, 0:6, :]
            row = cell * 12 + phase * 3
            dwh_ref[cp, row : row + 3, lanes] = edge_ref[8 - t, 6:9, :]
        wi_ref[...] = dwi_ref[...].astype(BF)
        wht_ref[...] = dwh_ref[...].astype(BF)
        for ref, taps, lo, size in ((wh_ref, 1, 6, 3), (wit_ref, -1, 0, 6)):
            ref[...] = jnp.zeros(ref.shape, BF)
            tmp_ref[...] = jnp.zeros(tmp_ref.shape, F32)
            for t, cp, rp, _, _, tile in edge_terms():
                row = (cp * 2 + rp) * size
                tap = t if taps > 0 else 8 - t
                tmp_ref[row : row + size, tile : tile + 128] = edge_ref[tap, lo : lo + size, :]
            ref[0:32, :] = tmp_ref[...].astype(BF)


    def add(to, b):
        to[...] = (to[...].astype(F32) + b[...].astype(F32)).astype(BF)

    def deal_pack(part, r_lo, r_hi):
        rows = slice(*ROWS_OF[part])

        def row(r, carry):
            zr, yr = r // 2, lax.rem(r, 2)
            at16, at32, a16, b16 = row_places(r)
            if part == LOW:
                pieces = [dlow_ref[j, :, at16, :].reshape(144, 128) for j in range(4)]
            elif part == HIGH_PART:
                pieces = [dhigh_ref[j, :, at32, :].reshape(288, 256) for j in range(2)]
            else:
                pieces = [
                    ddown_ref[:, at16, :].reshape(144, 256),
                    dup_ref[:, a16, :].reshape(144, 128),
                    dup_ref[:, b16, :].reshape(144, 128),
                ]
            v = dot_nt(jnp.concatenate(pieces, axis=1), lanes_ref[part]).astype(BF)
            for c in range(4):
                sb_ref[zr, yr, c // 2, c % 2, rows, :] = v[:, c * 128 : c * 128 + 128]
            return carry

        lax.fori_loop(r_lo, r_hi, row, 0)

    def core_copy(part, zs):
        rows = slice(*ROWS_OF[part])
        return pltpu.make_async_remote_copy(
            src_ref=sb_ref.at[zs, :, :, 1 - co, rows],
            dst_ref=rb_ref.at[zs, :, :, rows],
            send_sem=core_send.at[part, zs],
            recv_sem=core_recv.at[part, zs],
            device_id=device_at(z, y, x, 1 - co),
            device_id_type=MESH,
        )

    def first_copy(part, zs):
        rows = slice(*ROWS_OF[part])
        by_x = zs % 2 == 0
        return pltpu.make_async_remote_copy(
            src_ref=rb_ref.at[zs, :, 1 - x, rows] if by_x else rb_ref.at[zs, 1 - y, :, rows],
            dst_ref=rx_ref.at[zs, :, rows],
            send_sem=x_send.at[part, zs],
            recv_sem=x_recv.at[part, zs],
            device_id=device_at(z, y, 1 - x, co) if by_x else device_at(z, 1 - y, x, co),
            device_id_type=MESH,
        )

    def second_copy(part, zs):
        rows = slice(*ROWS_OF[part])
        by_x = zs % 2 == 1
        return pltpu.make_async_remote_copy(
            src_ref=rb_ref.at[zs, y, 1 - x, rows] if by_x else rb_ref.at[zs, 1 - y, x, rows],
            dst_ref=ry_ref.at[zs, rows],
            send_sem=y_send.at[part, zs],
            recv_sem=y_recv.at[part, zs],
            device_id=device_at(z, y, 1 - x, co) if by_x else device_at(z, 1 - y, x, co),
            device_id_type=MESH,
        )

    def z_copy(part, zs, source):
        rows = slice(*ROWS_OF[part])
        return pltpu.make_async_remote_copy(
            src_ref=rb_ref.at[zs, y, x, rows],
            dst_ref=rz_ref.at[source, rows],
            send_sem=z_send.at[part, zs],
            recv_sem=z_recv.at[part, source],
            device_id=device_at(zs, y, x, co),
            device_id_type=MESH,
        )

    def deal_core(part):
        for zs in range(4):
            deal_pack(part, 2 * zs, 2 * zs + 2)
            core_copy(part, zs).start()

    def deal_first(part):
        rows = slice(*ROWS_OF[part])
        for zs in range(4):
            core_copy(part, zs).wait_recv()
            for ys in range(2):
                for xs in range(2):
                    add(rb_ref.at[zs, ys, xs, rows], sb_ref.at[zs, ys, xs, co, rows])
            first_copy(part, zs).start()

    def deal_second(part):
        rows = slice(*ROWS_OF[part])
        for zs in range(4):
            first_copy(part, zs).wait_recv()
            for other in range(2):
                to = rb_ref.at[zs, other, x, rows] if zs % 2 == 0 else rb_ref.at[zs, y, other, rows]
                add(to, rx_ref.at[zs, other, rows])
            second_copy(part, zs).start()

    def deal_z(part):
        rows = slice(*ROWS_OF[part])
        for zs in range(4):
            second_copy(part, zs).wait_recv()
            add(rb_ref.at[zs, y, x, rows], ry_ref.at[zs, rows])

            @pl.when(zs != z)
            def _(zs=zs):
                z_copy(part, zs, z).start()

            @pl.when(zs == z)
            def _(zs=zs):
                rz_ref[zs, rows, :] = rb_ref[zs, y, x, rows, :]

    def deal_end(part):
        rows = slice(*ROWS_OF[part])
        for zs in range(4):

            @pl.when(zs != z)
            def _(zs=zs):
                z_copy(part, zs, zs).wait_recv()

        own = rz_ref[0, rows, :].astype(F32)
        for zs in range(1, 4):
            own = own + rz_ref[zs, rows, :].astype(F32)
        own_ref[rows, :] = own

    def deal_sent(part):
        for zs in range(4):
            core_copy(part, zs).wait_send()
            first_copy(part, zs).wait_send()
            second_copy(part, zs).wait_send()

            @pl.when(zs != z)
            def _(zs=zs):
                z_copy(part, zs, z).wait_send()


    pack_block()
    loads[5].wait()
    pack_own(LOW)
    meet_all(me)
    gather_far(LOW)
    gather_near(LOW)
    for copy in strip_copies(0, to_left):
        copy.start()

    @pl.when(to_right != me)
    def _():
        for copy in strip_copies(1, to_right):
            copy.start()

    loads[1].wait()
    loads[17].wait()
    cond_start()
    for n in (11, 14, 8):
        loads[n].wait()
    pack_own(REST)
    pack_own(HIGH_PART)
    gather_far(BIG)
    for n in (2, 20, 23, 0):
        loads[n].wait()
    load_edges()
    gather_z(LOW)
    gather_near(BIG)
    film_start()
    gather_xy(LOW)

    live_all = live_ref[...].astype(F32)
    slot_r = lax.broadcasted_iota(jnp.int32, (5, 5), 0)
    slot_c = lax.broadcasted_iota(jnp.int32, (5, 5), 1)

    def side(s):
        return jnp.where(jnp.logical_or(s == 0, s == 4), 32.0, 64.0)

    def all_sum(v):
        return jnp.sum(jnp.sum(v, axis=0, keepdims=True), axis=1, keepdims=True)

    count = 3.0 * all_sum(live_all * side(slot_r) * side(slot_c))
    my_l, my_r = slots_of(me)
    slot_id = slot_r * 5 + slot_c
    live_l = all_sum(jnp.where(slot_id == my_l, live_all, 0.0))
    live_r = all_sum(jnp.where(slot_id == my_r, live_all, 0.0))

    def zero(i, carry):
        wc_ref[at(i), :] = jnp.zeros((32, 256), BF)
        return carry

    loop(zero, count=48)
    wr_ref[...] = jnp.zeros(wr_ref.shape, BF)
    for cp in range(2):
        for di in range(3):
            wu_ref[cp, di] = jnp.zeros((512, 256), BF)
    for b in range(3):
        wd_ref[b * 512 + 384 : b * 512 + 512, :] = jnp.zeros((128, 256), BF)


    for copy in strip_copies(0, to_left):
        copy.wait()

    @pl.when(to_right != me)
    def _():
        for copy in strip_copies(1, to_right):
            copy.wait()

    @pl.when(to_right == me)
    def _():
        strips_ref[1] = block_ref[0]

    for g in range(4):
        for h in range(2):
            planes_ref[72 * g : 72 * g + 72, 32 * h : 32 * h + 32] = strips_ref[
                h, :, 32 * g : 32 * g + 32
            ]
    row_no = lax.broadcasted_iota(jnp.int32, (512, 288), 0)
    item = jnp.bitwise_and(row_no, 31)
    in_image = item < 12
    item2 = jnp.where(in_image, item, item - 12)
    size = jnp.where(in_image, 6, 3)
    parity = jnp.where(item2 >= size, 1, 0)
    source = (
        jnp.where(in_image, 0, 192)
        + (item2 - parity * size) * 32
        + 2 * lax.shift_right_logical(row_no, 5)
        + parity
    )
    source = jnp.where(item < 18, source, -1)
    pick = jnp.where(source == lax.broadcasted_iota(jnp.int32, (512, 288), 1), 1.0, 0.0)
    by_row = jnp.dot(pick, planes_ref[...], precision=HIGH, preferred_element_type=F32)
    row_no = lax.broadcasted_iota(jnp.int32, (64, 64), 0)
    column = 2 * jnp.bitwise_and(row_no, 31) + lax.shift_right_logical(row_no, 5)
    pick = jnp.where(column == lax.broadcasted_iota(jnp.int32, (64, 64), 1), 1.0, 0.0)
    by_cell = lax.dot_general(
        pick, by_row, (((1,), (1,)), ((), ())), precision=HIGH, preferred_element_type=F32
    )
    lane = lax.broadcasted_iota(jnp.int32, (32, 128), 1)
    none = jnp.zeros((32, 128), F32)
    for i in range(16):
        pair = by_cell[:, i // 4 * 128 : i // 4 * 128 + 128]
        if i % 4:
            pair = pltpu.roll(pair, 128 - 32 * (i % 4), 1)
        even, odd = pair[0:32], pair[32:64]
        v = jnp.where(lane < 12, even, jnp.where(lane < 24, pltpu.roll(odd, 12, 1), 0.0))
        img_ref[32 * i : 32 * i + 32, :] = jnp.concatenate([v, none], axis=1)
        v = jnp.where(
            lane < 6, pltpu.roll(even, 116, 1), jnp.where(lane < 12, pltpu.roll(odd, 122, 1), 0.0)
        )
        tgt_ref[32 * i : 32 * i + 32, :] = jnp.concatenate([v, none], axis=1)


    send(0, edge_cell(img_ref))
    arrive(0)
    put_patch(0, img_ref, recv_ref[0, 0:32, :], 24)
    for cp in range(2):
        full_ref[0, cp] = dot(patch_ref[0], wi_ref[cp])

    def fwd_norm_full(k, source, e):
        stats = stats_of(source, 2)
        send(e, edge_full(source), stats)
        return stats

    def fwd_apply_full(k, source, stats, e):
        arrive(e)
        norm_ready(k, stats, e, 2)

        def body(i, carry):
            put_wide(
                i,
                activated(source[0, at(i), :], k),
                activated(source[1, at(i), :], k),
            )
            return carry

        loop(body)
        put_wide_edge(activated(recv_ref[e, 0:32, :], k))

    for index in range(2):
        h = full_ref.at[2 * index]
        mid = full_ref.at[2 * index + 1]
        out = full_ref.at[2 * index + 2]
        k = 2 * index
        stats = fwd_norm_full(k, h, 1 + k)
        if index:
            load_wc(2)
        else:
            gather_last(LOW)
            gather_core(LOW)
            gather_place(LOW)
            load_wc(0)
            gather_z(BIG)
        fwd_apply_full(k, h, stats, 1 + k)
        keep_wide(k)

        def put_mid(cp, value, mid=mid):
            mid[cp] = value

        conv_low(put_mid)
        if index:
            gather_last(BIG)
        stats = fwd_norm_full(k + 1, mid, 2 + k)
        load_wc(2 * index + 1)
        if not index:
            film_ready()
        fwd_apply_full(k + 1, mid, stats, 2 + k)
        keep_wide(k + 1)

        def put_out(cp, value, h=h, out=out):
            out[cp] = h[cp] + value

        conv_low(put_out)
        if not index:
            gather_xy(BIG)

    skip = full_ref.at[4]
    send(5, edge_full(skip))
    gather_core(BIG)
    gather_place(REST)
    load_down()

    def skip_body(i, carry):
        put_wide(i, skip[0, at(i), :], skip[1, at(i), :])
        return carry

    loop(skip_body)
    arrive(5)
    put_wide_edge(recv_ref[5, 0:32, :])
    keep_wide(4)
    half_ref[0, 0] = dot(wide_ref[32:544, 0:1536], wd_ref[...])

    def fwd_half(k, source, e):
        stats = stats_of(source, 1)
        send(e, edge_cell(source.at[0]), stats)
        arrive(e)
        norm_ready(k, stats, e, 1)

        def body(i, carry):
            put_thin(i, activated(source[0, at(i), :], k))
            return carry

        loop(body)
        put_thin_edge(activated(recv_ref[e, 0:32, :], k))

    fwd_half(4, half_ref.at[0], 6)
    keep_thin(0)
    gather_place(HIGH_PART)
    half_ref[1, 0] = conv_high(0)
    fwd_half(5, half_ref.at[1], 7)
    keep_thin(1)
    half_ref[2, 0] = half_ref[0, 0] + conv_high(1)
    deep = half_ref.at[2]
    send(8, edge_cell(deep.at[0]))
    load_up()

    def deep_body(i, carry):
        put_thin(i, deep[0, at(i), :])
        return carry

    loop(deep_body)
    arrive(8)
    put_thin_edge(recv_ref[8, 0:32, :])
    keep_thin(2)
    merged = full_ref.at[5]
    for cp in range(2):
        total = skip[cp]
        for di in range(3):
            total = total + dot(
                thin_ref[32 * di : 32 * di + 512, cp * 256 : cp * 256 + 512], wu_ref[cp, di]
            )
        merged[cp] = total

    stats = fwd_norm_full(6, merged, 9)
    fwd_apply_full(6, merged, stats, 9)
    keep_wide(5)
    work_ref[0] = jnp.concatenate(
        [dot_nt(wide_ref[32:544, :], wh_ref[...]), jnp.zeros((512, 128), F32)], axis=1
    )

    live = spread(jnp.broadcast_to(jnp.concatenate([live_l, live_r], axis=0), (2, 256)))
    weight = 2.0 / count

    def loss_body(i, carry):
        diff = work_ref[0, at(i), :] - tgt_ref[at(i), :]
        half = live * diff
        work_ref[0, at(i), :] = (half * weight).astype(BF).astype(F32)
        return carry + half * diff

    lost = loop(loss_body, jnp.zeros((32, 256), F32))
    lost = jnp.sum(lost, axis=0, keepdims=True)
    part_ref[...] = jnp.zeros(part_ref.shape, F32)
    part_ref[99:100, :] = lost[:, 0:128] + lost[:, 128:256]
    fgrad_ref[...] = jnp.zeros(fgrad_ref.shape, F32)


    send(10, edge_cell(work_ref.at[0]))
    arrive(10)
    put_patch(1, work_ref.at[0], recv_ref[10, 0:32, :], 12)
    for cp in range(2):
        work_ref[cp] = dot(patch_ref[1], wht_ref[cp])
    stats = norm_back_start(6, merged, 2)
    send(11, edge_full(work_ref), stats)
    turn_ref[0:256, :] = patch_ref[1].T
    for cp in range(2):
        dwh_ref[cp] = dot(turn_ref[0:256, :], act_ref[5, cp])
    arrive(11)
    norm_back_ready(6, stats, 11, 2)

    def head_body(i, carry):
        pair = []
        for p in range(2):
            g = back_value(6, work_ref[p, at(i), :], merged[p, at(i), :])
            grad_ref[p, at(i), :] = g
            pair.append(g)
        put_wide(i, pair[0], pair[1])
        return carry

    loop(head_body)
    put_wide_edge(back_value(6, recv_ref[11, 0:32, :], recv_ref[9, 0:32, :]))

    hgrad = half_ref.at[3]
    hgrad[0] = dot_nt(wide_ref[32:544, :], wut_ref[...])
    send(12, edge_cell(hgrad.at[0]))
    turn_ref[0:256, :] = acth_ref[2].T
    for b in range(3):
        cols = {0: (3, 2), 1: (1, 2), 2: (1, 0)}[b]
        block = dot(turn_ref[0:256, :], wide_ref[32:544, cols[0] * 512 : cols[0] * 512 + 512]) + dot(
            turn_ref[0:256, :], wide_ref[32:544, cols[1] * 512 : cols[1] * 512 + 512]
        )
        for a in range(3):
            one, two = {0: (3, 1), 1: (0, 1), 2: (0, 2)}[a]
            dup_ref[3 * a + b] = (
                block[:, one * 128 : one * 128 + 128] + block[:, two * 128 : two * 128 + 128]
            ).astype(dup_ref.dtype)

    def deep_grad(i, carry):
        put_thin(i, hgrad[0, at(i), :])
        return carry

    loop(deep_grad)
    arrive(12)
    put_thin_edge(recv_ref[12, 0:32, :])
    work_ref[0] = conv_high_back(1)
    stats = norm_back_start(5, half_ref.at[1], 1)
    send(13, edge_cell(work_ref.at[0]), stats)
    grad_high(1, 1)
    arrive(13)
    norm_back_ready(5, stats, 13, 1)

    def mid_grad(i, carry):
        put_thin(i, back_value(5, work_ref[0, at(i), :], half_ref[1, 0, at(i), :]))
        return carry

    loop(mid_grad)
    put_thin_edge(back_value(5, recv_ref[13, 0:32, :], recv_ref[7, 0:32, :]))
    work_ref[0] = conv_high_back(0)
    stats = norm_back_start(4, half_ref.at[0], 1)
    send(14, edge_cell(work_ref.at[0]), stats)
    grad_high(0, 0)
    arrive(14)
    norm_back_ready(4, stats, 14, 1)

    def first_grad(i, carry):
        put_thin(
            i, hgrad[0, at(i), :] + back_value(4, work_ref[0, at(i), :], half_ref[0, 0, at(i), :])
        )
        return carry

    loop(first_grad)
    put_thin_edge(
        recv_ref[12, 0:32, :] + back_value(4, recv_ref[14, 0:32, :], recv_ref[6, 0:32, :])
    )

    for part in (LOW, BIG):
        gather_sent(part)
    deal_core(HIGH_PART)

    for cp in range(2):
        for rp in range(2):
            total = None
            for di in range(1 + rp):
                for dj in range(1 + cp):
                    a = 0 if di else 1 + rp
                    b = 0 if dj else 1 + cp
                    term = dot_nt(
                        thin_ref[32 * (1 + di) : 32 * (1 + di) + 512, (1 + dj) * 256 : (2 + dj) * 256],
                        down_ref[3 * a + b],
                    )
                    total = term if total is None else total + term
            grad_ref[cp, :, rp * 128 : rp * 128 + 128] = (
                grad_ref[cp, :, rp * 128 : rp * 128 + 128] + total
            )
    send(15, edge_full(grad_ref))
    turn_wide(4)
    for cp in range(2):
        for rp in range(2):
            for di in range(1 + rp):
                for dj in range(1 + cp):
                    a = 0 if di else 1 + rp
                    b = 0 if dj else 1 + cp
                    at_row = cp * 256 + rp * 128
                    ddown_ref[3 * a + b] = dot(
                        turn_ref[at_row : at_row + 128, :],
                        thin_ref[32 * (1 + di) : 32 * (1 + di) + 512, (1 + dj) * 256 : (2 + dj) * 256],
                    ).astype(ddown_ref.dtype)

    deal_first(HIGH_PART)
    deal_core(REST)

    def put_work(cp, value):
        work_ref[cp] = value

    edge_grad = None
    for index in (1, 0):
        h = full_ref.at[2 * index]
        mid = full_ref.at[2 * index + 1]
        k = 2 * index
        e = 16 if index else 18
        load_wr(k + 1)
        if index:

            def out_grad(i, carry):
                put_wide(i, grad_ref[0, at(i), :], grad_ref[1, at(i), :])
                return carry

            loop(out_grad)
            arrive(15)
            edge_grad = recv_ref[15, 0:32, :]
            put_wide_edge(edge_grad)
        conv_low(put_work, True)
        stats = norm_back_start(k + 1, mid, 2)
        send(e, edge_full(work_ref), stats)
        grad_low(k + 1, k + 1)
        if index:
            deal_first(REST)
        else:
            deal_z(HIGH_PART)
            deal_second(REST)
        load_wr(k)
        arrive(e)
        norm_back_ready(k + 1, stats, e, 2)

        def mid_body(i, carry, mid=mid, k=k):
            put_wide(
                i,
                back_value(k + 1, work_ref[0, at(i), :], mid[0, at(i), :]),
                back_value(k + 1, work_ref[1, at(i), :], mid[1, at(i), :]),
            )
            return carry

        loop(mid_body)
        put_wide_edge(back_value(k + 1, recv_ref[e, 0:32, :], recv_ref[k + 2, 0:32, :]))
        conv_low(put_work, True)
        stats = norm_back_start(k, h, 2)
        send(e + 1, edge_full(work_ref), stats)
        grad_low(k, k)
        if index:
            deal_second(HIGH_PART)
        else:
            deal_core(LOW)
        arrive(e + 1)
        norm_back_ready(k, stats, e + 1, 2)

        def in_body(i, carry, h=h, k=k):
            pair = []
            for p in range(2):
                g = grad_ref[p, at(i), :] + back_value(k, work_ref[p, at(i), :], h[p, at(i), :])
                grad_ref[p, at(i), :] = g
                pair.append(g)
            put_wide(i, pair[0], pair[1])
            return carry

        loop(in_body)
        edge_grad = edge_grad + back_value(k, recv_ref[e + 1, 0:32, :], recv_ref[k + 1, 0:32, :])
        put_wide_edge(edge_grad)

    deal_first(LOW)
    turn_ref[0:256, :] = patch_ref[0].T
    for cp in range(2):
        dwi_ref[cp] = dot(turn_ref[0:256, :], wide_ref[32:544, 512 + cp * 512 : 768 + cp * 512])

    for a in range(3):
        for b in range(3):
            first, last = None, None
            for cp in range(2):
                for rp in range(2):
                    rho, gamma = rp + a - 1, cp + b - 1
                    cell = (rho // 2 + 1) * 3 + gamma // 2 + 1
                    phase = (gamma % 2) * 2 + rho % 2
                    row = cell * 24 + phase * 6
                    term = dwi_ref[cp, row : row + 6, rp * 128 : rp * 128 + 128]
                    first = term if first is None else first + term
                    row = cell * 12 + phase * 3
                    term = dwh_ref[cp, row : row + 3, rp * 128 : rp * 128 + 128]
                    last = term if last is None else last + term
            t = 3 * a + b
            part_ref[9 * t : 9 * t + 6, :] = first
            part_ref[9 * (8 - t) + 6 : 9 * (8 - t) + 9, :] = last
    for which in range(2):
        for j in range(9):
            row = 81 + 9 * which + j
            part_ref[row : row + 1, :] = ngrad_ref[which : which + 1, 128 * j : 128 * j + 128]


    def message(n, src, dst, d, source):
        return pltpu.make_async_remote_copy(
            src_ref=src,
            dst_ref=dst.at[source],
            send_sem=m_send.at[n, d],
            recv_sem=m_recv.at[n, source],
            device_id=device_no(d),
            device_id_type=MESH,
        )

    def fill(d, carry):
        c = lax.rem(d, 4)
        for n in range(4):
            at_lane = pl.ds(pl.multiple_of(c * 256 + n % 2 * 128, 128), 128)
            m1_ref[d, n : n + 1, :] = fgrad_ref[n // 2 : n // 2 + 1, at_lane]
        m1_ref[d, 4:8, :] = part4_ref[d]

        @pl.when(d != me)
        def _():
            message(0, m1_ref.at[d], r1_ref, d, me).start()

        return carry

    for d in range(32):
        part4_ref[d] = part_ref[4 * d : 4 * d + 4, :]
    lax.fori_loop(0, 32, fill, 0)
    r1_ref[me] = m1_ref[me]

    deal_z(REST)
    deal_second(LOW)
    imgrad_ref[...] = dot_nt(wit_ref[0:32, :], wide_ref[32:544, :])[0:24] * count

    s_r, s_c = strip_of(me)
    home_left = s_r * 4 + s_c
    home_right = s_r * 4 + lax.rem(s_c + 1, 4)

    def back_copy(side, device):
        return pltpu.make_async_remote_copy(
            src_ref=imgrad_ref,
            dst_ref=back_ref.at[1 - side],
            send_sem=back_send.at[side],
            recv_sem=back_recv.at[side],
            device_id=device_no(device),
            device_id_type=MESH,
        )

    back_copy(0, home_left).start()

    @pl.when(home_right != me)
    def _():
        back_copy(1, home_right).start()

    others(lambda d: message(0, m1_ref.at[d], r1_ref, d, d).wait_recv())
    fsum_ref[...] = jnp.zeros(fsum_ref.shape, F32)

    def collect(d, total):
        s_l, s_rt = slots_of(d)
        for n, slot in enumerate((s_l, s_rt)):
            line = jnp.concatenate(
                [r1_ref[d, 2 * n : 2 * n + 1, :], r1_ref[d, 2 * n + 1 : 2 * n + 2, :]], axis=1
            )
            fsum_ref[pl.ds(slot, 1), :] = fsum_ref[pl.ds(slot, 1), :] + line
        return total + r1_ref[d]

    m2_ref[0:4, :] = lax.fori_loop(0, 32, collect, jnp.zeros((8, 128), F32))[4:8]
    film_mine = fsum_ref[...]
    film_w = weights[6][...].astype(BF).astype(F32)
    gc_part = lax.dot_general(
        film_mine, film_w, (((1,), (1,)), ((), ())), precision=HIGH, preferred_element_type=F32
    )
    wide = jnp.concatenate([gc_part, jnp.zeros((32, 64), F32)], axis=1)
    for c in range(4):
        gcs_ref[c] = pltpu.roll(wide, 128 - 16 * c, 1) if c else wide

    def gc_copy(c, source):
        return pltpu.make_async_remote_copy(
            src_ref=gcs_ref.at[c],
            dst_ref=gcr_ref.at[source],
            send_sem=gc_send.at[c],
            recv_sem=gc_recv.at[source],
            device_id={"rows": rr, "cols": c},
            device_id_type=MESH,
        )

    for c in range(4):

        @pl.when(cc != c)
        def _(c=c):
            gc_copy(c, cc).start()

        @pl.when(cc == c)
        def _(c=c):
            gcr_ref[c] = gcs_ref[c]

    grads = [None] * 8
    grads[6] = lax.dot_general(
        condv_ref[...], film_mine, (((0,), (0,)), ((), ())), precision=HIGH, preferred_element_type=F32
    )

    deal_z(LOW)
    deal_end(HIGH_PART)

    for c in range(4):

        @pl.when(cc != c)
        def _(c=c):
            gc_copy(c, c).wait_recv()

    pre = csend_ref[:, 0:16]
    gc = gcr_ref[0] + gcr_ref[1] + gcr_ref[2] + gcr_ref[3]
    gc = gc[:, 0:16] * silu_grad_tanh(pre)
    grads[5] = lax.dot_general(
        gc,
        joined_ref[...],
        (((0,), (0,)), ((), ())),
        precision=HIGH,
        preferred_element_type=F32,
    )

    deal_end(REST)
    deal_end(LOW)
    own = own_ref[...]
    grads[1] = jnp.stack([own[0:144, 32 * j : 32 * j + 32].reshape(9, 16, 32) for j in range(4)])
    grads[2] = jnp.stack([own[288:576, 64 * j : 64 * j + 64].reshape(9, 32, 64) for j in range(2)])
    grads[3] = own[144:288, 0:64].reshape(9, 16, 64)
    grads[4] = jnp.concatenate(
        [own[144:288, 64:96].reshape(9, 16, 32), own[144:288, 96:128].reshape(9, 16, 32)], axis=1
    )

    owned = square_sum(own)
    for n in (5, 6):
        owned = owned + square_sum(grads[n])
    m2_ref[4:8, :] = jnp.broadcast_to(owned, (4, 128))
    others(lambda d: message(1, m2_ref, r2_ref, d, me).start())
    r2_ref[me] = m2_ref[...]
    others(lambda d: message(1, m2_ref, r2_ref, d, d).wait_recv())

    squares = jnp.zeros((4, 128), F32)
    for d in range(32):
        total_ref[4 * d : 4 * d + 4, :] = r2_ref[d, 0:4, :]
        squares = squares + r2_ref[d, 4:8, :]
    shared = square_sum(total_ref[0:LOSS_ROW, :])
    clip = jnp.sqrt(squares[0:1, 0:1] + shared)
    factor = jnp.minimum(1.0, CLIP_AT / clip)
    grads[0] = jnp.stack([total_ref[9 * t : 9 * t + 9, :] for t in range(9)])
    grads[7] = jnp.concatenate(
        [
            jnp.concatenate(
                [total_ref[NORM_ROW + 9 * n + j : NORM_ROW + 9 * n + j + 1, :] for j in range(9)],
                axis=1,
            )
            for n in range(2)
        ],
        axis=0,
    )

    for n in range(3, 26):
        if n % 3 != 2:
            loads[n].wait()
    pairs = []
    spot = 0
    for n in range(8):
        outs[n][...] = grads[n]
        if n in (0, 7):
            continue
        update = lamb_update(
            weights[n][...],
            firsts[n][...],
            seconds[n][...],
            grads[n] * factor.reshape((1,) * grads[n].ndim),
        )[1]
        for j in range(update.shape[0] if n < 3 else 1):
            pairs.append((spot, square_sum(weights[n][j] if n < 3 else weights[n][...])))
            pairs.append((64 + spot, square_sum(update[j] if n < 3 else update)))
            spot += 1

    m3_ref[...] = lane_value(pairs)[0:1]
    others(lambda d: message(2, m3_ref, r3_ref, d, me).start())
    r3_ref[me] = m3_ref[...]

    others(lambda d: message(2, m3_ref, r3_ref, d, d).wait_recv())
    sums = r3_ref[0]
    for d in range(1, 32):
        sums = sums + r3_ref[d]
    scalars_out[0:8, :] = jnp.broadcast_to(sums, (8, 128))
    lost = jnp.sum(total_ref[LOSS_ROW : LOSS_ROW + 1, :], axis=1, keepdims=True)
    for n, v in enumerate((factor, lost, count, clip)):
        scalars_out[8 + n : 9 + n, :] = jnp.broadcast_to(v, (1, 128))
    scalars_out[12:16, :] = jnp.zeros((4, 128), F32)

    back_copy(0, home_left).wait()

    @pl.when(home_right != me)
    def _():
        back_copy(1, home_right).wait()

    @pl.when(home_right == me)
    def _():
        back_ref[0] = imgrad_ref[...]

    back_out[...] = back_ref[...]

    for part in range(3):
        deal_sent(part)
    others(lambda d: film_copy(d, me).wait_send())
    row_mates(lambda c: cond_copy(c, cc).wait_send())
    row_mates(lambda c: gc_copy(c, cc).wait_send())
    for n, src in ((1, m2_ref), (2, m3_ref)):
        others(lambda d, n=n, src=src: message(n, src, r2_ref if n == 1 else r3_ref, d, me).wait_send())
    others(lambda d: message(0, m1_ref.at[d], r1_ref, d, me).wait_send())


def step(*operands):
    far = operands[4:]
    outs = [jax.ShapeDtypeStruct(far[2 + 3 * n].shape, F32) for n in range(8)]
    outs += [jax.ShapeDtypeStruct((16, 128), F32)]
    outs += [jax.ShapeDtypeStruct((2, 24, 512), F32)]
    vmem = pl.BlockSpec(memory_space=pltpu.VMEM)
    dma = pltpu.SemaphoreType.DMA

    def half(*shape):
        return pltpu.VMEM(shape, BF)

    def full(*shape):
        return pltpu.VMEM(shape, F32)

    return pl.pallas_call(
        step_kernel,
        out_shape=tuple(outs),
        in_specs=[vmem] * 4 + [pl.BlockSpec(memory_space=pltpu.HBM)] * 26,
        out_specs=[vmem] * len(outs),
        scratch_shapes=[pltpu.VMEM(a.shape, a.dtype) for a in far]
        + [
            half(4, 9, 128, 128),
            half(2, 9, 256, 256),
            half(9, 128, 256),
            half(9, 256, 128),
            full(6, 2, 512, 256),
            full(4, 1, 512, 256),
            full(2, 512, 256),
            full(2, 512, 256),
            half(576, 2048),
            half(576, 768),
            half(6, 2, 512, 256),
            half(3, 512, 256),
            half(512, 512),
            half(1536, 256),
            half(256, 1536),
            half(2, 3, 512, 256),
            half(256, 2048),
            half(1536, 256),
            full(7, 7, 32, 256),
            full(7, 8, 256),
            half(2, 512, 256),
            full(576, 256),
            full(N_EXCHANGE, 40, 256),
            full(N_EXCHANGE, 40, 256),
            full(512, 256),
            full(512, 256),
            full(2, 256, 256),
            full(2, 256, 256),
            full(2, 1152),
            full(8, 1024),
            full(128, 128),
            full(32, 4, 128),
            full(24, 512),
            half(2, 256, 256),
            half(2, 256, 256),
            half(128, 2048),
            half(128, 2048),
            full(32, 2048),
            half(4, 2, 2, 2, ALL_ROWS, 128),
            full(2, 72, 128),
            full(2, 72, 128),
            full(288, 64),
            full(4, 32, 128),
            full(32, 128),
            full(32, 256),
            full(32, 4, 128),
            full(32, 4, 128),
            full(8, 1024),
            full(32, 4224),
            full(32, 64),
            half(4, 2, 2, ALL_ROWS, 128),
            half(4, 2, ALL_ROWS, 128),
            half(4, ALL_ROWS, 128),
            half(4, ALL_ROWS, 128),
            full(ALL_ROWS, 128),
            full(32, 8, 128),
            full(32, 8, 128),
            full(8, 128),
            full(32, 8, 128),
            full(1, 128),
            full(32, 1, 128),
            full(4, 32, 128),
            full(4, 32, 128),
            full(32, 256),
            full(128, 128),
            full(2, 24, 512),
            dma((N_EXCHANGE,)),
            dma((N_EXCHANGE,)),
            dma((26,)),
            dma((2, 7, 4, 2, 2)),
            dma((2, 4, 2, 2, 2)),
            dma((2,)),
            dma((2,)),
            dma((4,)),
            dma((4,)),
            dma((32,)),
            dma((32,)),
            dma((3, 4)),
            dma((3, 4)),
            dma((3, 4)),
            dma((3, 4)),
            dma((3, 4)),
            dma((3, 4)),
            dma((3, 4)),
            dma((3, 4)),
            dma((3, 32)),
            dma((3, 32)),
            dma((4,)),
            dma((4,)),
            dma((2,)),
            dma((2,)),
        ],
        compiler_params=pltpu.CompilerParams(
            collective_id=1, has_side_effects=True, vmem_limit_bytes=62 * 1024 * 1024
        ),
        name="step",
    )(*operands)


def per_device_strips(
    image_pair,
    noise_target,
    timesteps,
    text_pooled,
    slot_live,
    *params,
):
    lanes = jnp.asarray(lane_tables(), BF)

    def view(n, a):
        return jnp.swapaxes(a, 1, 2) if n == 0 else a.T if n == 5 else a

    def planes(a):
        return jnp.transpose(a[0], (2, 0, 1))

    state = [view(n // 3, a) for n, a in enumerate(params)]
    *grads, scalars, back = step(
        slot_live[0],
        time_embed(timesteps)[0].astype(BF),
        planes(image_pair),
        planes(noise_target),
        lanes,
        text_pooled[0],
        *state,
    )
    results = last(scalars, back, grads, state)
    new = [view(n // 3, a) for n, a in enumerate(results[:24])]
    loss, count, clip = (a.reshape(()) for a in results[24:27])
    return tuple(new) + (loss, count, clip, jnp.transpose(results[27], (1, 2, 0))[None])


def solution(mesh):
    strips = mesh.shape["rows"] == 8 and mesh.shape["cols"] == 4
    placed = (
        P(None, "rows", "cols", None),
        P(None, "rows", "cols", None),
        P(),
        P(),
        P(),
        P(),
        P(),
        P(),
        P(None, None, "rows", "cols"),
        P(None, None, "rows", "cols"),
        P(None, None, "rows", "cols"),
        P(None, None, "rows", "cols"),
        P(None, None, "rows", "cols"),
        P(None, None, "rows", "cols"),
        P(None, "rows", "cols"),
        P(None, "rows", "cols"),
        P(None, "rows", "cols"),
        P(None, "rows", "cols"),
        P(None, "rows", "cols"),
        P(None, "rows", "cols"),
        P(None, ("rows", "cols")),
        P(None, ("rows", "cols")),
        P(None, ("rows", "cols")),
        P("rows", "cols"),
        P("rows", "cols"),
        P("rows", "cols"),
        P(),
        P(),
        P(),
    )
    return jax.shard_map(
        per_device_strips if strips else per_device,
        mesh=mesh,
        in_specs=placed,
        out_specs=(
            P(),
            P(),
            P(),
            P(None, None, "rows", "cols"),
            P(None, None, "rows", "cols"),
            P(None, None, "rows", "cols"),
            P(None, None, "rows", "cols"),
            P(None, None, "rows", "cols"),
            P(None, None, "rows", "cols"),
            P(None, "rows", "cols"),
            P(None, "rows", "cols"),
            P(None, "rows", "cols"),
            P(None, "rows", "cols"),
            P(None, "rows", "cols"),
            P(None, "rows", "cols"),
            P(None, ("rows", "cols")),
            P(None, ("rows", "cols")),
            P(None, ("rows", "cols")),
            P("rows", "cols"),
            P("rows", "cols"),
            P("rows", "cols"),
            P(),
            P(),
            P(),
            P(),
            P(),
            P(),
            P(None, "rows", "cols", None),
        ),
        check_vma=False,
    )
```

```python
import math

import jax
import jax.numpy as jnp
import numpy as np
from jax import lax
from jax.experimental import pallas as pl
from jax.experimental.pallas import tpu as pltpu
from jax.sharding import PartitionSpec as P

SLOT = 64
SLOTS = 5
C1 = 128
C2 = 256
GROUPS = 32
TEMB = 128
STEP = 10


HIGH = lax.Precision.HIGHEST
EPS_NORM = 1e-05
CLIP_AT = 0.05
RATE = 0.5
BETA_ONE = 0.9
BETA_TWO = 0.999
EPS_ADAM = 1e-06
DECAY = 0.01


def entering(part, axis, combine, identity, reverse):
    count = lax.axis_size(axis)
    place = lax.axis_index(axis)
    ahead = count - 1 - place if reverse else place
    gathered = jax.tree.map(lambda a: lax.all_gather(a, axis), part)
    state = jax.tree.map(lambda a, e: jnp.zeros_like(a) + jnp.asarray(e, a.dtype), part, identity)

    def one(turn, state):
        source = count - 1 - turn if reverse else turn
        return combine(
            state, jax.tree.map(lambda a: lax.dynamic_index_in_dim(a, source, 0, False), gathered)
        )

    return lax.fori_loop(0, ahead, one, state)


def padded_2(block, sides, width):
    for axis, dim in sides:
        count = lax.axis_size(axis)
        forward = [(i, i + 1) for i in range(count - 1)]
        backward = [(target, source) for source, target in forward]
        low = lax.ppermute(
            lax.slice_in_dim(block, block.shape[dim] - width, None, axis=dim), axis, forward
        )
        high = lax.ppermute(lax.slice_in_dim(block, 0, width, axis=dim), axis, backward)
        block = jnp.concatenate([low, block, high], axis=dim)
    return block


def time_embed(steps):
    half = TEMB // 2
    freq = jnp.exp(-math.log(10000.0) * jnp.arange(half, dtype=jnp.float32) / half)
    angle = steps.astype(jnp.float32)[..., None] * freq
    return jnp.concatenate([jnp.sin(angle), jnp.cos(angle)], axis=-1)


def silu_grad(values):
    sigma = jax.nn.sigmoid(values)
    return sigma * (1.0 + values * (1.0 - sigma))


def tap_masks(rows, cols, slot):
    half = slot // 2
    row_pos = lax.axis_index("rows") * rows + jnp.arange(rows)
    col_pos = lax.axis_index("cols") * cols + jnp.arange(cols)
    row_ok = [
        (row_pos + offset + half) // slot == (row_pos + half) // slot for offset in (-1, 0, 1)
    ]
    col_ok = [
        (col_pos + offset + half) // slot == (col_pos + half) // slot for offset in (-1, 0, 1)
    ]
    return [
        (row_ok[tap // 3][:, None] & col_ok[tap % 3][None, :]).astype(jnp.bfloat16)
        for tap in range(9)
    ]


def slot_level(rows, cols, slot, size):
    half = slot // 2
    labels = jnp.arange(SLOTS)
    row_pos = lax.axis_index("rows") * rows + jnp.arange(rows)
    col_pos = lax.axis_index("cols") * cols + jnp.arange(cols)
    row_map = (((row_pos + half) // slot)[:, None] == labels[None, :]).astype(jnp.float32)
    col_map = (((col_pos + half) // slot)[:, None] == labels[None, :]).astype(jnp.float32)
    every = (jnp.arange(size) + half) // slot
    side = jnp.sum((every[:, None] == labels[None, :]).astype(jnp.float32), axis=0)
    return (row_map, col_map, side[:, None] * side[None, :])


def to_slots(values, level):
    return jnp.einsum("nhwk,ha,wb->nabk", values, level[0], level[1], precision=HIGH)


def to_pixels(table, level):
    return jnp.einsum("nabk,ha,wb->nhwk", table, level[0], level[1], precision=HIGH)


def add_pair(earlier, later):
    return (earlier[0] + later[0], earlier[1] + later[1])


def slot_total(tables):
    empty = (jnp.zeros_like(tables[0]), jnp.zeros_like(tables[1]))
    before = entering(tables, ("rows", "cols"), add_pair, empty, False)
    after = entering(tables, ("rows", "cols"), add_pair, empty, True)
    return (before[0] + tables[0] + after[0], before[1] + tables[1] + after[1])


def pad_rim(values):
    return padded_2(values, (("rows", 1), ("cols", 2)), 1)


def tap_patch(padded, masks, tap, stride):
    rows = padded.shape[1] - 2
    cols = padded.shape[2] - 2
    row_off, col_off = (tap // 3, tap % 3)
    patch = padded[:, row_off : row_off + rows : stride, col_off : col_off + cols : stride, :]
    return patch * masks[tap][::stride, ::stride][None, :, :, None]


def conv_taps(padded, weight, masks, stride):
    total = None
    for tap in range(9):
        term = jnp.einsum(
            "nhwc,cd->nhwd",
            tap_patch(padded, masks, tap, stride),
            weight[tap],
            preferred_element_type=jnp.float32,
        )
        total = term if total is None else total + term
    return total


def conv_weight_grad(padded, grad_out, masks, stride):
    return jnp.stack(
        [
            jnp.einsum(
                "nhwc,nhwd->cd",
                tap_patch(padded, masks, tap, stride),
                grad_out,
                preferred_element_type=jnp.float32,
            )
            for tap in range(9)
        ]
    )


def conv_input_grad(grad_out, weight, masks, stride):
    spread = grad_out
    if stride == 2:
        canvases, rows, cols, width = grad_out.shape
        spread = jnp.stack([grad_out, jnp.zeros_like(grad_out)], axis=2).reshape(
            canvases, 2 * rows, cols, width
        )
        spread = jnp.stack([spread, jnp.zeros_like(spread)], axis=3).reshape(
            canvases, 2 * rows, 2 * cols, width
        )
    flipped = jnp.swapaxes(weight[::-1], 1, 2)
    padded = padded_2(spread, (("rows", 1), ("cols", 2)), 1)
    return conv_taps(padded, flipped, masks, 1)


def norm_forward(values, gain, bias, scale, shift, level):
    count_n, rows, cols, width = values.shape
    grouped = values.reshape(count_n, rows, cols, GROUPS, width // GROUPS)
    total, squares = slot_total(
        (
            to_slots(jnp.sum(grouped, axis=4), level),
            to_slots(jnp.sum(grouped * grouped, axis=4), level),
        )
    )
    count = level[2][None, :, :, None] * (width // GROUPS)
    mean = total / count
    var = squares / count - mean * mean
    inverse = lax.rsqrt(var + EPS_NORM)
    mean_pix = to_pixels(mean, level)
    inv_pix = to_pixels(inverse, level)
    hat = ((grouped - mean_pix[..., None]) * inv_pix[..., None]).reshape(values.shape)
    normed = hat * gain + bias
    if scale is None:
        return (normed, (hat, inv_pix, normed, None))
    factor = 1.0 + to_pixels(scale, level)
    return (normed * factor + to_pixels(shift, level), (hat, inv_pix, normed, factor))


def norm_backward(grad_out, kept, gain, level):
    hat, inv_pix, normed, factor = kept
    count_n, rows, cols, width = hat.shape
    if factor is None:
        film_grad = None
        grad_normed = grad_out
    else:
        film_grad = jnp.concatenate(
            [to_slots(grad_out * normed, level), to_slots(grad_out, level)], axis=-1
        )
        grad_normed = grad_out * factor
    grad_gain = jnp.sum(grad_normed * hat, axis=(0, 1, 2))
    grad_bias = jnp.sum(grad_normed, axis=(0, 1, 2))
    shape = (count_n, rows, cols, GROUPS, width // GROUPS)
    grad_hat = (grad_normed * gain).reshape(shape)
    grouped_hat = hat.reshape(shape)
    first, second = slot_total(
        (
            to_slots(jnp.sum(grad_hat, axis=4), level),
            to_slots(jnp.sum(grad_hat * grouped_hat, axis=4), level),
        )
    )
    count = level[2][None, :, :, None] * (width // GROUPS)
    mean_one = to_pixels(first / count, level)[..., None]
    mean_two = to_pixels(second / count, level)[..., None]
    grad_in = inv_pix[..., None] * (grad_hat - mean_one - grouped_hat * mean_two)
    return (grad_in.reshape(hat.shape), grad_gain, grad_bias, film_grad)


def block_forward(hidden, weights, gains, film, level, masks):
    pre_one, saved_one = norm_forward(hidden, gains[0], gains[1], None, None, level)
    rim_one = pad_rim(jax.nn.silu(pre_one).astype(jnp.bfloat16))
    conv_one = conv_taps(rim_one, weights[0], masks, 1)
    pre_two, saved_two = norm_forward(conv_one, gains[2], gains[3], film[0], film[1], level)
    rim_two = pad_rim(jax.nn.silu(pre_two).astype(jnp.bfloat16))
    out = hidden + conv_taps(rim_two, weights[1], masks, 1)
    return (out, (pre_one, saved_one, rim_one, pre_two, saved_two, rim_two))


def block_backward(grad_out, weights, gains, kept, level, masks):
    pre_one, saved_one, rim_one, pre_two, saved_two, rim_two = kept
    grad_two = grad_out.astype(jnp.bfloat16)
    weight_two = conv_weight_grad(rim_two, grad_two, masks, 1)
    grad_pre_two = conv_input_grad(grad_two, weights[1], masks, 1) * silu_grad(pre_two)
    grad_conv, gain_two, bias_two, film_grad = norm_backward(
        grad_pre_two, saved_two, gains[2], level
    )
    grad_one = grad_conv.astype(jnp.bfloat16)
    weight_one = conv_weight_grad(rim_one, grad_one, masks, 1)
    grad_pre_one = conv_input_grad(grad_one, weights[0], masks, 1) * silu_grad(pre_one)
    grad_in, gain_one, bias_one, _ = norm_backward(grad_pre_one, saved_one, gains[0], level)
    return (
        grad_out + grad_in,
        (weight_one, weight_two),
        (gain_one, bias_one, gain_two, bias_two),
        film_grad,
    )


def per_device(
    image_pair,
    noise_target,
    timesteps,
    text_pooled,
    slot_live,
    edgeconv_weight,
    edgeconv_first,
    edgeconv_second,
    convlow_weight,
    convlow_first,
    convlow_second,
    convhigh_weight,
    convhigh_first,
    convhigh_second,
    downconv_weight,
    downconv_first,
    downconv_second,
    upconv_weight,
    upconv_first,
    upconv_second,
    condproj_weight,
    condproj_first,
    condproj_second,
    filmproj_weight,
    filmproj_first,
    filmproj_second,
    normparams_weight,
    normparams_first,
    normparams_second,
):
    canvases, rows_one, cols_one = image_pair.shape[:3]
    size_full = rows_one * lax.axis_size("rows")
    level_full = slot_level(rows_one, cols_one, SLOT, size_full)
    level_half = slot_level(rows_one // 2, cols_one // 2, SLOT // 2, size_full // 2)
    by_rows = (
        lax.all_gather(convlow_weight.astype(jnp.bfloat16), "rows", axis=2, tiled=True),
        lax.all_gather(convhigh_weight.astype(jnp.bfloat16), "rows", axis=2, tiled=True),
        lax.all_gather(downconv_weight.astype(jnp.bfloat16), "rows", axis=1, tiled=True),
        lax.all_gather(upconv_weight.astype(jnp.bfloat16), "rows", axis=1, tiled=True),
        lax.all_gather(filmproj_weight.astype(jnp.bfloat16), "rows", axis=0, tiled=True),
    )
    low_convs, high_convs, down_conv, up_conv, film_full = (
        lax.all_gather(by_rows[0], "cols", axis=3, tiled=True),
        lax.all_gather(by_rows[1], "cols", axis=3, tiled=True),
        lax.all_gather(by_rows[2], "cols", axis=2, tiled=True),
        lax.all_gather(by_rows[3], "cols", axis=2, tiled=True),
        lax.all_gather(by_rows[4], "cols", axis=1, tiled=True),
    )
    joined = jnp.concatenate([time_embed(timesteps).astype(jnp.bfloat16), text_pooled], axis=-1)
    cond_full = lax.all_gather(
        condproj_weight.astype(jnp.bfloat16), ("rows", "cols"), axis=1, tiled=True
    )
    pre_cond = jnp.einsum("nabk,kf->nabf", joined, cond_full, preferred_element_type=jnp.float32)
    cond_low = jax.nn.silu(pre_cond).astype(jnp.bfloat16)
    film_all = jnp.einsum("nabk,kf->nabf", cond_low, film_full, preferred_element_type=jnp.float32)
    offsets = [0, C1, 2 * C1, 3 * C1, 4 * C1, 4 * C1 + C2, 4 * C1 + 2 * C2, 5 * C1 + 2 * C2]

    def norm_part(index, which):
        return normparams_weight[which, offsets[index] : offsets[index + 1]]

    def block_gains(index):
        return (
            norm_part(2 * index, 0),
            norm_part(2 * index, 1),
            norm_part(2 * index + 1, 0),
            norm_part(2 * index + 1, 1),
        )

    def block_film(index):
        base = (0, 2 * C1, 4 * C1)[index]
        width = (C1, C1, C2)[index]
        return (film_all[..., base : base + width], film_all[..., base + width : base + 2 * width])

    masks_one = tap_masks(rows_one, cols_one, SLOT)
    masks_two = tap_masks(rows_one // 2, cols_one // 2, SLOT // 2)
    edge_low = edgeconv_weight.astype(jnp.bfloat16)
    inconv_low = jnp.swapaxes(edge_low[:, :, 0:6], 1, 2)
    head_low = edge_low[:, :, 6:9]
    rim_in = pad_rim(image_pair)
    hidden = conv_taps(rim_in, inconv_low, masks_one, 1)
    kept_blocks = []
    for index in range(2):
        hidden, kept = block_forward(
            hidden,
            (low_convs[2 * index], low_convs[2 * index + 1]),
            block_gains(index),
            block_film(index),
            level_full,
            masks_one,
        )
        kept_blocks.append(kept)
    rim_skip = pad_rim(hidden.astype(jnp.bfloat16))
    deep, kept_deep = block_forward(
        conv_taps(rim_skip, down_conv, masks_one, 2),
        (high_convs[0], high_convs[1]),
        block_gains(2),
        block_film(2),
        level_half,
        masks_two,
    )
    upsampled = jnp.repeat(jnp.repeat(deep.astype(jnp.bfloat16), 2, axis=1), 2, axis=2)
    rim_up = pad_rim(upsampled)
    merged = conv_taps(rim_up, up_conv, masks_one, 1) + hidden
    pre_head, kept_head = norm_forward(
        merged, norm_part(6, 0), norm_part(6, 1), None, None, level_full
    )
    rim_head = pad_rim(jax.nn.silu(pre_head).astype(jnp.bfloat16))
    pred = conv_taps(rim_head, head_low, masks_one, 1)
    live_slots = slot_live.astype(jnp.float32)
    live = to_pixels(live_slots[..., None], level_full)
    count = 3.0 * jnp.sum(live_slots * level_full[2][None, :, :])
    diff = pred - noise_target
    loss_local = jnp.sum(live * diff * diff)
    grad_pred = (2.0 * live * diff / count).astype(jnp.bfloat16)
    grad_head = conv_weight_grad(rim_head, grad_pred, masks_one, 1)
    grad_act = conv_input_grad(grad_pred, head_low, masks_one, 1) * silu_grad(pre_head)
    grad_merged, head_gain, head_bias, _ = norm_backward(
        grad_act, kept_head, norm_part(6, 0), level_full
    )
    merged_low = grad_merged.astype(jnp.bfloat16)
    grad_upconv = conv_weight_grad(rim_up, merged_low, masks_one, 1)
    grad_up = conv_input_grad(merged_low, up_conv, masks_one, 1)
    grad_deep = grad_up.reshape(canvases, rows_one // 2, 2, cols_one // 2, 2, C2).sum(axis=(2, 4))
    grad_down, deep_convs, deep_norms, deep_film = block_backward(
        grad_deep, (high_convs[0], high_convs[1]), block_gains(2), kept_deep, level_half, masks_two
    )
    down_low = grad_down.astype(jnp.bfloat16)
    grad_downconv = conv_weight_grad(rim_skip, down_low, masks_one, 2)
    grad_hidden = grad_merged + conv_input_grad(down_low, down_conv, masks_one, 2)
    block_convs = [None, None]
    block_norms = [None, None]
    block_films = [None, None]
    for index in (1, 0):
        grad_hidden, block_convs[index], block_norms[index], block_films[index] = block_backward(
            grad_hidden,
            (low_convs[2 * index], low_convs[2 * index + 1]),
            block_gains(index),
            kept_blocks[index],
            level_full,
            masks_one,
        )
    hidden_low = grad_hidden.astype(jnp.bfloat16)
    grad_inconv = conv_weight_grad(rim_in, hidden_low, masks_one, 1)
    image_grad = conv_input_grad(hidden_low, inconv_low, masks_one, 1) * count
    all_norms = block_norms + [deep_norms]
    gain_vector = jnp.concatenate([part[k] for part in all_norms for k in (0, 2)] + [head_gain])
    bias_vector = jnp.concatenate([part[k] for part in all_norms for k in (1, 3)] + [head_bias])
    film_grads = jnp.concatenate([block_films[0], block_films[1], deep_film], axis=-1)
    edge_local = jnp.concatenate([jnp.swapaxes(grad_inconv, 1, 2), grad_head], axis=2)
    film_sum, edge_sum, norm_sum, loss_sum = lax.psum(
        (film_grads, edge_local, jnp.stack([gain_vector, bias_vector]), loss_local),
        ("rows", "cols"),
    )
    grad_film_full = jnp.einsum(
        "nabk,nabf->kf", cond_low.astype(jnp.float32), film_sum, precision=HIGH
    )
    grad_cond = jnp.einsum(
        "nabf,kf->nabk", film_sum, film_full.astype(jnp.float32), precision=HIGH
    ) * silu_grad(pre_cond)
    grad_cond_full = jnp.einsum(
        "nabk,nabf->kf", joined.astype(jnp.float32), grad_cond, precision=HIGH
    )
    film_rows, film_cols = filmproj_weight.shape
    film_own = lax.dynamic_slice_in_dim(
        grad_film_full, lax.axis_index("rows") * film_rows, film_rows, 0
    )
    film_own = lax.dynamic_slice_in_dim(film_own, lax.axis_index("cols") * film_cols, film_cols, 1)
    cond_cols = condproj_weight.shape[1]
    cond_own = lax.dynamic_slice_in_dim(
        grad_cond_full, lax.axis_index(("rows", "cols")) * cond_cols, cond_cols, 1
    )
    by_cols = (
        lax.psum_scatter(
            jnp.stack(
                [block_convs[0][0], block_convs[0][1], block_convs[1][0], block_convs[1][1]]
            ).astype(jnp.bfloat16),
            "cols",
            scatter_dimension=3,
            tiled=True,
        ).astype(jnp.float32),
        lax.psum_scatter(
            jnp.stack([deep_convs[0], deep_convs[1]]).astype(jnp.bfloat16),
            "cols",
            scatter_dimension=3,
            tiled=True,
        ).astype(jnp.float32),
        lax.psum_scatter(
            grad_downconv.astype(jnp.bfloat16), "cols", scatter_dimension=2, tiled=True
        ).astype(jnp.float32),
        lax.psum_scatter(
            grad_upconv.astype(jnp.bfloat16), "cols", scatter_dimension=2, tiled=True
        ).astype(jnp.float32),
    )
    lowconv_own, highconv_own, downconv_own, upconv_own = (
        lax.psum_scatter(
            by_cols[0].astype(jnp.bfloat16), "rows", scatter_dimension=2, tiled=True
        ).astype(jnp.float32),
        lax.psum_scatter(
            by_cols[1].astype(jnp.bfloat16), "rows", scatter_dimension=2, tiled=True
        ).astype(jnp.float32),
        lax.psum_scatter(
            by_cols[2].astype(jnp.bfloat16), "rows", scatter_dimension=1, tiled=True
        ).astype(jnp.float32),
        lax.psum_scatter(
            by_cols[3].astype(jnp.bfloat16), "rows", scatter_dimension=1, tiled=True
        ).astype(jnp.float32),
    )
    weights = (
        edgeconv_weight,
        convlow_weight,
        convhigh_weight,
        downconv_weight,
        upconv_weight,
        condproj_weight,
        filmproj_weight,
        normparams_weight,
    )
    firsts = (
        edgeconv_first,
        convlow_first,
        convhigh_first,
        downconv_first,
        upconv_first,
        condproj_first,
        filmproj_first,
        normparams_first,
    )
    seconds = (
        edgeconv_second,
        convlow_second,
        convhigh_second,
        downconv_second,
        upconv_second,
        condproj_second,
        filmproj_second,
        normparams_second,
    )
    grads = (
        edge_sum,
        lowconv_own,
        highconv_own,
        downconv_own,
        upconv_own,
        cond_own,
        film_own,
        norm_sum,
    )
    sharded = (1, 2, 3, 4, 5, 6)
    stacked = (1, 2)
    owned_sq = sum((jnp.sum(grads[k] * grads[k]) for k in sharded))
    shared_sq = sum((jnp.sum(grads[k] * grads[k]) for k in range(8) if k not in sharded))
    clip_norm = jnp.sqrt(lax.psum(owned_sq, ("rows", "cols")) + shared_sq)
    factor = jnp.minimum(1.0, CLIP_AT / clip_norm)
    clipped, moments, updates = ([], [], [])
    for k in range(8):
        grad = grads[k] * factor
        first_new = BETA_ONE * firsts[k] + (1.0 - BETA_ONE) * grad
        second_new = BETA_TWO * seconds[k] + (1.0 - BETA_TWO) * grad * grad
        first_hat = first_new / (1.0 - BETA_ONE**STEP)
        second_hat = second_new / (1.0 - BETA_TWO**STEP)
        clipped.append(grad)
        moments.append(second_new)
        updates.append(first_hat / (jnp.sqrt(second_hat) + EPS_ADAM) + DECAY * weights[k])

    def matrix_squares(values, k):
        if k in stacked:
            return jnp.sum(values * values, axis=tuple(range(1, values.ndim)))
        return jnp.sum(values * values).reshape(1)

    weight_sq, update_sq = lax.psum(
        (
            jnp.concatenate([matrix_squares(weights[k], k) for k in sharded]),
            jnp.concatenate([matrix_squares(updates[k], k) for k in sharded]),
        ),
        ("rows", "cols"),
    )
    ratios = jnp.sqrt(weight_sq) / jnp.sqrt(update_sq)
    position = 0
    results = []
    for k in range(8):
        if k in sharded:
            span = weights[k].shape[0] if k in stacked else 1
            ratio = ratios[position : position + span]
            position += span
            ratio = (
                ratio.reshape((span,) + (1,) * (weights[k].ndim - 1)) if k in stacked else ratio[0]
            )
        elif k == 0:
            part = (jnp.arange(9) < 6)[None, None, :]
            other = jnp.logical_not(part)
            weight_sq_two = weights[k] * weights[k]
            update_sq_two = updates[k] * updates[k]
            ratio_in = jnp.sqrt(jnp.sum(jnp.where(part, weight_sq_two, 0.0))) / jnp.sqrt(
                jnp.sum(jnp.where(part, update_sq_two, 0.0))
            )
            ratio_out = jnp.sqrt(jnp.sum(jnp.where(other, weight_sq_two, 0.0))) / jnp.sqrt(
                jnp.sum(jnp.where(other, update_sq_two, 0.0))
            )
            ratio = jnp.where(part, ratio_in, ratio_out)
        else:
            ratio = jnp.sqrt(jnp.sum(weights[k] * weights[k])) / jnp.sqrt(
                jnp.sum(updates[k] * updates[k])
            )
        results.extend([clipped[k], moments[k], weights[k] - RATE * ratio * updates[k]])
    return (
        results[0],
        results[1],
        results[2],
        results[3],
        results[4],
        results[5],
        results[6],
        results[7],
        results[8],
        results[9],
        results[10],
        results[11],
        results[12],
        results[13],
        results[14],
        results[15],
        results[16],
        results[17],
        results[18],
        results[19],
        results[20],
        results[21],
        results[22],
        results[23],
        loss_sum,
        count,
        clip_norm,
        image_grad,
    )


F32 = jnp.float32
BF = jnp.bfloat16
MESH = pl.DeviceIdType.MESH
NORM_AT = (0, 128, 256, 384, 512, 768, 1024, 1152)
FILM_AT = {1: 0, 3: 256, 5: 512}
ROW_OF = (0, 1, -1, 2)
COL_OF = (-1, 0, 1, 2)
N_EXCHANGE = 20


def place_of():
    rr, cc = lax.axis_index("rows"), lax.axis_index("cols")
    return rr, cc, rr // 2, lax.rem(rr, 2), cc // 2, lax.rem(cc, 2)


def device_at(z, y, x, k):
    return {"rows": z * 2 + y, "cols": x * 2 + k}


def device_no(d):
    return {"rows": d // 4, "cols": lax.rem(d, 4)}


def meet_all(me, count=32):
    barrier = pltpu.get_barrier_semaphore()

    def hello(d, carry):
        @pl.when(d != me)
        def _():
            pl.semaphore_signal(barrier, inc=1, device_id=device_no(d), device_id_type=MESH)

        return carry

    lax.fori_loop(0, count, hello, 0)
    pl.semaphore_wait(barrier, count - 1)


def strip_at(r, c):
    pair = lax.rem((r + 1) // 2, 4)
    return (pair * 2 + c // 2) * 4 + lax.rem(c, 2) * 2 + lax.rem(r + 1, 2)


def strip_of(d):
    rr, cc = d // 4, lax.rem(d, 4)
    pair, core = rr // 2, lax.rem(cc, 2)
    r = jnp.where(pair == 0, 7 * (1 - core), 2 * pair - 1 + core)
    return r, lax.rem(rr, 2) * 2 + cc // 2


def slots_of(d):
    r, c = strip_of(d)
    row = (r + 1) // 2
    return row * 5 + c + 1, row * 5 + lax.rem(c + 1, 4)


def lane_tables():
    low = np.zeros((512, 512), np.float32)
    high = np.zeros((512, 512), np.float32)
    rest = np.zeros((512, 512), np.float32)
    for lane in range(512):
        c, q = lane // 128, lane % 128
        low[lane, (q // 32) * 128 + c * 32 + q % 32] = 1.0
        high[lane, (q // 64) * 256 + c * 64 + q % 64] = 1.0
        to = c * 64 + q if q < 64 else (256 if q < 96 else 384) + c * 32 + q % 32
        rest[lane, to] = 1.0
    return np.stack([low, rest, high])


def place_lanes(x, at, width=128):
    n = x.shape[1]
    one = (
        lax.broadcasted_iota(jnp.int32, (n, width), 0) + at
        == lax.broadcasted_iota(jnp.int32, (n, width), 1)
    )
    return jnp.dot(x, jnp.where(one, 1.0, 0.0).astype(x.dtype), preferred_element_type=F32)


ALL_ROWS = 576
LOW, REST, HIGH_PART = range(3)
ROWS_OF = ((0, 144), (144, 288), (288, 576))
BIG = 1
GATHER_ROWS = ((0, 144), (144, 576))
Z_ORDER = (0, 1, -1, 2, -2, 3, -3)


NORM_ROW = 81
LOSS_ROW = 99


def lane_value(pairs):
    lane = lax.broadcasted_iota(jnp.int32, (8, 128), 1)
    total = jnp.zeros((8, 128), F32)
    for at, value in pairs:
        total = total + jnp.where(lane == at, value, 0.0)
    return total


def square_sum(x):
    x = x * x
    while x.ndim > 2:
        x = jnp.sum(x, axis=0)
    return jnp.sum(jnp.sum(x, axis=0, keepdims=True), axis=1, keepdims=True)


def silu_grad_tanh(v):
    s = 0.5 * jnp.tanh(0.5 * v) + 0.5
    return s * (1.0 + v * (1.0 - s))


def lamb_update(weight, first, second, grad):
    first_new = BETA_ONE * first + (1.0 - BETA_ONE) * grad
    second_new = BETA_TWO * second + (1.0 - BETA_TWO) * grad * grad
    first_hat = first_new / (1.0 - BETA_ONE**STEP)
    second_hat = second_new / (1.0 - BETA_TWO**STEP)
    return second_new, first_hat / (jnp.sqrt(second_hat) + EPS_ADAM) + DECAY * weight


LAST_ORDER = (5, 1, 2, 4, 3, 6, 0, 7)


def last_kernel(*refs):
    scalars_ref, back_ref = refs[:2]
    far, outs, (loss_out, count_out, clip_out, image_out) = refs[2:34], refs[34:58], refs[58:62]
    near, made = refs[62:94], refs[94:118]
    pixel_ref, load_sem, store_sem = refs[118:]

    def load(n, kind):
        at = 4 * n + kind
        return pltpu.make_async_copy(far[at], near[at], load_sem.at[at])

    for n in LAST_ORDER:
        for kind in range(4):
            load(n, kind).start()

    column = lax.broadcasted_iota(jnp.int32, (64, 128), 1)
    row_no = lax.broadcasted_iota(jnp.int32, (64, 128), 0)
    pixel = jnp.bitwise_and(column, 63)
    pick = jnp.where(pixel == 2 * (row_no - 16) + lax.shift_right_logical(column, 6), 1.0, 0.0)
    for i in range(16):
        for side in range(2):
            pixel_ref[24 * i : 24 * i + 24, 32 * side : 32 * side + 32] = back_ref[
                side, :, 32 * i : 32 * i + 32
            ]
    wide = jnp.dot(pixel_ref[...], pick, precision=HIGH, preferred_element_type=F32)
    row_no = lax.broadcasted_iota(jnp.int32, (192, 384), 0)
    h = jnp.bitwise_and(row_no, 31)
    source = (
        lax.shift_right_logical(h, 1) * 24
        + jnp.bitwise_and(h, 1) * 6
        + lax.shift_right_logical(row_no, 5)
    )
    at_row = lax.broadcasted_iota(jnp.int32, (192, 384), 1)
    total = None
    for cp in range(2):
        pick = jnp.where(at_row == source + 12 * cp, 1.0, 0.0)
        term = jnp.dot(
            pick, wide[:, 64 * cp : 64 * cp + 64], precision=HIGH, preferred_element_type=F32
        )
        total = term if total is None else total + term
    image_out[...] = total.reshape(6, 32, 64)

    scalars = scalars_ref[...]
    factor = scalars[8:9, 0:1]
    for n, out in ((9, loss_out), (10, count_out), (11, clip_out)):
        out[...] = scalars[n : n + 1, 0:1]

    def root_ratio(a, b):
        return RATE * jnp.sqrt(a) / jnp.sqrt(b)

    def like(ratio, v):
        return ratio.reshape((1,) * v.ndim)

    spot_of = (None, 0, 4, 6, 7, 8, 9, None)
    stores = []
    for n in LAST_ORDER:
        for kind in range(4):
            load(n, kind).wait()
        grad_ref, weight_ref, first_ref, second_ref = near[4 * n : 4 * n + 4]
        grad_out, moment_out, new_out = made[3 * n : 3 * n + 3]
        weight = weight_ref[...]
        grad = grad_ref[...] * like(factor, weight)
        second_new, update = lamb_update(weight, first_ref[...], second_ref[...], grad)
        grad_out[...] = grad
        moment_out[...] = second_new
        if n == 0:
            for lo, hi in ((0, 6), (6, 9)):
                w, u = weight[:, lo:hi, :], update[:, lo:hi, :]
                new_out[:, lo:hi, :] = w - like(root_ratio(square_sum(w), square_sum(u)), w) * u
        elif n == 7:
            new_out[...] = weight - root_ratio(square_sum(weight), square_sum(update)) * update
        else:
            for j in range(weight.shape[0] if n < 3 else 1):
                s = spot_of[n] + j
                ratio = root_ratio(scalars[0:1, s : s + 1], scalars[0:1, 64 + s : 65 + s])
                if n < 3:
                    new_out[j] = weight[j] - like(ratio, weight[j]) * update[j]
                else:
                    new_out[...] = weight - like(ratio, weight) * update
        for kind in range(3):
            at = 3 * n + kind
            copy = pltpu.make_async_copy(made[at], outs[at], store_sem.at[at])
            copy.start()
            stores.append(copy)
    for copy in stores:
        copy.wait()


def last(scalars, back, grads, state):
    def shape(a):
        return jax.ShapeDtypeStruct(a.shape, F32)

    far = []
    for n in range(8):
        far += [grads[n], *state[3 * n : 3 * n + 3]]
    outs = [shape(a) for a in state]
    small = [jax.ShapeDtypeStruct((1, 1), F32)] * 3 + [jax.ShapeDtypeStruct((6, 32, 64), F32)]
    vmem = pl.BlockSpec(memory_space=pltpu.VMEM)
    away = pl.BlockSpec(memory_space=pltpu.HBM)
    return pl.pallas_call(
        last_kernel,
        out_shape=tuple(outs + small),
        in_specs=[vmem] * 2 + [away] * 32,
        out_specs=[away] * 24 + [vmem] * 4,
        scratch_shapes=[pltpu.VMEM(a.shape, F32) for a in far]
        + [pltpu.VMEM(a.shape, F32) for a in state]
        + [
            pltpu.VMEM((384, 64), F32),
            pltpu.SemaphoreType.DMA((32,)),
            pltpu.SemaphoreType.DMA((24,)),
        ],
        compiler_params=pltpu.CompilerParams(vmem_limit_bytes=60 * 1024 * 1024),
        name="last",
    )(scalars, back, *far)


def step_kernel(*refs):
    live_ref, temb_ref, image_ref, target_ref = refs[:4]
    far, outs = refs[4:30], refs[30:38]
    scalars_out, back_out = refs[38:40]
    near, made = refs[40:66], refs[66:74]
    (
        low_ref,
        high_ref,
        down_ref,
        up_ref,
        full_ref,
        half_ref,
        work_ref,
        grad_ref,
        wide_ref,
        thin_ref,
        act_ref,
        acth_ref,
        turn_ref,
        wc_ref,
        wr_ref,
        wu_ref,
        wut_ref,
        wd_ref,
        coef_ref,
        rows_ref,
        patch_ref,
        ext_ref,
        send_ref,
        recv_ref,
        img_ref,
        tgt_ref,
        dwi_ref,
        dwh_ref,
        ngrad_ref,
        fgrad_ref,
        part_ref,
    part4_ref,
        imgrad_ref,
        wi_ref,
        wht_ref,
        wit_ref,
        wh_ref,
        tmp_ref,
        all_ref,
        block_ref,
        strips_ref,
        planes_ref,
        cbuf_ref,
        csend_ref,
        cpart_ref,
        fsend_ref,
        frecv_ref,
        film_ref,
        joined_ref,
        condv_ref,
        rb_ref,
        rx_ref,
        ry_ref,
        rz_ref,
        own_ref,
        m1_ref,
        r1_ref,
        m2_ref,
        r2_ref,
        m3_ref,
        r3_ref,
        gcs_ref,
        gcr_ref,
        fsum_ref,
        total_ref,
        back_ref,
        send_sem,
        recv_sem,
        load_sem,
        store_sem,
        g_send,
        g_recv,
        strip_send,
        strip_recv,
        cond_send,
        cond_recv,
        film_send,
        film_recv,
        core_send,
        core_recv,
        x_send,
        x_recv,
        y_send,
        y_recv,
        z_send,
        z_recv,
        m_send,
        m_recv,
        gc_send,
        gc_recv,
        back_send,
        back_recv,
    ) = refs[74:]
    lanes_ref, text_ref = near[:2]
    weights, firsts, seconds = near[2::3], near[3::3], near[4::3]
    edge_ref, norm_ref = weights[0], weights[7]
    dlow_ref, dhigh_ref, ddown_ref, dup_ref = low_ref, high_ref, down_ref, up_ref
    sb_ref = all_ref
    rr, cc, z, y, x, co = place_of()
    me = rr * 4 + cc
    core = co
    partner = 1 - co + 2 * x
    halo = rr >= 2
    split = jnp.logical_and(lax.rem(rr, 2) == 1, cc >= 2)

    def flag(cond):
        return jnp.where(cond, 1.0, 0.0).astype(F32)

    f_halo = flag(halo)
    f_core1 = flag(core == 1)
    f_core0 = 1.0 - f_core1
    f_top = f_halo * f_core1
    f_bot = f_halo * f_core0
    f_split = flag(split)
    f_joined = 1.0 - f_split

    place = lax.broadcasted_iota(jnp.int32, (32, 256), 0)
    lo_mask = jnp.where(place == 0, 0.0, jnp.where(place == 16, f_joined, 1.0))
    hi_mask = jnp.where(place == 31, 0.0, jnp.where(place == 15, f_joined, 1.0))

    def before(x):
        return pltpu.roll(x, 1, 0) * lo_mask

    def after(x):
        return pltpu.roll(x, 31, 0) * hi_mask

    def at(i):
        return pl.ds(pl.multiple_of(i * 32, 32), 32)

    def loop(body, init=0, count=16):
        return lax.fori_loop(0, count, body, init, unroll=16)

    def dot(a, b):
        return jnp.dot(a, b, preferred_element_type=F32)

    def dot_nt(a, b):
        return lax.dot_general(a, b, (((1,), (1,)), ((), ())), preferred_element_type=F32)

    def sigmoid(z):
        return 0.5 * jnp.tanh(0.5 * z) + 0.5

    def double(v):
        return jnp.concatenate([v, v], axis=1)


    def copy_of(e):
        return pltpu.make_async_remote_copy(
            src_ref=send_ref.at[e],
            dst_ref=recv_ref.at[e],
            send_sem=send_sem.at[e],
            recv_sem=recv_sem.at[e],
            device_id={"cols": partner},
            device_id_type=MESH,
        )

    def send(e, row, stats=None):
        send_ref[e, 0:32, :] = row
        send_ref[e, 32:40, :] = jnp.zeros((8, 256), F32) if stats is None else stats
        copy_of(e).start()

    def arrive(e):
        copy_of(e).wait()

    def edge_full(ref):
        low = f_core0 * ref[0, 480:512, 128:256] + f_core1 * ref[0, 0:32, 0:128]
        high = f_core0 * ref[1, 480:512, 128:256] + f_core1 * ref[1, 0:32, 0:128]
        return jnp.concatenate([low, high], axis=1)

    def edge_cell(ref):
        return f_core0 * ref[480:512, :] + f_core1 * ref[0:32, :]

    def edge(ref, planes):
        return edge_full(ref) if planes == 2 else edge_cell(ref.at[0])


    def halves(x):
        return x[0:8] + x[8:16], x[16:24] + x[24:32]

    def gathered(sums, planes):
        rows = []
        for s in sums:
            row = jnp.sum(s, axis=0, keepdims=True)
            rows.append(double(row[:, 0:128] + row[:, 128:256]) if planes == 2 else row)
        return jnp.concatenate(rows + [jnp.zeros((4, 256), F32)], axis=0)

    zero8 = jnp.zeros((8, 256), F32)

    def stats_of(x_ref, planes):
        def body(i, carry):
            s_l, s_r, q_l, q_r = carry
            for p in range(planes):
                x = x_ref[p, at(i), :]
                a, b = halves(x)
                c, d = halves(x * x)
                s_l, s_r, q_l, q_r = s_l + a, s_r + b, q_l + c, q_r + d
            return s_l, s_r, q_l, q_r

        return gathered(loop(body, (zero8,) * 4), planes)

    def over_slot(block, planes):
        swapped = jnp.concatenate(
            [block[1:2], block[0:1], block[3:4], block[2:3], block[4:8]], axis=0
        )
        x = block + f_joined * swapped
        lane = lax.broadcasted_iota(jnp.int32, (8, 256), 1)
        step = 1
        while step < (4 if planes == 2 else 8):
            up = pltpu.roll(x, 256 - step, 1)
            down = pltpu.roll(x, step, 1)
            x = x + jnp.where(lax.rem(lane, 2 * step) < step, up, down)
            step *= 2
        size = 16.0 if planes == 2 else 8.0
        count = (16.0 + 16.0 * f_halo) * (16.0 + 16.0 * f_joined) * size
        return x / count

    def spread(two):
        return jnp.concatenate(
            [
                jnp.broadcast_to(two[0:1], (16, 256)),
                jnp.broadcast_to(two[1:2], (16, 256)),
            ],
            axis=0,
        )

    def norm_row(k, which):
        width = NORM_AT[k + 1] - NORM_AT[k] if k < 6 else 128
        row = norm_ref[which : which + 1, NORM_AT[k] : NORM_AT[k] + width]
        return double(row) if width == 128 else row

    def film_rows(k, which):
        if k not in FILM_AT:
            return jnp.zeros((2, 256), F32)
        width = 256 if k == 5 else 128
        base = FILM_AT[k] + which * width
        two = film_ref[0:2, base : base + width]
        return double(two) if width == 128 else two

    def norm_ready(k, stats, e, planes):
        total = over_slot(stats + f_halo * recv_ref[e, 32:40, :], planes)
        mean = total[0:2]
        var = total[2:4] - mean * mean
        inverse = lax.rsqrt(var + EPS_NORM)
        gain, bias = norm_row(k, 0), norm_row(k, 1)
        factor = 1.0 + film_rows(k, 0)
        slope = inverse * gain * factor
        coef_ref[k, 0] = spread(slope)
        coef_ref[k, 1] = spread((bias - mean * inverse * gain) * factor + film_rows(k, 1))
        coef_ref[k, 2] = spread(mean)
        coef_ref[k, 3] = spread(inverse)
        rows_ref[k, 0:2, :] = mean
        rows_ref[k, 2:4, :] = inverse

    def activated(x, k):
        z = x * coef_ref[k, 0] + coef_ref[k, 1]
        return z * sigmoid(z)


    def put_wide(i, even, odd):
        for t, g in enumerate((before(odd), even, odd, after(even))):
            b = g.astype(BF)
            wide_ref[at(i + 1), 512 * t : 512 * t + 256] = b
            wide_ref[at(i + 2), 512 * t + 256 : 512 * t + 384] = b[:, 128:256]
            wide_ref[at(i), 512 * t + 384 : 512 * t + 512] = b[:, 0:128]

    def put_wide_edge(row):
        even, odd = row[:, 0:128], row[:, 128:256]
        lo, hi = lo_mask[:, 0:128], hi_mask[:, 0:128]
        for t, g in enumerate((pltpu.roll(odd, 1, 0) * lo, even, odd, pltpu.roll(even, 31, 0) * hi)):
            wide_ref[32:64, 512 * t + 256 : 512 * t + 384] = (g * f_top).astype(BF)
            wide_ref[512:544, 512 * t + 384 : 512 * t + 512] = (g * f_bot).astype(BF)

    def put_thin(i, x):
        for t, g in enumerate((before(x), x, after(x))):
            thin_ref[at(i + 1), 256 * t : 256 * t + 256] = g.astype(BF)

    def put_thin_edge(row):
        for t, g in enumerate((before(row), row, after(row))):
            thin_ref[0:32, 256 * t : 256 * t + 256] = (g * f_top).astype(BF)
            thin_ref[544:576, 256 * t : 256 * t + 256] = (g * f_bot).astype(BF)

    def keep_wide(slot):
        act_ref[slot, 0] = wide_ref[32:544, 512:768]
        act_ref[slot, 1] = wide_ref[32:544, 1024:1280]

    def keep_thin(slot):
        acth_ref[slot] = thin_ref[32:544, 256:512]

    def turn_wide(slot):
        turn_ref[0:256, :] = act_ref[slot, 0].T
        turn_ref[256:512, :] = act_ref[slot, 1].T


    def load_wc(index):
        for b in range(3):
            for r in range(4):
                for rp in range(2):
                    a = ROW_OF[r] - rp + 1
                    if 0 <= a <= 2:
                        wc_ref[
                            b * 512 + r * 128 : b * 512 + r * 128 + 128, rp * 128 : rp * 128 + 128
                        ] = low_ref[index, 3 * a + b]

    def load_wr(index):
        for b in range(3):
            for r in range(4):
                for rp in range(2):
                    a = ROW_OF[r] - rp + 1
                    if 0 <= a <= 2:
                        wr_ref[
                            rp * 128 : rp * 128 + 128, b * 512 + r * 128 : b * 512 + r * 128 + 128
                        ] = low_ref[index, 8 - 3 * a - b]

    def taps_of(parity, d):
        if parity == 0:
            return {-1: (0,), 0: (1, 2)}.get(d, ())
        return {0: (0, 1), 1: (2,)}.get(d, ())

    def load_up():
        for cp in range(2):
            for rp in range(2):
                for di in (-1, 0, 1):
                    for dj in (-1, 0, 1):
                        taps = [3 * a + b for a in taps_of(rp, di) for b in taps_of(cp, dj)]
                        if not taps:
                            continue
                        total = up_ref[taps[0]].astype(F32)
                        for t in taps[1:]:
                            total = total + up_ref[t].astype(F32)
                        low = total.astype(BF)
                        at_k = (dj + 1 - cp) * 256
                        wu_ref[cp, di + 1, at_k : at_k + 256, rp * 128 : rp * 128 + 128] = low
                        row = ROW_OF.index(rp - 2 * di)
                        col = COL_OF.index(cp - 2 * dj)
                        wut_ref[:, col * 512 + row * 128 : col * 512 + row * 128 + 128] = low

    def load_down():
        for b in range(3):
            for r in range(3):
                a = ROW_OF[r] + 1
                wd_ref[b * 512 + r * 128 : b * 512 + r * 128 + 128, :] = down_ref[3 * a + b]


    def conv_low(out, weight_nt=False):
        for cp in range(2):
            left = wide_ref[32:544, cp * 512 : cp * 512 + 1536]
            out(cp, dot_nt(left, wr_ref[...]) if weight_nt else dot(left, wc_ref[...]))

    def conv_high(index):
        total = None
        for a in range(3):
            term = dot(
                thin_ref[32 * a : 32 * a + 512, :],
                high_ref[index, 3 * a : 3 * a + 3].reshape(768, 256),
            )
            total = term if total is None else total + term
        return total

    def conv_high_back(index):
        total = None
        for a in range(3):
            for b in range(3):
                term = dot_nt(
                    thin_ref[32 * a : 32 * a + 512, b * 256 : b * 256 + 256],
                    high_ref[index, 8 - 3 * a - b],
                )
                total = term if total is None else total + term
        return total

    def grad_low(index, slot):
        turn_wide(slot)
        for b in range(3):
            block = dot(turn_ref[0:256, :], wide_ref[32:544, b * 512 : b * 512 + 512]) + dot(
                turn_ref[256:512, :], wide_ref[32:544, b * 512 + 512 : b * 512 + 1024]
            )
            for a in range(3):
                first = ROW_OF.index(a - 1) * 128
                second = ROW_OF.index(a) * 128
                dlow_ref[index, 8 - 3 * a - b] = (
                    block[0:128, first : first + 128] + block[128:256, second : second + 128]
                ).astype(dlow_ref.dtype)

    def grad_high(index, slot):
        turn_ref[0:256, :] = acth_ref[slot].T
        for a in range(3):
            block = dot(turn_ref[0:256, :], thin_ref[32 * a : 32 * a + 512, :])
            for b in range(3):
                dhigh_ref[index, 8 - 3 * a - b] = block[:, b * 256 : b * 256 + 256].astype(
                    dhigh_ref.dtype
                )


    def put_patch(slot, source, row, lanes):
        ext_ref[0:32, :] = row * f_top
        ext_ref[544:576, :] = row * f_bot

        def fill(i, carry):
            ext_ref[at(i + 1), :] = source[at(i), :]
            return carry

        loop(fill)

        def body(i, carry):
            total = None
            for di in (-1, 0, 1):
                x = ext_ref[at(i + 1 + di), :]
                for dj, g in enumerate((before(x), x, after(x))):
                    shift = ((di + 1) * 3 + dj) * lanes
                    term = pltpu.roll(g, shift, 1) if shift else g
                    total = term if total is None else total + term
            patch_ref[slot, at(i), :] = total.astype(BF)
            return carry

        loop(body)


    def norm_back_start(k, x_ref, planes):
        def body(i, carry):
            s_l, s_r, q_l, q_r = carry
            for p in range(planes):
                x = x_ref[p, at(i), :]
                z = x * coef_ref[k, 0] + coef_ref[k, 1]
                s = sigmoid(z)
                d = work_ref[p, at(i), :] * (s * (1.0 + z * (1.0 - s)))
                work_ref[p, at(i), :] = d
                a, b = halves(d)
                c, e = halves(d * ((x - coef_ref[k, 2]) * coef_ref[k, 3]))
                s_l, s_r, q_l, q_r = s_l + a, s_r + b, q_l + c, q_r + e
            return s_l, s_r, q_l, q_r

        return gathered(loop(body, (zero8,) * 4), planes)

    def norm_back_ready(k, stats, e, planes):
        gain, bias = norm_row(k, 0), norm_row(k, 1)
        factor = 1.0 + film_rows(k, 0)
        width = 128 if planes == 2 else 256
        one, two = stats[0:2], stats[2:4]
        dgain, dbias = factor * two, factor * one
        o = NORM_AT[k]
        ngrad_ref[0:1, o : o + width] = (dgain[0:1] + dgain[1:2])[:, 0:width]
        ngrad_ref[1:2, o : o + width] = (dbias[0:1] + dbias[1:2])[:, 0:width]
        if k in FILM_AT:
            f = FILM_AT[k]
            fgrad_ref[0:2, f : f + width] = (gain * two + bias * one)[:, 0:width]
            fgrad_ref[0:2, f + width : f + 2 * width] = one[:, 0:width]
        both = stats + f_halo * recv_ref[e, 32:40, :]
        kk = gain * factor
        scaled = jnp.concatenate([kk * both[0:2], kk * both[2:4], both[4:8]], axis=0)
        total = over_slot(scaled, planes)
        mean, inverse = rows_ref[k, 0:2, :], rows_ref[k, 2:4, :]
        second = -inverse * inverse * total[2:4]
        third = -inverse * total[0:2] - mean * second
        coef_ref[k, 4] = spread(inverse * kk)
        coef_ref[k, 5] = spread(second)
        coef_ref[k, 6] = spread(third)

    def back_value(k, d, x):
        return d * coef_ref[k, 4] + x * coef_ref[k, 5] + coef_ref[k, 6]


    def shard(kind, part, zs, ys, xs, ks, device):
        rows = slice(*GATHER_ROWS[part])
        return pltpu.make_async_remote_copy(
            src_ref=all_ref.at[zs, ys, xs, ks, rows],
            dst_ref=all_ref.at[zs, ys, xs, ks, rows],
            send_sem=g_send.at[part, kind, zs, ys, xs],
            recv_sem=g_recv.at[part, zs, ys, xs, ks],
            device_id=device,
            device_id_type=MESH,
        )

    def to_z(part, zd):
        return shard(zd, part, z, y, x, co, device_at(zd, y, x, co))

    def to_x(part, zs, ys):
        return shard(4, part, zs, ys, x, co, device_at(z, y, 1 - x, co))

    def to_y(part, zs, xs):
        return shard(5, part, zs, y, xs, co, device_at(z, 1 - y, x, co))

    def to_core(part, zs, ys, xs):
        return shard(6, part, zs, ys, xs, co, device_at(z, y, x, 1 - co))

    def arrived(part, zs, ys, xs, ks=co):
        shard(6, part, zs, ys, xs, ks, device_at(z, y, x, 1 - co)).wait_recv()

    def start(copy):
        copy.start()

    def in_line(dz, act):
        zs = z + dz

        @pl.when(jnp.logical_and(zs >= 0, zs <= 3))
        def _():
            act(zs)

    def gather_far(part, act=start):
        for zd in range(4):

            @pl.when(zd != z)
            def _(zd=zd):
                act(to_z(part, zd))

    def gather_near(part, act=start):
        act(to_x(part, z, y))
        act(to_y(part, z, x))
        act(to_core(part, z, y, x))

    def gather_z(part, act=start, wait=arrived):
        for dz in Z_ORDER[1:]:

            def one(zs):
                wait(part, zs, y, x)
                act(to_x(part, zs, y))
                act(to_y(part, zs, x))
                act(to_core(part, zs, y, x))

            in_line(dz, one)

    def gather_line(part, dzs, act=start, wait=arrived):
        for dz in dzs:

            def one(zs, dz=dz):
                if dz:
                    wait(part, zs, y, x)
                if dz <= 0:

                    @pl.when(z < 3)
                    def _():
                        act(shard(0, part, zs, y, x, co, device_at(z + 1, y, x, co)))

                if dz >= 0:

                    @pl.when(z > 0)
                    def _():
                        act(shard(1, part, zs, y, x, co, device_at(z - 1, y, x, co)))

                act(to_x(part, zs, y))
                act(to_y(part, zs, x))
                act(to_core(part, zs, y, x))

            in_line(dz, one)

    def gather_xy(part, act=start, wait=arrived):
        for dz in Z_ORDER:

            def one(zs):
                wait(part, zs, y, 1 - x)

                @pl.when(lax.rem(zs, 2) == 0)
                def _():
                    act(to_y(part, zs, 1 - x))

                act(to_core(part, zs, y, 1 - x))
                wait(part, zs, 1 - y, x)

                @pl.when(lax.rem(zs, 2) == 1)
                def _():
                    act(to_x(part, zs, 1 - y))

                act(to_core(part, zs, 1 - y, x))

            in_line(dz, one)

    def gather_last(part, act=start, wait=arrived):
        for dz in Z_ORDER:

            def one(zs):
                wait(part, zs, 1 - y, 1 - x)
                act(to_core(part, zs, 1 - y, 1 - x))

            in_line(dz, one)

    def gather_core(part):
        for zs in range(4):
            for ys in range(2):
                for xs in range(2):
                    arrived(part, zs, ys, xs, 1 - co)

    def gather_sent(part):
        def sent(copy):
            copy.wait_send()

        def none(*a):
            return None

        if part == LOW:
            gather_far(part, sent)
            gather_near(part, sent)
            gather_z(part, sent, none)
        else:
            gather_line(part, Z_ORDER, sent, none)
        gather_xy(part, sent, none)
        gather_last(part, sent, none)

    def row_places(r):
        def rows(at_row, size):
            return pl.ds(pl.multiple_of(at_row, 16), size)

        return rows(r * 16, 16), rows(r * 32, 32), rows(r * 32, 16), rows(r * 32 + 16, 16)

    def gather_place(part):
        rows = slice(*ROWS_OF[part])

        def row(r, carry):
            zr, yr = r // 2, lax.rem(r, 2)
            at16, at32, a16, b16 = row_places(r)
            packed = jnp.concatenate(
                [all_ref[zr, yr, c // 2, c % 2, rows, :] for c in range(4)], axis=1
            )
            v = jnp.dot(packed, lanes_ref[part], preferred_element_type=F32).astype(BF)
            if part == LOW:
                for j in range(4):
                    low_ref[j, :, at16, :] = v[:, j * 128 : j * 128 + 128].reshape(9, 16, 128)
            elif part == HIGH_PART:
                for j in range(2):
                    high_ref[j, :, at32, :] = v[:, j * 256 : j * 256 + 256].reshape(9, 32, 256)
            else:
                down_ref[:, at16, :] = v[:, 0:256].reshape(9, 16, 256)
                up_ref[:, a16, :] = v[:, 256:384].reshape(9, 16, 128)
                up_ref[:, b16, :] = v[:, 384:512].reshape(9, 16, 128)
            return carry

        lax.fori_loop(0, 8, row, 0, unroll=4)

    def pack_own(part):
        rows = slice(*ROWS_OF[part])
        own = all_ref.at[z, y, x, co]
        if part == LOW:
            total = None
            for j in range(4):
                term = place_lanes(weights[1][j].reshape(144, 32).astype(BF), 32 * j)
                total = term if total is None else total + term
        elif part == HIGH_PART:
            total = place_lanes(weights[2][0].reshape(288, 64).astype(BF), 0) + place_lanes(
                weights[2][1].reshape(288, 64).astype(BF), 64
            )
        else:
            total = (
                place_lanes(weights[3][...].reshape(144, 64).astype(BF), 0)
                + place_lanes(weights[4][:, 0:16, :].reshape(144, 32).astype(BF), 64)
                + place_lanes(weights[4][:, 16:32, :].reshape(144, 32).astype(BF), 96)
            )
        own[rows, :] = total.astype(BF)

    to_left = strip_at(rr, cc)
    to_right = strip_at(rr, lax.rem(cc + 3, 4))

    def strip_copies(side, device):
        return [
            pltpu.make_async_remote_copy(
                src_ref=block_ref.at[1 - side],
                dst_ref=strips_ref.at[side],
                send_sem=strip_send.at[side],
                recv_sem=strip_recv.at[side],
                device_id=device_no(device),
                device_id_type=MESH,
            )
        ]

    def pack_block():
        planes_ref[0:192, :] = image_ref[...].astype(F32).reshape(192, 64)
        planes_ref[192:288, :] = target_ref[...].reshape(96, 64)
        for g in range(4):
            for h in range(2):
                block_ref[h, :, 32 * g : 32 * g + 32] = planes_ref[
                    72 * g : 72 * g + 72, 32 * h : 32 * h + 32
                ]

    loads = [
        pltpu.make_async_copy(a, b, load_sem.at[n]) for n, (a, b) in enumerate(zip(far, near))
    ]
    for n in (5, 11, 14, 8, 1, 17, 0, 2, 20, 23):
        loads[n].start()
    for n in range(26):
        if n > 1 and n % 3 != 2:
            loads[n].start()


    def others(body):
        def one(d, carry):
            @pl.when(d != me)
            def _():
                body(d)

            return carry

        lax.fori_loop(0, 32, one, 0)

    def row_mates(body):
        for c in range(4):

            @pl.when(cc != c)
            def _(c=c):
                body(c)

    def cond_copy(c, source):
        return pltpu.make_async_remote_copy(
            src_ref=csend_ref,
            dst_ref=cbuf_ref.at[source],
            send_sem=cond_send.at[c],
            recv_sem=cond_recv.at[source],
            device_id={"rows": rr, "cols": c},
            device_id_type=MESH,
        )

    def film_copy(d, source):
        return pltpu.make_async_remote_copy(
            src_ref=fsend_ref.at[d],
            dst_ref=frecv_ref.at[source],
            send_sem=film_send.at[d],
            recv_sem=film_recv.at[source],
            device_id=device_no(d),
            device_id_type=MESH,
        )

    def cond_start():
        joined_ref[24:32, :] = jnp.zeros((8, joined_ref.shape[1]), F32)
        for a in range(5):
            joined_ref[5 * a : 5 * a + 5, 0:128] = temb_ref[a].astype(F32)
            joined_ref[5 * a : 5 * a + 5, 128:] = text_ref[a].astype(F32)
        own = dot_nt(joined_ref[...].astype(BF), weights[5][...].astype(BF))
        csend_ref[...] = jnp.concatenate([own, jnp.zeros((32, 112), F32)], axis=1)
        row_mates(lambda c: cond_copy(c, cc).start())
        cbuf_ref[cc] = csend_ref[...]

    def film_start():
        row_mates(lambda c: cond_copy(c, c).wait_recv())
        whole = cbuf_ref[0]
        for c in range(1, 4):
            whole = whole + pltpu.roll(cbuf_ref[c], 16 * c, 1)
        whole = whole[:, 0:64]
        cond = (whole * sigmoid(whole)).astype(BF)
        condv_ref[...] = cond.astype(F32)
        cpart_ref[...] = dot(cond, weights[6][...].astype(BF))

        def deal(d, carry):
            s_l, s_r = slots_of(d)
            for n, slot in enumerate((s_l, s_r)):
                line = cpart_ref[pl.ds(slot, 1), :]
                fsend_ref[d, 2 * n : 2 * n + 1, :] = line[:, 0:128]
                fsend_ref[d, 2 * n + 1 : 2 * n + 2, :] = line[:, 128:256]

            @pl.when(d != me)
            def _():
                film_copy(d, me).start()

            return carry

        lax.fori_loop(0, 32, deal, 0)
        frecv_ref[me] = fsend_ref[me]

    def film_ready():
        others(lambda d: film_copy(d, d).wait_recv())
        for c in range(4):
            total = frecv_ref[c]
            for r in range(1, 8):
                total = total + frecv_ref[4 * r + c]
            for n in range(4):
                at_lane = c * 256 + n % 2 * 128
                film_ref[n // 2 : n // 2 + 1, at_lane : at_lane + 128] = total[n : n + 1]


    def edge_terms():
        for a in range(3):
            for b in range(3):
                for cp in range(2):
                    for rp in range(2):
                        rho, gamma = rp + a - 1, cp + b - 1
                        cell = (rho // 2 + 1) * 3 + gamma // 2 + 1
                        phase = (gamma % 2) * 2 + rho % 2
                        tile = COL_OF.index(gamma) * 512 + ROW_OF.index(rho) * 128
                        yield 3 * a + b, cp, rp, cell, phase, tile

    def load_edges():
        dwi_ref[...] = jnp.zeros(dwi_ref.shape, F32)
        dwh_ref[...] = jnp.zeros(dwh_ref.shape, F32)
        for t, cp, rp, cell, phase, _ in edge_terms():
            lanes = slice(rp * 128, rp * 128 + 128)
            row = cell * 24 + phase * 6
            dwi_ref[cp, row : row + 6, lanes] = edge_ref[t, 0:6, :]
            row = cell * 12 + phase * 3
            dwh_ref[cp, row : row + 3, lanes] = edge_ref[8 - t, 6:9, :]
        wi_ref[...] = dwi_ref[...].astype(BF)
        wht_ref[...] = dwh_ref[...].astype(BF)
        for ref, taps, lo, size in ((wh_ref, 1, 6, 3), (wit_ref, -1, 0, 6)):
            ref[...] = jnp.zeros(ref.shape, BF)
            tmp_ref[...] = jnp.zeros(tmp_ref.shape, F32)
            for t, cp, rp, _, _, tile in edge_terms():
                row = (cp * 2 + rp) * size
                tap = t if taps > 0 else 8 - t
                tmp_ref[row : row + size, tile : tile + 128] = edge_ref[tap, lo : lo + size, :]
            ref[0:32, :] = tmp_ref[...].astype(BF)


    def add(to, b):
        to[...] = (to[...].astype(F32) + b[...].astype(F32)).astype(BF)

    def deal_pack(part, r_lo, r_hi):
        rows = slice(*ROWS_OF[part])

        def row(r, carry):
            zr, yr = r // 2, lax.rem(r, 2)
            at16, at32, a16, b16 = row_places(r)
            if part == LOW:
                pieces = [dlow_ref[j, :, at16, :].reshape(144, 128) for j in range(4)]
            elif part == HIGH_PART:
                pieces = [dhigh_ref[j, :, at32, :].reshape(288, 256) for j in range(2)]
            else:
                pieces = [
                    ddown_ref[:, at16, :].reshape(144, 256),
                    dup_ref[:, a16, :].reshape(144, 128),
                    dup_ref[:, b16, :].reshape(144, 128),
                ]
            v = dot_nt(jnp.concatenate(pieces, axis=1), lanes_ref[part]).astype(BF)
            for c in range(4):
                sb_ref[zr, yr, c // 2, c % 2, rows, :] = v[:, c * 128 : c * 128 + 128]
            return carry

        lax.fori_loop(r_lo, r_hi, row, 0, unroll=2)

    def core_copy(part, zs):
        rows = slice(*ROWS_OF[part])
        return pltpu.make_async_remote_copy(
            src_ref=sb_ref.at[zs, :, :, 1 - co, rows],
            dst_ref=rb_ref.at[zs, :, :, rows],
            send_sem=core_send.at[part, zs],
            recv_sem=core_recv.at[part, zs],
            device_id=device_at(z, y, x, 1 - co),
            device_id_type=MESH,
        )

    def first_copy(part, zs):
        rows = slice(*ROWS_OF[part])
        by_x = zs % 2 == 0
        return pltpu.make_async_remote_copy(
            src_ref=rb_ref.at[zs, :, 1 - x, rows] if by_x else rb_ref.at[zs, 1 - y, :, rows],
            dst_ref=rx_ref.at[zs, :, rows],
            send_sem=x_send.at[part, zs],
            recv_sem=x_recv.at[part, zs],
            device_id=device_at(z, y, 1 - x, co) if by_x else device_at(z, 1 - y, x, co),
            device_id_type=MESH,
        )

    def second_copy(part, zs):
        rows = slice(*ROWS_OF[part])
        by_x = zs % 2 == 1
        return pltpu.make_async_remote_copy(
            src_ref=rb_ref.at[zs, y, 1 - x, rows] if by_x else rb_ref.at[zs, 1 - y, x, rows],
            dst_ref=ry_ref.at[zs, rows],
            send_sem=y_send.at[part, zs],
            recv_sem=y_recv.at[part, zs],
            device_id=device_at(z, y, 1 - x, co) if by_x else device_at(z, 1 - y, x, co),
            device_id_type=MESH,
        )

    def z_copy(part, zs, source):
        rows = slice(*ROWS_OF[part])
        return pltpu.make_async_remote_copy(
            src_ref=rb_ref.at[zs, y, x, rows],
            dst_ref=rz_ref.at[source, rows],
            send_sem=z_send.at[part, zs],
            recv_sem=z_recv.at[part, source],
            device_id=device_at(zs, y, x, co),
            device_id_type=MESH,
        )

    def deal_core(part):
        for zs in range(4):
            deal_pack(part, 2 * zs, 2 * zs + 2)
            core_copy(part, zs).start()

    def deal_first(part):
        rows = slice(*ROWS_OF[part])
        for zs in range(4):
            core_copy(part, zs).wait_recv()
            for ys in range(2):
                for xs in range(2):
                    add(rb_ref.at[zs, ys, xs, rows], sb_ref.at[zs, ys, xs, co, rows])
            first_copy(part, zs).start()

    def deal_second(part):
        rows = slice(*ROWS_OF[part])
        for zs in range(4):
            first_copy(part, zs).wait_recv()
            for other in range(2):
                to = rb_ref.at[zs, other, x, rows] if zs % 2 == 0 else rb_ref.at[zs, y, other, rows]
                add(to, rx_ref.at[zs, other, rows])
            second_copy(part, zs).start()

    def deal_z(part):
        rows = slice(*ROWS_OF[part])
        for zs in range(4):
            second_copy(part, zs).wait_recv()
            add(rb_ref.at[zs, y, x, rows], ry_ref.at[zs, rows])

            @pl.when(zs != z)
            def _(zs=zs):
                z_copy(part, zs, z).start()

            @pl.when(zs == z)
            def _(zs=zs):
                rz_ref[zs, rows, :] = rb_ref[zs, y, x, rows, :]

    def deal_end(part):
        rows = slice(*ROWS_OF[part])
        for zs in range(4):

            @pl.when(zs != z)
            def _(zs=zs):
                z_copy(part, zs, zs).wait_recv()

        own = rz_ref[0, rows, :].astype(F32)
        for zs in range(1, 4):
            own = own + rz_ref[zs, rows, :].astype(F32)
        own_ref[rows, :] = own

    def deal_sent(part):
        for zs in range(4):
            core_copy(part, zs).wait_send()
            first_copy(part, zs).wait_send()
            second_copy(part, zs).wait_send()

            @pl.when(zs != z)
            def _(zs=zs):
                z_copy(part, zs, z).wait_send()


    pack_block()
    loads[5].wait()
    pack_own(LOW)
    meet_all(me)
    gather_far(LOW)
    gather_near(LOW)
    for copy in strip_copies(0, to_left):
        copy.start()

    @pl.when(to_right != me)
    def _():
        for copy in strip_copies(1, to_right):
            copy.start()

    loads[1].wait()
    loads[17].wait()
    cond_start()
    for n in (11, 14, 8):
        loads[n].wait()
    pack_own(REST)
    pack_own(HIGH_PART)
    gather_line(BIG, (0,))
    for n in (2, 20, 23, 0):
        loads[n].wait()
    load_edges()
    gather_z(LOW)
    gather_line(BIG, (1, -1))
    film_start()
    gather_xy(LOW)
    gather_line(BIG, (2, -2))

    live_all = jnp.concatenate([live_ref[a] for a in range(5)], axis=0).astype(F32)
    slot_r = lax.broadcasted_iota(jnp.int32, (5, 5), 0)
    slot_c = lax.broadcasted_iota(jnp.int32, (5, 5), 1)

    def side(s):
        return jnp.where(jnp.logical_or(s == 0, s == 4), 32.0, 64.0)

    def all_sum(v):
        return jnp.sum(jnp.sum(v, axis=0, keepdims=True), axis=1, keepdims=True)

    count = 3.0 * all_sum(live_all * side(slot_r) * side(slot_c))
    my_l, my_r = slots_of(me)
    slot_id = slot_r * 5 + slot_c
    live_l = all_sum(jnp.where(slot_id == my_l, live_all, 0.0))
    live_r = all_sum(jnp.where(slot_id == my_r, live_all, 0.0))

    def zero(i, carry):
        wc_ref[at(i), :] = jnp.zeros((32, 256), BF)
        return carry

    loop(zero, count=48)
    wr_ref[...] = jnp.zeros(wr_ref.shape, BF)
    for cp in range(2):
        for di in range(3):
            wu_ref[cp, di] = jnp.zeros((512, 256), BF)
    for b in range(3):
        wd_ref[b * 512 + 384 : b * 512 + 512, :] = jnp.zeros((128, 256), BF)


    for copy in strip_copies(0, to_left):
        copy.wait()

    @pl.when(to_right != me)
    def _():
        for copy in strip_copies(1, to_right):
            copy.wait()

    @pl.when(to_right == me)
    def _():
        strips_ref[1] = block_ref[0]

    for g in range(4):
        for h in range(2):
            planes_ref[72 * g : 72 * g + 72, 32 * h : 32 * h + 32] = strips_ref[
                h, :, 32 * g : 32 * g + 32
            ]
    row_no = lax.broadcasted_iota(jnp.int32, (512, 288), 0)
    item = jnp.bitwise_and(row_no, 31)
    in_image = item < 12
    item2 = jnp.where(in_image, item, item - 12)
    size = jnp.where(in_image, 6, 3)
    parity = jnp.where(item2 >= size, 1, 0)
    source = (
        jnp.where(in_image, 0, 192)
        + (item2 - parity * size) * 32
        + 2 * lax.shift_right_logical(row_no, 5)
        + parity
    )
    source = jnp.where(item < 18, source, -1)
    pick = jnp.where(source == lax.broadcasted_iota(jnp.int32, (512, 288), 1), 1.0, 0.0)
    by_row = jnp.dot(pick, planes_ref[...], precision=HIGH, preferred_element_type=F32)
    row_no = lax.broadcasted_iota(jnp.int32, (64, 64), 0)
    column = 2 * jnp.bitwise_and(row_no, 31) + lax.shift_right_logical(row_no, 5)
    pick = jnp.where(column == lax.broadcasted_iota(jnp.int32, (64, 64), 1), 1.0, 0.0)
    by_cell = lax.dot_general(
        pick, by_row, (((1,), (1,)), ((), ())), precision=HIGH, preferred_element_type=F32
    )
    lane = lax.broadcasted_iota(jnp.int32, (32, 128), 1)
    none = jnp.zeros((32, 128), F32)
    for i in range(16):
        pair = by_cell[:, i // 4 * 128 : i // 4 * 128 + 128]
        if i % 4:
            pair = pltpu.roll(pair, 128 - 32 * (i % 4), 1)
        even, odd = pair[0:32], pair[32:64]
        v = jnp.where(lane < 12, even, jnp.where(lane < 24, pltpu.roll(odd, 12, 1), 0.0))
        img_ref[32 * i : 32 * i + 32, :] = jnp.concatenate([v, none], axis=1)
        v = jnp.where(
            lane < 6, pltpu.roll(even, 116, 1), jnp.where(lane < 12, pltpu.roll(odd, 122, 1), 0.0)
        )
        tgt_ref[32 * i : 32 * i + 32, :] = jnp.concatenate([v, none], axis=1)


    send(0, edge_cell(img_ref))
    arrive(0)
    put_patch(0, img_ref, recv_ref[0, 0:32, :], 24)
    for cp in range(2):
        full_ref[0, cp] = dot(patch_ref[0], wi_ref[cp])

    def fwd_norm_full(k, source, e):
        stats = stats_of(source, 2)
        send(e, edge_full(source), stats)
        return stats

    def fwd_apply_full(k, source, stats, e):
        arrive(e)
        norm_ready(k, stats, e, 2)

        def body(i, carry):
            put_wide(
                i,
                activated(source[0, at(i), :], k),
                activated(source[1, at(i), :], k),
            )
            return carry

        loop(body)
        put_wide_edge(activated(recv_ref[e, 0:32, :], k))

    for index in range(2):
        h = full_ref.at[2 * index]
        mid = full_ref.at[2 * index + 1]
        out = full_ref.at[2 * index + 2]
        k = 2 * index
        stats = fwd_norm_full(k, h, 1 + k)
        if index:
            gather_last(BIG)
            load_wc(2)
        else:
            gather_last(LOW)
            gather_core(LOW)
            gather_line(BIG, (3, -3))
            gather_place(LOW)
            load_wc(0)
        fwd_apply_full(k, h, stats, 1 + k)
        keep_wide(k)

        def put_mid(cp, value, mid=mid):
            mid[cp] = value

        conv_low(put_mid)
        stats = fwd_norm_full(k + 1, mid, 2 + k)
        load_wc(2 * index + 1)
        if not index:
            film_ready()
            gather_xy(BIG)
        fwd_apply_full(k + 1, mid, stats, 2 + k)
        keep_wide(k + 1)

        def put_out(cp, value, h=h, out=out):
            out[cp] = h[cp] + value

        conv_low(put_out)

    skip = full_ref.at[4]
    send(5, edge_full(skip))
    gather_core(BIG)
    gather_place(REST)
    load_down()

    def skip_body(i, carry):
        put_wide(i, skip[0, at(i), :], skip[1, at(i), :])
        return carry

    loop(skip_body)
    arrive(5)
    put_wide_edge(recv_ref[5, 0:32, :])
    keep_wide(4)
    half_ref[0, 0] = dot(wide_ref[32:544, 0:1536], wd_ref[...])

    def fwd_half(k, source, e):
        stats = stats_of(source, 1)
        send(e, edge_cell(source.at[0]), stats)
        arrive(e)
        norm_ready(k, stats, e, 1)

        def body(i, carry):
            put_thin(i, activated(source[0, at(i), :], k))
            return carry

        loop(body)
        put_thin_edge(activated(recv_ref[e, 0:32, :], k))

    fwd_half(4, half_ref.at[0], 6)
    keep_thin(0)
    gather_place(HIGH_PART)
    half_ref[1, 0] = conv_high(0)
    fwd_half(5, half_ref.at[1], 7)
    keep_thin(1)
    half_ref[2, 0] = half_ref[0, 0] + conv_high(1)
    deep = half_ref.at[2]
    send(8, edge_cell(deep.at[0]))
    load_up()

    def deep_body(i, carry):
        put_thin(i, deep[0, at(i), :])
        return carry

    loop(deep_body)
    arrive(8)
    put_thin_edge(recv_ref[8, 0:32, :])
    keep_thin(2)
    merged = full_ref.at[5]
    for cp in range(2):
        total = skip[cp]
        for di in range(3):
            total = total + dot(
                thin_ref[32 * di : 32 * di + 512, cp * 256 : cp * 256 + 512], wu_ref[cp, di]
            )
        merged[cp] = total

    stats = fwd_norm_full(6, merged, 9)
    fwd_apply_full(6, merged, stats, 9)
    keep_wide(5)
    work_ref[0] = jnp.concatenate(
        [dot_nt(wide_ref[32:544, :], wh_ref[...]), jnp.zeros((512, 128), F32)], axis=1
    )

    live = spread(jnp.broadcast_to(jnp.concatenate([live_l, live_r], axis=0), (2, 256)))
    weight = 2.0 / count

    def loss_body(i, carry):
        diff = work_ref[0, at(i), :] - tgt_ref[at(i), :]
        half = live * diff
        work_ref[0, at(i), :] = (half * weight).astype(BF).astype(F32)
        return carry + half * diff

    lost = loop(loss_body, jnp.zeros((32, 256), F32))
    lost = jnp.sum(lost, axis=0, keepdims=True)
    part_ref[...] = jnp.zeros(part_ref.shape, F32)
    part_ref[99:100, :] = lost[:, 0:128] + lost[:, 128:256]
    fgrad_ref[...] = jnp.zeros(fgrad_ref.shape, F32)


    send(10, edge_cell(work_ref.at[0]))
    arrive(10)
    put_patch(1, work_ref.at[0], recv_ref[10, 0:32, :], 12)
    for cp in range(2):
        work_ref[cp] = dot(patch_ref[1], wht_ref[cp])
    stats = norm_back_start(6, merged, 2)
    send(11, edge_full(work_ref), stats)
    turn_ref[0:256, :] = patch_ref[1].T
    for cp in range(2):
        dwh_ref[cp] = dot(turn_ref[0:256, :], act_ref[5, cp])
    arrive(11)
    norm_back_ready(6, stats, 11, 2)

    def head_body(i, carry):
        pair = []
        for p in range(2):
            g = back_value(6, work_ref[p, at(i), :], merged[p, at(i), :])
            grad_ref[p, at(i), :] = g
            pair.append(g)
        put_wide(i, pair[0], pair[1])
        return carry

    loop(head_body)
    put_wide_edge(back_value(6, recv_ref[11, 0:32, :], recv_ref[9, 0:32, :]))

    hgrad = half_ref.at[3]
    hgrad[0] = dot_nt(wide_ref[32:544, :], wut_ref[...])
    send(12, edge_cell(hgrad.at[0]))
    turn_ref[0:256, :] = acth_ref[2].T
    for b in range(3):
        cols = {0: (3, 2), 1: (1, 2), 2: (1, 0)}[b]
        block = dot(turn_ref[0:256, :], wide_ref[32:544, cols[0] * 512 : cols[0] * 512 + 512]) + dot(
            turn_ref[0:256, :], wide_ref[32:544, cols[1] * 512 : cols[1] * 512 + 512]
        )
        for a in range(3):
            one, two = {0: (3, 1), 1: (0, 1), 2: (0, 2)}[a]
            dup_ref[3 * a + b] = (
                block[:, one * 128 : one * 128 + 128] + block[:, two * 128 : two * 128 + 128]
            ).astype(dup_ref.dtype)

    def deep_grad(i, carry):
        put_thin(i, hgrad[0, at(i), :])
        return carry

    loop(deep_grad)
    arrive(12)
    put_thin_edge(recv_ref[12, 0:32, :])
    work_ref[0] = conv_high_back(1)
    stats = norm_back_start(5, half_ref.at[1], 1)
    send(13, edge_cell(work_ref.at[0]), stats)
    grad_high(1, 1)
    arrive(13)
    norm_back_ready(5, stats, 13, 1)

    def mid_grad(i, carry):
        put_thin(i, back_value(5, work_ref[0, at(i), :], half_ref[1, 0, at(i), :]))
        return carry

    loop(mid_grad)
    put_thin_edge(back_value(5, recv_ref[13, 0:32, :], recv_ref[7, 0:32, :]))
    work_ref[0] = conv_high_back(0)
    stats = norm_back_start(4, half_ref.at[0], 1)
    send(14, edge_cell(work_ref.at[0]), stats)
    grad_high(0, 0)
    arrive(14)
    norm_back_ready(4, stats, 14, 1)

    def first_grad(i, carry):
        put_thin(
            i, hgrad[0, at(i), :] + back_value(4, work_ref[0, at(i), :], half_ref[0, 0, at(i), :])
        )
        return carry

    loop(first_grad)
    put_thin_edge(
        recv_ref[12, 0:32, :] + back_value(4, recv_ref[14, 0:32, :], recv_ref[6, 0:32, :])
    )

    for part in (LOW, BIG):
        gather_sent(part)
    deal_core(HIGH_PART)

    for cp in range(2):
        for rp in range(2):
            total = None
            for di in range(1 + rp):
                for dj in range(1 + cp):
                    a = 0 if di else 1 + rp
                    b = 0 if dj else 1 + cp
                    term = dot_nt(
                        thin_ref[32 * (1 + di) : 32 * (1 + di) + 512, (1 + dj) * 256 : (2 + dj) * 256],
                        down_ref[3 * a + b],
                    )
                    total = term if total is None else total + term
            grad_ref[cp, :, rp * 128 : rp * 128 + 128] = (
                grad_ref[cp, :, rp * 128 : rp * 128 + 128] + total
            )
    send(15, edge_full(grad_ref))
    turn_wide(4)
    for cp in range(2):
        for rp in range(2):
            for di in range(1 + rp):
                for dj in range(1 + cp):
                    a = 0 if di else 1 + rp
                    b = 0 if dj else 1 + cp
                    at_row = cp * 256 + rp * 128
                    ddown_ref[3 * a + b] = dot(
                        turn_ref[at_row : at_row + 128, :],
                        thin_ref[32 * (1 + di) : 32 * (1 + di) + 512, (1 + dj) * 256 : (2 + dj) * 256],
                    ).astype(ddown_ref.dtype)

    deal_first(HIGH_PART)
    deal_core(REST)

    def put_work(cp, value):
        work_ref[cp] = value

    edge_grad = None
    for index in (1, 0):
        h = full_ref.at[2 * index]
        mid = full_ref.at[2 * index + 1]
        k = 2 * index
        e = 16 if index else 18
        load_wr(k + 1)
        if index:

            def out_grad(i, carry):
                put_wide(i, grad_ref[0, at(i), :], grad_ref[1, at(i), :])
                return carry

            loop(out_grad)
            arrive(15)
            edge_grad = recv_ref[15, 0:32, :]
            put_wide_edge(edge_grad)
        conv_low(put_work, True)
        stats = norm_back_start(k + 1, mid, 2)
        send(e, edge_full(work_ref), stats)
        grad_low(k + 1, k + 1)
        if index:
            deal_first(REST)
        else:
            deal_z(HIGH_PART)
            deal_second(REST)
        load_wr(k)
        arrive(e)
        norm_back_ready(k + 1, stats, e, 2)

        def mid_body(i, carry, mid=mid, k=k):
            put_wide(
                i,
                back_value(k + 1, work_ref[0, at(i), :], mid[0, at(i), :]),
                back_value(k + 1, work_ref[1, at(i), :], mid[1, at(i), :]),
            )
            return carry

        loop(mid_body)
        put_wide_edge(back_value(k + 1, recv_ref[e, 0:32, :], recv_ref[k + 2, 0:32, :]))
        conv_low(put_work, True)
        stats = norm_back_start(k, h, 2)
        send(e + 1, edge_full(work_ref), stats)
        grad_low(k, k)
        if index:
            deal_second(HIGH_PART)
        else:
            deal_core(LOW)
        arrive(e + 1)
        norm_back_ready(k, stats, e + 1, 2)

        def in_body(i, carry, h=h, k=k):
            pair = []
            for p in range(2):
                g = grad_ref[p, at(i), :] + back_value(k, work_ref[p, at(i), :], h[p, at(i), :])
                grad_ref[p, at(i), :] = g
                pair.append(g)
            put_wide(i, pair[0], pair[1])
            return carry

        loop(in_body)
        edge_grad = edge_grad + back_value(k, recv_ref[e + 1, 0:32, :], recv_ref[k + 1, 0:32, :])
        put_wide_edge(edge_grad)

    deal_first(LOW)
    turn_ref[0:256, :] = patch_ref[0].T
    for cp in range(2):
        dwi_ref[cp] = dot(turn_ref[0:256, :], wide_ref[32:544, 512 + cp * 512 : 768 + cp * 512])

    for a in range(3):
        for b in range(3):
            first, last = None, None
            for cp in range(2):
                for rp in range(2):
                    rho, gamma = rp + a - 1, cp + b - 1
                    cell = (rho // 2 + 1) * 3 + gamma // 2 + 1
                    phase = (gamma % 2) * 2 + rho % 2
                    row = cell * 24 + phase * 6
                    term = dwi_ref[cp, row : row + 6, rp * 128 : rp * 128 + 128]
                    first = term if first is None else first + term
                    row = cell * 12 + phase * 3
                    term = dwh_ref[cp, row : row + 3, rp * 128 : rp * 128 + 128]
                    last = term if last is None else last + term
            t = 3 * a + b
            part_ref[9 * t : 9 * t + 6, :] = first
            part_ref[9 * (8 - t) + 6 : 9 * (8 - t) + 9, :] = last
    for which in range(2):
        for j in range(9):
            row = 81 + 9 * which + j
            part_ref[row : row + 1, :] = ngrad_ref[which : which + 1, 128 * j : 128 * j + 128]


    def message(n, src, dst, d, source):
        return pltpu.make_async_remote_copy(
            src_ref=src,
            dst_ref=dst.at[source],
            send_sem=m_send.at[n, d],
            recv_sem=m_recv.at[n, source],
            device_id=device_no(d),
            device_id_type=MESH,
        )

    def fill(d, carry):
        c = lax.rem(d, 4)
        for n in range(4):
            at_lane = pl.ds(pl.multiple_of(c * 256 + n % 2 * 128, 128), 128)
            m1_ref[d, n : n + 1, :] = fgrad_ref[n // 2 : n // 2 + 1, at_lane]
        m1_ref[d, 4:8, :] = part4_ref[d]

        @pl.when(d != me)
        def _():
            message(0, m1_ref.at[d], r1_ref, d, me).start()

        return carry

    for d in range(32):
        part4_ref[d] = part_ref[4 * d : 4 * d + 4, :]
    lax.fori_loop(0, 32, fill, 0)
    r1_ref[me] = m1_ref[me]

    deal_z(REST)
    deal_second(LOW)
    imgrad_ref[...] = dot_nt(wit_ref[0:32, :], wide_ref[32:544, :])[0:24] * count

    s_r, s_c = strip_of(me)
    home_left = s_r * 4 + s_c
    home_right = s_r * 4 + lax.rem(s_c + 1, 4)

    def back_copy(side, device):
        return pltpu.make_async_remote_copy(
            src_ref=imgrad_ref,
            dst_ref=back_ref.at[1 - side],
            send_sem=back_send.at[side],
            recv_sem=back_recv.at[side],
            device_id=device_no(device),
            device_id_type=MESH,
        )

    back_copy(0, home_left).start()

    @pl.when(home_right != me)
    def _():
        back_copy(1, home_right).start()

    others(lambda d: message(0, m1_ref.at[d], r1_ref, d, d).wait_recv())
    fsum_ref[...] = jnp.zeros(fsum_ref.shape, F32)

    def collect(d, total):
        s_l, s_rt = slots_of(d)
        for n, slot in enumerate((s_l, s_rt)):
            line = jnp.concatenate(
                [r1_ref[d, 2 * n : 2 * n + 1, :], r1_ref[d, 2 * n + 1 : 2 * n + 2, :]], axis=1
            )
            fsum_ref[pl.ds(slot, 1), :] = fsum_ref[pl.ds(slot, 1), :] + line
        return total + r1_ref[d]

    m2_ref[0:4, :] = lax.fori_loop(0, 32, collect, jnp.zeros((8, 128), F32))[4:8]
    film_mine = fsum_ref[...]
    film_w = weights[6][...].astype(BF).astype(F32)
    gc_part = lax.dot_general(
        film_mine, film_w, (((1,), (1,)), ((), ())), precision=HIGH, preferred_element_type=F32
    )
    wide = jnp.concatenate([gc_part, jnp.zeros((32, 64), F32)], axis=1)
    for c in range(4):
        gcs_ref[c] = pltpu.roll(wide, 128 - 16 * c, 1) if c else wide

    def gc_copy(c, source):
        return pltpu.make_async_remote_copy(
            src_ref=gcs_ref.at[c],
            dst_ref=gcr_ref.at[source],
            send_sem=gc_send.at[c],
            recv_sem=gc_recv.at[source],
            device_id={"rows": rr, "cols": c},
            device_id_type=MESH,
        )

    for c in range(4):

        @pl.when(cc != c)
        def _(c=c):
            gc_copy(c, cc).start()

        @pl.when(cc == c)
        def _(c=c):
            gcr_ref[c] = gcs_ref[c]

    grads = [None] * 8
    grads[6] = lax.dot_general(
        condv_ref[...], film_mine, (((0,), (0,)), ((), ())), precision=HIGH, preferred_element_type=F32
    )

    deal_z(LOW)
    deal_end(HIGH_PART)

    for c in range(4):

        @pl.when(cc != c)
        def _(c=c):
            gc_copy(c, c).wait_recv()

    pre = csend_ref[:, 0:16]
    gc = gcr_ref[0] + gcr_ref[1] + gcr_ref[2] + gcr_ref[3]
    gc = gc[:, 0:16] * silu_grad_tanh(pre)
    grads[5] = lax.dot_general(
        gc,
        joined_ref[...],
        (((0,), (0,)), ((), ())),
        precision=HIGH,
        preferred_element_type=F32,
    )

    deal_end(REST)
    deal_end(LOW)
    own = own_ref[...]
    grads[1] = jnp.stack([own[0:144, 32 * j : 32 * j + 32].reshape(9, 16, 32) for j in range(4)])
    grads[2] = jnp.stack([own[288:576, 64 * j : 64 * j + 64].reshape(9, 32, 64) for j in range(2)])
    grads[3] = own[144:288, 0:64].reshape(9, 16, 64)
    grads[4] = jnp.concatenate(
        [own[144:288, 64:96].reshape(9, 16, 32), own[144:288, 96:128].reshape(9, 16, 32)], axis=1
    )

    owned = square_sum(own)
    for n in (5, 6):
        owned = owned + square_sum(grads[n])
    m2_ref[4:8, :] = jnp.broadcast_to(owned, (4, 128))
    others(lambda d: message(1, m2_ref, r2_ref, d, me).start())
    r2_ref[me] = m2_ref[...]

    def leaving(n):
        return pltpu.make_async_copy(made[n], outs[n], store_sem.at[n])

    def leave(n):
        made[n][...] = grads[n]
        leaving(n).start()

    for n in range(1, 7):
        leave(n)
    others(lambda d: message(1, m2_ref, r2_ref, d, d).wait_recv())

    squares = jnp.zeros((4, 128), F32)
    for d in range(32):
        total_ref[4 * d : 4 * d + 4, :] = r2_ref[d, 0:4, :]
        squares = squares + r2_ref[d, 4:8, :]
    shared = square_sum(total_ref[0:LOSS_ROW, :])
    clip = jnp.sqrt(squares[0:1, 0:1] + shared)
    factor = jnp.minimum(1.0, CLIP_AT / clip)
    grads[0] = jnp.stack([total_ref[9 * t : 9 * t + 9, :] for t in range(9)])
    grads[7] = jnp.concatenate(
        [
            jnp.concatenate(
                [total_ref[NORM_ROW + 9 * n + j : NORM_ROW + 9 * n + j + 1, :] for j in range(9)],
                axis=1,
            )
            for n in range(2)
        ],
        axis=0,
    )

    for n in range(3, 26):
        if n % 3 != 2:
            loads[n].wait()
    pairs = []
    spot = 0
    for n in range(8):
        if n in (0, 7):
            leave(n)
            continue
        update = lamb_update(
            weights[n][...],
            firsts[n][...],
            seconds[n][...],
            grads[n] * factor.reshape((1,) * grads[n].ndim),
        )[1]
        for j in range(update.shape[0] if n < 3 else 1):
            pairs.append((spot, square_sum(weights[n][j] if n < 3 else weights[n][...])))
            pairs.append((64 + spot, square_sum(update[j] if n < 3 else update)))
            spot += 1

    m3_ref[...] = lane_value(pairs)[0:1]
    others(lambda d: message(2, m3_ref, r3_ref, d, me).start())
    r3_ref[me] = m3_ref[...]

    others(lambda d: message(2, m3_ref, r3_ref, d, d).wait_recv())
    sums = r3_ref[0]
    for d in range(1, 32):
        sums = sums + r3_ref[d]
    scalars_out[0:8, :] = jnp.broadcast_to(sums, (8, 128))
    lost = jnp.sum(total_ref[LOSS_ROW : LOSS_ROW + 1, :], axis=1, keepdims=True)
    for n, v in enumerate((factor, lost, count, clip)):
        scalars_out[8 + n : 9 + n, :] = jnp.broadcast_to(v, (1, 128))
    scalars_out[12:16, :] = jnp.zeros((4, 128), F32)

    back_copy(0, home_left).wait()

    @pl.when(home_right != me)
    def _():
        back_copy(1, home_right).wait()

    @pl.when(home_right == me)
    def _():
        back_ref[0] = imgrad_ref[...]

    back_out[...] = back_ref[...]

    for n in range(8):
        leaving(n).wait()

    for part in range(3):
        deal_sent(part)
    others(lambda d: film_copy(d, me).wait_send())
    row_mates(lambda c: cond_copy(c, cc).wait_send())
    row_mates(lambda c: gc_copy(c, cc).wait_send())
    for n, src in ((1, m2_ref), (2, m3_ref)):
        others(lambda d, n=n, src=src: message(n, src, r2_ref if n == 1 else r3_ref, d, me).wait_send())
    others(lambda d: message(0, m1_ref.at[d], r1_ref, d, me).wait_send())


def step(*operands):
    far = operands[4:]
    outs = [jax.ShapeDtypeStruct(far[2 + 3 * n].shape, F32) for n in range(8)]
    outs += [jax.ShapeDtypeStruct((16, 128), F32)]
    outs += [jax.ShapeDtypeStruct((2, 24, 512), F32)]
    vmem = pl.BlockSpec(memory_space=pltpu.VMEM)
    dma = pltpu.SemaphoreType.DMA

    def half(*shape):
        return pltpu.VMEM(shape, BF)

    def full(*shape):
        return pltpu.VMEM(shape, F32)

    return pl.pallas_call(
        step_kernel,
        out_shape=tuple(outs),
        in_specs=[vmem] * 4 + [pl.BlockSpec(memory_space=pltpu.HBM)] * 26,
        out_specs=[pl.BlockSpec(memory_space=pltpu.HBM)] * 8 + [vmem] * 2,
        scratch_shapes=[pltpu.VMEM(a.shape, a.dtype) for a in far]
        + [pltpu.VMEM(a.shape, F32) for a in outs[:8]]
        + [
            half(4, 9, 128, 128),
            half(2, 9, 256, 256),
            half(9, 128, 256),
            half(9, 256, 128),
            full(6, 2, 512, 256),
            full(4, 1, 512, 256),
            full(2, 512, 256),
            full(2, 512, 256),
            half(576, 2048),
            half(576, 768),
            half(6, 2, 512, 256),
            half(3, 512, 256),
            half(512, 512),
            half(1536, 256),
            half(256, 1536),
            half(2, 3, 512, 256),
            half(256, 2048),
            half(1536, 256),
            full(7, 7, 32, 256),
            full(7, 8, 256),
            half(2, 512, 256),
            full(576, 256),
            full(N_EXCHANGE, 40, 256),
            full(N_EXCHANGE, 40, 256),
            full(512, 256),
            full(512, 256),
            full(2, 256, 256),
            full(2, 256, 256),
            full(2, 1152),
            full(8, 1024),
            full(128, 128),
            full(32, 4, 128),
            full(24, 512),
            half(2, 256, 256),
            half(2, 256, 256),
            half(128, 2048),
            half(128, 2048),
            full(32, 2048),
            half(4, 2, 2, 2, ALL_ROWS, 128),
            full(2, 72, 128),
            full(2, 72, 128),
            full(288, 64),
            full(4, 32, 128),
            full(32, 128),
            full(32, 256),
            full(32, 4, 128),
            full(32, 4, 128),
            full(8, 1024),
            full(32, 4224),
            full(32, 64),
            half(4, 2, 2, ALL_ROWS, 128),
            half(4, 2, ALL_ROWS, 128),
            half(4, ALL_ROWS, 128),
            half(4, ALL_ROWS, 128),
            full(ALL_ROWS, 128),
            full(32, 8, 128),
            full(32, 8, 128),
            full(8, 128),
            full(32, 8, 128),
            full(1, 128),
            full(32, 1, 128),
            full(4, 32, 128),
            full(4, 32, 128),
            full(32, 256),
            full(128, 128),
            full(2, 24, 512),
            dma((N_EXCHANGE,)),
            dma((N_EXCHANGE,)),
            dma((26,)),
            dma((8,)),
            dma((2, 7, 4, 2, 2)),
            dma((2, 4, 2, 2, 2)),
            dma((2,)),
            dma((2,)),
            dma((4,)),
            dma((4,)),
            dma((32,)),
            dma((32,)),
            dma((3, 4)),
            dma((3, 4)),
            dma((3, 4)),
            dma((3, 4)),
            dma((3, 4)),
            dma((3, 4)),
            dma((3, 4)),
            dma((3, 4)),
            dma((3, 32)),
            dma((3, 32)),
            dma((4,)),
            dma((4,)),
            dma((2,)),
            dma((2,)),
        ],
        compiler_params=pltpu.CompilerParams(
            collective_id=1, has_side_effects=True, vmem_limit_bytes=62 * 1024 * 1024
        ),
        name="step",
    )(*operands)


def per_device_strips(
    image_pair,
    noise_target,
    timesteps,
    text_pooled,
    slot_live,
    *params,
):
    lanes = jnp.asarray(lane_tables(), BF)

    def view(n, a):
        return jnp.swapaxes(a, 1, 2) if n == 0 else a.T if n == 5 else a

    def planes(a):
        return jnp.transpose(a[0], (2, 0, 1))

    state = [view(n // 3, a) for n, a in enumerate(params)]
    *grads, scalars, back = step(
        jnp.transpose(slot_live, (1, 0, 2)),
        time_embed(timesteps)[0].astype(BF),
        planes(image_pair),
        planes(noise_target),
        lanes,
        text_pooled[0],
        *state,
    )
    results = last(scalars, back, grads, state)
    new = [view(n // 3, a) for n, a in enumerate(results[:24])]
    loss, count, clip = (a.reshape(()) for a in results[24:27])
    return tuple(new) + (loss, count, clip, jnp.transpose(results[27], (1, 2, 0))[None])


def solution(mesh):
    strips = mesh.shape["rows"] == 8 and mesh.shape["cols"] == 4
    placed = (
        P(None, "rows", "cols", None),
        P(None, "rows", "cols", None),
        P(),
        P(),
        P(),
        P(),
        P(),
        P(),
        P(None, None, "rows", "cols"),
        P(None, None, "rows", "cols"),
        P(None, None, "rows", "cols"),
        P(None, None, "rows", "cols"),
        P(None, None, "rows", "cols"),
        P(None, None, "rows", "cols"),
        P(None, "rows", "cols"),
        P(None, "rows", "cols"),
        P(None, "rows", "cols"),
        P(None, "rows", "cols"),
        P(None, "rows", "cols"),
        P(None, "rows", "cols"),
        P(None, ("rows", "cols")),
        P(None, ("rows", "cols")),
        P(None, ("rows", "cols")),
        P("rows", "cols"),
        P("rows", "cols"),
        P("rows", "cols"),
        P(),
        P(),
        P(),
    )
    return jax.shard_map(
        per_device_strips if strips else per_device,
        mesh=mesh,
        in_specs=placed,
        out_specs=(
            P(),
            P(),
            P(),
            P(None, None, "rows", "cols"),
            P(None, None, "rows", "cols"),
            P(None, None, "rows", "cols"),
            P(None, None, "rows", "cols"),
            P(None, None, "rows", "cols"),
            P(None, None, "rows", "cols"),
            P(None, "rows", "cols"),
            P(None, "rows", "cols"),
            P(None, "rows", "cols"),
            P(None, "rows", "cols"),
            P(None, "rows", "cols"),
            P(None, "rows", "cols"),
            P(None, ("rows", "cols")),
            P(None, ("rows", "cols")),
            P(None, ("rows", "cols")),
            P("rows", "cols"),
            P("rows", "cols"),
            P("rows", "cols"),
            P(),
            P(),
            P(),
            P(),
            P(),
            P(),
            P(None, "rows", "cols", None),
        ),
        check_vma=False,
    )
```

```python
import math

import jax
import jax.numpy as jnp
import numpy as np
from jax import lax
from jax.experimental import pallas as pl
from jax.experimental.pallas import tpu as pltpu
from jax.sharding import PartitionSpec as P

SLOT = 64
SLOTS = 5
C1 = 128
C2 = 256
GROUPS = 32
TEMB = 128
STEP = 10


HIGH = lax.Precision.HIGHEST
EPS_NORM = 1e-05
CLIP_AT = 0.05
RATE = 0.5
BETA_ONE = 0.9
BETA_TWO = 0.999
EPS_ADAM = 1e-06
DECAY = 0.01


def entering(part, axis, combine, identity, reverse):
    count = lax.axis_size(axis)
    place = lax.axis_index(axis)
    ahead = count - 1 - place if reverse else place
    gathered = jax.tree.map(lambda a: lax.all_gather(a, axis), part)
    state = jax.tree.map(lambda a, e: jnp.zeros_like(a) + jnp.asarray(e, a.dtype), part, identity)

    def one(turn, state):
        source = count - 1 - turn if reverse else turn
        return combine(
            state, jax.tree.map(lambda a: lax.dynamic_index_in_dim(a, source, 0, False), gathered)
        )

    return lax.fori_loop(0, ahead, one, state)


def padded_2(block, sides, width):
    for axis, dim in sides:
        count = lax.axis_size(axis)
        forward = [(i, i + 1) for i in range(count - 1)]
        backward = [(target, source) for source, target in forward]
        low = lax.ppermute(
            lax.slice_in_dim(block, block.shape[dim] - width, None, axis=dim), axis, forward
        )
        high = lax.ppermute(lax.slice_in_dim(block, 0, width, axis=dim), axis, backward)
        block = jnp.concatenate([low, block, high], axis=dim)
    return block


def time_embed(steps):
    half = TEMB // 2
    freq = jnp.exp(-math.log(10000.0) * jnp.arange(half, dtype=jnp.float32) / half)
    angle = steps.astype(jnp.float32)[..., None] * freq
    return jnp.concatenate([jnp.sin(angle), jnp.cos(angle)], axis=-1)


def silu_grad(values):
    sigma = jax.nn.sigmoid(values)
    return sigma * (1.0 + values * (1.0 - sigma))


def tap_masks(rows, cols, slot):
    half = slot // 2
    row_pos = lax.axis_index("rows") * rows + jnp.arange(rows)
    col_pos = lax.axis_index("cols") * cols + jnp.arange(cols)
    row_ok = [
        (row_pos + offset + half) // slot == (row_pos + half) // slot for offset in (-1, 0, 1)
    ]
    col_ok = [
        (col_pos + offset + half) // slot == (col_pos + half) // slot for offset in (-1, 0, 1)
    ]
    return [
        (row_ok[tap // 3][:, None] & col_ok[tap % 3][None, :]).astype(jnp.bfloat16)
        for tap in range(9)
    ]


def slot_level(rows, cols, slot, size):
    half = slot // 2
    labels = jnp.arange(SLOTS)
    row_pos = lax.axis_index("rows") * rows + jnp.arange(rows)
    col_pos = lax.axis_index("cols") * cols + jnp.arange(cols)
    row_map = (((row_pos + half) // slot)[:, None] == labels[None, :]).astype(jnp.float32)
    col_map = (((col_pos + half) // slot)[:, None] == labels[None, :]).astype(jnp.float32)
    every = (jnp.arange(size) + half) // slot
    side = jnp.sum((every[:, None] == labels[None, :]).astype(jnp.float32), axis=0)
    return (row_map, col_map, side[:, None] * side[None, :])


def to_slots(values, level):
    return jnp.einsum("nhwk,ha,wb->nabk", values, level[0], level[1], precision=HIGH)


def to_pixels(table, level):
    return jnp.einsum("nabk,ha,wb->nhwk", table, level[0], level[1], precision=HIGH)


def add_pair(earlier, later):
    return (earlier[0] + later[0], earlier[1] + later[1])


def slot_total(tables):
    empty = (jnp.zeros_like(tables[0]), jnp.zeros_like(tables[1]))
    before = entering(tables, ("rows", "cols"), add_pair, empty, False)
    after = entering(tables, ("rows", "cols"), add_pair, empty, True)
    return (before[0] + tables[0] + after[0], before[1] + tables[1] + after[1])


def pad_rim(values):
    return padded_2(values, (("rows", 1), ("cols", 2)), 1)


def tap_patch(padded, masks, tap, stride):
    rows = padded.shape[1] - 2
    cols = padded.shape[2] - 2
    row_off, col_off = (tap // 3, tap % 3)
    patch = padded[:, row_off : row_off + rows : stride, col_off : col_off + cols : stride, :]
    return patch * masks[tap][::stride, ::stride][None, :, :, None]


def conv_taps(padded, weight, masks, stride):
    total = None
    for tap in range(9):
        term = jnp.einsum(
            "nhwc,cd->nhwd",
            tap_patch(padded, masks, tap, stride),
            weight[tap],
            preferred_element_type=jnp.float32,
        )
        total = term if total is None else total + term
    return total


def conv_weight_grad(padded, grad_out, masks, stride):
    return jnp.stack(
        [
            jnp.einsum(
                "nhwc,nhwd->cd",
                tap_patch(padded, masks, tap, stride),
                grad_out,
                preferred_element_type=jnp.float32,
            )
            for tap in range(9)
        ]
    )


def conv_input_grad(grad_out, weight, masks, stride):
    spread = grad_out
    if stride == 2:
        canvases, rows, cols, width = grad_out.shape
        spread = jnp.stack([grad_out, jnp.zeros_like(grad_out)], axis=2).reshape(
            canvases, 2 * rows, cols, width
        )
        spread = jnp.stack([spread, jnp.zeros_like(spread)], axis=3).reshape(
            canvases, 2 * rows, 2 * cols, width
        )
    flipped = jnp.swapaxes(weight[::-1], 1, 2)
    padded = padded_2(spread, (("rows", 1), ("cols", 2)), 1)
    return conv_taps(padded, flipped, masks, 1)


def norm_forward(values, gain, bias, scale, shift, level):
    count_n, rows, cols, width = values.shape
    grouped = values.reshape(count_n, rows, cols, GROUPS, width // GROUPS)
    total, squares = slot_total(
        (
            to_slots(jnp.sum(grouped, axis=4), level),
            to_slots(jnp.sum(grouped * grouped, axis=4), level),
        )
    )
    count = level[2][None, :, :, None] * (width // GROUPS)
    mean = total / count
    var = squares / count - mean * mean
    inverse = lax.rsqrt(var + EPS_NORM)
    mean_pix = to_pixels(mean, level)
    inv_pix = to_pixels(inverse, level)
    hat = ((grouped - mean_pix[..., None]) * inv_pix[..., None]).reshape(values.shape)
    normed = hat * gain + bias
    if scale is None:
        return (normed, (hat, inv_pix, normed, None))
    factor = 1.0 + to_pixels(scale, level)
    return (normed * factor + to_pixels(shift, level), (hat, inv_pix, normed, factor))


def norm_backward(grad_out, kept, gain, level):
    hat, inv_pix, normed, factor = kept
    count_n, rows, cols, width = hat.shape
    if factor is None:
        film_grad = None
        grad_normed = grad_out
    else:
        film_grad = jnp.concatenate(
            [to_slots(grad_out * normed, level), to_slots(grad_out, level)], axis=-1
        )
        grad_normed = grad_out * factor
    grad_gain = jnp.sum(grad_normed * hat, axis=(0, 1, 2))
    grad_bias = jnp.sum(grad_normed, axis=(0, 1, 2))
    shape = (count_n, rows, cols, GROUPS, width // GROUPS)
    grad_hat = (grad_normed * gain).reshape(shape)
    grouped_hat = hat.reshape(shape)
    first, second = slot_total(
        (
            to_slots(jnp.sum(grad_hat, axis=4), level),
            to_slots(jnp.sum(grad_hat * grouped_hat, axis=4), level),
        )
    )
    count = level[2][None, :, :, None] * (width // GROUPS)
    mean_one = to_pixels(first / count, level)[..., None]
    mean_two = to_pixels(second / count, level)[..., None]
    grad_in = inv_pix[..., None] * (grad_hat - mean_one - grouped_hat * mean_two)
    return (grad_in.reshape(hat.shape), grad_gain, grad_bias, film_grad)


def block_forward(hidden, weights, gains, film, level, masks):
    pre_one, saved_one = norm_forward(hidden, gains[0], gains[1], None, None, level)
    rim_one = pad_rim(jax.nn.silu(pre_one).astype(jnp.bfloat16))
    conv_one = conv_taps(rim_one, weights[0], masks, 1)
    pre_two, saved_two = norm_forward(conv_one, gains[2], gains[3], film[0], film[1], level)
    rim_two = pad_rim(jax.nn.silu(pre_two).astype(jnp.bfloat16))
    out = hidden + conv_taps(rim_two, weights[1], masks, 1)
    return (out, (pre_one, saved_one, rim_one, pre_two, saved_two, rim_two))


def block_backward(grad_out, weights, gains, kept, level, masks):
    pre_one, saved_one, rim_one, pre_two, saved_two, rim_two = kept
    grad_two = grad_out.astype(jnp.bfloat16)
    weight_two = conv_weight_grad(rim_two, grad_two, masks, 1)
    grad_pre_two = conv_input_grad(grad_two, weights[1], masks, 1) * silu_grad(pre_two)
    grad_conv, gain_two, bias_two, film_grad = norm_backward(
        grad_pre_two, saved_two, gains[2], level
    )
    grad_one = grad_conv.astype(jnp.bfloat16)
    weight_one = conv_weight_grad(rim_one, grad_one, masks, 1)
    grad_pre_one = conv_input_grad(grad_one, weights[0], masks, 1) * silu_grad(pre_one)
    grad_in, gain_one, bias_one, _ = norm_backward(grad_pre_one, saved_one, gains[0], level)
    return (
        grad_out + grad_in,
        (weight_one, weight_two),
        (gain_one, bias_one, gain_two, bias_two),
        film_grad,
    )


def per_device(
    image_pair,
    noise_target,
    timesteps,
    text_pooled,
    slot_live,
    edgeconv_weight,
    edgeconv_first,
    edgeconv_second,
    convlow_weight,
    convlow_first,
    convlow_second,
    convhigh_weight,
    convhigh_first,
    convhigh_second,
    downconv_weight,
    downconv_first,
    downconv_second,
    upconv_weight,
    upconv_first,
    upconv_second,
    condproj_weight,
    condproj_first,
    condproj_second,
    filmproj_weight,
    filmproj_first,
    filmproj_second,
    normparams_weight,
    normparams_first,
    normparams_second,
):
    canvases, rows_one, cols_one = image_pair.shape[:3]
    size_full = rows_one * lax.axis_size("rows")
    level_full = slot_level(rows_one, cols_one, SLOT, size_full)
    level_half = slot_level(rows_one // 2, cols_one // 2, SLOT // 2, size_full // 2)
    by_rows = (
        lax.all_gather(convlow_weight.astype(jnp.bfloat16), "rows", axis=2, tiled=True),
        lax.all_gather(convhigh_weight.astype(jnp.bfloat16), "rows", axis=2, tiled=True),
        lax.all_gather(downconv_weight.astype(jnp.bfloat16), "rows", axis=1, tiled=True),
        lax.all_gather(upconv_weight.astype(jnp.bfloat16), "rows", axis=1, tiled=True),
        lax.all_gather(filmproj_weight.astype(jnp.bfloat16), "rows", axis=0, tiled=True),
    )
    low_convs, high_convs, down_conv, up_conv, film_full = (
        lax.all_gather(by_rows[0], "cols", axis=3, tiled=True),
        lax.all_gather(by_rows[1], "cols", axis=3, tiled=True),
        lax.all_gather(by_rows[2], "cols", axis=2, tiled=True),
        lax.all_gather(by_rows[3], "cols", axis=2, tiled=True),
        lax.all_gather(by_rows[4], "cols", axis=1, tiled=True),
    )
    joined = jnp.concatenate([time_embed(timesteps).astype(jnp.bfloat16), text_pooled], axis=-1)
    cond_full = lax.all_gather(
        condproj_weight.astype(jnp.bfloat16), ("rows", "cols"), axis=1, tiled=True
    )
    pre_cond = jnp.einsum("nabk,kf->nabf", joined, cond_full, preferred_element_type=jnp.float32)
    cond_low = jax.nn.silu(pre_cond).astype(jnp.bfloat16)
    film_all = jnp.einsum("nabk,kf->nabf", cond_low, film_full, preferred_element_type=jnp.float32)
    offsets = [0, C1, 2 * C1, 3 * C1, 4 * C1, 4 * C1 + C2, 4 * C1 + 2 * C2, 5 * C1 + 2 * C2]

    def norm_part(index, which):
        return normparams_weight[which, offsets[index] : offsets[index + 1]]

    def block_gains(index):
        return (
            norm_part(2 * index, 0),
            norm_part(2 * index, 1),
            norm_part(2 * index + 1, 0),
            norm_part(2 * index + 1, 1),
        )

    def block_film(index):
        base = (0, 2 * C1, 4 * C1)[index]
        width = (C1, C1, C2)[index]
        return (film_all[..., base : base + width], film_all[..., base + width : base + 2 * width])

    masks_one = tap_masks(rows_one, cols_one, SLOT)
    masks_two = tap_masks(rows_one // 2, cols_one // 2, SLOT // 2)
    edge_low = edgeconv_weight.astype(jnp.bfloat16)
    inconv_low = jnp.swapaxes(edge_low[:, :, 0:6], 1, 2)
    head_low = edge_low[:, :, 6:9]
    rim_in = pad_rim(image_pair)
    hidden = conv_taps(rim_in, inconv_low, masks_one, 1)
    kept_blocks = []
    for index in range(2):
        hidden, kept = block_forward(
            hidden,
            (low_convs[2 * index], low_convs[2 * index + 1]),
            block_gains(index),
            block_film(index),
            level_full,
            masks_one,
        )
        kept_blocks.append(kept)
    rim_skip = pad_rim(hidden.astype(jnp.bfloat16))
    deep, kept_deep = block_forward(
        conv_taps(rim_skip, down_conv, masks_one, 2),
        (high_convs[0], high_convs[1]),
        block_gains(2),
        block_film(2),
        level_half,
        masks_two,
    )
    upsampled = jnp.repeat(jnp.repeat(deep.astype(jnp.bfloat16), 2, axis=1), 2, axis=2)
    rim_up = pad_rim(upsampled)
    merged = conv_taps(rim_up, up_conv, masks_one, 1) + hidden
    pre_head, kept_head = norm_forward(
        merged, norm_part(6, 0), norm_part(6, 1), None, None, level_full
    )
    rim_head = pad_rim(jax.nn.silu(pre_head).astype(jnp.bfloat16))
    pred = conv_taps(rim_head, head_low, masks_one, 1)
    live_slots = slot_live.astype(jnp.float32)
    live = to_pixels(live_slots[..., None], level_full)
    count = 3.0 * jnp.sum(live_slots * level_full[2][None, :, :])
    diff = pred - noise_target
    loss_local = jnp.sum(live * diff * diff)
    grad_pred = (2.0 * live * diff / count).astype(jnp.bfloat16)
    grad_head = conv_weight_grad(rim_head, grad_pred, masks_one, 1)
    grad_act = conv_input_grad(grad_pred, head_low, masks_one, 1) * silu_grad(pre_head)
    grad_merged, head_gain, head_bias, _ = norm_backward(
        grad_act, kept_head, norm_part(6, 0), level_full
    )
    merged_low = grad_merged.astype(jnp.bfloat16)
    grad_upconv = conv_weight_grad(rim_up, merged_low, masks_one, 1)
    grad_up = conv_input_grad(merged_low, up_conv, masks_one, 1)
    grad_deep = grad_up.reshape(canvases, rows_one // 2, 2, cols_one // 2, 2, C2).sum(axis=(2, 4))
    grad_down, deep_convs, deep_norms, deep_film = block_backward(
        grad_deep, (high_convs[0], high_convs[1]), block_gains(2), kept_deep, level_half, masks_two
    )
    down_low = grad_down.astype(jnp.bfloat16)
    grad_downconv = conv_weight_grad(rim_skip, down_low, masks_one, 2)
    grad_hidden = grad_merged + conv_input_grad(down_low, down_conv, masks_one, 2)
    block_convs = [None, None]
    block_norms = [None, None]
    block_films = [None, None]
    for index in (1, 0):
        grad_hidden, block_convs[index], block_norms[index], block_films[index] = block_backward(
            grad_hidden,
            (low_convs[2 * index], low_convs[2 * index + 1]),
            block_gains(index),
            kept_blocks[index],
            level_full,
            masks_one,
        )
    hidden_low = grad_hidden.astype(jnp.bfloat16)
    grad_inconv = conv_weight_grad(rim_in, hidden_low, masks_one, 1)
    image_grad = conv_input_grad(hidden_low, inconv_low, masks_one, 1) * count
    all_norms = block_norms + [deep_norms]
    gain_vector = jnp.concatenate([part[k] for part in all_norms for k in (0, 2)] + [head_gain])
    bias_vector = jnp.concatenate([part[k] for part in all_norms for k in (1, 3)] + [head_bias])
    film_grads = jnp.concatenate([block_films[0], block_films[1], deep_film], axis=-1)
    edge_local = jnp.concatenate([jnp.swapaxes(grad_inconv, 1, 2), grad_head], axis=2)
    film_sum, edge_sum, norm_sum, loss_sum = lax.psum(
        (film_grads, edge_local, jnp.stack([gain_vector, bias_vector]), loss_local),
        ("rows", "cols"),
    )
    grad_film_full = jnp.einsum(
        "nabk,nabf->kf", cond_low.astype(jnp.float32), film_sum, precision=HIGH
    )
    grad_cond = jnp.einsum(
        "nabf,kf->nabk", film_sum, film_full.astype(jnp.float32), precision=HIGH
    ) * silu_grad(pre_cond)
    grad_cond_full = jnp.einsum(
        "nabk,nabf->kf", joined.astype(jnp.float32), grad_cond, precision=HIGH
    )
    film_rows, film_cols = filmproj_weight.shape
    film_own = lax.dynamic_slice_in_dim(
        grad_film_full, lax.axis_index("rows") * film_rows, film_rows, 0
    )
    film_own = lax.dynamic_slice_in_dim(film_own, lax.axis_index("cols") * film_cols, film_cols, 1)
    cond_cols = condproj_weight.shape[1]
    cond_own = lax.dynamic_slice_in_dim(
        grad_cond_full, lax.axis_index(("rows", "cols")) * cond_cols, cond_cols, 1
    )
    by_cols = (
        lax.psum_scatter(
            jnp.stack(
                [block_convs[0][0], block_convs[0][1], block_convs[1][0], block_convs[1][1]]
            ).astype(jnp.bfloat16),
            "cols",
            scatter_dimension=3,
            tiled=True,
        ).astype(jnp.float32),
        lax.psum_scatter(
            jnp.stack([deep_convs[0], deep_convs[1]]).astype(jnp.bfloat16),
            "cols",
            scatter_dimension=3,
            tiled=True,
        ).astype(jnp.float32),
        lax.psum_scatter(
            grad_downconv.astype(jnp.bfloat16), "cols", scatter_dimension=2, tiled=True
        ).astype(jnp.float32),
        lax.psum_scatter(
            grad_upconv.astype(jnp.bfloat16), "cols", scatter_dimension=2, tiled=True
        ).astype(jnp.float32),
    )
    lowconv_own, highconv_own, downconv_own, upconv_own = (
        lax.psum_scatter(
            by_cols[0].astype(jnp.bfloat16), "rows", scatter_dimension=2, tiled=True
        ).astype(jnp.float32),
        lax.psum_scatter(
            by_cols[1].astype(jnp.bfloat16), "rows", scatter_dimension=2, tiled=True
        ).astype(jnp.float32),
        lax.psum_scatter(
            by_cols[2].astype(jnp.bfloat16), "rows", scatter_dimension=1, tiled=True
        ).astype(jnp.float32),
        lax.psum_scatter(
            by_cols[3].astype(jnp.bfloat16), "rows", scatter_dimension=1, tiled=True
        ).astype(jnp.float32),
    )
    weights = (
        edgeconv_weight,
        convlow_weight,
        convhigh_weight,
        downconv_weight,
        upconv_weight,
        condproj_weight,
        filmproj_weight,
        normparams_weight,
    )
    firsts = (
        edgeconv_first,
        convlow_first,
        convhigh_first,
        downconv_first,
        upconv_first,
        condproj_first,
        filmproj_first,
        normparams_first,
    )
    seconds = (
        edgeconv_second,
        convlow_second,
        convhigh_second,
        downconv_second,
        upconv_second,
        condproj_second,
        filmproj_second,
        normparams_second,
    )
    grads = (
        edge_sum,
        lowconv_own,
        highconv_own,
        downconv_own,
        upconv_own,
        cond_own,
        film_own,
        norm_sum,
    )
    sharded = (1, 2, 3, 4, 5, 6)
    stacked = (1, 2)
    owned_sq = sum((jnp.sum(grads[k] * grads[k]) for k in sharded))
    shared_sq = sum((jnp.sum(grads[k] * grads[k]) for k in range(8) if k not in sharded))
    clip_norm = jnp.sqrt(lax.psum(owned_sq, ("rows", "cols")) + shared_sq)
    factor = jnp.minimum(1.0, CLIP_AT / clip_norm)
    clipped, moments, updates = ([], [], [])
    for k in range(8):
        grad = grads[k] * factor
        first_new = BETA_ONE * firsts[k] + (1.0 - BETA_ONE) * grad
        second_new = BETA_TWO * seconds[k] + (1.0 - BETA_TWO) * grad * grad
        first_hat = first_new / (1.0 - BETA_ONE**STEP)
        second_hat = second_new / (1.0 - BETA_TWO**STEP)
        clipped.append(grad)
        moments.append(second_new)
        updates.append(first_hat / (jnp.sqrt(second_hat) + EPS_ADAM) + DECAY * weights[k])

    def matrix_squares(values, k):
        if k in stacked:
            return jnp.sum(values * values, axis=tuple(range(1, values.ndim)))
        return jnp.sum(values * values).reshape(1)

    weight_sq, update_sq = lax.psum(
        (
            jnp.concatenate([matrix_squares(weights[k], k) for k in sharded]),
            jnp.concatenate([matrix_squares(updates[k], k) for k in sharded]),
        ),
        ("rows", "cols"),
    )
    ratios = jnp.sqrt(weight_sq) / jnp.sqrt(update_sq)
    position = 0
    results = []
    for k in range(8):
        if k in sharded:
            span = weights[k].shape[0] if k in stacked else 1
            ratio = ratios[position : position + span]
            position += span
            ratio = (
                ratio.reshape((span,) + (1,) * (weights[k].ndim - 1)) if k in stacked else ratio[0]
            )
        elif k == 0:
            part = (jnp.arange(9) < 6)[None, None, :]
            other = jnp.logical_not(part)
            weight_sq_two = weights[k] * weights[k]
            update_sq_two = updates[k] * updates[k]
            ratio_in = jnp.sqrt(jnp.sum(jnp.where(part, weight_sq_two, 0.0))) / jnp.sqrt(
                jnp.sum(jnp.where(part, update_sq_two, 0.0))
            )
            ratio_out = jnp.sqrt(jnp.sum(jnp.where(other, weight_sq_two, 0.0))) / jnp.sqrt(
                jnp.sum(jnp.where(other, update_sq_two, 0.0))
            )
            ratio = jnp.where(part, ratio_in, ratio_out)
        else:
            ratio = jnp.sqrt(jnp.sum(weights[k] * weights[k])) / jnp.sqrt(
                jnp.sum(updates[k] * updates[k])
            )
        results.extend([clipped[k], moments[k], weights[k] - RATE * ratio * updates[k]])
    return (
        results[0],
        results[1],
        results[2],
        results[3],
        results[4],
        results[5],
        results[6],
        results[7],
        results[8],
        results[9],
        results[10],
        results[11],
        results[12],
        results[13],
        results[14],
        results[15],
        results[16],
        results[17],
        results[18],
        results[19],
        results[20],
        results[21],
        results[22],
        results[23],
        loss_sum,
        count,
        clip_norm,
        image_grad,
    )


F32 = jnp.float32
BF = jnp.bfloat16
MESH = pl.DeviceIdType.MESH
NORM_AT = (0, 128, 256, 384, 512, 768, 1024, 1152)
FILM_AT = {1: 0, 3: 256, 5: 512}
ROW_OF = (0, 1, -1, 2)
COL_OF = (-1, 0, 1, 2)
N_EXCHANGE = 20


def place_of():
    rr, cc = lax.axis_index("rows"), lax.axis_index("cols")
    return rr, cc, rr // 2, lax.rem(rr, 2), cc // 2, lax.rem(cc, 2)


def device_at(z, y, x, k):
    return {"rows": z * 2 + y, "cols": x * 2 + k}


def device_no(d):
    return {"rows": d // 4, "cols": lax.rem(d, 4)}


def meet_all(me, count=32):
    barrier = pltpu.get_barrier_semaphore()

    def hello(d, carry):
        @pl.when(d != me)
        def _():
            pl.semaphore_signal(barrier, inc=1, device_id=device_no(d), device_id_type=MESH)

        return carry

    lax.fori_loop(0, count, hello, 0)
    pl.semaphore_wait(barrier, count - 1)


def strip_at(r, c):
    pair = lax.rem((r + 1) // 2, 4)
    return (pair * 2 + c // 2) * 4 + lax.rem(c, 2) * 2 + lax.rem(r + 1, 2)


def strip_of(d):
    rr, cc = d // 4, lax.rem(d, 4)
    pair, core = rr // 2, lax.rem(cc, 2)
    r = jnp.where(pair == 0, 7 * (1 - core), 2 * pair - 1 + core)
    return r, lax.rem(rr, 2) * 2 + cc // 2


def slots_of(d):
    r, c = strip_of(d)
    row = (r + 1) // 2
    return row * 5 + c + 1, row * 5 + lax.rem(c + 1, 4)


def lane_tables():
    low = np.zeros((512, 512), np.float32)
    high = np.zeros((512, 512), np.float32)
    rest = np.zeros((512, 512), np.float32)
    for lane in range(512):
        c, q = lane // 128, lane % 128
        low[lane, (q // 32) * 128 + c * 32 + q % 32] = 1.0
        high[lane, (q // 64) * 256 + c * 64 + q % 64] = 1.0
        to = c * 64 + q if q < 64 else (256 if q < 96 else 384) + c * 32 + q % 32
        rest[lane, to] = 1.0
    return np.stack([low, rest, high])


def place_lanes(x, at, width=128):
    n = x.shape[1]
    one = (
        lax.broadcasted_iota(jnp.int32, (n, width), 0) + at
        == lax.broadcasted_iota(jnp.int32, (n, width), 1)
    )
    return jnp.dot(x, jnp.where(one, 1.0, 0.0).astype(x.dtype), preferred_element_type=F32)


ALL_ROWS = 576
LOW, REST, HIGH_PART = range(3)
ROWS_OF = ((0, 144), (144, 288), (288, 576))
BIG = 1
GATHER_ROWS = ((0, 144), (144, 576))
Z_ORDER = (0, 1, -1, 2, -2, 3, -3)


NORM_ROW = 81
LOSS_ROW = 99


def lane_value(pairs):
    lane = lax.broadcasted_iota(jnp.int32, (8, 128), 1)
    total = jnp.zeros((8, 128), F32)
    for at, value in pairs:
        total = total + jnp.where(lane == at, value, 0.0)
    return total


def square_sum(x):
    x = x * x
    while x.ndim > 2:
        x = jnp.sum(x, axis=0)
    return jnp.sum(jnp.sum(x, axis=0, keepdims=True), axis=1, keepdims=True)


def silu_grad_tanh(v):
    s = 0.5 * jnp.tanh(0.5 * v) + 0.5
    return s * (1.0 + v * (1.0 - s))


def lamb_update(weight, first, second, grad):
    first_new = BETA_ONE * first + (1.0 - BETA_ONE) * grad
    second_new = BETA_TWO * second + (1.0 - BETA_TWO) * grad * grad
    first_hat = first_new / (1.0 - BETA_ONE**STEP)
    second_hat = second_new / (1.0 - BETA_TWO**STEP)
    return second_new, first_hat / (jnp.sqrt(second_hat) + EPS_ADAM) + DECAY * weight


LAST_ORDER = (5, 1, 2, 4, 3, 6, 0, 7)


def last_kernel(*refs):
    scalars_ref, back_ref = refs[:2]
    far, outs, (small_out, image_out) = refs[2:34], refs[34:58], refs[58:60]
    near, made = refs[60:92], refs[92:116]
    pixel_ref, load_sem, store_sem = refs[116:]

    def load(n, kind):
        at = 4 * n + kind
        return pltpu.make_async_copy(far[at], near[at], load_sem.at[at])

    for n in LAST_ORDER:
        for kind in range(4):
            load(n, kind).start()

    column = lax.broadcasted_iota(jnp.int32, (64, 128), 1)
    row_no = lax.broadcasted_iota(jnp.int32, (64, 128), 0)
    pixel = jnp.bitwise_and(column, 63)
    pick = jnp.where(pixel == 2 * (row_no - 16) + lax.shift_right_logical(column, 6), 1.0, 0.0)
    for i in range(16):
        for side in range(2):
            pixel_ref[24 * i : 24 * i + 24, 32 * side : 32 * side + 32] = back_ref[
                side, :, 32 * i : 32 * i + 32
            ]
    wide = jnp.dot(pixel_ref[...], pick, precision=HIGH, preferred_element_type=F32)
    row_no = lax.broadcasted_iota(jnp.int32, (192, 384), 0)
    h = jnp.bitwise_and(row_no, 31)
    source = (
        lax.shift_right_logical(h, 1) * 24
        + jnp.bitwise_and(h, 1) * 6
        + lax.shift_right_logical(row_no, 5)
    )
    at_row = lax.broadcasted_iota(jnp.int32, (192, 384), 1)
    total = None
    for cp in range(2):
        pick = jnp.where(at_row == source + 12 * cp, 1.0, 0.0)
        term = jnp.dot(
            pick, wide[:, 64 * cp : 64 * cp + 64], precision=HIGH, preferred_element_type=F32
        )
        total = term if total is None else total + term
    image_out[...] = total.reshape(6, 32, 64)

    scalars = scalars_ref[...]
    factor = scalars[8:9, 0:1]
    small_out[...] = scalars[8:16]

    def root_ratio(a, b):
        return RATE * jnp.sqrt(a) / jnp.sqrt(b)

    def like(ratio, v):
        return ratio.reshape((1,) * v.ndim)

    spot_of = (None, 0, 4, 6, 7, 8, 9, None)
    stores = []
    for n in LAST_ORDER:
        for kind in range(4):
            load(n, kind).wait()
        grad_ref, weight_ref, first_ref, second_ref = near[4 * n : 4 * n + 4]
        grad_out, moment_out, new_out = made[3 * n : 3 * n + 3]
        weight = weight_ref[...]
        grad = grad_ref[...] * like(factor, weight)
        second_new, update = lamb_update(weight, first_ref[...], second_ref[...], grad)
        grad_out[...] = grad
        moment_out[...] = second_new
        if n == 0:
            for lo, hi in ((0, 6), (6, 9)):
                w, u = weight[:, lo:hi, :], update[:, lo:hi, :]
                new_out[:, lo:hi, :] = w - like(root_ratio(square_sum(w), square_sum(u)), w) * u
        elif n == 7:
            new_out[...] = weight - root_ratio(square_sum(weight), square_sum(update)) * update
        else:
            for j in range(weight.shape[0] if n < 3 else 1):
                s = spot_of[n] + j
                ratio = root_ratio(scalars[0:1, s : s + 1], scalars[0:1, 64 + s : 65 + s])
                if n < 3:
                    new_out[j] = weight[j] - like(ratio, weight[j]) * update[j]
                else:
                    new_out[...] = weight - like(ratio, weight) * update
        for kind in range(3):
            at = 3 * n + kind
            copy = pltpu.make_async_copy(made[at], outs[at], store_sem.at[at])
            copy.start()
            stores.append(copy)
    for copy in stores:
        copy.wait()


def last(scalars, back, grads, state):
    def shape(a):
        return jax.ShapeDtypeStruct(a.shape, F32)

    far = []
    for n in range(8):
        far += [grads[n], *state[3 * n : 3 * n + 3]]
    outs = [shape(a) for a in state]
    small = [jax.ShapeDtypeStruct((8, 128), F32), jax.ShapeDtypeStruct((6, 32, 64), F32)]
    vmem = pl.BlockSpec(memory_space=pltpu.VMEM)
    away = pl.BlockSpec(memory_space=pltpu.HBM)
    return pl.pallas_call(
        last_kernel,
        out_shape=tuple(outs + small),
        in_specs=[vmem] * 2 + [away] * 32,
        out_specs=[away] * 24 + [vmem] * 2,
        scratch_shapes=[pltpu.VMEM(a.shape, F32) for a in far]
        + [pltpu.VMEM(a.shape, F32) for a in state]
        + [
            pltpu.VMEM((384, 64), F32),
            pltpu.SemaphoreType.DMA((32,)),
            pltpu.SemaphoreType.DMA((24,)),
        ],
        compiler_params=pltpu.CompilerParams(vmem_limit_bytes=60 * 1024 * 1024),
        name="last",
    )(scalars, back, *far)


def step_kernel(*refs):
    live_ref, temb_ref, image_ref, target_ref = refs[:4]
    far, outs = refs[4:30], refs[30:38]
    scalars_out, back_out = refs[38:40]
    near, made = refs[40:66], refs[66:74]
    (
        low_ref,
        high_ref,
        down_ref,
        up_ref,
        full_ref,
        half_ref,
        work_ref,
        grad_ref,
        wide_ref,
        thin_ref,
        act_ref,
        acth_ref,
        turn_ref,
        wc_ref,
        wr_ref,
        wu_ref,
        wut_ref,
        wd_ref,
        coef_ref,
        rows_ref,
        patch_ref,
        ext_ref,
        send_ref,
        recv_ref,
        img_ref,
        tgt_ref,
        dwi_ref,
        dwh_ref,
        ngrad_ref,
        fgrad_ref,
        part_ref,
    part4_ref,
        imgrad_ref,
        wi_ref,
        wht_ref,
        wit_ref,
        wh_ref,
        tmp_ref,
        all_ref,
        block_ref,
        strips_ref,
        planes_ref,
        cbuf_ref,
        csend_ref,
        cpart_ref,
        fsend_ref,
        frecv_ref,
        film_ref,
        joined_ref,
        condv_ref,
        rb_ref,
        rx_ref,
        ry_ref,
        rz_ref,
        own_ref,
        m1_ref,
        r1_ref,
        m2_ref,
        r2_ref,
        m3_ref,
        r3_ref,
        gcs_ref,
        gcr_ref,
        fsum_ref,
        total_ref,
        back_ref,
        send_sem,
        recv_sem,
        load_sem,
        store_sem,
        g_send,
        g_recv,
        strip_send,
        strip_recv,
        cond_send,
        cond_recv,
        film_send,
        film_recv,
        core_send,
        core_recv,
        x_send,
        x_recv,
        y_send,
        y_recv,
        z_send,
        z_recv,
        m_send,
        m_recv,
        gc_send,
        gc_recv,
        back_send,
        back_recv,
    ) = refs[74:]
    lanes_ref, text_ref = near[:2]
    weights, firsts, seconds = near[2::3], near[3::3], near[4::3]
    edge_ref, norm_ref = weights[0], weights[7]
    dlow_ref, dhigh_ref, ddown_ref, dup_ref = low_ref, high_ref, down_ref, up_ref
    sb_ref = all_ref
    rr, cc, z, y, x, co = place_of()
    me = rr * 4 + cc
    core = co
    partner = 1 - co + 2 * x
    halo = rr >= 2
    split = jnp.logical_and(lax.rem(rr, 2) == 1, cc >= 2)

    def flag(cond):
        return jnp.where(cond, 1.0, 0.0).astype(F32)

    f_halo = flag(halo)
    f_core1 = flag(core == 1)
    f_core0 = 1.0 - f_core1
    f_top = f_halo * f_core1
    f_bot = f_halo * f_core0
    f_split = flag(split)
    f_joined = 1.0 - f_split

    place = lax.broadcasted_iota(jnp.int32, (32, 256), 0)
    lo_mask = jnp.where(place == 0, 0.0, jnp.where(place == 16, f_joined, 1.0))
    hi_mask = jnp.where(place == 31, 0.0, jnp.where(place == 15, f_joined, 1.0))

    def before(x):
        return pltpu.roll(x, 1, 0) * lo_mask

    def after(x):
        return pltpu.roll(x, 31, 0) * hi_mask

    def at(i):
        return pl.ds(pl.multiple_of(i * 32, 32), 32)

    def loop(body, init=0, count=16):
        return lax.fori_loop(0, count, body, init, unroll=16)

    def dot(a, b):
        return jnp.dot(a, b, preferred_element_type=F32)

    def dot_nt(a, b):
        return lax.dot_general(a, b, (((1,), (1,)), ((), ())), preferred_element_type=F32)

    def sigmoid(z):
        return 0.5 * jnp.tanh(0.5 * z) + 0.5

    def double(v):
        return jnp.concatenate([v, v], axis=1)


    def copy_of(e):
        return pltpu.make_async_remote_copy(
            src_ref=send_ref.at[e],
            dst_ref=recv_ref.at[e],
            send_sem=send_sem.at[e],
            recv_sem=recv_sem.at[e],
            device_id={"cols": partner},
            device_id_type=MESH,
        )

    def send(e, row, stats=None):
        send_ref[e, 0:32, :] = row
        send_ref[e, 32:40, :] = jnp.zeros((8, 256), F32) if stats is None else stats
        copy_of(e).start()

    def arrive(e):
        copy_of(e).wait()

    def edge_full(ref):
        low = f_core0 * ref[0, 480:512, 128:256] + f_core1 * ref[0, 0:32, 0:128]
        high = f_core0 * ref[1, 480:512, 128:256] + f_core1 * ref[1, 0:32, 0:128]
        return jnp.concatenate([low, high], axis=1)

    def edge_cell(ref):
        return f_core0 * ref[480:512, :] + f_core1 * ref[0:32, :]

    def edge(ref, planes):
        return edge_full(ref) if planes == 2 else edge_cell(ref.at[0])


    def halves(x):
        return x[0:8] + x[8:16], x[16:24] + x[24:32]

    def gathered(sums, planes):
        rows = []
        for s in sums:
            row = jnp.sum(s, axis=0, keepdims=True)
            rows.append(double(row[:, 0:128] + row[:, 128:256]) if planes == 2 else row)
        return jnp.concatenate(rows + [jnp.zeros((4, 256), F32)], axis=0)

    zero8 = jnp.zeros((8, 256), F32)

    def stats_of(x_ref, planes):
        def body(i, carry):
            s_l, s_r, q_l, q_r = carry
            for p in range(planes):
                x = x_ref[p, at(i), :]
                a, b = halves(x)
                c, d = halves(x * x)
                s_l, s_r, q_l, q_r = s_l + a, s_r + b, q_l + c, q_r + d
            return s_l, s_r, q_l, q_r

        return gathered(loop(body, (zero8,) * 4), planes)

    def over_slot(block, planes):
        swapped = jnp.concatenate(
            [block[1:2], block[0:1], block[3:4], block[2:3], block[4:8]], axis=0
        )
        x = block + f_joined * swapped
        lane = lax.broadcasted_iota(jnp.int32, (8, 256), 1)
        step = 1
        while step < (4 if planes == 2 else 8):
            up = pltpu.roll(x, 256 - step, 1)
            down = pltpu.roll(x, step, 1)
            x = x + jnp.where(lax.rem(lane, 2 * step) < step, up, down)
            step *= 2
        size = 16.0 if planes == 2 else 8.0
        count = (16.0 + 16.0 * f_halo) * (16.0 + 16.0 * f_joined) * size
        return x / count

    def spread(two):
        return jnp.concatenate(
            [
                jnp.broadcast_to(two[0:1], (16, 256)),
                jnp.broadcast_to(two[1:2], (16, 256)),
            ],
            axis=0,
        )

    def norm_row(k, which):
        width = NORM_AT[k + 1] - NORM_AT[k] if k < 6 else 128
        row = norm_ref[which : which + 1, NORM_AT[k] : NORM_AT[k] + width]
        return double(row) if width == 128 else row

    def film_rows(k, which):
        if k not in FILM_AT:
            return jnp.zeros((2, 256), F32)
        width = 256 if k == 5 else 128
        base = FILM_AT[k] + which * width
        two = film_ref[0:2, base : base + width]
        return double(two) if width == 128 else two

    def norm_ready(k, stats, e, planes):
        total = over_slot(stats + f_halo * recv_ref[e, 32:40, :], planes)
        mean = total[0:2]
        var = total[2:4] - mean * mean
        inverse = lax.rsqrt(var + EPS_NORM)
        gain, bias = norm_row(k, 0), norm_row(k, 1)
        factor = 1.0 + film_rows(k, 0)
        slope = inverse * gain * factor
        coef_ref[k, 0] = spread(slope)
        coef_ref[k, 1] = spread((bias - mean * inverse * gain) * factor + film_rows(k, 1))
        coef_ref[k, 2] = spread(mean)
        coef_ref[k, 3] = spread(inverse)
        rows_ref[k, 0:2, :] = mean
        rows_ref[k, 2:4, :] = inverse

    def activated(x, k):
        z = x * coef_ref[k, 0] + coef_ref[k, 1]
        return z * sigmoid(z)


    def put_wide(i, even, odd):
        for t, g in enumerate((before(odd), even, odd, after(even))):
            b = g.astype(BF)
            wide_ref[at(i + 1), 512 * t : 512 * t + 256] = b
            wide_ref[at(i + 2), 512 * t + 256 : 512 * t + 384] = b[:, 128:256]
            wide_ref[at(i), 512 * t + 384 : 512 * t + 512] = b[:, 0:128]

    def put_wide_edge(row):
        even, odd = row[:, 0:128], row[:, 128:256]
        lo, hi = lo_mask[:, 0:128], hi_mask[:, 0:128]
        for t, g in enumerate((pltpu.roll(odd, 1, 0) * lo, even, odd, pltpu.roll(even, 31, 0) * hi)):
            wide_ref[32:64, 512 * t + 256 : 512 * t + 384] = (g * f_top).astype(BF)
            wide_ref[512:544, 512 * t + 384 : 512 * t + 512] = (g * f_bot).astype(BF)

    def put_thin(i, x):
        for t, g in enumerate((before(x), x, after(x))):
            thin_ref[at(i + 1), 256 * t : 256 * t + 256] = g.astype(BF)

    def put_thin_edge(row):
        for t, g in enumerate((before(row), row, after(row))):
            thin_ref[0:32, 256 * t : 256 * t + 256] = (g * f_top).astype(BF)
            thin_ref[544:576, 256 * t : 256 * t + 256] = (g * f_bot).astype(BF)

    def keep_wide(slot):
        act_ref[slot, 0] = wide_ref[32:544, 512:768]
        act_ref[slot, 1] = wide_ref[32:544, 1024:1280]

    def keep_thin(slot):
        acth_ref[slot] = thin_ref[32:544, 256:512]

    def turn_wide(slot):
        turn_ref[0:256, :] = act_ref[slot, 0].T
        turn_ref[256:512, :] = act_ref[slot, 1].T


    def load_wc(index):
        for b in range(3):
            for r in range(4):
                for rp in range(2):
                    a = ROW_OF[r] - rp + 1
                    if 0 <= a <= 2:
                        wc_ref[
                            b * 512 + r * 128 : b * 512 + r * 128 + 128, rp * 128 : rp * 128 + 128
                        ] = low_ref[index, 3 * a + b]

    def load_wr(index):
        for b in range(3):
            for r in range(4):
                for rp in range(2):
                    a = ROW_OF[r] - rp + 1
                    if 0 <= a <= 2:
                        wr_ref[
                            rp * 128 : rp * 128 + 128, b * 512 + r * 128 : b * 512 + r * 128 + 128
                        ] = low_ref[index, 8 - 3 * a - b]

    def taps_of(parity, d):
        if parity == 0:
            return {-1: (0,), 0: (1, 2)}.get(d, ())
        return {0: (0, 1), 1: (2,)}.get(d, ())

    def load_up():
        for cp in range(2):
            for rp in range(2):
                for di in (-1, 0, 1):
                    for dj in (-1, 0, 1):
                        taps = [3 * a + b for a in taps_of(rp, di) for b in taps_of(cp, dj)]
                        if not taps:
                            continue
                        total = up_ref[taps[0]].astype(F32)
                        for t in taps[1:]:
                            total = total + up_ref[t].astype(F32)
                        low = total.astype(BF)
                        at_k = (dj + 1 - cp) * 256
                        wu_ref[cp, di + 1, at_k : at_k + 256, rp * 128 : rp * 128 + 128] = low
                        row = ROW_OF.index(rp - 2 * di)
                        col = COL_OF.index(cp - 2 * dj)
                        wut_ref[:, col * 512 + row * 128 : col * 512 + row * 128 + 128] = low

    def load_down():
        for b in range(3):
            for r in range(3):
                a = ROW_OF[r] + 1
                wd_ref[b * 512 + r * 128 : b * 512 + r * 128 + 128, :] = down_ref[3 * a + b]


    def conv_low(out, weight_nt=False):
        for cp in range(2):
            left = wide_ref[32:544, cp * 512 : cp * 512 + 1536]
            out(cp, dot_nt(left, wr_ref[...]) if weight_nt else dot(left, wc_ref[...]))

    def conv_high(index):
        total = None
        for a in range(3):
            term = dot(
                thin_ref[32 * a : 32 * a + 512, :],
                high_ref[index, 3 * a : 3 * a + 3].reshape(768, 256),
            )
            total = term if total is None else total + term
        return total

    def conv_high_back(index):
        total = None
        for a in range(3):
            for b in range(3):
                term = dot_nt(
                    thin_ref[32 * a : 32 * a + 512, b * 256 : b * 256 + 256],
                    high_ref[index, 8 - 3 * a - b],
                )
                total = term if total is None else total + term
        return total

    def grad_low(index, slot):
        turn_wide(slot)
        for b in range(3):
            block = dot(turn_ref[0:256, :], wide_ref[32:544, b * 512 : b * 512 + 512]) + dot(
                turn_ref[256:512, :], wide_ref[32:544, b * 512 + 512 : b * 512 + 1024]
            )
            for a in range(3):
                first = ROW_OF.index(a - 1) * 128
                second = ROW_OF.index(a) * 128
                dlow_ref[index, 8 - 3 * a - b] = (
                    block[0:128, first : first + 128] + block[128:256, second : second + 128]
                ).astype(dlow_ref.dtype)

    def grad_high(index, slot):
        turn_ref[0:256, :] = acth_ref[slot].T
        for a in range(3):
            block = dot(turn_ref[0:256, :], thin_ref[32 * a : 32 * a + 512, :])
            for b in range(3):
                dhigh_ref[index, 8 - 3 * a - b] = block[:, b * 256 : b * 256 + 256].astype(
                    dhigh_ref.dtype
                )


    def put_patch(slot, source, row, lanes):
        ext_ref[0:32, :] = row * f_top
        ext_ref[544:576, :] = row * f_bot

        def fill(i, carry):
            ext_ref[at(i + 1), :] = source[at(i), :]
            return carry

        loop(fill)

        def body(i, carry):
            total = None
            for di in (-1, 0, 1):
                x = ext_ref[at(i + 1 + di), :]
                for dj, g in enumerate((before(x), x, after(x))):
                    shift = ((di + 1) * 3 + dj) * lanes
                    term = pltpu.roll(g, shift, 1) if shift else g
                    total = term if total is None else total + term
            patch_ref[slot, at(i), :] = total.astype(BF)
            return carry

        loop(body)


    def norm_back_start(k, x_ref, planes):
        def body(i, carry):
            s_l, s_r, q_l, q_r = carry
            for p in range(planes):
                x = x_ref[p, at(i), :]
                z = x * coef_ref[k, 0] + coef_ref[k, 1]
                s = sigmoid(z)
                d = work_ref[p, at(i), :] * (s * (1.0 + z * (1.0 - s)))
                work_ref[p, at(i), :] = d
                a, b = halves(d)
                c, e = halves(d * ((x - coef_ref[k, 2]) * coef_ref[k, 3]))
                s_l, s_r, q_l, q_r = s_l + a, s_r + b, q_l + c, q_r + e
            return s_l, s_r, q_l, q_r

        return gathered(loop(body, (zero8,) * 4), planes)

    def norm_back_ready(k, stats, e, planes):
        gain, bias = norm_row(k, 0), norm_row(k, 1)
        factor = 1.0 + film_rows(k, 0)
        width = 128 if planes == 2 else 256
        one, two = stats[0:2], stats[2:4]
        dgain, dbias = factor * two, factor * one
        o = NORM_AT[k]
        ngrad_ref[0:1, o : o + width] = (dgain[0:1] + dgain[1:2])[:, 0:width]
        ngrad_ref[1:2, o : o + width] = (dbias[0:1] + dbias[1:2])[:, 0:width]
        if k in FILM_AT:
            f = FILM_AT[k]
            fgrad_ref[0:2, f : f + width] = (gain * two + bias * one)[:, 0:width]
            fgrad_ref[0:2, f + width : f + 2 * width] = one[:, 0:width]
        both = stats + f_halo * recv_ref[e, 32:40, :]
        kk = gain * factor
        scaled = jnp.concatenate([kk * both[0:2], kk * both[2:4], both[4:8]], axis=0)
        total = over_slot(scaled, planes)
        mean, inverse = rows_ref[k, 0:2, :], rows_ref[k, 2:4, :]
        second = -inverse * inverse * total[2:4]
        third = -inverse * total[0:2] - mean * second
        coef_ref[k, 4] = spread(inverse * kk)
        coef_ref[k, 5] = spread(second)
        coef_ref[k, 6] = spread(third)

    def back_value(k, d, x):
        return d * coef_ref[k, 4] + x * coef_ref[k, 5] + coef_ref[k, 6]


    def shard(kind, part, zs, ys, xs, ks, device):
        rows = slice(*GATHER_ROWS[part])
        return pltpu.make_async_remote_copy(
            src_ref=all_ref.at[zs, ys, xs, ks, rows],
            dst_ref=all_ref.at[zs, ys, xs, ks, rows],
            send_sem=g_send.at[part, kind, zs, ys, xs],
            recv_sem=g_recv.at[part, zs, ys, xs, ks],
            device_id=device,
            device_id_type=MESH,
        )

    def to_z(part, zd):
        return shard(zd, part, z, y, x, co, device_at(zd, y, x, co))

    def to_x(part, zs, ys):
        return shard(4, part, zs, ys, x, co, device_at(z, y, 1 - x, co))

    def to_y(part, zs, xs):
        return shard(5, part, zs, y, xs, co, device_at(z, 1 - y, x, co))

    def to_core(part, zs, ys, xs):
        return shard(6, part, zs, ys, xs, co, device_at(z, y, x, 1 - co))

    def arrived(part, zs, ys, xs, ks=co):
        shard(6, part, zs, ys, xs, ks, device_at(z, y, x, 1 - co)).wait_recv()

    def start(copy):
        copy.start()

    def in_line(dz, act):
        zs = z + dz

        @pl.when(jnp.logical_and(zs >= 0, zs <= 3))
        def _():
            act(zs)

    def gather_far(part, act=start):
        for zd in range(4):

            @pl.when(zd != z)
            def _(zd=zd):
                act(to_z(part, zd))

    def gather_near(part, act=start):
        act(to_x(part, z, y))
        act(to_y(part, z, x))
        act(to_core(part, z, y, x))

    def gather_z(part, act=start, wait=arrived):
        for dz in Z_ORDER[1:]:

            def one(zs):
                wait(part, zs, y, x)
                act(to_x(part, zs, y))
                act(to_y(part, zs, x))
                act(to_core(part, zs, y, x))

            in_line(dz, one)

    def gather_line(part, dzs, act=start, wait=arrived):
        for dz in dzs:

            def one(zs, dz=dz):
                if dz:
                    wait(part, zs, y, x)
                if dz <= 0:

                    @pl.when(z < 3)
                    def _():
                        act(shard(0, part, zs, y, x, co, device_at(z + 1, y, x, co)))

                if dz >= 0:

                    @pl.when(z > 0)
                    def _():
                        act(shard(1, part, zs, y, x, co, device_at(z - 1, y, x, co)))

                act(to_x(part, zs, y))
                act(to_y(part, zs, x))
                act(to_core(part, zs, y, x))

            in_line(dz, one)

    def gather_xy(part, act=start, wait=arrived):
        for dz in Z_ORDER:

            def one(zs):
                wait(part, zs, y, 1 - x)

                @pl.when(lax.rem(zs, 2) == 0)
                def _():
                    act(to_y(part, zs, 1 - x))

                act(to_core(part, zs, y, 1 - x))
                wait(part, zs, 1 - y, x)

                @pl.when(lax.rem(zs, 2) == 1)
                def _():
                    act(to_x(part, zs, 1 - y))

                act(to_core(part, zs, 1 - y, x))

            in_line(dz, one)

    def gather_last(part, act=start, wait=arrived):
        for dz in Z_ORDER:

            def one(zs):
                wait(part, zs, 1 - y, 1 - x)
                act(to_core(part, zs, 1 - y, 1 - x))

            in_line(dz, one)

    def gather_core(part):
        for zs in range(4):
            for ys in range(2):
                for xs in range(2):
                    arrived(part, zs, ys, xs, 1 - co)

    def gather_sent(part):
        def sent(copy):
            copy.wait_send()

        def none(*a):
            return None

        if part == LOW:
            gather_far(part, sent)
            gather_near(part, sent)
            gather_z(part, sent, none)
        else:
            gather_line(part, Z_ORDER, sent, none)
        gather_xy(part, sent, none)
        gather_last(part, sent, none)

    def row_places(r):
        def rows(at_row, size):
            return pl.ds(pl.multiple_of(at_row, 16), size)

        return rows(r * 16, 16), rows(r * 32, 32), rows(r * 32, 16), rows(r * 32 + 16, 16)

    def gather_place(part):
        rows = slice(*ROWS_OF[part])

        def row(r, carry):
            zr, yr = r // 2, lax.rem(r, 2)
            at16, at32, a16, b16 = row_places(r)
            packed = jnp.concatenate(
                [all_ref[zr, yr, c // 2, c % 2, rows, :] for c in range(4)], axis=1
            )
            v = jnp.dot(packed, lanes_ref[part], preferred_element_type=F32).astype(BF)
            if part == LOW:
                for j in range(4):
                    low_ref[j, :, at16, :] = v[:, j * 128 : j * 128 + 128].reshape(9, 16, 128)
            elif part == HIGH_PART:
                for j in range(2):
                    high_ref[j, :, at32, :] = v[:, j * 256 : j * 256 + 256].reshape(9, 32, 256)
            else:
                down_ref[:, at16, :] = v[:, 0:256].reshape(9, 16, 256)
                up_ref[:, a16, :] = v[:, 256:384].reshape(9, 16, 128)
                up_ref[:, b16, :] = v[:, 384:512].reshape(9, 16, 128)
            return carry

        lax.fori_loop(0, 8, row, 0, unroll=4)

    def pack_own(part):
        rows = slice(*ROWS_OF[part])
        own = all_ref.at[z, y, x, co]
        if part == LOW:
            total = None
            for j in range(4):
                term = place_lanes(weights[1][j].reshape(144, 32).astype(BF), 32 * j)
                total = term if total is None else total + term
        elif part == HIGH_PART:
            total = place_lanes(weights[2][0].reshape(288, 64).astype(BF), 0) + place_lanes(
                weights[2][1].reshape(288, 64).astype(BF), 64
            )
        else:
            total = (
                place_lanes(weights[3][...].reshape(144, 64).astype(BF), 0)
                + place_lanes(weights[4][:, 0:16, :].reshape(144, 32).astype(BF), 64)
                + place_lanes(weights[4][:, 16:32, :].reshape(144, 32).astype(BF), 96)
            )
        own[rows, :] = total.astype(BF)

    to_left = strip_at(rr, cc)
    to_right = strip_at(rr, lax.rem(cc + 3, 4))

    def strip_copies(side, device):
        return [
            pltpu.make_async_remote_copy(
                src_ref=block_ref.at[1 - side],
                dst_ref=strips_ref.at[side],
                send_sem=strip_send.at[side],
                recv_sem=strip_recv.at[side],
                device_id=device_no(device),
                device_id_type=MESH,
            )
        ]

    def pack_block():
        planes_ref[0:192, :] = image_ref[...].astype(F32).reshape(192, 64)
        planes_ref[192:288, :] = target_ref[...].reshape(96, 64)
        for g in range(4):
            for h in range(2):
                block_ref[h, :, 32 * g : 32 * g + 32] = planes_ref[
                    72 * g : 72 * g + 72, 32 * h : 32 * h + 32
                ]

    loads = [
        pltpu.make_async_copy(a, b, load_sem.at[n]) for n, (a, b) in enumerate(zip(far, near))
    ]
    for n in (5, 11, 14, 8, 1, 17, 0, 2, 20, 23):
        loads[n].start()
    for n in range(26):
        if n > 1 and n % 3 != 2:
            loads[n].start()


    def others(body):
        def one(d, carry):
            @pl.when(d != me)
            def _():
                body(d)

            return carry

        lax.fori_loop(0, 32, one, 0)

    def row_mates(body):
        for c in range(4):

            @pl.when(cc != c)
            def _(c=c):
                body(c)

    def cond_copy(c, source):
        return pltpu.make_async_remote_copy(
            src_ref=csend_ref,
            dst_ref=cbuf_ref.at[source],
            send_sem=cond_send.at[c],
            recv_sem=cond_recv.at[source],
            device_id={"rows": rr, "cols": c},
            device_id_type=MESH,
        )

    def film_copy(d, source):
        return pltpu.make_async_remote_copy(
            src_ref=fsend_ref.at[d],
            dst_ref=frecv_ref.at[source],
            send_sem=film_send.at[d],
            recv_sem=film_recv.at[source],
            device_id=device_no(d),
            device_id_type=MESH,
        )

    def cond_start():
        joined_ref[24:32, :] = jnp.zeros((8, joined_ref.shape[1]), F32)
        for a in range(5):
            joined_ref[5 * a : 5 * a + 5, 0:128] = temb_ref[a].astype(F32)
            joined_ref[5 * a : 5 * a + 5, 128:] = text_ref[a].astype(F32)
        own = dot_nt(joined_ref[...].astype(BF), weights[5][...].astype(BF))
        csend_ref[...] = jnp.concatenate([own, jnp.zeros((32, 112), F32)], axis=1)
        row_mates(lambda c: cond_copy(c, cc).start())
        cbuf_ref[cc] = csend_ref[...]

    def film_start():
        row_mates(lambda c: cond_copy(c, c).wait_recv())
        whole = cbuf_ref[0]
        for c in range(1, 4):
            whole = whole + pltpu.roll(cbuf_ref[c], 16 * c, 1)
        whole = whole[:, 0:64]
        cond = (whole * sigmoid(whole)).astype(BF)
        condv_ref[...] = cond.astype(F32)
        cpart_ref[...] = dot(cond, weights[6][...].astype(BF))

        def deal(d, carry):
            s_l, s_r = slots_of(d)
            for n, slot in enumerate((s_l, s_r)):
                line = cpart_ref[pl.ds(slot, 1), :]
                fsend_ref[d, 2 * n : 2 * n + 1, :] = line[:, 0:128]
                fsend_ref[d, 2 * n + 1 : 2 * n + 2, :] = line[:, 128:256]

            @pl.when(d != me)
            def _():
                film_copy(d, me).start()

            return carry

        lax.fori_loop(0, 32, deal, 0)
        frecv_ref[me] = fsend_ref[me]

    def film_ready():
        others(lambda d: film_copy(d, d).wait_recv())
        for c in range(4):
            total = frecv_ref[c]
            for r in range(1, 8):
                total = total + frecv_ref[4 * r + c]
            for n in range(4):
                at_lane = c * 256 + n % 2 * 128
                film_ref[n // 2 : n // 2 + 1, at_lane : at_lane + 128] = total[n : n + 1]


    def edge_terms():
        for a in range(3):
            for b in range(3):
                for cp in range(2):
                    for rp in range(2):
                        rho, gamma = rp + a - 1, cp + b - 1
                        cell = (rho // 2 + 1) * 3 + gamma // 2 + 1
                        phase = (gamma % 2) * 2 + rho % 2
                        tile = COL_OF.index(gamma) * 512 + ROW_OF.index(rho) * 128
                        yield 3 * a + b, cp, rp, cell, phase, tile

    def load_edges():
        dwi_ref[...] = jnp.zeros(dwi_ref.shape, F32)
        dwh_ref[...] = jnp.zeros(dwh_ref.shape, F32)
        for t, cp, rp, cell, phase, _ in edge_terms():
            lanes = slice(rp * 128, rp * 128 + 128)
            row = cell * 24 + phase * 6
            dwi_ref[cp, row : row + 6, lanes] = edge_ref[t, 0:6, :]
            row = cell * 12 + phase * 3
            dwh_ref[cp, row : row + 3, lanes] = edge_ref[8 - t, 6:9, :]
        wi_ref[...] = dwi_ref[...].astype(BF)
        wht_ref[...] = dwh_ref[...].astype(BF)
        for ref, taps, lo, size in ((wh_ref, 1, 6, 3), (wit_ref, -1, 0, 6)):
            ref[...] = jnp.zeros(ref.shape, BF)
            tmp_ref[...] = jnp.zeros(tmp_ref.shape, F32)
            for t, cp, rp, _, _, tile in edge_terms():
                row = (cp * 2 + rp) * size
                tap = t if taps > 0 else 8 - t
                tmp_ref[row : row + size, tile : tile + 128] = edge_ref[tap, lo : lo + size, :]
            ref[0:32, :] = tmp_ref[...].astype(BF)


    def add(to, b):
        to[...] = (to[...].astype(F32) + b[...].astype(F32)).astype(BF)

    def deal_pack(part, r_lo, r_hi):
        rows = slice(*ROWS_OF[part])

        def row(r, carry):
            zr, yr = r // 2, lax.rem(r, 2)
            at16, at32, a16, b16 = row_places(r)
            if part == LOW:
                pieces = [dlow_ref[j, :, at16, :].reshape(144, 128) for j in range(4)]
            elif part == HIGH_PART:
                pieces = [dhigh_ref[j, :, at32, :].reshape(288, 256) for j in range(2)]
            else:
                pieces = [
                    ddown_ref[:, at16, :].reshape(144, 256),
                    dup_ref[:, a16, :].reshape(144, 128),
                    dup_ref[:, b16, :].reshape(144, 128),
                ]
            v = dot_nt(jnp.concatenate(pieces, axis=1), lanes_ref[part]).astype(BF)
            for c in range(4):
                sb_ref[zr, yr, c // 2, c % 2, rows, :] = v[:, c * 128 : c * 128 + 128]
            return carry

        lax.fori_loop(r_lo, r_hi, row, 0, unroll=2)

    def core_copy(part, zs):
        rows = slice(*ROWS_OF[part])
        return pltpu.make_async_remote_copy(
            src_ref=sb_ref.at[zs, :, :, 1 - co, rows],
            dst_ref=rb_ref.at[zs, :, :, rows],
            send_sem=core_send.at[part, zs],
            recv_sem=core_recv.at[part, zs],
            device_id=device_at(z, y, x, 1 - co),
            device_id_type=MESH,
        )

    def first_copy(part, zs):
        rows = slice(*ROWS_OF[part])
        by_x = zs % 2 == 0
        return pltpu.make_async_remote_copy(
            src_ref=rb_ref.at[zs, :, 1 - x, rows] if by_x else rb_ref.at[zs, 1 - y, :, rows],
            dst_ref=rx_ref.at[zs, :, rows],
            send_sem=x_send.at[part, zs],
            recv_sem=x_recv.at[part, zs],
            device_id=device_at(z, y, 1 - x, co) if by_x else device_at(z, 1 - y, x, co),
            device_id_type=MESH,
        )

    def second_copy(part, zs):
        rows = slice(*ROWS_OF[part])
        by_x = zs % 2 == 1
        return pltpu.make_async_remote_copy(
            src_ref=rb_ref.at[zs, y, 1 - x, rows] if by_x else rb_ref.at[zs, 1 - y, x, rows],
            dst_ref=ry_ref.at[zs, rows],
            send_sem=y_send.at[part, zs],
            recv_sem=y_recv.at[part, zs],
            device_id=device_at(z, y, 1 - x, co) if by_x else device_at(z, 1 - y, x, co),
            device_id_type=MESH,
        )

    def z_copy(part, zs, source):
        rows = slice(*ROWS_OF[part])
        return pltpu.make_async_remote_copy(
            src_ref=rb_ref.at[zs, y, x, rows],
            dst_ref=rz_ref.at[source, rows],
            send_sem=z_send.at[part, zs],
            recv_sem=z_recv.at[part, source],
            device_id=device_at(zs, y, x, co),
            device_id_type=MESH,
        )

    def deal_core(part):
        for zs in range(4):
            deal_pack(part, 2 * zs, 2 * zs + 2)
            core_copy(part, zs).start()

    def deal_first(part):
        rows = slice(*ROWS_OF[part])
        for zs in range(4):
            core_copy(part, zs).wait_recv()
            for ys in range(2):
                for xs in range(2):
                    add(rb_ref.at[zs, ys, xs, rows], sb_ref.at[zs, ys, xs, co, rows])
            first_copy(part, zs).start()

    def deal_second(part):
        rows = slice(*ROWS_OF[part])
        for zs in range(4):
            first_copy(part, zs).wait_recv()
            for other in range(2):
                to = rb_ref.at[zs, other, x, rows] if zs % 2 == 0 else rb_ref.at[zs, y, other, rows]
                add(to, rx_ref.at[zs, other, rows])
            second_copy(part, zs).start()

    def deal_z(part):
        rows = slice(*ROWS_OF[part])
        for zs in range(4):
            second_copy(part, zs).wait_recv()
            add(rb_ref.at[zs, y, x, rows], ry_ref.at[zs, rows])

            @pl.when(zs != z)
            def _(zs=zs):
                z_copy(part, zs, z).start()

            @pl.when(zs == z)
            def _(zs=zs):
                rz_ref[zs, rows, :] = rb_ref[zs, y, x, rows, :]

    def deal_end(part):
        rows = slice(*ROWS_OF[part])
        for zs in range(4):

            @pl.when(zs != z)
            def _(zs=zs):
                z_copy(part, zs, zs).wait_recv()

        own = rz_ref[0, rows, :].astype(F32)
        for zs in range(1, 4):
            own = own + rz_ref[zs, rows, :].astype(F32)
        own_ref[rows, :] = own

    def deal_sent(part):
        for zs in range(4):
            core_copy(part, zs).wait_send()
            first_copy(part, zs).wait_send()
            second_copy(part, zs).wait_send()

            @pl.when(zs != z)
            def _(zs=zs):
                z_copy(part, zs, z).wait_send()


    pack_block()
    loads[5].wait()
    pack_own(LOW)
    meet_all(me)
    gather_far(LOW)
    gather_near(LOW)
    for copy in strip_copies(0, to_left):
        copy.start()

    @pl.when(to_right != me)
    def _():
        for copy in strip_copies(1, to_right):
            copy.start()

    loads[1].wait()
    loads[17].wait()
    cond_start()
    for n in (11, 14, 8):
        loads[n].wait()
    pack_own(REST)
    pack_own(HIGH_PART)
    gather_line(BIG, (0,))
    for n in (2, 20, 23, 0):
        loads[n].wait()
    load_edges()
    gather_z(LOW)
    gather_line(BIG, (1, -1))
    film_start()
    gather_xy(LOW)
    gather_line(BIG, (2, -2))

    live_all = jnp.concatenate([live_ref[a] for a in range(5)], axis=0).astype(F32)
    slot_r = lax.broadcasted_iota(jnp.int32, (5, 5), 0)
    slot_c = lax.broadcasted_iota(jnp.int32, (5, 5), 1)

    def side(s):
        return jnp.where(jnp.logical_or(s == 0, s == 4), 32.0, 64.0)

    def all_sum(v):
        return jnp.sum(jnp.sum(v, axis=0, keepdims=True), axis=1, keepdims=True)

    count = 3.0 * all_sum(live_all * side(slot_r) * side(slot_c))
    my_l, my_r = slots_of(me)
    slot_id = slot_r * 5 + slot_c
    live_l = all_sum(jnp.where(slot_id == my_l, live_all, 0.0))
    live_r = all_sum(jnp.where(slot_id == my_r, live_all, 0.0))

    def zero(i, carry):
        wc_ref[at(i), :] = jnp.zeros((32, 256), BF)
        return carry

    loop(zero, count=48)
    wr_ref[...] = jnp.zeros(wr_ref.shape, BF)
    for cp in range(2):
        for di in range(3):
            wu_ref[cp, di] = jnp.zeros((512, 256), BF)
    for b in range(3):
        wd_ref[b * 512 + 384 : b * 512 + 512, :] = jnp.zeros((128, 256), BF)


    for copy in strip_copies(0, to_left):
        copy.wait()

    @pl.when(to_right != me)
    def _():
        for copy in strip_copies(1, to_right):
            copy.wait()

    @pl.when(to_right == me)
    def _():
        strips_ref[1] = block_ref[0]

    for g in range(4):
        for h in range(2):
            planes_ref[72 * g : 72 * g + 72, 32 * h : 32 * h + 32] = strips_ref[
                h, :, 32 * g : 32 * g + 32
            ]
    row_no = lax.broadcasted_iota(jnp.int32, (512, 288), 0)
    item = jnp.bitwise_and(row_no, 31)
    in_image = item < 12
    item2 = jnp.where(in_image, item, item - 12)
    size = jnp.where(in_image, 6, 3)
    parity = jnp.where(item2 >= size, 1, 0)
    source = (
        jnp.where(in_image, 0, 192)
        + (item2 - parity * size) * 32
        + 2 * lax.shift_right_logical(row_no, 5)
        + parity
    )
    source = jnp.where(item < 18, source, -1)
    pick = jnp.where(source == lax.broadcasted_iota(jnp.int32, (512, 288), 1), 1.0, 0.0)
    by_row = jnp.dot(pick, planes_ref[...], precision=HIGH, preferred_element_type=F32)
    row_no = lax.broadcasted_iota(jnp.int32, (64, 64), 0)
    column = 2 * jnp.bitwise_and(row_no, 31) + lax.shift_right_logical(row_no, 5)
    pick = jnp.where(column == lax.broadcasted_iota(jnp.int32, (64, 64), 1), 1.0, 0.0)
    by_cell = lax.dot_general(
        pick, by_row, (((1,), (1,)), ((), ())), precision=HIGH, preferred_element_type=F32
    )
    lane = lax.broadcasted_iota(jnp.int32, (32, 128), 1)
    none = jnp.zeros((32, 128), F32)
    for i in range(16):
        pair = by_cell[:, i // 4 * 128 : i // 4 * 128 + 128]
        if i % 4:
            pair = pltpu.roll(pair, 128 - 32 * (i % 4), 1)
        even, odd = pair[0:32], pair[32:64]
        v = jnp.where(lane < 12, even, jnp.where(lane < 24, pltpu.roll(odd, 12, 1), 0.0))
        img_ref[32 * i : 32 * i + 32, :] = jnp.concatenate([v, none], axis=1)
        v = jnp.where(
            lane < 6, pltpu.roll(even, 116, 1), jnp.where(lane < 12, pltpu.roll(odd, 122, 1), 0.0)
        )
        tgt_ref[32 * i : 32 * i + 32, :] = jnp.concatenate([v, none], axis=1)


    send(0, edge_cell(img_ref))
    arrive(0)
    put_patch(0, img_ref, recv_ref[0, 0:32, :], 24)
    for cp in range(2):
        full_ref[0, cp] = dot(patch_ref[0], wi_ref[cp])

    def fwd_norm_full(k, source, e):
        stats = stats_of(source, 2)
        send(e, edge_full(source), stats)
        return stats

    def fwd_apply_full(k, source, stats, e):
        arrive(e)
        norm_ready(k, stats, e, 2)

        def body(i, carry):
            put_wide(
                i,
                activated(source[0, at(i), :], k),
                activated(source[1, at(i), :], k),
            )
            return carry

        loop(body)
        put_wide_edge(activated(recv_ref[e, 0:32, :], k))

    for index in range(2):
        h = full_ref.at[2 * index]
        mid = full_ref.at[2 * index + 1]
        out = full_ref.at[2 * index + 2]
        k = 2 * index
        stats = fwd_norm_full(k, h, 1 + k)
        if index:
            gather_last(BIG)
            load_wc(2)
        else:
            gather_last(LOW)
            gather_core(LOW)
            gather_line(BIG, (3, -3))
            gather_place(LOW)
            load_wc(0)
        fwd_apply_full(k, h, stats, 1 + k)
        keep_wide(k)

        def put_mid(cp, value, mid=mid):
            mid[cp] = value

        conv_low(put_mid)
        stats = fwd_norm_full(k + 1, mid, 2 + k)
        load_wc(2 * index + 1)
        if not index:
            film_ready()
            gather_xy(BIG)
        fwd_apply_full(k + 1, mid, stats, 2 + k)
        keep_wide(k + 1)

        def put_out(cp, value, h=h, out=out):
            out[cp] = h[cp] + value

        conv_low(put_out)

    skip = full_ref.at[4]
    send(5, edge_full(skip))
    gather_core(BIG)
    gather_place(REST)
    load_down()

    def skip_body(i, carry):
        put_wide(i, skip[0, at(i), :], skip[1, at(i), :])
        return carry

    loop(skip_body)
    arrive(5)
    put_wide_edge(recv_ref[5, 0:32, :])
    keep_wide(4)
    half_ref[0, 0] = dot(wide_ref[32:544, 0:1536], wd_ref[...])

    def fwd_half(k, source, e):
        stats = stats_of(source, 1)
        send(e, edge_cell(source.at[0]), stats)
        arrive(e)
        norm_ready(k, stats, e, 1)

        def body(i, carry):
            put_thin(i, activated(source[0, at(i), :], k))
            return carry

        loop(body)
        put_thin_edge(activated(recv_ref[e, 0:32, :], k))

    fwd_half(4, half_ref.at[0], 6)
    keep_thin(0)
    gather_place(HIGH_PART)
    half_ref[1, 0] = conv_high(0)
    fwd_half(5, half_ref.at[1], 7)
    keep_thin(1)
    half_ref[2, 0] = half_ref[0, 0] + conv_high(1)
    deep = half_ref.at[2]
    send(8, edge_cell(deep.at[0]))
    load_up()

    def deep_body(i, carry):
        put_thin(i, deep[0, at(i), :])
        return carry

    loop(deep_body)
    arrive(8)
    put_thin_edge(recv_ref[8, 0:32, :])
    keep_thin(2)
    merged = full_ref.at[5]
    for cp in range(2):
        total = skip[cp]
        for di in range(3):
            total = total + dot(
                thin_ref[32 * di : 32 * di + 512, cp * 256 : cp * 256 + 512], wu_ref[cp, di]
            )
        merged[cp] = total

    stats = fwd_norm_full(6, merged, 9)
    fwd_apply_full(6, merged, stats, 9)
    keep_wide(5)
    work_ref[0] = jnp.concatenate(
        [dot_nt(wide_ref[32:544, :], wh_ref[...]), jnp.zeros((512, 128), F32)], axis=1
    )

    live = spread(jnp.broadcast_to(jnp.concatenate([live_l, live_r], axis=0), (2, 256)))
    weight = 2.0 / count

    def loss_body(i, carry):
        diff = work_ref[0, at(i), :] - tgt_ref[at(i), :]
        half = live * diff
        work_ref[0, at(i), :] = (half * weight).astype(BF).astype(F32)
        return carry + half * diff

    lost = loop(loss_body, jnp.zeros((32, 256), F32))
    lost = jnp.sum(lost, axis=0, keepdims=True)
    part_ref[...] = jnp.zeros(part_ref.shape, F32)
    part_ref[99:100, :] = lost[:, 0:128] + lost[:, 128:256]
    fgrad_ref[...] = jnp.zeros(fgrad_ref.shape, F32)


    send(10, edge_cell(work_ref.at[0]))
    arrive(10)
    put_patch(1, work_ref.at[0], recv_ref[10, 0:32, :], 12)
    for cp in range(2):
        work_ref[cp] = dot(patch_ref[1], wht_ref[cp])
    stats = norm_back_start(6, merged, 2)
    send(11, edge_full(work_ref), stats)
    turn_ref[0:256, :] = patch_ref[1].T
    for cp in range(2):
        dwh_ref[cp] = dot(turn_ref[0:256, :], act_ref[5, cp])
    arrive(11)
    norm_back_ready(6, stats, 11, 2)

    def head_body(i, carry):
        pair = []
        for p in range(2):
            g = back_value(6, work_ref[p, at(i), :], merged[p, at(i), :])
            grad_ref[p, at(i), :] = g
            pair.append(g)
        put_wide(i, pair[0], pair[1])
        return carry

    loop(head_body)
    put_wide_edge(back_value(6, recv_ref[11, 0:32, :], recv_ref[9, 0:32, :]))

    hgrad = half_ref.at[3]
    hgrad[0] = dot_nt(wide_ref[32:544, :], wut_ref[...])
    send(12, edge_cell(hgrad.at[0]))
    turn_ref[0:256, :] = acth_ref[2].T
    for b in range(3):
        cols = {0: (3, 2), 1: (1, 2), 2: (1, 0)}[b]
        block = dot(turn_ref[0:256, :], wide_ref[32:544, cols[0] * 512 : cols[0] * 512 + 512]) + dot(
            turn_ref[0:256, :], wide_ref[32:544, cols[1] * 512 : cols[1] * 512 + 512]
        )
        for a in range(3):
            one, two = {0: (3, 1), 1: (0, 1), 2: (0, 2)}[a]
            dup_ref[3 * a + b] = (
                block[:, one * 128 : one * 128 + 128] + block[:, two * 128 : two * 128 + 128]
            ).astype(dup_ref.dtype)

    def deep_grad(i, carry):
        put_thin(i, hgrad[0, at(i), :])
        return carry

    loop(deep_grad)
    arrive(12)
    put_thin_edge(recv_ref[12, 0:32, :])
    work_ref[0] = conv_high_back(1)
    stats = norm_back_start(5, half_ref.at[1], 1)
    send(13, edge_cell(work_ref.at[0]), stats)
    grad_high(1, 1)
    arrive(13)
    norm_back_ready(5, stats, 13, 1)

    def mid_grad(i, carry):
        put_thin(i, back_value(5, work_ref[0, at(i), :], half_ref[1, 0, at(i), :]))
        return carry

    loop(mid_grad)
    put_thin_edge(back_value(5, recv_ref[13, 0:32, :], recv_ref[7, 0:32, :]))
    work_ref[0] = conv_high_back(0)
    stats = norm_back_start(4, half_ref.at[0], 1)
    send(14, edge_cell(work_ref.at[0]), stats)
    grad_high(0, 0)
    arrive(14)
    norm_back_ready(4, stats, 14, 1)

    def first_grad(i, carry):
        put_thin(
            i, hgrad[0, at(i), :] + back_value(4, work_ref[0, at(i), :], half_ref[0, 0, at(i), :])
        )
        return carry

    loop(first_grad)
    put_thin_edge(
        recv_ref[12, 0:32, :] + back_value(4, recv_ref[14, 0:32, :], recv_ref[6, 0:32, :])
    )

    for part in (LOW, BIG):
        gather_sent(part)
    deal_core(HIGH_PART)

    for cp in range(2):
        for rp in range(2):
            total = None
            for di in range(1 + rp):
                for dj in range(1 + cp):
                    a = 0 if di else 1 + rp
                    b = 0 if dj else 1 + cp
                    term = dot_nt(
                        thin_ref[32 * (1 + di) : 32 * (1 + di) + 512, (1 + dj) * 256 : (2 + dj) * 256],
                        down_ref[3 * a + b],
                    )
                    total = term if total is None else total + term
            grad_ref[cp, :, rp * 128 : rp * 128 + 128] = (
                grad_ref[cp, :, rp * 128 : rp * 128 + 128] + total
            )
    send(15, edge_full(grad_ref))
    turn_wide(4)
    for cp in range(2):
        for rp in range(2):
            for di in range(1 + rp):
                for dj in range(1 + cp):
                    a = 0 if di else 1 + rp
                    b = 0 if dj else 1 + cp
                    at_row = cp * 256 + rp * 128
                    ddown_ref[3 * a + b] = dot(
                        turn_ref[at_row : at_row + 128, :],
                        thin_ref[32 * (1 + di) : 32 * (1 + di) + 512, (1 + dj) * 256 : (2 + dj) * 256],
                    ).astype(ddown_ref.dtype)

    deal_first(HIGH_PART)
    deal_core(REST)

    def put_work(cp, value):
        work_ref[cp] = value

    edge_grad = None
    for index in (1, 0):
        h = full_ref.at[2 * index]
        mid = full_ref.at[2 * index + 1]
        k = 2 * index
        e = 16 if index else 18
        load_wr(k + 1)
        if index:

            def out_grad(i, carry):
                put_wide(i, grad_ref[0, at(i), :], grad_ref[1, at(i), :])
                return carry

            loop(out_grad)
            arrive(15)
            edge_grad = recv_ref[15, 0:32, :]
            put_wide_edge(edge_grad)
        conv_low(put_work, True)
        stats = norm_back_start(k + 1, mid, 2)
        send(e, edge_full(work_ref), stats)
        grad_low(k + 1, k + 1)
        if index:
            deal_first(REST)
        else:
            deal_z(HIGH_PART)
            deal_second(REST)
        load_wr(k)
        arrive(e)
        norm_back_ready(k + 1, stats, e, 2)

        def mid_body(i, carry, mid=mid, k=k):
            put_wide(
                i,
                back_value(k + 1, work_ref[0, at(i), :], mid[0, at(i), :]),
                back_value(k + 1, work_ref[1, at(i), :], mid[1, at(i), :]),
            )
            return carry

        loop(mid_body)
        put_wide_edge(back_value(k + 1, recv_ref[e, 0:32, :], recv_ref[k + 2, 0:32, :]))
        conv_low(put_work, True)
        stats = norm_back_start(k, h, 2)
        send(e + 1, edge_full(work_ref), stats)
        grad_low(k, k)
        if index:
            deal_second(HIGH_PART)
        else:
            deal_core(LOW)
        arrive(e + 1)
        norm_back_ready(k, stats, e + 1, 2)

        def in_body(i, carry, h=h, k=k):
            pair = []
            for p in range(2):
                g = grad_ref[p, at(i), :] + back_value(k, work_ref[p, at(i), :], h[p, at(i), :])
                grad_ref[p, at(i), :] = g
                pair.append(g)
            put_wide(i, pair[0], pair[1])
            return carry

        loop(in_body)
        edge_grad = edge_grad + back_value(k, recv_ref[e + 1, 0:32, :], recv_ref[k + 1, 0:32, :])
        put_wide_edge(edge_grad)

    deal_first(LOW)
    turn_ref[0:256, :] = patch_ref[0].T
    for cp in range(2):
        dwi_ref[cp] = dot(turn_ref[0:256, :], wide_ref[32:544, 512 + cp * 512 : 768 + cp * 512])

    for a in range(3):
        for b in range(3):
            first, last = None, None
            for cp in range(2):
                for rp in range(2):
                    rho, gamma = rp + a - 1, cp + b - 1
                    cell = (rho // 2 + 1) * 3 + gamma // 2 + 1
                    phase = (gamma % 2) * 2 + rho % 2
                    row = cell * 24 + phase * 6
                    term = dwi_ref[cp, row : row + 6, rp * 128 : rp * 128 + 128]
                    first = term if first is None else first + term
                    row = cell * 12 + phase * 3
                    term = dwh_ref[cp, row : row + 3, rp * 128 : rp * 128 + 128]
                    last = term if last is None else last + term
            t = 3 * a + b
            part_ref[9 * t : 9 * t + 6, :] = first
            part_ref[9 * (8 - t) + 6 : 9 * (8 - t) + 9, :] = last
    for which in range(2):
        for j in range(9):
            row = 81 + 9 * which + j
            part_ref[row : row + 1, :] = ngrad_ref[which : which + 1, 128 * j : 128 * j + 128]


    def message(n, src, dst, d, source):
        return pltpu.make_async_remote_copy(
            src_ref=src,
            dst_ref=dst.at[source],
            send_sem=m_send.at[n, d],
            recv_sem=m_recv.at[n, source],
            device_id=device_no(d),
            device_id_type=MESH,
        )

    def fill(d, carry):
        c = lax.rem(d, 4)
        for n in range(4):
            at_lane = pl.ds(pl.multiple_of(c * 256 + n % 2 * 128, 128), 128)
            m1_ref[d, n : n + 1, :] = fgrad_ref[n // 2 : n // 2 + 1, at_lane]
        m1_ref[d, 4:8, :] = part4_ref[d]

        @pl.when(d != me)
        def _():
            message(0, m1_ref.at[d], r1_ref, d, me).start()

        return carry

    for d in range(32):
        part4_ref[d] = part_ref[4 * d : 4 * d + 4, :]
    lax.fori_loop(0, 32, fill, 0)
    r1_ref[me] = m1_ref[me]

    deal_z(REST)
    deal_second(LOW)
    imgrad_ref[...] = dot_nt(wit_ref[0:32, :], wide_ref[32:544, :])[0:24] * count

    s_r, s_c = strip_of(me)
    home_left = s_r * 4 + s_c
    home_right = s_r * 4 + lax.rem(s_c + 1, 4)

    def back_copy(side, device):
        return pltpu.make_async_remote_copy(
            src_ref=imgrad_ref,
            dst_ref=back_ref.at[1 - side],
            send_sem=back_send.at[side],
            recv_sem=back_recv.at[side],
            device_id=device_no(device),
            device_id_type=MESH,
        )

    back_copy(0, home_left).start()

    @pl.when(home_right != me)
    def _():
        back_copy(1, home_right).start()

    others(lambda d: message(0, m1_ref.at[d], r1_ref, d, d).wait_recv())
    fsum_ref[...] = jnp.zeros(fsum_ref.shape, F32)

    def collect(d, total):
        s_l, s_rt = slots_of(d)
        for n, slot in enumerate((s_l, s_rt)):
            line = jnp.concatenate(
                [r1_ref[d, 2 * n : 2 * n + 1, :], r1_ref[d, 2 * n + 1 : 2 * n + 2, :]], axis=1
            )
            fsum_ref[pl.ds(slot, 1), :] = fsum_ref[pl.ds(slot, 1), :] + line
        return total + r1_ref[d]

    m2_ref[0:4, :] = lax.fori_loop(0, 32, collect, jnp.zeros((8, 128), F32))[4:8]
    film_mine = fsum_ref[...]
    film_w = weights[6][...].astype(BF).astype(F32)
    gc_part = lax.dot_general(
        film_mine, film_w, (((1,), (1,)), ((), ())), precision=HIGH, preferred_element_type=F32
    )
    wide = jnp.concatenate([gc_part, jnp.zeros((32, 64), F32)], axis=1)
    for c in range(4):
        gcs_ref[c] = pltpu.roll(wide, 128 - 16 * c, 1) if c else wide

    def gc_copy(c, source):
        return pltpu.make_async_remote_copy(
            src_ref=gcs_ref.at[c],
            dst_ref=gcr_ref.at[source],
            send_sem=gc_send.at[c],
            recv_sem=gc_recv.at[source],
            device_id={"rows": rr, "cols": c},
            device_id_type=MESH,
        )

    for c in range(4):

        @pl.when(cc != c)
        def _(c=c):
            gc_copy(c, cc).start()

        @pl.when(cc == c)
        def _(c=c):
            gcr_ref[c] = gcs_ref[c]

    grads = [None] * 8
    grads[6] = lax.dot_general(
        condv_ref[...], film_mine, (((0,), (0,)), ((), ())), precision=HIGH, preferred_element_type=F32
    )

    deal_z(LOW)
    deal_end(HIGH_PART)

    for c in range(4):

        @pl.when(cc != c)
        def _(c=c):
            gc_copy(c, c).wait_recv()

    pre = csend_ref[:, 0:16]
    gc = gcr_ref[0] + gcr_ref[1] + gcr_ref[2] + gcr_ref[3]
    gc = gc[:, 0:16] * silu_grad_tanh(pre)
    grads[5] = lax.dot_general(
        gc,
        joined_ref[...],
        (((0,), (0,)), ((), ())),
        precision=HIGH,
        preferred_element_type=F32,
    )

    deal_end(REST)
    deal_end(LOW)
    own = own_ref[...]
    grads[1] = jnp.stack([own[0:144, 32 * j : 32 * j + 32].reshape(9, 16, 32) for j in range(4)])
    grads[2] = jnp.stack([own[288:576, 64 * j : 64 * j + 64].reshape(9, 32, 64) for j in range(2)])
    grads[3] = own[144:288, 0:64].reshape(9, 16, 64)
    grads[4] = jnp.concatenate(
        [own[144:288, 64:96].reshape(9, 16, 32), own[144:288, 96:128].reshape(9, 16, 32)], axis=1
    )

    owned = square_sum(own)
    for n in (5, 6):
        owned = owned + square_sum(grads[n])
    m2_ref[4:8, :] = jnp.broadcast_to(owned, (4, 128))
    others(lambda d: message(1, m2_ref, r2_ref, d, me).start())
    r2_ref[me] = m2_ref[...]

    def leaving(n):
        return pltpu.make_async_copy(made[n], outs[n], store_sem.at[n])

    def leave(n):
        made[n][...] = grads[n]
        leaving(n).start()

    for n in range(1, 7):
        leave(n)
    others(lambda d: message(1, m2_ref, r2_ref, d, d).wait_recv())

    squares = jnp.zeros((4, 128), F32)
    for d in range(32):
        total_ref[4 * d : 4 * d + 4, :] = r2_ref[d, 0:4, :]
        squares = squares + r2_ref[d, 4:8, :]
    shared = square_sum(total_ref[0:LOSS_ROW, :])
    clip = jnp.sqrt(squares[0:1, 0:1] + shared)
    factor = jnp.minimum(1.0, CLIP_AT / clip)
    grads[0] = jnp.stack([total_ref[9 * t : 9 * t + 9, :] for t in range(9)])
    grads[7] = jnp.concatenate(
        [
            jnp.concatenate(
                [total_ref[NORM_ROW + 9 * n + j : NORM_ROW + 9 * n + j + 1, :] for j in range(9)],
                axis=1,
            )
            for n in range(2)
        ],
        axis=0,
    )

    for n in range(3, 26):
        if n % 3 != 2:
            loads[n].wait()
    pairs = []
    spot = 0
    for n in range(8):
        if n in (0, 7):
            leave(n)
            continue
        update = lamb_update(
            weights[n][...],
            firsts[n][...],
            seconds[n][...],
            grads[n] * factor.reshape((1,) * grads[n].ndim),
        )[1]
        for j in range(update.shape[0] if n < 3 else 1):
            pairs.append((spot, square_sum(weights[n][j] if n < 3 else weights[n][...])))
            pairs.append((64 + spot, square_sum(update[j] if n < 3 else update)))
            spot += 1

    m3_ref[...] = lane_value(pairs)[0:1]
    others(lambda d: message(2, m3_ref, r3_ref, d, me).start())
    r3_ref[me] = m3_ref[...]

    others(lambda d: message(2, m3_ref, r3_ref, d, d).wait_recv())
    sums = r3_ref[0]
    for d in range(1, 32):
        sums = sums + r3_ref[d]
    scalars_out[0:8, :] = jnp.broadcast_to(sums, (8, 128))
    lost = jnp.sum(total_ref[LOSS_ROW : LOSS_ROW + 1, :], axis=1, keepdims=True)
    for n, v in enumerate((factor, lost, count, clip)):
        scalars_out[8 + n : 9 + n, :] = jnp.broadcast_to(v, (1, 128))
    scalars_out[12:16, :] = jnp.zeros((4, 128), F32)

    back_copy(0, home_left).wait()

    @pl.when(home_right != me)
    def _():
        back_copy(1, home_right).wait()

    @pl.when(home_right == me)
    def _():
        back_ref[0] = imgrad_ref[...]

    back_out[...] = back_ref[...]

    for n in range(8):
        leaving(n).wait()

    for part in range(3):
        deal_sent(part)
    others(lambda d: film_copy(d, me).wait_send())
    row_mates(lambda c: cond_copy(c, cc).wait_send())
    row_mates(lambda c: gc_copy(c, cc).wait_send())
    for n, src in ((1, m2_ref), (2, m3_ref)):
        others(lambda d, n=n, src=src: message(n, src, r2_ref if n == 1 else r3_ref, d, me).wait_send())
    others(lambda d: message(0, m1_ref.at[d], r1_ref, d, me).wait_send())


def step(*operands):
    far = operands[4:]
    outs = [jax.ShapeDtypeStruct(far[2 + 3 * n].shape, F32) for n in range(8)]
    outs += [jax.ShapeDtypeStruct((16, 128), F32)]
    outs += [jax.ShapeDtypeStruct((2, 24, 512), F32)]
    vmem = pl.BlockSpec(memory_space=pltpu.VMEM)
    dma = pltpu.SemaphoreType.DMA

    def half(*shape):
        return pltpu.VMEM(shape, BF)

    def full(*shape):
        return pltpu.VMEM(shape, F32)

    return pl.pallas_call(
        step_kernel,
        out_shape=tuple(outs),
        in_specs=[vmem] * 4 + [pl.BlockSpec(memory_space=pltpu.HBM)] * 26,
        out_specs=[pl.BlockSpec(memory_space=pltpu.HBM)] * 8 + [vmem] * 2,
        scratch_shapes=[pltpu.VMEM(a.shape, a.dtype) for a in far]
        + [pltpu.VMEM(a.shape, F32) for a in outs[:8]]
        + [
            half(4, 9, 128, 128),
            half(2, 9, 256, 256),
            half(9, 128, 256),
            half(9, 256, 128),
            full(6, 2, 512, 256),
            full(4, 1, 512, 256),
            full(2, 512, 256),
            full(2, 512, 256),
            half(576, 2048),
            half(576, 768),
            half(6, 2, 512, 256),
            half(3, 512, 256),
            half(512, 512),
            half(1536, 256),
            half(256, 1536),
            half(2, 3, 512, 256),
            half(256, 2048),
            half(1536, 256),
            full(7, 7, 32, 256),
            full(7, 8, 256),
            half(2, 512, 256),
            full(576, 256),
            full(N_EXCHANGE, 40, 256),
            full(N_EXCHANGE, 40, 256),
            full(512, 256),
            full(512, 256),
            full(2, 256, 256),
            full(2, 256, 256),
            full(2, 1152),
            full(8, 1024),
            full(128, 128),
            full(32, 4, 128),
            full(24, 512),
            half(2, 256, 256),
            half(2, 256, 256),
            half(128, 2048),
            half(128, 2048),
            full(32, 2048),
            half(4, 2, 2, 2, ALL_ROWS, 128),
            full(2, 72, 128),
            full(2, 72, 128),
            full(288, 64),
            full(4, 32, 128),
            full(32, 128),
            full(32, 256),
            full(32, 4, 128),
            full(32, 4, 128),
            full(8, 1024),
            full(32, 4224),
            full(32, 64),
            half(4, 2, 2, ALL_ROWS, 128),
            half(4, 2, ALL_ROWS, 128),
            half(4, ALL_ROWS, 128),
            half(4, ALL_ROWS, 128),
            full(ALL_ROWS, 128),
            full(32, 8, 128),
            full(32, 8, 128),
            full(8, 128),
            full(32, 8, 128),
            full(1, 128),
            full(32, 1, 128),
            full(4, 32, 128),
            full(4, 32, 128),
            full(32, 256),
            full(128, 128),
            full(2, 24, 512),
            dma((N_EXCHANGE,)),
            dma((N_EXCHANGE,)),
            dma((26,)),
            dma((8,)),
            dma((2, 7, 4, 2, 2)),
            dma((2, 4, 2, 2, 2)),
            dma((2,)),
            dma((2,)),
            dma((4,)),
            dma((4,)),
            dma((32,)),
            dma((32,)),
            dma((3, 4)),
            dma((3, 4)),
            dma((3, 4)),
            dma((3, 4)),
            dma((3, 4)),
            dma((3, 4)),
            dma((3, 4)),
            dma((3, 4)),
            dma((3, 32)),
            dma((3, 32)),
            dma((4,)),
            dma((4,)),
            dma((2,)),
            dma((2,)),
        ],
        compiler_params=pltpu.CompilerParams(
            collective_id=1, has_side_effects=True, vmem_limit_bytes=62 * 1024 * 1024
        ),
        name="step",
    )(*operands)


def per_device_strips(
    image_pair,
    noise_target,
    timesteps,
    text_pooled,
    slot_live,
    *params,
):
    lanes = jnp.asarray(lane_tables(), BF)

    def view(n, a):
        return jnp.swapaxes(a, 1, 2) if n == 0 else a.T if n == 5 else a

    def planes(a):
        return jnp.transpose(a[0], (2, 0, 1))

    state = [view(n // 3, a) for n, a in enumerate(params)]
    *grads, scalars, back = step(
        jnp.transpose(slot_live, (1, 0, 2)),
        time_embed(timesteps)[0].astype(BF),
        planes(image_pair),
        planes(noise_target),
        lanes,
        text_pooled[0],
        *state,
    )
    results = last(scalars, back, grads, state)
    new = [view(n // 3, a) for n, a in enumerate(results[:24])]
    loss, count, clip = results[24][1, 0], results[24][2, 0], results[24][3, 0]
    return tuple(new) + (loss, count, clip, jnp.transpose(results[25], (1, 2, 0))[None])


def solution(mesh):
    strips = mesh.shape["rows"] == 8 and mesh.shape["cols"] == 4
    placed = (
        P(None, "rows", "cols", None),
        P(None, "rows", "cols", None),
        P(),
        P(),
        P(),
        P(),
        P(),
        P(),
        P(None, None, "rows", "cols"),
        P(None, None, "rows", "cols"),
        P(None, None, "rows", "cols"),
        P(None, None, "rows", "cols"),
        P(None, None, "rows", "cols"),
        P(None, None, "rows", "cols"),
        P(None, "rows", "cols"),
        P(None, "rows", "cols"),
        P(None, "rows", "cols"),
        P(None, "rows", "cols"),
        P(None, "rows", "cols"),
        P(None, "rows", "cols"),
        P(None, ("rows", "cols")),
        P(None, ("rows", "cols")),
        P(None, ("rows", "cols")),
        P("rows", "cols"),
        P("rows", "cols"),
        P("rows", "cols"),
        P(),
        P(),
        P(),
    )
    return jax.shard_map(
        per_device_strips if strips else per_device,
        mesh=mesh,
        in_specs=placed,
        out_specs=(
            P(),
            P(),
            P(),
            P(None, None, "rows", "cols"),
            P(None, None, "rows", "cols"),
            P(None, None, "rows", "cols"),
            P(None, None, "rows", "cols"),
            P(None, None, "rows", "cols"),
            P(None, None, "rows", "cols"),
            P(None, "rows", "cols"),
            P(None, "rows", "cols"),
            P(None, "rows", "cols"),
            P(None, "rows", "cols"),
            P(None, "rows", "cols"),
            P(None, "rows", "cols"),
            P(None, ("rows", "cols")),
            P(None, ("rows", "cols")),
            P(None, ("rows", "cols")),
            P("rows", "cols"),
            P("rows", "cols"),
            P("rows", "cols"),
            P(),
            P(),
            P(),
            P(),
            P(),
            P(),
            P(None, "rows", "cols", None),
        ),
        check_vma=False,
    )
```
